32 devices in a mesh: groups: 2 (over y), seq: 4 (over z), dp: 4 (over x, core).
Axes of the slice: x: 2, y: 2, z: 4, core: 2. Of those that a mesh axis runs over, the one named last changes fastest.
Arguments:
- x_raw: bfloat16 [1024, 8192], P(('groups', 'seq'), 'dp'), parts along dimension 0, may hold values from -6 to 6
- bc_raw: bfloat16 [1024, 2048], P(('groups', 'seq'), 'dp'), parts along dimension 0, may hold values from -6 to 6
- z_gate: bfloat16 [1024, 8192], P(('groups', 'seq'), 'dp'), parts along dimension 0, may hold values from -6 to 6
- dt_raw: float32 [1024, 128], P(('groups', 'seq'), 'dp'), parts along dimension 0, may hold values from -3 to 6
- conv_x_weight: float32 [4, 8192], P(None, 'dp'), may hold values from -3 to 3
- conv_x_bias: float32 [8192], P('dp'), may hold values from -3 to 3
- conv_bc_weight: float32 [4, 2048], P(None, 'dp'), may hold values from -3 to 3
- conv_bc_bias: float32 [2048], P('dp'), may hold values from -3 to 3
- dt_bias: float32 [128], P('dp'), may hold values from -1 to 1
- a_log: float32 [128], P('dp')
- skip_d: float32 [128], P('dp'), may hold values from 0.5 to 1.5
- norm_gain: float32 [8192], P('dp'), may hold values from 0.5 to 1.5
- queries: bfloat16 [1024, 4096], P(('groups', 'seq'), 'dp'), parts along dimension 0, may hold values from -6 to 6
- keys: bfloat16 [1024, 1024], P(('groups', 'seq'), 'dp'), parts along dimension 0, may hold values from -6 to 6
- values: bfloat16 [1024, 1024], P(('groups', 'seq'), 'dp'), parts along dimension 0, may hold values from -6 to 6
- doc_lens: int32 [8], P('groups'), parts along dimension 0, may hold values from 1 to 256, 512 in all
Outputs:
- mamba_out: bfloat16 [1024, 8192], P(('groups', 'seq'), 'dp'), parts along dimension 0
- attn_out: bfloat16 [1024, 4096], P(('groups', 'seq'), 'dp'), parts along dimension 0
The draws below stay inside these ranges and needn't reach their ends.
There are 2 independent parts, one for each index of `groups`. The reference program is written for one: setup_inputs(seed, part) draws one part's arguments, and reference() takes and returns one part's arrays. A program takes and returns all parts, laid end to end along the dimension named above; an argument that names none is the same for every part. Nothing has to cross between parts.
Inputs may be any that keep to these rules, and one draw needn't show every extreme that they name: doc_lens holds 4 document lengths that sum to 512; the longest is exactly 256.
All inputs are finite; a program needn't handle non-finite values.
Results may differ from the reference program's by a relative error of at most 0.018.
Values may be sent and summed in bfloat16 or wider, within the bound.
No kernel may reach another device: no remote copies, remote signals or barrier semaphores. Data moves between devices by JAX's collectives and lax.ppermute only.
A program may use at most 128 MiB of HBM per device.

```python
import math
import jax
import jax.numpy as jnp
import numpy as np
from jax import lax

HEADS = 128
HDIM = 64
STATE = 128
GROUPS = 8
CONV = 4
QHEADS = 32
KVHEADS = 8
ADIM = 128
TOK_DEV = 128
DOCS = 4
STREAM_LENGTH = 512


def draw_queries(key, part):
    noise_key = jax.random.fold_in(key, 1)
    field = jnp.clip(jax.random.normal(noise_key, (STREAM_LENGTH, QHEADS * ADIM), jnp.float32), -6.0, 6.0)
    return field.astype(jnp.bfloat16)


def draw_keys(key, part):
    noise_key = jax.random.fold_in(key, 2)
    field = jnp.clip(jax.random.normal(noise_key, (STREAM_LENGTH, KVHEADS * ADIM), jnp.float32), -6.0, 6.0)
    return field.astype(jnp.bfloat16)


def draw_dt_raw(key, part):
    noise_key = jax.random.fold_in(key, 3)
    cluster_prng_seed = jax.random.fold_in(key, 4)
    field = jnp.clip(0.5 * jax.random.normal(noise_key, (STREAM_LENGTH, HEADS), jnp.float32), -3.0, 3.0)
    flagged_spots = jax.random.randint(cluster_prng_seed, (8,), 0, STREAM_LENGTH)
    field = field.at[flagged_spots].add(3.0)
    return jnp.clip(field, -3.0, 6.0)


def draw_a_log(key, part):
    marker_random_key = jax.random.fold_in(key, 5)
    level_key = jax.random.fold_in(key, 6)
    slow = jax.random.bernoulli(marker_random_key, 0.5, (HEADS,))
    level = jax.random.uniform(level_key, (HEADS,), jnp.float32, 0.0, 1.0)
    slow_rate = jnp.exp(jnp.log(0.2 / STREAM_LENGTH) + level * jnp.log(10.0))
    fast_rate = jnp.exp(jnp.log(1.0 / 400.0) + level * jnp.log(400.0 / 30.0))
    return jnp.log(jnp.where(slow, slow_rate, fast_rate) / 0.7)


def shard_levels(stream_key, extent, pieces, least, top_value):
    loudness = 1.0
    for axis_at, blocks in pieces:
        draws = jax.random.uniform(jax.random.fold_in(jax.random.fold_in(stream_key, 6), axis_at), (blocks,), jnp.float32, least / len(pieces), top_value / len(pieces))
        loudness = loudness * jnp.repeat(jnp.exp(draws), extent[axis_at] // blocks).reshape((-1,) + (1,) * (len(extent) - 1 - axis_at))
    return loudness


def profile(number_of, total, reach, lean):
    loads = [(1 << 20) // math.isqrt(grade ** lean) + 1 for grade in range(2, number_of + 1)]
    spare, counts = total - reach - (number_of - 1), [1] * (number_of - 1)
    while spare > 0:
        free = [i for i in range(number_of - 1) if counts[i] < reach]
        whole, budget = sum([loads[i] for i in free]), spare
        for i in free:
            addition = min(reach - counts[i], max(1, budget * loads[i] // whole), spare)
            counts[i] = counts[i] + addition
            spare = spare - addition
    return np.array([reach] + counts)


def uneven_parts(stream_key, number_of, total, bound, skew):
    if number_of == 2:
        one = jax.random.randint(stream_key, (), max(1, total - bound), min(bound, total - 1) + 1)
        return jnp.stack([one, total - one])
    tallies = jnp.asarray(profile(number_of, total, bound, skew), jnp.int32)
    pairs = (number_of - 1) // 2
    donor, taker = tallies[1:1 + 2 * pairs:2], tallies[2:2 + 2 * pairs:2]
    margin = jnp.minimum(donor - 1, bound - taker)
    shifted = jax.random.randint(jax.random.fold_in(stream_key, 1), (pairs,), 0, 1 << 20) % (margin + 1)
    tallies = tallies.at[1:1 + 2 * pairs:2].set(donor - shifted).at[2:2 + 2 * pairs:2].set(taker + shifted)
    return tallies[jax.random.permutation(jax.random.fold_in(stream_key, 2), number_of)]


def bell_draw(own_key, dims, scale, limit, cuts=(), kind=jnp.bfloat16):
    array = scale * jax.random.normal(own_key, dims, jnp.float32)
    if cuts:
        array = array * shard_levels(own_key, dims, cuts, -0.22, 0.18)
    return jnp.clip(array, -limit, limit).astype(kind)


def setup_inputs(seed: int = 0, part: int = 0) -> dict:
    key_of = jax.random.split(jax.random.key(seed), 17)
    part_splits = jax.random.split(jax.random.fold_in(key_of[16], part), 17)
    return {
        "x_raw": bell_draw(part_splits[0], (STREAM_LENGTH, HEADS * HDIM), 1.0, 6.0, ((0, 4), (1, 4))),
        "bc_raw": bell_draw(part_splits[1], (STREAM_LENGTH, 2 * GROUPS * STATE), 1.0, 6.0, ((0, 4), (1, 4))),
        "z_gate": bell_draw(part_splits[2], (STREAM_LENGTH, HEADS * HDIM), 1.0, 6.0, ((0, 4), (1, 4))),
        "dt_raw": draw_dt_raw(jax.random.fold_in(jax.random.fold_in(key_of[16], part), 71), part),
        "conv_x_weight": bell_draw(key_of[4], (CONV, HEADS * HDIM), CONV ** -0.5, 3.0, ((1, 4),), jnp.float32),
        "conv_x_bias": bell_draw(key_of[5], (HEADS * HDIM,), 0.5, 3.0, ((0, 4),), jnp.float32),
        "conv_bc_weight": bell_draw(key_of[6], (CONV, 2 * GROUPS * STATE), CONV ** -0.5, 3.0, ((1, 4),), jnp.float32),
        "conv_bc_bias": bell_draw(key_of[7], (2 * GROUPS * STATE,), 0.5, 3.0, ((0, 4),), jnp.float32),
        "dt_bias": jnp.clip(jax.random.uniform(key_of[8], (HEADS,), jnp.float32, -1.0, 1.0) * shard_levels(key_of[8], (HEADS,), ((0, 4),), -0.4, 0.0), -1.0, 1.0),
        "a_log": draw_a_log(jax.random.fold_in(key_of[16], 71), part),
        "skip_d": jnp.clip(0.5 + 1.0 * jax.random.uniform(key_of[10], (HEADS,), jnp.float32) ** shard_levels(key_of[10], (HEADS,), ((0, 4),), -0.2, 0.2), 0.5, 1.5),
        "norm_gain": jnp.clip(1.0 + 0.1 * jax.random.normal(key_of[11], (HEADS * HDIM,), jnp.float32), 0.5, 1.5),
        "queries": draw_queries(jax.random.fold_in(jax.random.fold_in(key_of[16], part), 71), part),
        "keys": draw_keys(jax.random.fold_in(jax.random.fold_in(key_of[16], part), 71), part),
        "values": bell_draw(part_splits[14], (STREAM_LENGTH, KVHEADS * ADIM), 1.0, 6.0, ((0, 4), (1, 4))),
        "doc_lens": uneven_parts(part_splits[15], DOCS, STREAM_LENGTH, STREAM_LENGTH // 2, 2).astype(jnp.int32),
    }


EPSILON = 1e-05
NEGATIVE = -1e+30
HIGHEST = lax.Precision.HIGHEST

def doc_starts(doc_lens):
    ends = jnp.cumsum(doc_lens).astype(jnp.int32)
    return (ends - doc_lens).astype(jnp.int32)

def doc_index(positions, starts):
    inside = (starts[None, :] <= positions[:, None]).astype(jnp.int32)
    return (lax.optimization_barrier(jnp.sum(inside, axis=1)) - 1).astype(jnp.int32)

def causal_conv(padded, pad_docs, docs, weight, bias):
    count = docs.shape[0]
    total = jnp.zeros((count, bias.shape[0]), jnp.float32) + bias[None, :]
    for lag in range(weight.shape[0]):
        term = padded[lag:lag + count].astype(jnp.float32) * weight[lag][None, :]
        same = pad_docs[lag:lag + count] == docs
        total = total + jnp.where(same[:, None], term, 0.0)
    return jax.nn.silu(total).astype(jnp.bfloat16)

def ssd_terms(head_values, b_groups, c_groups, step_size, log_decay, begins):
    rows, heads, width = head_values.shape
    group_total_count = b_groups.shape[1]
    per_group = heads // group_total_count
    running = jnp.cumsum(log_decay, axis=0)
    segment = jnp.cumsum(begins.astype(jnp.int32), axis=0).astype(jnp.int32)
    order = jnp.arange(rows, dtype=jnp.int32)
    linked = (segment[:, None] == segment[None, :]) & (order[:, None] >= order[None, :])
    spread = running.T[:, :, None] - running.T[:, None, :]
    multiplier = jnp.where(linked[None], jnp.exp(jnp.where(linked[None], spread, 0.0)), 0.0)
    intersection = jnp.einsum('ign,jgn->gij', c_groups, b_groups, preferred_element_type=jnp.float32)
    intersection = jnp.repeat(intersection, per_group, axis=0)
    scaled = head_values.astype(jnp.float32) * step_size[:, :, None]
    output = jnp.einsum('hij,jhp->ihp', multiplier * intersection, scaled, precision=HIGHEST)
    entry = jnp.where((segment == 0)[:, None], jnp.exp(running), 0.0)
    tail_weight = jnp.where((segment == segment[-1])[:, None], jnp.exp(running[-1][None, :] - running), 0.0)
    weighted = (scaled * tail_weight[:, :, None]).reshape(rows, group_total_count, per_group, width)
    local_state = jnp.einsum('jgqp,jgn->gqpn', weighted, b_groups.astype(jnp.float32), precision=HIGHEST)
    local_state = local_state.reshape(heads, width, -1)
    through = jnp.where(segment[-1] == 0, jnp.exp(running[-1]), 0.0)
    return (output, entry, local_state, through)

def apply_state(c_groups, state):
    heads, width, size = state.shape
    group_total_count = c_groups.shape[1]
    grouped = state.reshape(group_total_count, heads // group_total_count, width, size)
    result = jnp.einsum('ign,gqpn->igqp', c_groups.astype(jnp.float32), grouped, precision=HIGHEST)
    return result.reshape(c_groups.shape[0], heads, width)

def gated_norm(mixed, z_gate, norm_gain, group_total_count):
    count = mixed.shape[0]
    gated = mixed * jax.nn.silu(z_gate.astype(jnp.float32)).reshape(mixed.shape)
    grouped = gated.reshape(count, group_total_count, -1)
    multiplier = lax.rsqrt(lax.optimization_barrier(jnp.mean(grouped * grouped, axis=-1, keepdims=True)) + EPSILON)
    return ((grouped * multiplier).reshape(count, -1) * norm_gain[None, :]).astype(jnp.bfloat16)

def reference(x_raw, bc_raw, z_gate, dt_raw, conv_x_weight, conv_x_bias, conv_bc_weight, conv_bc_bias, dt_bias, a_log, skip_d, norm_gain, queries, keys, values, doc_lens):
    starts = doc_starts(doc_lens)
    positions = jnp.arange(STREAM_LENGTH, dtype=jnp.int32)
    docs = doc_index(positions, starts)
    pad_positions = jnp.arange(STREAM_LENGTH + CONV - 1, dtype=jnp.int32) - (CONV - 1)
    pad_docs = doc_index(pad_positions, starts)
    begins = jnp.any(starts[None, :] == positions[:, None], axis=1)
    x_pad = jnp.concatenate([jnp.zeros((CONV - 1, x_raw.shape[1]), x_raw.dtype), x_raw], axis=0)
    bc_pad = jnp.concatenate([jnp.zeros((CONV - 1, bc_raw.shape[1]), bc_raw.dtype), bc_raw], axis=0)
    x_conv = causal_conv(x_pad, pad_docs, docs, conv_x_weight, conv_x_bias)
    bc_conv = causal_conv(bc_pad, pad_docs, docs, conv_bc_weight, conv_bc_bias)
    step_size = jax.nn.softplus(dt_raw + dt_bias[None, :])
    log_decay = -step_size * jnp.exp(a_log)[None, :]
    blocks = STREAM_LENGTH // TOK_DEV
    value_blocks = x_conv.reshape(blocks, TOK_DEV, HEADS, HDIM)
    paired = bc_conv.reshape(blocks, TOK_DEV, GROUPS, 2, STATE)

    def advance(state, block):
        head_values, pair_block, steps, logs, starts_here = block
        b_groups = pair_block[:, :, 0]
        c_groups = pair_block[:, :, 1]
        output, entry, local_state, through = ssd_terms(head_values, b_groups, c_groups, steps, logs, starts_here)
        output = output + apply_state(c_groups, state) * entry[:, :, None]
        return (state * through[:, None, None] + local_state, output)
    initial = jnp.zeros((HEADS, HDIM, STATE), jnp.float32)
    _, outputs = lax.scan(advance, initial, (value_blocks, paired, step_size.reshape(blocks, TOK_DEV, HEADS), log_decay.reshape(blocks, TOK_DEV, HEADS), begins.reshape(blocks, TOK_DEV)))
    mixed = outputs.reshape(STREAM_LENGTH, HEADS, HDIM) + skip_d[None, :, None] * x_conv.reshape(STREAM_LENGTH, HEADS, HDIM).astype(jnp.float32)
    mamba_out = gated_norm(mixed, z_gate, norm_gain, GROUPS)
    share = QHEADS // KVHEADS
    scale = ADIM ** (-0.5)
    query_heads = queries.reshape(STREAM_LENGTH, KVHEADS, share, ADIM).transpose(1, 0, 2, 3)
    key_heads = keys.reshape(STREAM_LENGTH, KVHEADS, ADIM).transpose(1, 0, 2)
    value_heads = values.reshape(STREAM_LENGTH, KVHEADS, ADIM).transpose(1, 0, 2)

    def head_attend(operands):
        asking_head_index, key_head, value_head = operands

        def block_attend(block_index):
            query_block = lax.dynamic_slice_in_dim(asking_head_index, block_index * TOK_DEV, TOK_DEV, 0)
            row_positions = block_index * TOK_DEV + jnp.arange(TOK_DEV, dtype=jnp.int32)
            row_docs = lax.dynamic_slice_in_dim(docs, block_index * TOK_DEV, TOK_DEV, 0)
            scores = jnp.einsum('tga,ja->gtj', query_block.astype(jnp.float32), key_head.astype(jnp.float32), precision=HIGHEST) * scale
            permitted_mask = (positions[None, :] <= row_positions[:, None]) & (docs[None, :] == row_docs[:, None])
            scores = jnp.where(permitted_mask[None], scores, NEGATIVE)
            peak = lax.optimization_barrier(jnp.max(scores, axis=-1, keepdims=True))
            expo = jnp.where(permitted_mask[None], jnp.exp(scores - peak), 0.0)
            probs = expo.astype(jnp.bfloat16)
            total = lax.optimization_barrier(jnp.sum(expo, axis=-1))
            summed = jnp.einsum('gtj,ja->gta', probs.astype(jnp.float32), value_head.astype(jnp.float32), precision=HIGHEST)
            return (summed / total[:, :, None]).transpose(1, 0, 2)
        return lax.map(block_attend, jnp.arange(blocks, dtype=jnp.int32))
    attended = lax.map(head_attend, (query_heads, key_heads, value_heads))
    attn_out = attended.transpose(1, 2, 0, 3, 4).reshape(STREAM_LENGTH, QHEADS * ADIM).astype(jnp.bfloat16)
    return (mamba_out, attn_out)
```

```python
import functools
import math

import jax
import jax.numpy as jnp
from jax import lax
from jax.experimental import pallas as pl
from jax.experimental.pallas import tpu as pltpu
from jax.sharding import PartitionSpec as P

HDIM = 64
STATE = 128
QHEADS = 32
KVHEADS = 8
ADIM = 128
EPSILON = 1e-05
BARRED = -2e30
HIGHEST = lax.Precision.HIGHEST
F32 = jnp.float32
BF16 = jnp.bfloat16
CHUNK = 256
VMEM_LIMIT = 48 * 1024 * 1024


def silu(value):
    return value * (0.5 * jnp.tanh(0.5 * value) + 0.5)


def softplus(value):
    return jnp.maximum(value, 0.0) + jnp.log(1.0 + jnp.exp(-jnp.abs(value)))


def doc_start(positions, lens_ref):
    begin = jnp.int32(0)
    found = jnp.zeros_like(positions)
    for doc in range(lens_ref.shape[0]):
        found = jnp.where(positions >= begin, begin, found)
        begin = begin + lens_ref[doc]
    return found


def doc_start_of(position, lens_ref):
    begin = jnp.int32(0)
    found = jnp.int32(0)
    for doc in range(lens_ref.shape[0]):
        found = jnp.where(position >= begin, begin, found)
        begin = begin + lens_ref[doc]
    return found


def widen(per_head, first, width):
    heads = per_head.shape[1]
    high = per_head.astype(BF16)
    low = (per_head - high.astype(F32)).astype(BF16)
    both = jnp.concatenate([high, low], axis=1)
    head = lax.broadcasted_iota(jnp.int32, (2 * heads, width), 0)
    head = jnp.where(head >= heads, head - heads, head)
    channel = lax.broadcasted_iota(jnp.int32, (2 * heads, width), 1) + first
    spread = (channel // HDIM == head).astype(F32).astype(BF16)
    return jnp.dot(both, spread, preferred_element_type=F32)


def steps_of(dt_ref, dt_bias_ref, a_log_ref):
    step = softplus(dt_ref[...] + dt_bias_ref[...].reshape(1, -1))
    return step, -step * jnp.exp(a_log_ref[...].reshape(1, -1))


def tails_kernel(x_ref, bc_ref, dt_ref, dt_bias_ref, a_log_ref, out_ref):
    width = x_ref.shape[1]
    rows = x_ref.shape[0]
    _, rate = steps_of(dt_ref, dt_bias_ref, a_log_ref)
    total = jnp.sum(rate, axis=0, keepdims=True)
    out_ref[:, :width] = x_ref[...].astype(F32)[rows - 4 :]
    out_ref[:, width:] = bc_ref[...].astype(F32)[rows - 4 :]
    out_ref[0:1, : total.shape[1]] = total


def conv_kernel(
    x_ref, bc_ref, tail_ref, dt_ref, wx_ref, bx_ref, wbc_ref, bbc_ref, dt_bias_ref, a_log_ref, lens_ref,
    xc_ref, bcc_ref, state_ref, step_ref, running_ref, pad_ref,
):
    rows, width = x_ref.shape
    bc_width = bc_ref.shape[1]
    taps = wx_ref.shape[0]
    first = lax.axis_index("seq") * rows
    positions = first + lax.broadcasted_iota(jnp.int32, (rows, CHUNK), 0)
    depth = positions - doc_start(positions, lens_ref)
    inside = [depth >= lag for lag in range(taps)]
    step, rate = steps_of(dt_ref, dt_bias_ref, a_log_ref)
    row = lax.broadcasted_iota(jnp.int32, (rows, rows), 0)
    column = lax.broadcasted_iota(jnp.int32, (rows, rows), 1)
    lower = (row >= column).astype(F32)
    running = jnp.dot(lower, rate, precision=HIGHEST, preferred_element_type=F32)
    step_ref[...] = step
    running_ref[...] = running
    last_begin = doc_start_of(first + rows - 1, lens_ref)
    position = first + lax.broadcasted_iota(jnp.int32, step.shape, 0)
    weight = jnp.where(
        position >= last_begin, step * jnp.exp(running[rows - 1 : rows] - running), 0.0
    )

    def conv(raw_ref, offset, start, weight_ref, bias_ref, slot):
        columns = slice(start, start + CHUNK)
        pad = pad_ref.at[slot]
        pad[4:8] = tail_ref[:, offset + start : offset + start + CHUNK]
        raw = raw_ref[:, columns].astype(F32)
        pad[8:] = raw
        total = raw * weight_ref[taps - 1 : taps, columns] + bias_ref[columns].reshape(1, -1)
        for lag in range(1, taps):
            term = pad[8 - lag : 8 - lag + rows] * weight_ref[taps - 1 - lag : taps - lag, columns]
            total = total + jnp.where(inside[lag], term, 0.0)
        return silu(total).astype(BF16)

    slots = pad_ref.shape[0]
    groups = bc_width // (2 * STATE)
    turned = []
    for group in range(groups):
        pair = conv(bc_ref, width, group * 2 * STATE, wbc_ref, bbc_ref, group % slots)
        bcc_ref[:, group * 2 * STATE : (group + 1) * 2 * STATE] = pair
        turned.append(pair[:, :STATE].astype(F32).T.astype(BF16))
    per_group = width // groups
    for start in range(0, width, CHUNK):
        xc = conv(x_ref, 0, start, wx_ref, bx_ref, (start // CHUNK) % slots)
        xc_ref[:, start : start + CHUNK] = xc
        weighted = (xc.astype(F32) * widen(weight, start, CHUNK)).astype(BF16)
        state_ref[:, start : start + CHUNK] = jnp.dot(
            turned[start // per_group], weighted, preferred_element_type=F32
        ).astype(BF16)


def local_kernel(xc_ref, bcc_ref, step_ref, running_ref, skip_ref, lens_ref, out_ref):
    rows, width = xc_ref.shape
    groups = bcc_ref.shape[1] // (2 * STATE)
    per_group = width // groups
    first = lax.axis_index("seq") * rows
    row = lax.broadcasted_iota(jnp.int32, (rows, rows), 0)
    column = lax.broadcasted_iota(jnp.int32, (rows, rows), 1)
    begin = doc_start(first + row, lens_ref)
    linked = (row >= column) & (first + column >= begin)
    running = running_ref[...]
    turned_running = running.T
    turned_step = step_ref[...].T
    skip = skip_ref[...].reshape(1, -1)
    skip = jnp.broadcast_to(skip, (8, skip.shape[1]))
    pair_width = 2 * HDIM
    lane = lax.broadcasted_iota(jnp.int32, (rows, pair_width), 1)
    for group in range(groups):
        base = group * 2 * STATE
        inputs = bcc_ref[:, base : base + STATE]
        outputs = bcc_ref[:, base + STATE : base + 2 * STATE]
        meet = lax.dot_general(
            outputs, inputs, (((1,), (1,)), ((), ())), preferred_element_type=F32
        )
        meet = jnp.where(linked, meet, 0.0)
        for start in range(group * per_group, (group + 1) * per_group, pair_width):
            parts = []
            for head in (start // HDIM, start // HDIM + 1):
                spread = running[:, head : head + 1] - turned_running[head : head + 1]
                decay = jnp.exp(jnp.minimum(spread, 0.0))
                parts.append((decay * (meet * turned_step[head : head + 1])).astype(BF16))
            mix = jnp.concatenate(parts, axis=1)
            xc = xc_ref[:, start : start + pair_width]
            zero = jnp.zeros_like(xc)
            stacked = jnp.concatenate(
                [jnp.where(lane < HDIM, xc, zero), jnp.where(lane < HDIM, zero, xc)], axis=0
            )
            value = jnp.dot(mix, stacked, preferred_element_type=F32)
            wide_skip = widen(skip, start, pair_width)[0:1]
            out_ref[:, start : start + pair_width] = value + xc.astype(F32) * wide_skip


def attend_kernel(hops, *refs):
    q_ref = refs[0]
    kv_refs = refs[1 : 2 + hops]
    lens_ref, out_ref = refs[2 + hops :]
    rows = q_ref.shape[0]
    kv_heads = kv_refs[0].shape[1] // (2 * ADIM)
    share = QHEADS // KVHEADS
    count = rows * (hops + 1)
    here = lax.axis_index("seq")
    row = here * rows + lax.broadcasted_iota(jnp.int32, (rows, count), 0)
    column = (here - hops) * rows + lax.broadcasted_iota(jnp.int32, (rows, count), 1)
    allowed = (column <= row) & (column >= doc_start(row, lens_ref))
    scale = ADIM ** (-0.5)
    for head in range(kv_heads):
        low = head * ADIM
        keys = jnp.concatenate([ref[:, low : low + ADIM] for ref in kv_refs], axis=0)
        low = (kv_heads + head) * ADIM
        values = jnp.concatenate([ref[:, low : low + ADIM] for ref in kv_refs], axis=0)
        for part in range(share):
            low = (head * share + part) * ADIM
            scores = lax.dot_general(
                q_ref[:, low : low + ADIM], keys, (((1,), (1,)), ((), ())), preferred_element_type=F32
            )
            scores = jnp.where(allowed, scores * scale, BARRED)
            expo = jnp.exp(scores - jnp.max(scores, axis=1, keepdims=True))
            total = jnp.sum(expo, axis=1, keepdims=True)
            summed = jnp.dot(expo.astype(BF16), values, preferred_element_type=F32)
            out_ref[:, low : low + ADIM] = (summed / total).astype(BF16)


def final_kernel(hops, *refs):
    mixed_ref, bcc_ref, running_ref, z_ref, gain_ref, lens_ref = refs[:6]
    state_refs = refs[6 : 6 + hops]
    total_refs = refs[6 + hops : 6 + hops + hops - 1]
    out_ref, gated_ref = refs[-2:]
    rows, width = mixed_ref.shape
    heads = running_ref.shape[1]
    groups = bcc_ref.shape[1] // (2 * STATE)
    per_group = width // groups
    here = lax.axis_index("seq")
    first = here * rows
    first_begin = doc_start_of(first, lens_ref)
    positions = first + lax.broadcasted_iota(jnp.int32, (rows, heads), 0)
    begin = doc_start(positions, lens_ref)
    entry = jnp.where(begin < first, jnp.exp(running_ref[...]), 0.0)
    decays = []
    total = jnp.zeros((1, heads), F32)
    for hop in range(2, hops + 1):
        total = total + total_refs[hop - 2][0:1, :heads]
        factor = jnp.where(first_begin < (here - hop + 1) * rows, jnp.exp(total), 0.0)
        decays.append(jnp.broadcast_to(factor, (8, heads)))
    for group in range(groups):
        base = group * 2 * STATE
        outputs = bcc_ref[:, base + STATE : base + 2 * STATE]
        squares = jnp.zeros((rows, 1), F32)
        for start in range(group * per_group, (group + 1) * per_group, CHUNK):
            columns = slice(start, start + CHUNK)
            state = state_refs[0][:, columns].astype(F32)
            for factor, ref in zip(decays, state_refs[1:]):
                state = state + widen(factor, start, CHUNK)[0:1] * ref[:, columns].astype(F32)
            carried = jnp.dot(outputs, state.astype(BF16), preferred_element_type=F32)
            mixed = mixed_ref[:, columns] + carried * widen(entry, start, CHUNK)
            gated = mixed * silu(z_ref[:, columns].astype(F32))
            gated_ref[:, columns] = gated
            squares = squares + jnp.sum(gated * gated, axis=1, keepdims=True)
        multiplier = lax.rsqrt(squares * (1.0 / per_group) + EPSILON)
        for start in range(group * per_group, (group + 1) * per_group, CHUNK):
            columns = slice(start, start + CHUNK)
            out_ref[:, columns] = (
                gated_ref[:, columns] * multiplier * gain_ref[columns].reshape(1, -1)
            ).astype(BF16)


def call(kernel, name, outs, operands, scalars=(), specs=None, scratch=(), flops=0):
    vmem = pl.BlockSpec(memory_space=pltpu.VMEM)
    smem = pl.BlockSpec(memory_space=pltpu.SMEM)
    in_specs = [vmem] * len(operands) if specs is None else list(specs)
    for at in scalars:
        in_specs[at] = smem
    moved = sum(math.prod(a.shape) * a.dtype.itemsize for a in (*operands, *outs))
    return pl.pallas_call(
        kernel,
        name=name,
        out_shape=outs,
        in_specs=in_specs,
        out_specs=[vmem] * len(outs),
        scratch_shapes=list(scratch),
        compiler_params=pltpu.CompilerParams(vmem_limit_bytes=VMEM_LIMIT),
        cost_estimate=pl.CostEstimate(flops=flops, bytes_accessed=moved, transcendentals=0),
    )(*operands)


def shifted(value, steps):
    count = lax.axis_size("seq")
    return lax.ppermute(value, "seq", [(source, source + steps) for source in range(count - steps)])


def shards(
    x_raw,
    bc_raw,
    z_gate,
    dt_raw,
    conv_x_weight,
    conv_x_bias,
    conv_bc_weight,
    conv_bc_bias,
    dt_bias,
    a_log,
    skip_d,
    norm_gain,
    queries,
    keys,
    values,
    doc_lens,
):
    rows, width = x_raw.shape
    bc_width = bc_raw.shape[1]
    heads = dt_raw.shape[1]
    count = lax.axis_size("seq")
    longest = rows * count // 2
    hops = min(count - 1, -(-(longest - 1) // rows))
    shape = jax.ShapeDtypeStruct
    whole = pl.BlockSpec(memory_space=pltpu.VMEM)
    edge = 16

    (tails,) = pl.pallas_call(
        tails_kernel,
        name="tails",
        grid=(1,),
        out_shape=[shape((4, width + bc_width), F32)],
        in_specs=[
            pl.BlockSpec((edge, width), lambda i: (rows // edge - 1, 0)),
            pl.BlockSpec((edge, bc_width), lambda i: (rows // edge - 1, 0)),
            whole,
            whole,
            whole,
        ],
        out_specs=[whole],
    )(x_raw, bc_raw, dt_raw, dt_bias, a_log)
    tail = shifted(tails, 1)
    kv = jnp.concatenate([keys, values], axis=1)
    kv_before = [shifted(kv, hop) for hop in range(1, hops + 1)]

    xc, bcc, state, step, running = call(
        conv_kernel,
        "conv_state",
        [
            shape((rows, width), BF16),
            shape((rows, bc_width), BF16),
            shape((STATE, width), BF16),
            shape((rows, heads), F32),
            shape((rows, heads), F32),
        ],
        [
            x_raw, bc_raw, tail, dt_raw, conv_x_weight, conv_x_bias, conv_bc_weight, conv_bc_bias,
            dt_bias, a_log, doc_lens,
        ],
        scalars=(10,),
        scratch=[pltpu.VMEM((4, rows + 8, CHUNK), F32)],
        flops=2 * rows * width * STATE,
    )
    states = []
    for _ in range(hops):
        states.append(shifted(states[-1] if states else state, 1))
    totals = []
    for hop in range(2, hops + 1):
        totals.append(tail[:, :STATE] if hop == 2 else shifted(totals[-1], 1))

    (mixed,) = call(
        local_kernel,
        "local_mix",
        [shape((rows, width), F32)],
        [xc, bcc, step, running, skip_d, doc_lens],
        scalars=(5,),
        flops=4 * rows * rows * width,
    )
    (attn_out,) = call(
        functools.partial(attend_kernel, hops),
        "attend",
        [shape(queries.shape, BF16)],
        [queries, *reversed(kv_before), kv, doc_lens],
        scalars=(hops + 2,),
        flops=4 * rows * rows * (hops + 1) * queries.shape[1],
    )
    (mamba_out,) = call(
        functools.partial(final_kernel, hops),
        "carry_norm",
        [shape((rows, width), BF16)],
        [mixed, bcc, running, z_gate, norm_gain, doc_lens, *states, *totals],
        scalars=(5,),
        scratch=[pltpu.VMEM((rows, width), F32)],
        flops=2 * rows * width * STATE,
    )
    return (mamba_out, attn_out)


def solution(mesh):
    split = P(("groups", "seq"), "dp")
    placed = (
        split,
        split,
        split,
        split,
        P(None, "dp"),
        P("dp"),
        P(None, "dp"),
        P("dp"),
        P("dp"),
        P("dp"),
        P("dp"),
        P("dp"),
        split,
        split,
        split,
        P("groups"),
    )
    return jax.shard_map(
        shards,
        mesh=mesh,
        in_specs=placed,
        out_specs=(split, split),
        check_vma=False,
    )
```

```python
import functools
import math

import jax
import jax.numpy as jnp
from jax import lax
from jax.experimental import pallas as pl
from jax.experimental.pallas import tpu as pltpu
from jax.sharding import PartitionSpec as P

HDIM = 64
STATE = 128
QHEADS = 32
KVHEADS = 8
ADIM = 128
EPSILON = 1e-05
BARRED = -2e30
HIGHEST = lax.Precision.HIGHEST
F32 = jnp.float32
BF16 = jnp.bfloat16
CHUNK = 256
EDGE = 16
MARK = 3
VMEM_LIMIT = 40 * 1024 * 1024


def silu(value):
    return value * (0.5 * jnp.tanh(0.5 * value) + 0.5)


def softplus(value):
    return jnp.maximum(value, 0.0) + jnp.log(1.0 + jnp.exp(-jnp.abs(value)))


def doc_start(positions, lens_ref):
    begin = jnp.int32(0)
    found = positions * 0
    for doc in range(lens_ref.shape[0]):
        found = jnp.where(positions >= begin, begin, found)
        begin = begin + lens_ref[doc]
    return found


def halves(value):
    high = value.astype(BF16)
    return high, (value - high.astype(F32)).astype(BF16)


def widen(per_head, first, width):
    heads = per_head.shape[1]
    both = jnp.concatenate(halves(per_head), axis=1)
    head = lax.broadcasted_iota(jnp.int32, (2 * heads, width), 0)
    head = jnp.where(head >= heads, head - heads, head)
    channel = lax.broadcasted_iota(jnp.int32, (2 * heads, width), 1) + first
    spread = (channel // HDIM == head).astype(F32).astype(BF16)
    return jnp.dot(both, spread, preferred_element_type=F32)


def rates(dt_ref, dt_bias_ref, a_log_ref):
    step = softplus(dt_ref[...].T + dt_bias_ref[...].reshape(1, -1))
    rate = -step * jnp.exp(a_log_ref[...].reshape(1, -1))
    rows = step.shape[0]
    row = lax.broadcasted_iota(jnp.int32, (rows, rows), 0)
    column = lax.broadcasted_iota(jnp.int32, (rows, rows), 1)
    lower = (row >= column).astype(F32)
    return step, jnp.dot(lower, rate, precision=HIGHEST, preferred_element_type=F32)


def insides(first, shape, taps, lens_ref):
    positions = first + lax.broadcasted_iota(jnp.int32, shape, 0)
    depth = positions - doc_start(positions, lens_ref)
    return [depth >= lag for lag in range(taps)]


def conv(pad, rows, weight, bias, inside):
    taps = weight.shape[0]
    total = pad[8 : 8 + rows] * weight[taps - 1 : taps] + bias
    for lag in range(1, taps):
        term = pad[8 - lag : 8 - lag + rows] * weight[taps - 1 - lag : taps - lag]
        total = total + jnp.where(inside[lag], term, 0.0)
    return silu(total).astype(BF16)


def state_weight(first, step, running, lens_ref):
    rows = step.shape[0]
    last_begin = doc_start(first + rows - 1, lens_ref)
    position = first + lax.broadcasted_iota(jnp.int32, step.shape, 0)
    return jnp.where(
        position >= last_begin, step * jnp.exp(running[rows - 1 : rows] - running), 0.0
    )


def message_pieces(ref, rows):
    block = ref[rows:].astype(F32)
    pieces = [block[at : at + 8] for at in range(0, block.shape[0], 8)]
    return jnp.concatenate(pieces, axis=1)


def state_kernel(group, send, *refs):
    x_ref, bc_ref, dt_ref, wx_ref, bx_ref, wbc_ref, bbc_ref, dt_bias_ref, a_log_ref, lens_ref = refs[:10]
    refs = refs[10:]
    if send:
        x_all_ref, bc_all_ref, keys_ref, values_ref = refs[:4]
        refs = refs[4:]
    xc_ref, bcc_ref, state_ref = refs[:3]
    pad_ref = refs[-1]
    rows, width = x_ref.shape
    taps = wx_ref.shape[0]
    per_group = width // HDIM
    first = lax.axis_index("seq") * rows
    inside = insides(first, (rows, CHUNK), taps, lens_ref)
    step, running = rates(dt_ref, dt_bias_ref, a_log_ref)
    weight = state_weight(first, step, running, lens_ref)
    row = lax.broadcasted_iota(jnp.int32, weight.shape, 0)
    kept = jnp.where(row >= taps - 1, weight, 0.0)[:, group * per_group : (group + 1) * per_group]
    slots = pad_ref.shape[0]

    def block(raw_ref, start, weight_ref, bias_ref, offset, slot):
        pad = pad_ref.at[slot]
        pad[0:8] = jnp.zeros((8, CHUNK), F32)
        pad[8:] = raw_ref[:, start : start + CHUNK].astype(F32)
        columns = slice(offset + start, offset + start + CHUNK)
        return conv(pad, rows, weight_ref[:, columns], bias_ref[columns].reshape(1, -1), inside)

    pair = block(bc_ref, 0, wbc_ref, bbc_ref, group * 2 * STATE, 0)
    bcc_ref[...] = pair
    turned = pair[:, :STATE].astype(F32).T.astype(BF16)
    for start in range(0, width, CHUNK):
        xc = block(x_ref, start, wx_ref, bx_ref, group * width, (start // CHUNK + 1) % slots)
        xc_ref[:, start : start + CHUNK] = xc
        weighted = (xc.astype(F32) * widen(kept, start, CHUNK)).astype(BF16)
        state_ref[:, start : start + CHUNK] = jnp.dot(
            turned, weighted, preferred_element_type=F32
        ).astype(BF16)
    if send:
        message_ref = refs[3]
        kv_width = keys_ref.shape[1]
        message_ref[:rows, :kv_width] = keys_ref[...]
        message_ref[:rows, kv_width:] = values_ref[...]
        marks = []
        for value in (weight[0:1], weight[1:2], weight[2:3], running[rows - 1 : rows]):
            marks.extend(half.astype(F32) for half in halves(value))
        marks = jnp.concatenate(marks, axis=1)
        spare = x_all_ref.shape[1] + bc_all_ref.shape[1] - marks.shape[1]
        marks = jnp.concatenate([marks, jnp.zeros((1, spare), F32)], axis=1)

        def edge(at):
            return jnp.concatenate(
                [x_all_ref[at : at + EDGE].astype(F32), bc_all_ref[at : at + EDGE].astype(F32)], axis=1
            )

        head = edge(0)[:8]
        tail = edge(rows - EDGE)[8:]
        line = lax.broadcasted_iota(jnp.int32, head.shape, 0)
        lines = jnp.where(line < MARK, head, jnp.where(line == MARK, marks, tail))
        pieces = [lines[:, at : at + 2 * kv_width] for at in range(0, lines.shape[1], 2 * kv_width)]
        if len(pieces) % 2:
            pieces.append(jnp.zeros_like(pieces[0]))
        message_ref[rows:] = jnp.concatenate(pieces, axis=0).astype(BF16)


def local_kernel(groups, *refs):
    (
        x_ref, bc_ref, message_ref, dt_ref, wx_ref, bx_ref, wbc_ref, bbc_ref,
        dt_bias_ref, a_log_ref, skip_ref, lens_ref,
    ) = refs[:12]
    xc_refs = refs[12 : 12 + groups]
    bcc_refs = refs[12 + groups : 12 + 2 * groups]
    out_ref, c_ref, pad_ref = refs[12 + 2 * groups :]
    rows, per_group = xc_refs[0].shape
    width = groups * per_group
    taps = wx_ref.shape[0]
    first = lax.axis_index("seq") * rows
    inside = insides(first, (EDGE, CHUNK), taps, lens_ref)
    lines = message_pieces(message_ref, rows)
    slots = pad_ref.shape[0]

    def top(raw_ref, start, weight_ref, bias_ref, offset, slot):
        columns = slice(start, start + CHUNK)
        pad = pad_ref.at[slot]
        pad[0:8] = lines[:, offset + start : offset + start + CHUNK]
        pad[8:] = raw_ref[:, columns].astype(F32)
        return conv(pad, EDGE, weight_ref[:, columns], bias_ref[columns].reshape(1, -1), inside)

    row = lax.broadcasted_iota(jnp.int32, (rows, rows), 0)
    column = lax.broadcasted_iota(jnp.int32, (rows, rows), 1)
    begin = doc_start(first + row, lens_ref)
    linked = (row >= column) & (first + column >= begin)
    step, running = rates(dt_ref, dt_bias_ref, a_log_ref)
    turned_running = running.T
    turned_step = step.T
    skip = skip_ref[...].reshape(1, -1)
    skip = jnp.broadcast_to(skip, (8, skip.shape[1]))
    pair_width = 2 * HDIM
    lane = lax.broadcasted_iota(jnp.int32, (rows, pair_width), 1)
    for group in range(groups):
        base = group * 2 * STATE
        pair = jnp.concatenate(
            [top(bc_ref, base, wbc_ref, bbc_ref, width, group % slots), bcc_refs[group][EDGE:]], axis=0
        )
        inputs = pair[:, :STATE]
        outputs = pair[:, STATE:]
        c_ref[:, group * STATE : (group + 1) * STATE] = outputs
        meet = lax.dot_general(
            outputs, inputs, (((1,), (1,)), ((), ())), preferred_element_type=F32
        )
        meet = jnp.where(linked, meet, 0.0)
        for chunk in range(0, per_group, CHUNK):
            at = group * per_group + chunk
            xc_all = jnp.concatenate(
                [
                    top(x_ref, at, wx_ref, bx_ref, 0, (chunk // CHUNK) % slots),
                    xc_refs[group][EDGE:, chunk : chunk + CHUNK],
                ],
                axis=0,
            )
            wide_skip = widen(skip, at, CHUNK)[0:1]
            for start in range(0, CHUNK, pair_width):
                parts = []
                for head in ((at + start) // HDIM, (at + start) // HDIM + 1):
                    spread = running[:, head : head + 1] - turned_running[head : head + 1]
                    decay = jnp.exp(jnp.minimum(spread, 0.0))
                    parts.append((decay * (meet * turned_step[head : head + 1])).astype(BF16))
                mix = jnp.concatenate(parts, axis=1)
                xc = xc_all[:, start : start + pair_width]
                zero = jnp.zeros_like(xc)
                stacked = jnp.concatenate(
                    [jnp.where(lane < HDIM, xc, zero), jnp.where(lane < HDIM, zero, xc)], axis=0
                )
                value = jnp.dot(mix, stacked, preferred_element_type=F32)
                out_ref[:, at + start : at + start + pair_width] = (
                    value + xc.astype(F32) * wide_skip[:, start : start + pair_width]
                )


def attend_kernel(hops, *refs):
    q_ref = refs[0]
    kv_refs = refs[1 : 2 + hops]
    lens_ref, out_ref = refs[2 + hops :]
    rows = q_ref.shape[0]
    kv_heads = kv_refs[0].shape[1] // (2 * ADIM)
    share = QHEADS // KVHEADS
    count = rows * (hops + 1)
    here = lax.axis_index("seq")
    row = here * rows + lax.broadcasted_iota(jnp.int32, (rows, count), 0)
    column = (here - hops) * rows + lax.broadcasted_iota(jnp.int32, (rows, count), 1)
    allowed = (column <= row) & (column >= doc_start(row, lens_ref))
    scale = ADIM ** (-0.5)
    ones = jnp.ones((count, ADIM), BF16)
    for head in range(kv_heads):
        low = head * ADIM
        keys = jnp.concatenate([ref[:rows, low : low + ADIM] for ref in kv_refs], axis=0)
        low = (kv_heads + head) * ADIM
        values = jnp.concatenate([ref[:rows, low : low + ADIM] for ref in kv_refs], axis=0)
        values = jnp.concatenate([values, ones], axis=1)
        for part in range(share):
            low = (head * share + part) * ADIM
            scores = lax.dot_general(
                q_ref[:, low : low + ADIM], keys, (((1,), (1,)), ((), ())), preferred_element_type=F32
            )
            scores = jnp.where(allowed, scores * scale, BARRED)
            expo = jnp.exp(scores - jnp.max(scores, axis=1, keepdims=True))
            summed = jnp.dot(expo.astype(BF16), values, preferred_element_type=F32)
            out_ref[:, low : low + ADIM] = (summed[:, :ADIM] / summed[:, ADIM:]).astype(BF16)


def carry_kernel(groups, hops, *refs):
    mixed_ref, c_ref, dt_ref, wx_ref, bx_ref, wbc_ref, bbc_ref, dt_bias_ref, a_log_ref, lens_ref = refs[:10]
    state_refs = refs[10 : 10 + groups]
    message_refs = refs[10 + groups : 10 + groups + hops]
    out_ref, entry_ref, pad_ref = refs[10 + groups + hops :]
    rows, width = mixed_ref.shape
    per_group = width // groups
    taps = wx_ref.shape[0]
    here = lax.axis_index("seq")
    first = here * rows
    _, running = rates(dt_ref, dt_bias_ref, a_log_ref)
    heads = running.shape[1]
    group_heads = heads // groups
    first_begin = doc_start(first, lens_ref)
    position = first + lax.broadcasted_iota(jnp.int32, running.shape, 0)
    entry = jnp.where(doc_start(position, lens_ref) < first, jnp.exp(running), 0.0)
    lines = [message_pieces(ref, rows) for ref in message_refs]

    def mark(hop, which):
        at = 2 * which * heads
        return lines[hop][MARK : MARK + 1, at : at + heads] + lines[hop][MARK : MARK + 1, at + heads : at + 2 * heads]

    line = lax.broadcasted_iota(jnp.int32, (8, heads), 0)
    total = jnp.zeros((1, heads), F32)
    weights = []
    inside = []
    for hop in range(1, hops + 1):
        factor = jnp.ones((1, heads), F32)
        if hop > 1:
            total = total + mark(hop - 2, 3)
            factor = jnp.where(first_begin < (here - hop + 1) * rows, jnp.exp(total), 0.0)
            entry_ref[hop - 2] = entry * factor
        weight = jnp.zeros((8, heads), F32)
        for at in range(taps - 1):
            weight = jnp.where(line == at, mark(hop - 1, at) * factor, weight)
        weights.append(weight)
        inside.append(insides((here - hop) * rows, (8, CHUNK), taps, lens_ref))
    slots = pad_ref.shape[0]

    def top(hop, at, weight_ref, bias_ref, start, slot):
        columns = slice(start, start + CHUNK)
        pad = pad_ref.at[slot]
        above = lines[hop + 1] if hop + 1 < hops else jnp.zeros_like(lines[0])
        pad[0:8] = above[:, at : at + CHUNK]
        pad[8:] = lines[hop][:, at : at + CHUNK]
        return conv(pad, 8, weight_ref[:, columns], bias_ref[columns].reshape(1, -1), inside[hop])

    for group in range(groups):
        outputs = c_ref[:, group * STATE : (group + 1) * STATE]
        meets = []
        for hop in range(hops):
            base = group * 2 * STATE
            inputs = top(hop, width + base, wbc_ref, bbc_ref, base, hop % slots)[:, :STATE]
            meets.append(
                lax.dot_general(outputs, inputs, (((1,), (1,)), ((), ())), preferred_element_type=F32)
            )
        meets = jnp.concatenate(meets, axis=1).astype(BF16)
        these = slice(group * group_heads, (group + 1) * group_heads)
        for chunk in range(0, per_group, CHUNK):
            at = group * per_group + chunk
            columns = slice(at, at + CHUNK)
            edges = []
            for hop in range(hops):
                xc = top(hop, at, wx_ref, bx_ref, at, hop % slots).astype(F32)
                edges.append(xc * widen(weights[hop][:, these], chunk, CHUNK))
            edges = jnp.concatenate(edges, axis=0).astype(BF16)
            carried = jnp.dot(
                outputs, state_refs[group][:, chunk : chunk + CHUNK], preferred_element_type=F32
            ) + jnp.dot(meets, edges, preferred_element_type=F32)
            out_ref[:, columns] = mixed_ref[:, columns] + carried * widen(entry[:, these], chunk, CHUNK)


def norm_kernel(group, hops, *refs):
    mixed_ref, c_ref, entry_ref, z_ref, gain_ref = refs[:5]
    state_refs = refs[5 : 5 + hops - 1]
    out_ref, gated_ref = refs[-2:]
    rows, per_group = mixed_ref.shape
    group_heads = per_group // HDIM
    these = slice(group * group_heads, (group + 1) * group_heads)
    outputs = c_ref[:, group * STATE : (group + 1) * STATE]
    squares = jnp.zeros((rows, 1), F32)
    for start in range(0, per_group, CHUNK):
        columns = slice(start, start + CHUNK)
        mixed = mixed_ref[:, columns]
        for hop, ref in enumerate(state_refs):
            carried = jnp.dot(outputs, ref[:, columns], preferred_element_type=F32)
            mixed = mixed + carried * widen(entry_ref[hop][:, these], start, CHUNK)
        gated = mixed * silu(z_ref[:, columns].astype(F32))
        gated_ref[:, columns] = gated
        squares = squares + jnp.sum(gated * gated, axis=1, keepdims=True)
    multiplier = lax.rsqrt(squares * (1.0 / per_group) + EPSILON)
    for start in range(0, per_group, CHUNK):
        columns = slice(start, start + CHUNK)
        gain = gain_ref[group * per_group + start : group * per_group + start + CHUNK]
        out_ref[:, columns] = (gated_ref[:, columns] * multiplier * gain.reshape(1, -1)).astype(BF16)


WHOLE = pl.BlockSpec(memory_space=pltpu.VMEM)
SCALARS = pl.BlockSpec(memory_space=pltpu.SMEM)
UNTOUCHED = pl.BlockSpec(memory_space=pl.ANY)


def part(rows, columns, row, column):
    return pl.BlockSpec((rows, columns), lambda step: (row, column))


def call(kernel, name, outs, operands, specs, out_specs=None, scratch=(), flops=0, aliases={}):
    moved = sum(math.prod(a.shape) * a.dtype.itemsize for a in (*operands, *outs))
    return pl.pallas_call(
        kernel,
        name=name,
        grid=(1,),
        out_shape=outs,
        in_specs=specs,
        out_specs=[WHOLE] * len(outs) if out_specs is None else out_specs,
        scratch_shapes=list(scratch),
        input_output_aliases=aliases,
        compiler_params=pltpu.CompilerParams(vmem_limit_bytes=VMEM_LIMIT),
        cost_estimate=pl.CostEstimate(flops=flops, bytes_accessed=moved, transcendentals=0),
    )(*operands)


def onward(value):
    count = lax.axis_size("seq")
    return lax.ppermute(value, "seq", [(source, source + 1) for source in range(count - 1)])


def shards(
    x_raw,
    bc_raw,
    z_gate,
    dt_raw,
    conv_x_weight,
    conv_x_bias,
    conv_bc_weight,
    conv_bc_bias,
    dt_bias,
    a_log,
    skip_d,
    norm_gain,
    queries,
    keys,
    values,
    doc_lens,
):
    rows, width = x_raw.shape
    bc_width = bc_raw.shape[1]
    heads = dt_raw.shape[1]
    groups = bc_width // (2 * STATE)
    per_group = width // groups
    count = lax.axis_size("seq")
    longest = rows * count // 2
    hops = min(count - 1, -(-(longest - 1) // rows))
    assert hops * rows >= longest
    kv_width = 2 * keys.shape[1]
    shape = jax.ShapeDtypeStruct
    dt = dt_raw.T
    convs = (conv_x_weight, conv_x_bias, conv_bc_weight, conv_bc_bias)
    pieces = -(-(width + bc_width) // kv_width)
    message_rows = rows + EDGE * -(-pieces // 2)

    xcs, bccs, states = [], [], []
    for group in range(groups):
        send = group == groups - 1
        outs = [shape((rows, per_group), BF16), shape((rows, 2 * STATE), BF16), shape((STATE, per_group), BF16)]
        operands = [x_raw, bc_raw, dt, *convs, dt_bias, a_log, doc_lens]
        specs = [part(rows, per_group, 0, group), part(rows, 2 * STATE, 0, group)] + [WHOLE] * 7 + [SCALARS]
        if send:
            outs.append(shape((message_rows, kv_width), BF16))
            operands += [x_raw, bc_raw, keys, values]
            specs += [WHOLE] * 4
        got = call(
            functools.partial(state_kernel, group, send),
            f"state_part{group}",
            outs,
            operands,
            specs,
            scratch=[pltpu.VMEM((4, rows + 8, CHUNK), F32)],
            flops=2 * rows * per_group * STATE,
        )
        xcs.append(got[0])
        bccs.append(got[1])
        states.append(got[2])
    messages = [onward(got[3])]
    for _ in range(1, hops):
        messages.append(onward(messages[-1]))
    arrived = [[onward(state)] for state in states]
    for hop in range(1, hops):
        for chain in arrived:
            chain.append(onward(chain[-1]))

    mixed, c_out = call(
        functools.partial(local_kernel, groups),
        "local_mix",
        [shape((rows, width), F32), shape((rows, groups * STATE), BF16)],
        [x_raw, bc_raw, messages[0], dt, *convs, dt_bias, a_log, skip_d, doc_lens, *xcs, *bccs],
        [part(EDGE, width, 0, 0), part(EDGE, bc_width, 0, 0)] + [WHOLE] * 9 + [SCALARS] + [WHOLE] * 2 * groups,
        scratch=[pltpu.VMEM((4, EDGE + 8, CHUNK), F32)],
        flops=4 * rows * rows * width,
    )
    (attn_out,) = call(
        functools.partial(attend_kernel, hops),
        "attend",
        [shape(queries.shape, BF16)],
        [queries, *reversed(messages), got[3], doc_lens],
        [WHOLE] * (hops + 2) + [SCALARS],
        flops=4 * rows * rows * (hops + 1) * queries.shape[1],
    )
    mixed, entry = call(
        functools.partial(carry_kernel, groups, hops),
        "carry_near",
        [shape((rows, width), F32), shape((max(hops - 1, 1), rows, heads), F32)],
        [mixed, c_out, dt, *convs, dt_bias, a_log, doc_lens, *(chain[0] for chain in arrived), *messages],
        [WHOLE] * 9 + [SCALARS] + [WHOLE] * (groups + hops),
        scratch=[pltpu.VMEM((4, 16, CHUNK), F32)],
        flops=2 * rows * width * STATE,
    )
    mamba_out = None
    for group, chain in enumerate(arrived):
        operands = [mixed, c_out, entry, z_gate, norm_gain, *chain[1:]]
        specs = [part(rows, per_group, 0, group), WHOLE, WHOLE, part(rows, per_group, 0, group)]
        specs += [WHOLE] * hops
        aliases = {}
        if mamba_out is not None:
            operands.append(mamba_out)
            specs.append(UNTOUCHED)
            aliases = {len(operands) - 1: 0}
        (mamba_out,) = call(
            functools.partial(norm_kernel, group, hops),
            f"norm_part{group}",
            [shape((rows, width), BF16)],
            operands,
            specs,
            out_specs=[part(rows, per_group, 0, group)],
            scratch=[pltpu.VMEM((rows, per_group), F32)],
            flops=2 * rows * per_group * STATE,
            aliases=aliases,
        )
    return (mamba_out, attn_out)


def solution(mesh):
    split = P(("groups", "seq"), "dp")
    placed = (
        split,
        split,
        split,
        split,
        P(None, "dp"),
        P("dp"),
        P(None, "dp"),
        P("dp"),
        P("dp"),
        P("dp"),
        P("dp"),
        P("dp"),
        split,
        split,
        split,
        P("groups"),
    )
    return jax.shard_map(
        shards,
        mesh=mesh,
        in_specs=placed,
        out_specs=(split, split),
        check_vma=False,
    )
```

```python
import functools
import math

import jax
import jax.numpy as jnp
from jax import lax
from jax.experimental import pallas as pl
from jax.experimental.pallas import tpu as pltpu
from jax.sharding import PartitionSpec as P

HDIM = 64
STATE = 128
QHEADS = 32
KVHEADS = 8
ADIM = 128
EPSILON = 1e-05
BARRED = -2e30
HIGHEST = lax.Precision.HIGHEST
F32 = jnp.float32
BF16 = jnp.bfloat16
CHUNK = 256
EDGE = 16
KERNEL_FLOPS = 2 * 10**9
VMEM_LIMIT = 40 * 1024 * 1024
VMEM_ALL = 62 * 1024 * 1024


def silu(value):
    return value * (0.5 * jnp.tanh(0.5 * value) + 0.5)


def softplus(value):
    return jnp.maximum(value, 0.0) + jnp.log(1.0 + jnp.exp(-jnp.abs(value)))


def doc_start(positions, lens_ref):
    begin = jnp.int32(0)
    found = positions * 0
    for doc in range(lens_ref.shape[0]):
        found = jnp.where(positions >= begin, begin, found)
        begin = begin + lens_ref[doc]
    return found


def halves(value):
    high = value.astype(BF16)
    return high, (value - high.astype(F32)).astype(BF16)


def widen(per_head, first, width):
    heads = per_head.shape[1]
    both = jnp.concatenate(halves(per_head), axis=1)
    head = lax.broadcasted_iota(jnp.int32, (2 * heads, width), 0)
    head = jnp.where(head >= heads, head - heads, head)
    channel = lax.broadcasted_iota(jnp.int32, (2 * heads, width), 1) + first
    spread = (channel // HDIM == head).astype(F32).astype(BF16)
    return jnp.dot(both, spread, preferred_element_type=F32)


def rates(dt_ref, dt_bias_ref, a_log_ref):
    step = softplus(dt_ref[...].T + dt_bias_ref[...].reshape(1, -1))
    rate = -step * jnp.exp(a_log_ref[...].reshape(1, -1))
    rows = step.shape[0]
    row = lax.broadcasted_iota(jnp.int32, (rows, rows), 0)
    column = lax.broadcasted_iota(jnp.int32, (rows, rows), 1)
    lower = (row >= column).astype(F32)
    return step, jnp.dot(lower, rate, precision=HIGHEST, preferred_element_type=F32)


def insides(first, shape, taps, lens_ref):
    positions = first + lax.broadcasted_iota(jnp.int32, shape, 0)
    depth = positions - doc_start(positions, lens_ref)
    return [depth >= lag for lag in range(taps)]


def conv(pad, rows, weight, bias, inside):
    taps = weight.shape[0]
    total = pad[8 : 8 + rows] * weight[taps - 1 : taps] + bias
    for lag in range(1, taps):
        term = pad[8 - lag : 8 - lag + rows] * weight[taps - 1 - lag : taps - lag]
        total = total + jnp.where(inside[lag], term, 0.0)
    return silu(total).astype(BF16)


def state_weight(first, step, running, lens_ref):
    rows = step.shape[0]
    last_begin = doc_start(first + rows - 1, lens_ref)
    position = first + lax.broadcasted_iota(jnp.int32, step.shape, 0)
    return jnp.where(
        position >= last_begin, step * jnp.exp(running[rows - 1 : rows] - running), 0.0
    )


def tail_lines(message, rows):
    block = message[rows:].astype(F32)
    return jnp.concatenate([block[at : at + 4] for at in range(0, block.shape[0], 4)], axis=1)


def reach(device, rows, lens_ref):
    return device - doc_start((device + 1) * rows - 1, lens_ref) // rows


def state_kernel(part, first_part, last_part, *refs):
    x_ref, bc_ref, dt_ref, wx_ref, bx_ref, wbc_ref, bbc_ref, dt_bias_ref, a_log_ref, lens_ref = refs[:10]
    refs = refs[10:]
    if first_part:
        x_edge_ref, bc_edge_ref = refs[:2]
        refs = refs[2:]
    if last_part:
        keys_ref, values_ref = refs[:2]
        refs = refs[2:]
    xc_ref, bcc_ref, state_ref = refs[:3]
    pad_ref = refs[-1]
    rows, width = x_ref.shape
    taps = wx_ref.shape[0]
    heads = width // HDIM
    here = lax.axis_index("seq")
    first = here * rows
    inside = insides(first, (rows, CHUNK), taps, lens_ref)
    step, running = rates(dt_ref, dt_bias_ref, a_log_ref)
    weight = state_weight(first, step, running, lens_ref)
    row = lax.broadcasted_iota(jnp.int32, weight.shape, 0)
    kept = (row >= taps - 1) | (reach(here, rows, lens_ref) == 0)
    weight = jnp.where(kept, weight, 0.0)[:, part * heads : (part + 1) * heads]
    slots = pad_ref.shape[0]

    def block(raw_ref, start, weight_ref, bias_ref, offset, slot):
        pad = pad_ref.at[slot]
        pad[0:8] = jnp.zeros((8, CHUNK), F32)
        pad[8:] = raw_ref[:, start : start + CHUNK].astype(F32)
        columns = slice(offset + start, offset + start + CHUNK)
        return conv(pad, rows, weight_ref[:, columns], bias_ref[columns].reshape(1, -1), inside)

    pair = block(bc_ref, 0, wbc_ref, bbc_ref, part * 2 * STATE, 0)
    bcc_ref[...] = pair
    turned = pair[:, :STATE].astype(F32).T.astype(BF16)
    for start in range(0, width, CHUNK):
        xc = block(x_ref, start, wx_ref, bx_ref, part * width, (start // CHUNK + 1) % slots)
        xc_ref[:, start : start + CHUNK] = xc
        weighted = (xc.astype(F32) * widen(weight, start, CHUNK)).astype(BF16)
        state_ref[:STATE, start : start + CHUNK] = jnp.dot(
            turned, weighted, preferred_element_type=F32
        ).astype(BF16)
    if first_part:
        edges = jnp.concatenate([x_edge_ref[...].astype(F32), bc_edge_ref[...].astype(F32)], axis=1)
        edges = edges[EDGE - 4 :]
        spare = -edges.shape[1] % width
        if spare:
            edges = jnp.concatenate([edges, jnp.zeros((4, spare), F32)], axis=1)
        pieces = [edges[:, at : at + width] for at in range(0, edges.shape[1], width)]
        while len(pieces) % (EDGE // 4):
            pieces.append(jnp.zeros_like(pieces[0]))
        state_ref[STATE:] = jnp.concatenate(pieces, axis=0).astype(BF16)
    if last_part:
        kv_ref = refs[3]
        kv_width = keys_ref.shape[1]
        kv_ref[:, :kv_width] = keys_ref[...]
        kv_ref[:, kv_width:] = values_ref[...]


def relay_kernel(part, offset, fresh, *refs):
    (
        x_ref, bc_ref, message_ref, got_ref, state_ref, dt_ref, wx_ref, bx_ref, wbc_ref, bbc_ref,
        dt_bias_ref, a_log_ref, lens_ref,
    ) = refs[:13]
    out_ref, pad_ref = refs[-2:]
    width = x_ref.shape[1]
    rows = dt_ref.shape[1]
    taps = wx_ref.shape[0]
    heads = width // HDIM
    here = lax.axis_index("seq")
    first = here * rows
    own = reach(here, rows, lens_ref) == 0
    inside = insides(first, (EDGE, CHUNK), taps, lens_ref)
    step, running = rates(dt_ref, dt_bias_ref, a_log_ref)
    row = lax.broadcasted_iota(jnp.int32, (EDGE, heads), 0)
    these = slice(part * heads, (part + 1) * heads)
    total = running[rows - 1 : rows, these]
    weight = step[:EDGE, these] * jnp.exp(total - running[:EDGE, these])
    weight = jnp.where((row < taps - 1) & jnp.logical_not(own), weight, 0.0)
    through = jnp.broadcast_to(jnp.exp(total), (8, heads))
    lines = tail_lines(message_ref, STATE)
    slots = pad_ref.shape[0]

    def top(raw_ref, start, line, weight_ref, bias_ref, base, slot):
        columns = slice(base + start, base + start + CHUNK)
        pad = pad_ref.at[slot]
        pad[4:8] = lines[:, line + start : line + start + CHUNK]
        pad[8:] = raw_ref[:, start : start + CHUNK].astype(F32)
        return conv(pad, EDGE, weight_ref[:, columns], bias_ref[columns].reshape(1, -1), inside)

    base = part * 2 * STATE
    inputs = top(bc_ref, 0, offset + base, wbc_ref, bbc_ref, base, 0)[:, :STATE]
    turned = inputs.astype(F32).T.astype(BF16)
    for start in range(0, width, CHUNK):
        columns = slice(start, start + CHUNK)
        xc = top(x_ref, start, part * width, wx_ref, bx_ref, part * width, (start // CHUNK + 1) % slots)
        weighted = (xc.astype(F32) * widen(weight, start, CHUNK)).astype(BF16)
        full = state_ref[:STATE, columns].astype(F32) + jnp.dot(
            turned, weighted, preferred_element_type=F32
        )
        full = full + widen(through, start, CHUNK)[0:1] * got_ref[:STATE, columns].astype(F32)
        other = refs[13] if fresh else state_ref
        out_ref[:, columns] = jnp.where(own, other[:STATE, columns].astype(F32), full).astype(BF16)


def local_kernel(groups, *refs):
    (
        x_ref, bc_ref, message_ref, dt_ref, wx_ref, bx_ref, wbc_ref, bbc_ref,
        dt_bias_ref, a_log_ref, skip_ref, lens_ref,
    ) = refs[:12]
    xc_refs = refs[12 : 12 + groups]
    bcc_refs = refs[12 + groups : 12 + 2 * groups]
    out_ref, c_ref, entry_ref, pad_ref = refs[12 + 2 * groups :]
    rows, per_group = xc_refs[0].shape
    width = groups * per_group
    taps = wx_ref.shape[0]
    first = lax.axis_index("seq") * rows
    inside = insides(first, (EDGE, CHUNK), taps, lens_ref)
    lines = tail_lines(message_ref, STATE)
    slots = pad_ref.shape[0]

    def top(raw_ref, start, weight_ref, bias_ref, offset, slot):
        columns = slice(start, start + CHUNK)
        pad = pad_ref.at[slot]
        pad[4:8] = lines[:, offset + start : offset + start + CHUNK]
        pad[8:] = raw_ref[:, columns].astype(F32)
        return conv(pad, EDGE, weight_ref[:, columns], bias_ref[columns].reshape(1, -1), inside)

    row = lax.broadcasted_iota(jnp.int32, (rows, rows), 0)
    column = lax.broadcasted_iota(jnp.int32, (rows, rows), 1)
    begin = doc_start(first + row, lens_ref)
    linked = (row >= column) & (first + column >= begin)
    step, running = rates(dt_ref, dt_bias_ref, a_log_ref)
    position = first + lax.broadcasted_iota(jnp.int32, running.shape, 0)
    entry_ref[...] = jnp.where(doc_start(position, lens_ref) < first, jnp.exp(running), 0.0)
    turned_running = running.T
    turned_step = step.T
    skip = skip_ref[...].reshape(1, -1)
    skip = jnp.broadcast_to(skip, (8, skip.shape[1]))
    pair_width = 2 * HDIM
    lane = lax.broadcasted_iota(jnp.int32, (rows, pair_width), 1)
    for group in range(groups):
        base = group * 2 * STATE
        pair = jnp.concatenate(
            [top(bc_ref, base, wbc_ref, bbc_ref, width, group % slots), bcc_refs[group][EDGE:]], axis=0
        )
        inputs = pair[:, :STATE]
        outputs = pair[:, STATE:]
        c_ref[:, group * STATE : (group + 1) * STATE] = outputs
        meet = lax.dot_general(
            outputs, inputs, (((1,), (1,)), ((), ())), preferred_element_type=F32
        )
        meet = jnp.where(linked, meet, 0.0)
        for chunk in range(0, per_group, CHUNK):
            at = group * per_group + chunk
            xc_all = jnp.concatenate(
                [
                    top(x_ref, at, wx_ref, bx_ref, 0, (chunk // CHUNK) % slots),
                    xc_refs[group][EDGE:, chunk : chunk + CHUNK],
                ],
                axis=0,
            )
            wide_skip = widen(skip, at, CHUNK)[0:1]
            for start in range(0, CHUNK, pair_width):
                parts = []
                for head in ((at + start) // HDIM, (at + start) // HDIM + 1):
                    spread = running[:, head : head + 1] - turned_running[head : head + 1]
                    decay = jnp.exp(jnp.minimum(spread, 0.0))
                    parts.append((decay * (meet * turned_step[head : head + 1])).astype(BF16))
                mix = jnp.concatenate(parts, axis=1)
                xc = xc_all[:, start : start + pair_width]
                zero = jnp.zeros_like(xc)
                stacked = jnp.concatenate(
                    [jnp.where(lane < HDIM, xc, zero), jnp.where(lane < HDIM, zero, xc)], axis=0
                )
                value = jnp.dot(mix, stacked, preferred_element_type=F32)
                out_ref[:, at + start : at + start + pair_width] = (
                    value + xc.astype(F32) * wide_skip[:, start : start + pair_width]
                )


def attend_kernel(hops, *refs):
    q_ref = refs[0]
    kv_refs = refs[1 : 2 + hops]
    lens_ref, out_ref = refs[2 + hops :]
    rows = q_ref.shape[0]
    kv_heads = kv_refs[0].shape[1] // (2 * ADIM)
    share = QHEADS // KVHEADS
    count = rows * (hops + 1)
    here = lax.axis_index("seq")
    row = here * rows + lax.broadcasted_iota(jnp.int32, (rows, count), 0)
    column = (here - hops) * rows + lax.broadcasted_iota(jnp.int32, (rows, count), 1)
    allowed = (column <= row) & (column >= doc_start(row, lens_ref))
    scale = ADIM ** (-0.5)
    ones = jnp.ones((count, ADIM), BF16)
    for head in range(kv_heads):
        low = head * ADIM
        keys = jnp.concatenate([ref[:, low : low + ADIM] for ref in kv_refs], axis=0)
        low = (kv_heads + head) * ADIM
        values = jnp.concatenate([ref[:, low : low + ADIM] for ref in kv_refs], axis=0)
        values = jnp.concatenate([values, ones], axis=1)
        for part in range(share):
            low = (head * share + part) * ADIM
            scores = lax.dot_general(
                q_ref[:, low : low + ADIM], keys, (((1,), (1,)), ((), ())), preferred_element_type=F32
            )
            scores = jnp.where(allowed, scores * scale, BARRED)
            expo = jnp.exp(scores - jnp.max(scores, axis=1, keepdims=True))
            summed = jnp.dot(expo.astype(BF16), values, preferred_element_type=F32)
            out_ref[:, low : low + ADIM] = (summed[:, :ADIM] / summed[:, ADIM:]).astype(BF16)


def norm_kernel(part, hops, *refs):
    mixed_ref, c_ref, entry_ref, z_ref, gain_ref, lens_ref = refs[:6]
    got_refs = refs[6 : 6 + hops]
    out_ref, gated_ref = refs[-2:]
    rows, width = mixed_ref.shape
    heads = width // HDIM
    entry = entry_ref[:, part * heads : (part + 1) * heads]
    outputs = c_ref[:, part * STATE : (part + 1) * STATE]
    before = reach(lax.axis_index("seq") - 1, rows, lens_ref)
    squares = jnp.zeros((rows, 1), F32)
    for start in range(0, width, CHUNK):
        columns = slice(start, start + CHUNK)
        state = got_refs[0][:STATE, columns]
        for hop in range(1, hops):
            state = jnp.where(before == hop, got_refs[hop][:STATE, columns], state)
        carried = jnp.dot(outputs, state, preferred_element_type=F32)
        mixed = mixed_ref[:, columns] + carried * widen(entry, start, CHUNK)
        gated = mixed * silu(z_ref[:, columns].astype(F32))
        gated_ref[:, columns] = gated
        squares = squares + jnp.sum(gated * gated, axis=1, keepdims=True)
    multiplier = lax.rsqrt(squares * (1.0 / width) + EPSILON)
    for start in range(0, width, CHUNK):
        columns = slice(start, start + CHUNK)
        gain = gain_ref[part * width + start : part * width + start + CHUNK]
        out_ref[:, columns] = (gated_ref[:, columns] * multiplier * gain.reshape(1, -1)).astype(BF16)


WHOLE = pl.BlockSpec(memory_space=pltpu.VMEM)
SCALARS = pl.BlockSpec(memory_space=pltpu.SMEM)
UNTOUCHED = pl.BlockSpec(memory_space=pl.ANY)


def tile(rows, columns, row, column):
    return pl.BlockSpec((rows, columns), lambda step: (row, column))


def call(kernel, name, outs, operands, specs, out_specs=None, scratch=(), flops=KERNEL_FLOPS, aliases={}, limit=VMEM_LIMIT, after=()):
    operands = [*operands, *after]
    specs = [*specs, *([UNTOUCHED] * len(after))]
    inputs = len(operands) - len(after)
    moved = sum(math.prod(a.shape) * a.dtype.itemsize for a in (*operands, *outs))
    def body(*refs):
        kernel(*refs[:inputs], *refs[inputs + len(after) :])

    return pl.pallas_call(
        body,
        name=name,
        grid=(1,),
        out_shape=outs,
        in_specs=specs,
        out_specs=[WHOLE] * len(outs) if out_specs is None else out_specs,
        scratch_shapes=list(scratch),
        input_output_aliases=aliases,
        compiler_params=pltpu.CompilerParams(vmem_limit_bytes=limit),
        cost_estimate=pl.CostEstimate(flops=flops, bytes_accessed=moved, transcendentals=0),
    )(*operands)


def onward(value, first=0):
    count = lax.axis_size("seq")
    return lax.ppermute(value, "seq", [(source, source + 1) for source in range(first, count - 1)])


def shards(
    x_raw,
    bc_raw,
    z_gate,
    dt_raw,
    conv_x_weight,
    conv_x_bias,
    conv_bc_weight,
    conv_bc_bias,
    dt_bias,
    a_log,
    skip_d,
    norm_gain,
    queries,
    keys,
    values,
    doc_lens,
):
    rows, width = x_raw.shape
    bc_width = bc_raw.shape[1]
    heads = dt_raw.shape[1]
    groups = bc_width // (2 * STATE)
    per_group = width // groups
    count = lax.axis_size("seq")
    longest = rows * count // 2
    hops = min(count - 1, -(-(longest - 1) // rows))
    assert hops * rows >= longest and (hops <= 2 or groups == 1)
    shape = jax.ShapeDtypeStruct
    dt = dt_raw.T
    params = [dt, conv_x_weight, conv_x_bias, conv_bc_weight, conv_bc_bias, dt_bias, a_log]
    pieces = -(-(width + bc_width) // per_group)
    tail_rows = EDGE * -(-4 * pieces // EDGE)
    last_edge = rows // EDGE - 1

    xcs, bccs, states = [], [], []
    for part in range(groups):
        first_part, last_part = part == 0, part == groups - 1
        outs = [
            shape((rows, per_group), BF16),
            shape((rows, 2 * STATE), BF16),
            shape((STATE + tail_rows * first_part, per_group), BF16),
        ]
        operands = [x_raw, bc_raw, *params, doc_lens]
        specs = [tile(rows, per_group, 0, part), tile(rows, 2 * STATE, 0, part)] + [WHOLE] * 7 + [SCALARS]
        if first_part:
            operands += [x_raw, bc_raw]
            specs += [tile(EDGE, width, last_edge, 0), tile(EDGE, bc_width, last_edge, 0)]
        if last_part:
            outs.append(shape((rows, 2 * keys.shape[1]), BF16))
            operands += [keys, values]
            specs += [WHOLE] * 2
        got = call(
            functools.partial(state_kernel, part, first_part, last_part),
            f"state_part{part}",
            outs,
            operands,
            specs,
            scratch=[pltpu.VMEM((4, rows + 8, CHUNK), F32)],
            limit=VMEM_ALL if first_part else VMEM_LIMIT,
        )
        xcs.append(got[0])
        bccs.append(got[1])
        states.append(got[2])
    kvs = [got[3]]
    for hop in range(hops):
        kvs.append(onward(kvs[-1], hop))

    slots = [onward(states[0])]
    mixed, c_out, entry = call(
        functools.partial(local_kernel, groups),
        "local_mix",
        [shape((rows, width), F32), shape((rows, groups * STATE), BF16), shape((rows, heads), F32)],
        [x_raw, bc_raw, slots[0], *params, skip_d, doc_lens, *xcs, *bccs],
        [tile(EDGE, width, 0, 0), tile(EDGE, bc_width, 0, 0)]
        + [WHOLE] * 9
        + [SCALARS]
        + [WHOLE] * 2 * groups,
        scratch=[pltpu.VMEM((4, EDGE + 8, CHUNK), F32)],
        after=[kvs[1]],
    )
    for slot in range(2, hops + groups):
        part = min(slot - 1, groups) - 1
        fresh = slot <= groups
        operands = [x_raw, bc_raw, slots[0], slots[-1], states[part], *params, doc_lens]
        specs = [tile(EDGE, per_group, 0, part), tile(EDGE, 2 * STATE, 0, part)] + [WHOLE] * 10 + [SCALARS]
        if fresh:
            operands.append(states[slot - 1])
            specs.append(WHOLE)
        (passed,) = call(
            functools.partial(relay_kernel, part, width, fresh),
            f"relay_slot{slot}",
            [shape((STATE, per_group), BF16)],
            operands,
            specs,
            scratch=[pltpu.VMEM((4, EDGE + 8, CHUNK), F32)],
            after=[entry] if slot == hops + groups - 1 else [],
        )
        slots.append(onward(passed, max(0, slot - groups)))

    (attn_out,) = call(
        functools.partial(attend_kernel, hops),
        "attend",
        [shape(queries.shape, BF16)],
        [queries, *reversed(kvs), doc_lens],
        [WHOLE] * (hops + 2) + [SCALARS],
    )
    mamba_out = None
    for part in range(groups):
        operands = [mixed, c_out, entry, z_gate, norm_gain, doc_lens, *slots[part : part + hops]]
        block = tile(rows, per_group, 0, part)
        specs = [block, WHOLE, WHOLE, block, WHOLE, SCALARS] + [WHOLE] * hops
        aliases = {}
        if mamba_out is not None:
            operands.append(mamba_out)
            specs.append(UNTOUCHED)
            aliases = {len(operands) - 1: 0}
        (mamba_out,) = call(
            functools.partial(norm_kernel, part, hops),
            f"norm_part{part}",
            [shape((rows, width), BF16)],
            operands,
            specs,
            out_specs=[block],
            scratch=[pltpu.VMEM((rows, per_group), F32)],
            aliases=aliases,
        )
    return (mamba_out, attn_out)


def solution(mesh):
    split = P(("groups", "seq"), "dp")
    placed = (
        split,
        split,
        split,
        split,
        P(None, "dp"),
        P("dp"),
        P(None, "dp"),
        P("dp"),
        P("dp"),
        P("dp"),
        P("dp"),
        P("dp"),
        split,
        split,
        split,
        P("groups"),
    )
    return jax.shard_map(
        shards,
        mesh=mesh,
        in_specs=placed,
        out_specs=(split, split),
        check_vma=False,
    )
```

```python
import functools
import math

import jax
import jax.numpy as jnp
from jax import lax
from jax.experimental import pallas as pl
from jax.experimental.pallas import tpu as pltpu
from jax.sharding import PartitionSpec as P

HDIM = 64
STATE = 128
QHEADS = 32
KVHEADS = 8
ADIM = 128
EPSILON = 1e-05
BARRED = -2e30
HIGHEST = lax.Precision.HIGHEST
F32 = jnp.float32
BF16 = jnp.bfloat16
CHUNK = 256
EDGE = 16
KERNEL_FLOPS = 2 * 10**9
VMEM_LIMIT = 40 * 1024 * 1024
VMEM_ALL = 62 * 1024 * 1024


def silu(value):
    return value * (0.5 * jnp.tanh(0.5 * value) + 0.5)


def softplus(value):
    return jnp.maximum(value, 0.0) + jnp.log(1.0 + jnp.exp(-jnp.abs(value)))


def doc_start(positions, lens_ref):
    begin = jnp.int32(0)
    found = positions * 0
    for doc in range(lens_ref.shape[0]):
        found = jnp.where(positions >= begin, begin, found)
        begin = begin + lens_ref[doc]
    return found


def halves(value):
    high = value.astype(BF16)
    return high, (value - high.astype(F32)).astype(BF16)


def widen(per_head, first, width):
    heads = per_head.shape[1]
    both = jnp.concatenate(halves(per_head), axis=1)
    head = lax.broadcasted_iota(jnp.int32, (2 * heads, width), 0)
    head = jnp.where(head >= heads, head - heads, head)
    channel = lax.broadcasted_iota(jnp.int32, (2 * heads, width), 1) + first
    spread = (channel // HDIM == head).astype(F32).astype(BF16)
    return jnp.dot(both, spread, preferred_element_type=F32)


def rates(dt_ref, dt_bias_ref, a_log_ref):
    step = softplus(dt_ref[...].T + dt_bias_ref[...].reshape(1, -1))
    rate = -step * jnp.exp(a_log_ref[...].reshape(1, -1))
    rows = step.shape[0]
    row = lax.broadcasted_iota(jnp.int32, (rows, rows), 0)
    column = lax.broadcasted_iota(jnp.int32, (rows, rows), 1)
    lower = (row >= column).astype(F32).astype(BF16)
    high = rate.astype(BF16)
    middle, low = halves(rate - high.astype(F32))
    parts = jnp.concatenate([high, middle, low], axis=0)
    lowers = jnp.concatenate([lower, lower, lower], axis=1)
    return step, jnp.dot(lowers, parts, preferred_element_type=F32)


def insides(first, shape, taps, lens_ref):
    positions = first + lax.broadcasted_iota(jnp.int32, shape, 0)
    depth = positions - doc_start(positions, lens_ref)
    return [depth >= lag for lag in range(taps)]


def conv(pad, rows, weight, bias, inside):
    taps = weight.shape[0]
    total = pad[8 : 8 + rows] * weight[taps - 1 : taps] + bias
    for lag in range(1, taps):
        term = pad[8 - lag : 8 - lag + rows] * weight[taps - 1 - lag : taps - lag]
        total = total + jnp.where(inside[lag], term, 0.0)
    return silu(total).astype(BF16)


def state_weight(first, step, running, lens_ref):
    rows = step.shape[0]
    last_begin = doc_start(first + rows - 1, lens_ref)
    position = first + lax.broadcasted_iota(jnp.int32, step.shape, 0)
    return jnp.where(
        position >= last_begin, step * jnp.exp(running[rows - 1 : rows] - running), 0.0
    )


def tail_lines(message, rows):
    block = message[rows:].astype(F32)
    return jnp.concatenate([block[at : at + 4] for at in range(0, block.shape[0], 4)], axis=1)


def reach(device, rows, lens_ref):
    return device - doc_start((device + 1) * rows - 1, lens_ref) // rows


def state_kernel(part, first_part, last_part, *refs):
    x_ref, bc_ref, dt_ref, wx_ref, bx_ref, wbc_ref, bbc_ref, dt_bias_ref, a_log_ref, lens_ref = refs[:10]
    refs = refs[10:]
    if first_part:
        x_edge_ref, bc_edge_ref = refs[:2]
        refs = refs[2:]
    if last_part:
        keys_ref, values_ref = refs[:2]
        refs = refs[2:]
    xc_ref, bcc_ref, state_ref = refs[:3]
    pad_ref = refs[-1]
    rows, width = x_ref.shape
    taps = wx_ref.shape[0]
    heads = width // HDIM
    here = lax.axis_index("seq")
    first = here * rows
    inside = insides(first, (rows, CHUNK), taps, lens_ref)
    step, running = rates(dt_ref, dt_bias_ref, a_log_ref)
    weight = state_weight(first, step, running, lens_ref)
    row = lax.broadcasted_iota(jnp.int32, weight.shape, 0)
    kept = (row >= taps - 1) | (reach(here, rows, lens_ref) == 0)
    weight = jnp.where(kept, weight, 0.0)[:, part * heads : (part + 1) * heads]
    slots = pad_ref.shape[0]

    def block(raw_ref, start, weight_ref, bias_ref, offset, slot):
        pad = pad_ref.at[slot]
        pad[0:8] = jnp.zeros((8, CHUNK), F32)
        pad[8:] = raw_ref[:, start : start + CHUNK].astype(F32)
        columns = slice(offset + start, offset + start + CHUNK)
        return conv(pad, rows, weight_ref[:, columns], bias_ref[columns].reshape(1, -1), inside)

    pair = block(bc_ref, 0, wbc_ref, bbc_ref, part * 2 * STATE, 0)
    bcc_ref[...] = pair
    turned = pair[:, :STATE].astype(F32).T.astype(BF16)
    for start in range(0, width, CHUNK):
        xc = block(x_ref, start, wx_ref, bx_ref, part * width, (start // CHUNK + 1) % slots)
        xc_ref[:, start : start + CHUNK] = xc
        weighted = (xc.astype(F32) * widen(weight, start, CHUNK)).astype(BF16)
        state_ref[:STATE, start : start + CHUNK] = jnp.dot(
            turned, weighted, preferred_element_type=F32
        ).astype(BF16)
    if first_part:
        edges = jnp.concatenate([x_edge_ref[...].astype(F32), bc_edge_ref[...].astype(F32)], axis=1)
        edges = edges[EDGE - 4 :]
        spare = -edges.shape[1] % width
        if spare:
            edges = jnp.concatenate([edges, jnp.zeros((4, spare), F32)], axis=1)
        pieces = [edges[:, at : at + width] for at in range(0, edges.shape[1], width)]
        while len(pieces) % (EDGE // 4):
            pieces.append(jnp.zeros_like(pieces[0]))
        state_ref[STATE:] = jnp.concatenate(pieces, axis=0).astype(BF16)
    if last_part:
        kv_ref = refs[3]
        kv_width = keys_ref.shape[1]
        kv_ref[:, :kv_width] = keys_ref[...]
        kv_ref[:, kv_width:] = values_ref[...]


def prepare_kernel(hops, *refs):
    x_ref, bc_ref, dt_ref, wx_ref, bx_ref, wbc_ref, bbc_ref, dt_bias_ref, a_log_ref, lens_ref = refs[:10]
    partial_ref, weight_ref, through_ref, inside_ref, flag_ref, entry_ref, pad_ref = refs[10:]
    width = x_ref.shape[1]
    rows, heads = entry_ref.shape
    taps = wx_ref.shape[0]
    here = lax.axis_index("seq")
    first = here * rows
    own = reach(here, rows, lens_ref) == 0
    inside = insides(first, (8, CHUNK), taps, lens_ref)
    for lag in range(1, taps):
        inside_ref[lag - 1] = inside[lag].astype(F32)
    flag_ref[0] = jnp.broadcast_to(own.astype(F32), (8, CHUNK))
    before = reach(here - 1, rows, lens_ref)
    for hop in range(1, hops):
        flag_ref[hop] = jnp.broadcast_to((before == hop).astype(F32), (8, CHUNK))
    step, running = rates(dt_ref, dt_bias_ref, a_log_ref)
    position = first + lax.broadcasted_iota(jnp.int32, running.shape, 0)
    entry_ref[...] = jnp.where(doc_start(position, lens_ref) < first, jnp.exp(running), 0.0)
    row = lax.broadcasted_iota(jnp.int32, (8, heads), 0)
    total = running[rows - 1 : rows]
    weight = step[:8] * jnp.exp(total - running[:8])
    weight = jnp.where((row < taps - 1) & jnp.logical_not(own), weight, 0.0)
    through = jnp.where(own, 0.0, jnp.broadcast_to(jnp.exp(total), (8, heads)))
    both = jnp.concatenate([weight, through], axis=0)
    for start in range(0, width, CHUNK):
        wide = widen(both, start, CHUNK)
        weight_ref[:, start : start + CHUNK] = wide[:8]
        through_ref[:, start : start + CHUNK] = wide[8:]
    pad_ref[0:8] = jnp.zeros((8, pad_ref.shape[1]), F32)
    pad_ref[8:, :width] = x_ref[...].astype(F32)[:8]
    pad_ref[8:, width:] = bc_ref[...].astype(F32)[:8]

    def some(columns, base, w_ref, b_ref):
        here_columns = slice(base + columns.start, base + columns.stop)
        total = pad_ref[8:, here_columns] * w_ref[taps - 1 : taps, columns] + b_ref[columns].reshape(1, -1)
        for lag in range(1, taps):
            term = pad_ref[8 - lag : 16 - lag, here_columns] * w_ref[taps - 1 - lag : taps - lag, columns]
            total = total + jnp.where(inside[lag], term, 0.0)
        partial_ref[:, here_columns] = total

    for start in range(0, width, CHUNK):
        some(slice(start, start + CHUNK), 0, wx_ref, bx_ref)
    for start in range(0, bc_ref.shape[1], CHUNK):
        some(slice(start, start + CHUNK), width, wbc_ref, bbc_ref)


def first_rows(lines, partial_ref, inside_ref, w_ref, pad_ref, slot, at, start):
    taps = w_ref.shape[0]
    columns = slice(start, start + CHUNK)
    pad = pad_ref.at[slot]
    pad[4:8] = lines[:, at + start : at + start + CHUNK]
    pad[8:] = jnp.zeros((8, CHUNK), F32)
    total = partial_ref[:, at + start : at + start + CHUNK]
    for lag in range(1, taps):
        term = pad[8 - lag : 16 - lag] * w_ref[taps - 1 - lag : taps - lag, columns]
        total = total + term * inside_ref[lag - 1]
    return silu(total).astype(BF16)


def relay_first_kernel(fresh, *refs):
    message_ref, state_ref, partial_ref, weight_ref, through_ref, inside_ref, flag_ref, wx_ref, wbc_ref = refs[:9]
    other_ref = refs[9] if fresh else state_ref
    out_ref, pad_ref = refs[-2:]
    width = out_ref.shape[1]
    slots = pad_ref.shape[0]
    lines = tail_lines(message_ref, STATE)
    top = functools.partial(first_rows, lines, partial_ref, inside_ref)
    inputs = top(wbc_ref, pad_ref, 0, wx_ref.shape[1], 0)[:, :STATE]
    turned = inputs.astype(F32).T.astype(BF16)
    own = flag_ref[0, 0:1] > 0.5
    for start in range(0, width, CHUNK):
        columns = slice(start, start + CHUNK)
        xc = top(wx_ref, pad_ref, (start // CHUNK + 1) % slots, 0, start)
        weighted = (xc.astype(F32) * weight_ref[:, columns]).astype(BF16)
        full = state_ref[:STATE, columns].astype(F32) + jnp.dot(
            turned, weighted, preferred_element_type=F32
        )
        full = full + through_ref[0:1, columns] * message_ref[:STATE, columns].astype(F32)
        out_ref[:, columns] = jnp.where(own, other_ref[:STATE, columns].astype(F32), full).astype(BF16)


def relay_kernel(part, fresh, *refs):
    got_ref, state_ref, through_ref, flag_ref = refs[:4]
    out_ref = refs[-1]
    width = out_ref.shape[1]
    own = flag_ref[0, 0:1] > 0.5
    for start in range(0, width, CHUNK):
        columns = slice(start, start + CHUNK)
        through = through_ref[0:1, part * width + start : part * width + start + CHUNK]
        full = state_ref[:, columns].astype(F32) + through * got_ref[:STATE, columns].astype(F32)
        if fresh:
            full = jnp.where(own, refs[4][:STATE, columns].astype(F32), full)
        out_ref[:, columns] = full.astype(BF16)


def local_kernel(groups, *refs):
    (
        message_ref, partial_ref, weight_ref, inside_ref, wx_ref, wbc_ref, dt_ref, dt_bias_ref,
        a_log_ref, skip_ref, lens_ref, kv_ref,
    ) = refs[:12]
    xc_refs = refs[12 : 12 + groups]
    bcc_refs = refs[12 + groups : 12 + 2 * groups]
    state_refs = refs[12 + 2 * groups : 12 + 3 * groups]
    out_ref, c_ref, kv_out_ref = refs[12 + 3 * groups : 15 + 3 * groups]
    full_refs = refs[15 + 3 * groups : 15 + 4 * groups]
    pad_ref = refs[-1]
    rows, per_group = xc_refs[0].shape
    width = groups * per_group
    first = lax.axis_index("seq") * rows
    lines = tail_lines(message_ref, STATE)
    slots = pad_ref.shape[0]
    kv_out_ref[...] = kv_ref[...]

    def top(w_ref, slot, at, start, below):
        new = first_rows(lines, partial_ref, inside_ref, w_ref, pad_ref, slot, at, start)
        old = below[8:EDGE].astype(F32)
        return jnp.concatenate([jnp.concatenate([new.astype(F32), old], axis=0).astype(BF16), below[EDGE:]], axis=0)

    row = lax.broadcasted_iota(jnp.int32, (rows, rows), 0)
    column = lax.broadcasted_iota(jnp.int32, (rows, rows), 1)
    begin = doc_start(first + row, lens_ref)
    linked = (row >= column) & (first + column >= begin)
    step, running = rates(dt_ref, dt_bias_ref, a_log_ref)
    turned_running = running.T
    turned_step = step.T
    skip = skip_ref[...].reshape(1, -1)
    skip = jnp.broadcast_to(skip, (8, skip.shape[1]))
    pair_width = 2 * HDIM
    lane = lax.broadcasted_iota(jnp.int32, (rows, pair_width), 1)
    for group in range(groups):
        base = group * 2 * STATE
        pair = top(wbc_ref, group % slots, width, base, bcc_refs[group][...])
        inputs = pair[:, :STATE]
        outputs = pair[:, STATE:]
        c_ref[:, group * STATE : (group + 1) * STATE] = outputs
        turned = inputs[:EDGE].astype(F32).T[:, :8].astype(BF16)
        meet = lax.dot_general(
            outputs, inputs, (((1,), (1,)), ((), ())), preferred_element_type=F32
        )
        meet = jnp.where(linked, meet, 0.0)
        for chunk in range(0, per_group, CHUNK):
            at = group * per_group + chunk
            columns = slice(chunk, chunk + CHUNK)
            xc_all = top(wx_ref, (chunk // CHUNK) % slots, 0, at, xc_refs[group][:, columns])
            weighted = xc_all[:EDGE].astype(F32)[:8] * weight_ref[:, at : at + CHUNK]
            full = state_refs[group][:STATE, columns].astype(F32) + jnp.dot(
                turned, weighted.astype(BF16), preferred_element_type=F32
            )
            full_refs[group][:, columns] = full.astype(BF16)
            wide_skip = widen(skip, at, CHUNK)[0:1]
            for start in range(0, CHUNK, pair_width):
                parts = []
                for head in ((at + start) // HDIM, (at + start) // HDIM + 1):
                    spread = running[:, head : head + 1] - turned_running[head : head + 1]
                    decay = jnp.exp(jnp.minimum(spread, 0.0))
                    parts.append((decay * (meet * turned_step[head : head + 1])).astype(BF16))
                mix = jnp.concatenate(parts, axis=1)
                xc = xc_all[:, start : start + pair_width]
                zero = jnp.zeros_like(xc)
                stacked = jnp.concatenate(
                    [jnp.where(lane < HDIM, xc, zero), jnp.where(lane < HDIM, zero, xc)], axis=0
                )
                value = jnp.dot(mix, stacked, preferred_element_type=F32)
                out_ref[:, at + start : at + start + pair_width] = (
                    value + xc.astype(F32) * wide_skip[:, start : start + pair_width]
                )


def attend_kernel(hops, *refs):
    q_ref = refs[0]
    kv_refs = refs[1 : 2 + hops]
    lens_ref, out_ref = refs[2 + hops :]
    rows = q_ref.shape[0]
    kv_heads = kv_refs[0].shape[1] // (2 * ADIM)
    share = QHEADS // KVHEADS
    count = rows * (hops + 1)
    here = lax.axis_index("seq")
    row = here * rows + lax.broadcasted_iota(jnp.int32, (rows, count), 0)
    column = (here - hops) * rows + lax.broadcasted_iota(jnp.int32, (rows, count), 1)
    allowed = (column <= row) & (column >= doc_start(row, lens_ref))
    scale = ADIM ** (-0.5)
    ones = jnp.ones((count, ADIM), BF16)
    for head in range(kv_heads):
        low = head * ADIM
        keys = jnp.concatenate([ref[:, low : low + ADIM] for ref in kv_refs], axis=0)
        low = (kv_heads + head) * ADIM
        values = jnp.concatenate([ref[:, low : low + ADIM] for ref in kv_refs], axis=0)
        values = jnp.concatenate([values, ones], axis=1)
        for part in range(share):
            low = (head * share + part) * ADIM
            scores = lax.dot_general(
                q_ref[:, low : low + ADIM], keys, (((1,), (1,)), ((), ())), preferred_element_type=F32
            )
            scores = jnp.where(allowed, scores * scale, BARRED)
            expo = jnp.exp(scores - jnp.max(scores, axis=1, keepdims=True))
            summed = jnp.dot(expo.astype(BF16), values, preferred_element_type=F32)
            out_ref[:, low : low + ADIM] = (summed[:, :ADIM] / summed[:, ADIM:]).astype(BF16)


def norm_kernel(part, hops, *refs):
    mixed_ref, c_ref, entry_ref, z_ref, gain_ref, flag_ref = refs[:6]
    got_refs = refs[6 : 6 + hops]
    out_ref, gated_ref = refs[-2:]
    rows, width = gated_ref.shape
    heads = width // HDIM
    entry = entry_ref[:, part * heads : (part + 1) * heads]
    outputs = c_ref[:, part * STATE : (part + 1) * STATE]
    squares = jnp.zeros((rows, 1), F32)
    for start in range(0, width, CHUNK):
        columns = slice(start, start + CHUNK)
        placed = slice(part * width + start, part * width + start + CHUNK)
        state = got_refs[0][:STATE, columns].astype(F32)
        for hop in range(1, hops):
            there = flag_ref[hop, 0:1] > 0.5
            state = jnp.where(there, got_refs[hop][:STATE, columns].astype(F32), state)
        carried = jnp.dot(outputs, state.astype(BF16), preferred_element_type=F32)
        mixed = mixed_ref[:, placed] + carried * widen(entry, start, CHUNK)
        gated = mixed * silu(z_ref[:, placed].astype(F32))
        gated_ref[:, columns] = gated
        squares = squares + jnp.sum(gated * gated, axis=1, keepdims=True)
    multiplier = lax.rsqrt(squares * (1.0 / width) + EPSILON)
    for start in range(0, width, CHUNK):
        columns = slice(start, start + CHUNK)
        gain = gain_ref[part * width + start : part * width + start + CHUNK]
        out_ref[:, columns] = (gated_ref[:, columns] * multiplier * gain.reshape(1, -1)).astype(BF16)


WHOLE = pl.BlockSpec(memory_space=pltpu.VMEM)
SCALARS = pl.BlockSpec(memory_space=pltpu.SMEM)
UNTOUCHED = pl.BlockSpec(memory_space=pl.ANY)


def tile(rows, columns, row, column):
    return pl.BlockSpec((rows, columns), lambda step: (row, column))


def call(kernel, name, outs, operands, specs, out_specs=None, scratch=(), flops=KERNEL_FLOPS, aliases={}, limit=VMEM_LIMIT):
    moved = sum(math.prod(a.shape) * a.dtype.itemsize for a in (*operands, *outs))
    return pl.pallas_call(
        kernel,
        name=name,
        grid=(1,),
        out_shape=outs,
        in_specs=specs,
        out_specs=[WHOLE] * len(outs) if out_specs is None else out_specs,
        scratch_shapes=list(scratch),
        input_output_aliases=aliases,
        compiler_params=pltpu.CompilerParams(vmem_limit_bytes=limit),
        cost_estimate=pl.CostEstimate(flops=flops, bytes_accessed=moved, transcendentals=0),
    )(*operands)


def onward(value, first=0):
    count = lax.axis_size("seq")
    return lax.ppermute(value, "seq", [(source, source + 1) for source in range(first, count - 1)])


def shards(
    x_raw,
    bc_raw,
    z_gate,
    dt_raw,
    conv_x_weight,
    conv_x_bias,
    conv_bc_weight,
    conv_bc_bias,
    dt_bias,
    a_log,
    skip_d,
    norm_gain,
    queries,
    keys,
    values,
    doc_lens,
):
    rows, width = x_raw.shape
    bc_width = bc_raw.shape[1]
    heads = dt_raw.shape[1]
    groups = bc_width // (2 * STATE)
    per_group = width // groups
    count = lax.axis_size("seq")
    longest = rows * count // 2
    hops = min(count - 1, -(-(longest - 1) // rows))
    assert hops * rows >= longest and (hops <= 2 or groups == 1)
    shape = jax.ShapeDtypeStruct
    dt = dt_raw.T
    params = [dt, conv_x_weight, conv_x_bias, conv_bc_weight, conv_bc_bias, dt_bias, a_log]
    pieces = -(-(width + bc_width) // per_group)
    tail_rows = EDGE * -(-4 * pieces // EDGE)
    last_edge = rows // EDGE - 1

    xcs, bccs, states = [], [], []
    for part in range(groups):
        first_part, last_part = part == 0, part == groups - 1
        outs = [
            shape((rows, per_group), BF16),
            shape((rows, 2 * STATE), BF16),
            shape((STATE + tail_rows * first_part, per_group), BF16),
        ]
        operands = [x_raw, bc_raw, *params, doc_lens]
        specs = [tile(rows, per_group, 0, part), tile(rows, 2 * STATE, 0, part)] + [WHOLE] * 7 + [SCALARS]
        if first_part:
            operands += [x_raw, bc_raw]
            specs += [tile(EDGE, width, last_edge, 0), tile(EDGE, bc_width, last_edge, 0)]
        if last_part:
            outs.append(shape((rows, 2 * keys.shape[1]), BF16))
            operands += [keys, values]
            specs += [WHOLE] * 2
        got = call(
            functools.partial(state_kernel, part, first_part, last_part),
            f"state_part{part}",
            outs,
            operands,
            specs,
            scratch=[pltpu.VMEM((4, rows + 8, CHUNK), F32)],
            limit=VMEM_ALL if first_part else VMEM_LIMIT,
        )
        xcs.append(got[0])
        bccs.append(got[1])
        states.append(got[2])
    kvs = [got[3], onward(got[3])]
    slots = [onward(states[0])]

    partial, weight, through, inside, flags, entry = call(
        functools.partial(prepare_kernel, hops),
        "prepare",
        [
            shape((8, width + bc_width), F32),
            shape((8, width), F32),
            shape((8, width), F32),
            shape((conv_x_weight.shape[0] - 1, 8, CHUNK), F32),
            shape((hops, 8, CHUNK), F32),
            shape((rows, heads), F32),
        ],
        [x_raw, bc_raw, *params, doc_lens],
        [tile(EDGE, width, 0, 0), tile(EDGE, bc_width, 0, 0)] + [WHOLE] * 7 + [SCALARS],
        scratch=[pltpu.VMEM((16, width + bc_width), F32)],
    )

    fulls = None
    for slot in range(2, hops + groups):
        part = min(slot - 1, groups) - 1
        fresh = slot <= groups
        if slot == 2:
            kernel = functools.partial(relay_first_kernel, fresh)
            operands = [slots[0], states[0], partial, weight, through, inside, flags, conv_x_weight, conv_bc_weight]
            scratch = [pltpu.VMEM((4, 16, CHUNK), F32)]
        else:
            kernel = functools.partial(relay_kernel, part, fresh)
            operands = [slots[-1], fulls[part], through, flags]
            scratch = []
        if fresh:
            operands.append(states[slot - 1])
        (passed,) = call(
            kernel,
            f"relay_slot{slot}",
            [shape((STATE, per_group), BF16)],
            operands,
            [WHOLE] * len(operands),
            scratch=scratch,
        )
        slots.append(onward(passed, max(0, slot - groups)))
        if fulls is None:
            mixed, c_out, kv_on, *fulls = call(
                functools.partial(local_kernel, groups),
                "local_mix",
                [
                    shape((rows, width), F32),
                    shape((rows, groups * STATE), BF16),
                    shape(got[3].shape, BF16),
                    *(shape((STATE, per_group), BF16) for _ in range(groups)),
                ],
                [
                    slots[0], partial, weight, inside, conv_x_weight, conv_bc_weight, dt, dt_bias, a_log,
                    skip_d, doc_lens, kvs[1], *xcs, *bccs, *states,
                ],
                [WHOLE] * 10 + [SCALARS] + [WHOLE] * (1 + 3 * groups),
                scratch=[pltpu.VMEM((4, 16, CHUNK), F32)],
            )
    for hop in range(1, hops):
        kvs.append(onward(kv_on if hop == 1 else kvs[-1], hop))

    (attn_out,) = call(
        functools.partial(attend_kernel, hops),
        "attend",
        [shape(queries.shape, BF16)],
        [queries, *reversed(kvs), doc_lens],
        [WHOLE] * (hops + 2) + [SCALARS],
    )
    mamba_out = None
    for part in range(groups):
        operands = [mixed, c_out, entry, z_gate, norm_gain, flags, *slots[part : part + hops]]
        block = tile(rows, per_group, 0, part)
        specs = [WHOLE] * (6 + hops)
        aliases = {}
        if mamba_out is not None:
            operands.append(mamba_out)
            specs.append(UNTOUCHED)
            aliases = {len(operands) - 1: 0}
        (mamba_out,) = call(
            functools.partial(norm_kernel, part, hops),
            f"norm_part{part}",
            [shape((rows, width), BF16)],
            operands,
            specs,
            out_specs=[block],
            scratch=[pltpu.VMEM((rows, per_group), F32)],
            aliases=aliases,
        )
    return (mamba_out, attn_out)


def solution(mesh):
    split = P(("groups", "seq"), "dp")
    placed = (
        split,
        split,
        split,
        split,
        P(None, "dp"),
        P("dp"),
        P(None, "dp"),
        P("dp"),
        P("dp"),
        P("dp"),
        P("dp"),
        P("dp"),
        split,
        split,
        split,
        P("groups"),
    )
    return jax.shard_map(
        shards,
        mesh=mesh,
        in_specs=placed,
        out_specs=(split, split),
        check_vma=False,
    )
```

```python
import functools
import math

import jax
import jax.numpy as jnp
from jax import lax
from jax.experimental import pallas as pl
from jax.experimental.pallas import tpu as pltpu
from jax.sharding import PartitionSpec as P

HDIM = 64
STATE = 128
QHEADS = 32
KVHEADS = 8
ADIM = 128
EPSILON = 1e-05
BARRED = -2e30
HIGHEST = lax.Precision.HIGHEST
F32 = jnp.float32
BF16 = jnp.bfloat16
CHUNK = 256
EDGE = 16
KERNEL_FLOPS = 2 * 10**9
VMEM_LIMIT = 40 * 1024 * 1024
VMEM_ALL = 62 * 1024 * 1024


def silu(value):
    return value * (0.5 * jnp.tanh(0.5 * value) + 0.5)


def softplus(value):
    return jnp.maximum(value, 0.0) + jnp.log(1.0 + jnp.exp(-jnp.abs(value)))


def doc_start(positions, lens_ref):
    begin = jnp.int32(0)
    found = positions * 0
    for doc in range(lens_ref.shape[0]):
        found = jnp.where(positions >= begin, begin, found)
        begin = begin + lens_ref[doc]
    return found


def halves(value):
    high = value.astype(BF16)
    return high, (value - high.astype(F32)).astype(BF16)


def widen(per_head, first, width):
    heads = per_head.shape[1]
    both = jnp.concatenate(halves(per_head), axis=1)
    head = lax.broadcasted_iota(jnp.int32, (2 * heads, width), 0)
    head = jnp.where(head >= heads, head - heads, head)
    channel = lax.broadcasted_iota(jnp.int32, (2 * heads, width), 1) + first
    spread = (channel // HDIM == head).astype(F32).astype(BF16)
    return jnp.dot(both, spread, preferred_element_type=F32)


def rates(dt_ref, dt_bias_ref, a_log_ref):
    heads = dt_ref.shape[0]
    step = softplus(dt_ref[...].T + dt_bias_ref[...].reshape(1, -1)[:, :heads])
    rate = -step * jnp.exp(a_log_ref[...].reshape(1, -1)[:, :heads])
    rows = step.shape[0]
    row = lax.broadcasted_iota(jnp.int32, (rows, rows), 0)
    column = lax.broadcasted_iota(jnp.int32, (rows, rows), 1)
    lower = (row >= column).astype(F32).astype(BF16)
    high = rate.astype(BF16)
    middle, low = halves(rate - high.astype(F32))
    parts = jnp.concatenate([high, middle, low], axis=0)
    lowers = jnp.concatenate([lower, lower, lower], axis=1)
    return step, jnp.dot(lowers, parts, preferred_element_type=F32)


def insides(first, shape, taps, lens_ref):
    positions = first + lax.broadcasted_iota(jnp.int32, shape, 0)
    depth = positions - doc_start(positions, lens_ref)
    return [depth >= lag for lag in range(taps)]


def conv(pad, rows, weight, bias, inside):
    taps = weight.shape[0]
    total = pad[8 : 8 + rows] * weight[taps - 1 : taps] + bias
    for lag in range(1, taps):
        term = pad[8 - lag : 8 - lag + rows] * weight[taps - 1 - lag : taps - lag]
        total = total + jnp.where(inside[lag], term, 0.0)
    return silu(total).astype(BF16)


def state_weight(first, step, running, lens_ref):
    rows = step.shape[0]
    last_begin = doc_start(first + rows - 1, lens_ref)
    position = first + lax.broadcasted_iota(jnp.int32, step.shape, 0)
    return jnp.where(
        position >= last_begin, step * jnp.exp(running[rows - 1 : rows] - running), 0.0
    )


def tail_lines(message, rows):
    block = message[rows:].astype(F32)
    return jnp.concatenate([block[at : at + 4] for at in range(0, block.shape[0], 4)], axis=1)


def reach(device, rows, lens_ref):
    return device - doc_start((device + 1) * rows - 1, lens_ref) // rows


def kept_weight(here, step, running, taps, lens_ref):
    rows = step.shape[0]
    weight = state_weight(here * rows, step, running, lens_ref)
    row = lax.broadcasted_iota(jnp.int32, weight.shape, 0)
    return jnp.where((row >= taps - 1) | (reach(here, rows, lens_ref) == 0), weight, 0.0)


def conv_rows(pad, raw, weight, bias, inside):
    pad[0:8] = jnp.zeros((8, raw.shape[1]), F32)
    pad[8:] = raw.astype(F32)
    return conv(pad, raw.shape[0], weight, bias.reshape(1, -1), inside)


def first_state_kernel(*refs):
    hbm_refs, out_hbm_ref = refs[:10], refs[10]
    vmem_refs = refs[11:21]
    x_edge_ref, bc_edge_ref, out_ref, b_pad_ref, pad_ref, in_sems, out_sems = refs[21:]
    x_ref, b_ref, dt_ref, wx_ref, bx_ref, wbc_ref, bbc_ref, dt_bias_ref, a_log_ref, lens_ref = vmem_refs
    rows, width = x_ref.shape
    taps = wx_ref.shape[0]

    def corner(ref, shape):
        return ref.at[tuple(pl.ds(0, extent) for extent in shape)]

    order = (9, 2, 7, 8, 1, 5, 6, 0, 3, 4)
    copies = {}
    for at in order:
        source = corner(hbm_refs[at], vmem_refs[at].shape)
        copies[at] = pltpu.make_async_copy(source, vmem_refs[at], in_sems.at[at])
        copies[at].start()
    edge_copies = []
    for at, (source, target) in enumerate(((hbm_refs[0], x_edge_ref), (hbm_refs[1], bc_edge_ref))):
        edge_copies.append(
            pltpu.make_async_copy(source.at[pl.ds(rows - EDGE, EDGE)], target, in_sems.at[10 + at])
        )
        edge_copies[-1].start()

    here = lax.axis_index("seq")
    for at in (9, 2, 7, 8):
        copies[at].wait()
    inside = insides(here * rows, (rows, CHUNK), taps, lens_ref)
    step, running = rates(dt_ref, dt_bias_ref, a_log_ref)
    weight = kept_weight(here, step, running, taps, lens_ref)
    for at in (1, 5, 6):
        copies[at].wait()
    narrow = [mask[:, :STATE] for mask in inside]
    inputs = conv_rows(b_pad_ref, b_ref[...], wbc_ref[...], bbc_ref[...], narrow)
    turned = inputs.astype(F32).T.astype(BF16)
    for at in (0, 3, 4):
        copies[at].wait()
    slots = pad_ref.shape[0]
    outs = []

    def send(at, view):
        copy = pltpu.make_async_copy(out_ref.at[view], out_hbm_ref.at[view], out_sems.at[at])
        copy.start()
        outs.append(copy)

    for at, start in enumerate(range(0, width, CHUNK)):
        columns = slice(start, start + CHUNK)
        pad = pad_ref.at[(at + 1) % slots]
        xc = conv_rows(pad, x_ref[:, columns], wx_ref[:, columns], bx_ref[:, columns], inside)
        weighted = (xc.astype(F32) * widen(weight, start, CHUNK)).astype(BF16)
        out_ref[:STATE, columns] = jnp.dot(turned, weighted, preferred_element_type=F32).astype(BF16)
        send(at, (pl.ds(0, STATE), pl.ds(start, CHUNK)))
    for copy in edge_copies:
        copy.wait()
    edges = jnp.concatenate([x_edge_ref[...].astype(F32), bc_edge_ref[...].astype(F32)], axis=1)[EDGE - 4 :]
    spare = -edges.shape[1] % width
    if spare:
        edges = jnp.concatenate([edges, jnp.zeros((4, spare), F32)], axis=1)
    pieces = [edges[:, at : at + width] for at in range(0, edges.shape[1], width)]
    while len(pieces) % (EDGE // 4):
        pieces.append(jnp.zeros_like(pieces[0]))
    out_ref[STATE:] = jnp.concatenate(pieces, axis=0).astype(BF16)
    send(width // CHUNK, (pl.ds(STATE, out_ref.shape[0] - STATE), pl.ds(0, width)))
    for copy in outs:
        copy.wait()


def conv_kernel(groups, *refs):
    x_ref, bc_ref, dt_ref, wx_ref, bx_ref, wbc_ref, bbc_ref, dt_bias_ref, a_log_ref, lens_ref = refs[:10]
    keys_ref, values_ref, xc_ref, bcc_ref, kv_ref = refs[10:15]
    state_refs = refs[15:-1]
    pad_ref = refs[-1]
    rows, width = x_ref.shape
    per_group = width // groups
    heads = per_group // HDIM
    taps = wx_ref.shape[0]
    slots = pad_ref.shape[0]
    here = lax.axis_index("seq")
    kv_width = keys_ref.shape[1]
    kv_ref[:, :kv_width] = keys_ref[...]
    kv_ref[:, kv_width:] = values_ref[...]
    inside = insides(here * rows, (rows, CHUNK), taps, lens_ref)
    step, running = rates(dt_ref, dt_bias_ref, a_log_ref)
    weight = kept_weight(here, step, running, taps, lens_ref)
    for group in range(groups):
        base = slice(group * 2 * STATE, (group + 1) * 2 * STATE)
        pair = conv_rows(pad_ref.at[0], bc_ref[:, base], wbc_ref[:, base], bbc_ref[base], inside)
        bcc_ref[:, base] = pair
        turned = pair[:, :STATE].astype(F32).T.astype(BF16)
        part_weight = weight[:, group * heads : (group + 1) * heads]
        for chunk in range(0, per_group, CHUNK):
            columns = slice(group * per_group + chunk, group * per_group + chunk + CHUNK)
            pad = pad_ref.at[(chunk // CHUNK + 1) % slots]
            xc = conv_rows(pad, x_ref[:, columns], wx_ref[:, columns], bx_ref[columns], inside)
            xc_ref[:, columns] = xc
            if group:
                weighted = (xc.astype(F32) * widen(part_weight, chunk, CHUNK)).astype(BF16)
                state_refs[group - 1][:, chunk : chunk + CHUNK] = jnp.dot(
                    turned, weighted, preferred_element_type=F32
                ).astype(BF16)


def prepare_kernel(hops, *refs):
    x_ref, bc_ref, dt_ref, wx_ref, bx_ref, wbc_ref, bbc_ref, dt_bias_ref, a_log_ref, skip_ref, lens_ref = refs[:11]
    partial_ref, weight_ref, through_ref, inside_ref, flag_ref, entry_ref, wide_skip_ref, pad_ref = refs[11:]
    width = x_ref.shape[1]
    rows, heads = entry_ref.shape
    taps = wx_ref.shape[0]
    here = lax.axis_index("seq")
    first = here * rows
    own = reach(here, rows, lens_ref) == 0
    inside = insides(first, (8, CHUNK), taps, lens_ref)
    for lag in range(1, taps):
        inside_ref[lag - 1] = inside[lag].astype(F32)
    flag_ref[0] = jnp.broadcast_to(own.astype(F32), (8, CHUNK))
    before = reach(here - 1, rows, lens_ref)
    for hop in range(1, hops):
        flag_ref[hop] = jnp.broadcast_to((before == hop).astype(F32), (8, CHUNK))
    step, running = rates(dt_ref, dt_bias_ref, a_log_ref)
    position = first + lax.broadcasted_iota(jnp.int32, running.shape, 0)
    entry_ref[...] = jnp.where(doc_start(position, lens_ref) < first, jnp.exp(running), 0.0)
    row = lax.broadcasted_iota(jnp.int32, (8, heads), 0)
    total = running[rows - 1 : rows]
    weight = step[:8] * jnp.exp(total - running[:8])
    weight = jnp.where((row < taps - 1) & jnp.logical_not(own), weight, 0.0)
    through = jnp.where(own, 0.0, jnp.broadcast_to(jnp.exp(total), (8, heads)))
    skip = jnp.broadcast_to(skip_ref[...].reshape(1, -1), (8, heads))
    every = jnp.concatenate([weight, through, skip], axis=0)
    for start in range(0, width, CHUNK):
        wide = widen(every, start, CHUNK)
        weight_ref[:, start : start + CHUNK] = wide[:8]
        through_ref[:, start : start + CHUNK] = wide[8:16]
        wide_skip_ref[:, start : start + CHUNK] = wide[16:]
    pad_ref[0:8] = jnp.zeros((8, pad_ref.shape[1]), F32)
    pad_ref[8:, :width] = x_ref[...].astype(F32)[:8]
    pad_ref[8:, width:] = bc_ref[...].astype(F32)[:8]

    def some(columns, base, w_ref, b_ref):
        here_columns = slice(base + columns.start, base + columns.stop)
        total = pad_ref[8:, here_columns] * w_ref[taps - 1 : taps, columns] + b_ref[columns].reshape(1, -1)
        for lag in range(1, taps):
            term = pad_ref[8 - lag : 16 - lag, here_columns] * w_ref[taps - 1 - lag : taps - lag, columns]
            total = total + jnp.where(inside[lag], term, 0.0)
        partial_ref[:, here_columns] = total

    for start in range(0, width, CHUNK):
        some(slice(start, start + CHUNK), 0, wx_ref, bx_ref)
    for start in range(0, bc_ref.shape[1], CHUNK):
        some(slice(start, start + CHUNK), width, wbc_ref, bbc_ref)


def first_rows(lines, partial_ref, inside_ref, w_ref, pad_ref, slot, at, start):
    taps = w_ref.shape[0]
    columns = slice(start, start + CHUNK)
    pad = pad_ref.at[slot]
    pad[4:8] = lines[:, at + start : at + start + CHUNK]
    pad[8:] = jnp.zeros((8, CHUNK), F32)
    total = partial_ref[:, at + start : at + start + CHUNK]
    for lag in range(1, taps):
        term = pad[8 - lag : 16 - lag] * w_ref[taps - 1 - lag : taps - lag, columns]
        total = total + term * inside_ref[lag - 1]
    return silu(total).astype(BF16)


def relay_first_kernel(fresh, *refs):
    message_ref, state_ref, partial_ref, weight_ref, through_ref, inside_ref, flag_ref, wx_ref, wbc_ref = refs[:9]
    other_ref = refs[9] if fresh else state_ref
    out_ref, pad_ref = refs[-2:]
    width = out_ref.shape[1]
    slots = pad_ref.shape[0]
    lines = tail_lines(message_ref, STATE)
    top = functools.partial(first_rows, lines, partial_ref, inside_ref)
    inputs = top(wbc_ref, pad_ref, 0, wx_ref.shape[1], 0)[:, :STATE]
    turned = inputs.astype(F32).T.astype(BF16)
    own = flag_ref[0, 0:1] > 0.5
    for start in range(0, width, CHUNK):
        columns = slice(start, start + CHUNK)
        xc = top(wx_ref, pad_ref, (start // CHUNK + 1) % slots, 0, start)
        weighted = (xc.astype(F32) * weight_ref[:, columns]).astype(BF16)
        full = state_ref[:STATE, columns].astype(F32) + jnp.dot(
            turned, weighted, preferred_element_type=F32
        )
        full = full + through_ref[0:1, columns] * message_ref[:STATE, columns].astype(F32)
        out_ref[:, columns] = jnp.where(own, other_ref[:STATE, columns].astype(F32), full).astype(BF16)


def relay_kernel(part, fresh, *refs):
    got_ref, state_ref, through_ref, flag_ref = refs[:4]
    out_ref = refs[-1]
    width = out_ref.shape[1]
    own = flag_ref[0, 0:1] > 0.5
    for start in range(0, width, CHUNK):
        columns = slice(start, start + CHUNK)
        through = through_ref[0:1, part * width + start : part * width + start + CHUNK]
        full = state_ref[:, columns].astype(F32) + through * got_ref[:STATE, columns].astype(F32)
        if fresh:
            full = jnp.where(own, refs[4][:STATE, columns].astype(F32), full)
        out_ref[:, columns] = full.astype(BF16)


def local_kernel(groups, *refs):
    (
        message_ref, partial_ref, weight_ref, inside_ref, wx_ref, wbc_ref, dt_ref, dt_bias_ref,
        a_log_ref, wide_skip_ref, lens_ref, kv_ref, xc_ref, bcc_ref,
    ) = refs[:14]
    state_refs = refs[14 : 14 + groups]
    out_ref, c_ref, kv_out_ref = refs[14 + groups : 17 + groups]
    full_refs = refs[17 + groups : 17 + 2 * groups]
    pad_ref = refs[-1]
    rows, width = xc_ref.shape
    per_group = width // groups
    first = lax.axis_index("seq") * rows
    lines = tail_lines(message_ref, STATE)
    slots = pad_ref.shape[0]
    kv_out_ref[...] = kv_ref[...]

    def top(w_ref, slot, at, start, below):
        new = first_rows(lines, partial_ref, inside_ref, w_ref, pad_ref, slot, at, start)
        old = below[8:EDGE].astype(F32)
        return jnp.concatenate([jnp.concatenate([new.astype(F32), old], axis=0).astype(BF16), below[EDGE:]], axis=0)

    row = lax.broadcasted_iota(jnp.int32, (rows, rows), 0)
    column = lax.broadcasted_iota(jnp.int32, (rows, rows), 1)
    begin = doc_start(first + row, lens_ref)
    linked = (row >= column) & (first + column >= begin)
    step, running = rates(dt_ref, dt_bias_ref, a_log_ref)
    turned_running = running.T
    turned_step = step.T
    pair_width = 2 * HDIM
    lane = lax.broadcasted_iota(jnp.int32, (rows, pair_width), 1)
    for group in range(groups):
        base = group * 2 * STATE
        pair = top(wbc_ref, group % slots, width, base, bcc_ref[:, base : base + 2 * STATE])
        inputs = pair[:, :STATE]
        outputs = pair[:, STATE:]
        c_ref[:, group * STATE : (group + 1) * STATE] = outputs
        turned = inputs[:EDGE].astype(F32).T[:, :8].astype(BF16)
        meet = lax.dot_general(
            outputs, inputs, (((1,), (1,)), ((), ())), preferred_element_type=F32
        )
        meet = jnp.where(linked, meet, 0.0)
        for chunk in range(0, per_group, CHUNK):
            at = group * per_group + chunk
            columns = slice(chunk, chunk + CHUNK)
            xc_all = top(wx_ref, (chunk // CHUNK) % slots, 0, at, xc_ref[:, at : at + CHUNK])
            weighted = xc_all[:EDGE].astype(F32)[:8] * weight_ref[:, at : at + CHUNK]
            full = state_refs[group][:STATE, columns].astype(F32) + jnp.dot(
                turned, weighted.astype(BF16), preferred_element_type=F32
            )
            full_refs[group][:, columns] = full.astype(BF16)
            wide_skip = wide_skip_ref[0:1, at : at + CHUNK]
            for start in range(0, CHUNK, pair_width):
                parts = []
                for head in ((at + start) // HDIM, (at + start) // HDIM + 1):
                    spread = running[:, head : head + 1] - turned_running[head : head + 1]
                    decay = jnp.exp(jnp.minimum(spread, 0.0))
                    parts.append((decay * (meet * turned_step[head : head + 1])).astype(BF16))
                mix = jnp.concatenate(parts, axis=1)
                xc = xc_all[:, start : start + pair_width]
                zero = jnp.zeros_like(xc)
                stacked = jnp.concatenate(
                    [jnp.where(lane < HDIM, xc, zero), jnp.where(lane < HDIM, zero, xc)], axis=0
                )
                value = jnp.dot(mix, stacked, preferred_element_type=F32)
                out_ref[:, at + start : at + start + pair_width] = (
                    value + xc.astype(F32) * wide_skip[:, start : start + pair_width]
                )


def attend_kernel(hops, *refs):
    q_ref = refs[0]
    kv_refs = refs[1 : 2 + hops]
    lens_ref, out_ref = refs[2 + hops :]
    rows = q_ref.shape[0]
    kv_heads = kv_refs[0].shape[1] // (2 * ADIM)
    share = QHEADS // KVHEADS
    count = rows * (hops + 1)
    here = lax.axis_index("seq")
    row = here * rows + lax.broadcasted_iota(jnp.int32, (rows, count), 0)
    column = (here - hops) * rows + lax.broadcasted_iota(jnp.int32, (rows, count), 1)
    allowed = (column <= row) & (column >= doc_start(row, lens_ref))
    scale = ADIM ** (-0.5)
    ones = jnp.ones((count, ADIM), BF16)
    allowed = jnp.concatenate([allowed] * share, axis=0)
    for head in range(kv_heads):
        low = head * ADIM
        keys = jnp.concatenate([ref[:, low : low + ADIM] for ref in kv_refs], axis=0)
        low = (kv_heads + head) * ADIM
        values = jnp.concatenate([ref[:, low : low + ADIM] for ref in kv_refs], axis=0)
        values = jnp.concatenate([values, ones], axis=1)
        lows = [(head * share + part) * ADIM for part in range(share)]
        asking = jnp.concatenate([q_ref[:, low : low + ADIM] for low in lows], axis=0)
        scores = lax.dot_general(asking, keys, (((1,), (1,)), ((), ())), preferred_element_type=F32)
        scores = jnp.where(allowed, scores * scale, BARRED)
        expo = jnp.exp(scores - jnp.max(scores, axis=1, keepdims=True))
        summed = jnp.dot(expo.astype(BF16), values, preferred_element_type=F32)
        result = (summed[:, :ADIM] / summed[:, ADIM:]).astype(BF16)
        for part, low in enumerate(lows):
            out_ref[:, low : low + ADIM] = result[part * rows : (part + 1) * rows]


def norm_kernel(part, hops, *refs):
    mixed_ref, c_ref, entry_ref, z_ref, gain_ref, flag_ref = refs[:6]
    got_refs = refs[6 : 6 + hops]
    out_ref, gated_ref = refs[-2:]
    rows, width = gated_ref.shape
    heads = width // HDIM
    entry = entry_ref[:, part * heads : (part + 1) * heads]
    outputs = c_ref[:, part * STATE : (part + 1) * STATE]
    squares = jnp.zeros((rows, 1), F32)
    for start in range(0, width, CHUNK):
        columns = slice(start, start + CHUNK)
        placed = slice(part * width + start, part * width + start + CHUNK)
        state = got_refs[0][:STATE, columns].astype(F32)
        for hop in range(1, hops):
            there = flag_ref[hop, 0:1] > 0.5
            state = jnp.where(there, got_refs[hop][:STATE, columns].astype(F32), state)
        carried = jnp.dot(outputs, state.astype(BF16), preferred_element_type=F32)
        mixed = mixed_ref[:, placed] + carried * widen(entry, start, CHUNK)
        gated = mixed * silu(z_ref[:, placed].astype(F32))
        gated_ref[:, columns] = gated
        squares = squares + jnp.sum(gated * gated, axis=1, keepdims=True)
    multiplier = lax.rsqrt(squares * (1.0 / width) + EPSILON)
    for start in range(0, width, CHUNK):
        columns = slice(start, start + CHUNK)
        gain = gain_ref[part * width + start : part * width + start + CHUNK]
        out_ref[:, columns] = (gated_ref[:, columns] * multiplier * gain.reshape(1, -1)).astype(BF16)


WHOLE = pl.BlockSpec(memory_space=pltpu.VMEM)
SCALARS = pl.BlockSpec(memory_space=pltpu.SMEM)
UNTOUCHED = pl.BlockSpec(memory_space=pl.ANY)


def tile(rows, columns, row, column):
    return pl.BlockSpec((rows, columns), lambda step: (row, column))


def call(kernel, name, outs, operands, specs, out_specs=None, scratch=(), flops=KERNEL_FLOPS, aliases={}, limit=VMEM_LIMIT):
    moved = sum(math.prod(a.shape) * a.dtype.itemsize for a in (*operands, *outs))
    return pl.pallas_call(
        kernel,
        name=name,
        grid=(1,),
        out_shape=outs,
        in_specs=specs,
        out_specs=[WHOLE] * len(outs) if out_specs is None else out_specs,
        scratch_shapes=list(scratch),
        input_output_aliases=aliases,
        compiler_params=pltpu.CompilerParams(vmem_limit_bytes=limit),
        cost_estimate=pl.CostEstimate(flops=flops, bytes_accessed=moved, transcendentals=0),
    )(*operands)


def onward(value, first=0):
    count = lax.axis_size("seq")
    return lax.ppermute(value, "seq", [(source, source + 1) for source in range(first, count - 1)])


def shards(
    x_raw,
    bc_raw,
    z_gate,
    dt_raw,
    conv_x_weight,
    conv_x_bias,
    conv_bc_weight,
    conv_bc_bias,
    dt_bias,
    a_log,
    skip_d,
    norm_gain,
    queries,
    keys,
    values,
    doc_lens,
):
    rows, width = x_raw.shape
    bc_width = bc_raw.shape[1]
    heads = dt_raw.shape[1]
    groups = bc_width // (2 * STATE)
    per_group = width // groups
    count = lax.axis_size("seq")
    longest = rows * count // 2
    hops = min(count - 1, -(-(longest - 1) // rows))
    assert hops * rows >= longest and (hops <= 2 or groups == 1)
    shape = jax.ShapeDtypeStruct
    dt = dt_raw.T
    params = [dt, conv_x_weight, conv_x_bias, conv_bc_weight, conv_bc_bias, dt_bias, a_log]
    pieces = -(-(width + bc_width) // per_group)
    tail_rows = EDGE * -(-4 * pieces // EDGE)

    (message,) = call(
        first_state_kernel,
        "first_state",
        [shape((STATE + tail_rows, per_group), BF16)],
        [x_raw, bc_raw, *(a if a.ndim > 1 else a[None] for a in params), doc_lens],
        [UNTOUCHED] * 10,
        out_specs=[UNTOUCHED],
        scratch=[
            pltpu.VMEM((rows, per_group), BF16),
            pltpu.VMEM((rows, STATE), BF16),
            pltpu.VMEM((per_group // HDIM, rows), F32),
            pltpu.VMEM((conv_x_weight.shape[0], per_group), F32),
            pltpu.VMEM((1, per_group), F32),
            pltpu.VMEM((conv_x_weight.shape[0], STATE), F32),
            pltpu.VMEM((1, STATE), F32),
            pltpu.VMEM((1, heads), F32),
            pltpu.VMEM((1, heads), F32),
            pltpu.SMEM(doc_lens.shape, jnp.int32),
            pltpu.VMEM((EDGE, width), BF16),
            pltpu.VMEM((EDGE, bc_width), BF16),
            pltpu.VMEM((STATE + tail_rows, per_group), BF16),
            pltpu.VMEM((rows + 8, STATE), F32),
            pltpu.VMEM((4, rows + 8, CHUNK), F32),
            pltpu.SemaphoreType.DMA((12,)),
            pltpu.SemaphoreType.DMA((per_group // CHUNK + 1,)),
        ],
        limit=VMEM_ALL,
    )
    slots = [onward(message)]
    xc, bcc, kv, *states = call(
        functools.partial(conv_kernel, groups),
        "conv_all",
        [
            shape((rows, width), BF16),
            shape((rows, bc_width), BF16),
            shape((rows, 2 * keys.shape[1]), BF16),
            *(shape((STATE, per_group), BF16) for _ in range(groups - 1)),
        ],
        [x_raw, bc_raw, *params, doc_lens, keys, values],
        [WHOLE] * 9 + [SCALARS] + [WHOLE] * 2,
        scratch=[pltpu.VMEM((4, rows + 8, CHUNK), F32)],
    )
    states = [message, *states]
    kvs = [kv, onward(kv)]

    partial, weight, through, inside, flags, entry, wide_skip = call(
        functools.partial(prepare_kernel, hops),
        "prepare",
        [
            shape((8, width + bc_width), F32),
            shape((8, width), F32),
            shape((8, width), F32),
            shape((conv_x_weight.shape[0] - 1, 8, CHUNK), F32),
            shape((hops, 8, CHUNK), F32),
            shape((rows, heads), F32),
            shape((8, width), F32),
        ],
        [x_raw, bc_raw, *params, skip_d, doc_lens],
        [tile(EDGE, width, 0, 0), tile(EDGE, bc_width, 0, 0)] + [WHOLE] * 8 + [SCALARS],
        scratch=[pltpu.VMEM((16, width + bc_width), F32)],
    )

    fulls = None
    for slot in range(2, hops + groups):
        part = min(slot - 1, groups) - 1
        fresh = slot <= groups
        if slot == 2:
            kernel = functools.partial(relay_first_kernel, fresh)
            operands = [slots[0], states[0], partial, weight, through, inside, flags, conv_x_weight, conv_bc_weight]
            scratch = [pltpu.VMEM((4, 16, CHUNK), F32)]
        else:
            kernel = functools.partial(relay_kernel, part, fresh)
            operands = [slots[-1], fulls[part], through, flags]
            scratch = []
        if fresh:
            operands.append(states[slot - 1])
        (passed,) = call(
            kernel,
            f"relay_slot{slot}",
            [shape((STATE, per_group), BF16)],
            operands,
            [WHOLE] * len(operands),
            scratch=scratch,
        )
        slots.append(onward(passed, max(0, slot - groups)))
        if fulls is None:
            mixed, c_out, kv_on, *fulls = call(
                functools.partial(local_kernel, groups),
                "local_mix",
                [
                    shape((rows, width), F32),
                    shape((rows, groups * STATE), BF16),
                    shape(kv.shape, BF16),
                    *(shape((STATE, per_group), BF16) for _ in range(groups)),
                ],
                [
                    slots[0], partial, weight, inside, conv_x_weight, conv_bc_weight, dt, dt_bias, a_log,
                    wide_skip, doc_lens, kvs[1], xc, bcc, *states,
                ],
                [WHOLE] * 10 + [SCALARS] + [WHOLE] * (3 + groups),
                scratch=[pltpu.VMEM((4, 16, CHUNK), F32)],
            )
    for hop in range(1, hops):
        kvs.append(onward(kv_on if hop == 1 else kvs[-1], hop))

    (attn_out,) = call(
        functools.partial(attend_kernel, hops),
        "attend",
        [shape(queries.shape, BF16)],
        [queries, *reversed(kvs), doc_lens],
        [WHOLE] * (hops + 2) + [SCALARS],
    )
    mamba_out = None
    for part in range(groups):
        operands = [mixed, c_out, entry, z_gate, norm_gain, flags, *slots[part : part + hops]]
        block = tile(rows, per_group, 0, part)
        specs = [WHOLE] * (6 + hops)
        aliases = {}
        if mamba_out is not None:
            operands.append(mamba_out)
            specs.append(UNTOUCHED)
            aliases = {len(operands) - 1: 0}
        (mamba_out,) = call(
            functools.partial(norm_kernel, part, hops),
            f"norm_part{part}",
            [shape((rows, width), BF16)],
            operands,
            specs,
            out_specs=[block],
            scratch=[pltpu.VMEM((rows, per_group), F32)],
            aliases=aliases,
        )
    return (mamba_out, attn_out)


def solution(mesh):
    split = P(("groups", "seq"), "dp")
    placed = (
        split,
        split,
        split,
        split,
        P(None, "dp"),
        P("dp"),
        P(None, "dp"),
        P("dp"),
        P("dp"),
        P("dp"),
        P("dp"),
        P("dp"),
        split,
        split,
        split,
        P("groups"),
    )
    return jax.shard_map(
        shards,
        mesh=mesh,
        in_specs=placed,
        out_specs=(split, split),
        check_vma=False,
    )
```

```python
import functools
import math

import jax
import jax.numpy as jnp
from jax import lax
from jax.experimental import pallas as pl
from jax.experimental.pallas import tpu as pltpu
from jax.sharding import PartitionSpec as P

HDIM = 64
STATE = 128
QHEADS = 32
KVHEADS = 8
ADIM = 128
EPSILON = 1e-05
BARRED = -2e30
HIGHEST = lax.Precision.HIGHEST
F32 = jnp.float32
BF16 = jnp.bfloat16
CHUNK = 256
EDGE = 16
KERNEL_FLOPS = 2 * 10**9
VMEM_LIMIT = 40 * 1024 * 1024
VMEM_ALL = 62 * 1024 * 1024


def silu(value):
    return value * (0.5 * jnp.tanh(0.5 * value) + 0.5)


def softplus(value):
    return jnp.maximum(value, 0.0) + jnp.log(1.0 + jnp.exp(-jnp.abs(value)))


def doc_start(positions, lens_ref):
    begin = jnp.int32(0)
    found = positions * 0
    for doc in range(lens_ref.shape[0]):
        found = jnp.where(positions >= begin, begin, found)
        begin = begin + lens_ref[doc]
    return found


def halves(value):
    high = value.astype(BF16)
    return high, (value - high.astype(F32)).astype(BF16)


def widen(per_head, first, width):
    heads = per_head.shape[1]
    both = jnp.concatenate(halves(per_head), axis=1)
    head = lax.broadcasted_iota(jnp.int32, (2 * heads, width), 0)
    head = jnp.where(head >= heads, head - heads, head)
    channel = lax.broadcasted_iota(jnp.int32, (2 * heads, width), 1) + first
    spread = (channel // HDIM == head).astype(F32).astype(BF16)
    return jnp.dot(both, spread, preferred_element_type=F32)


def column(ref, heads):
    return jnp.broadcast_to(ref[...].reshape(1, -1), (8, ref.size)).T[:heads, 0:1]


def rates(dt_ref, dt_bias_ref, a_log_ref):
    heads, rows = dt_ref.shape
    step = softplus(dt_ref[...] + column(dt_bias_ref, heads))
    rate = -step * jnp.exp(column(a_log_ref, heads))
    row = lax.broadcasted_iota(jnp.int32, (rows, rows), 0)
    lane = lax.broadcasted_iota(jnp.int32, (rows, rows), 1)
    upper = (row <= lane).astype(F32).astype(BF16)
    high = rate.astype(BF16)
    middle, low = halves(rate - high.astype(F32))
    parts = jnp.concatenate([high, middle, low], axis=1)
    uppers = jnp.concatenate([upper, upper, upper], axis=0)
    return step, jnp.dot(parts, uppers, preferred_element_type=F32)


def insides(first, shape, taps, lens_ref):
    positions = first + lax.broadcasted_iota(jnp.int32, shape, 0)
    depth = positions - doc_start(positions, lens_ref)
    return [depth >= lag for lag in range(taps)]


def conv(pad, rows, weight, bias, inside):
    taps = weight.shape[0]
    total = pad[8 : 8 + rows] * weight[taps - 1 : taps] + bias
    for lag in range(1, taps):
        term = pad[8 - lag : 8 - lag + rows] * weight[taps - 1 - lag : taps - lag]
        total = total + jnp.where(inside[lag], term, 0.0)
    return silu(total).astype(BF16)


def tail_lines(message, rows):
    block = message[rows:].astype(F32)
    return jnp.concatenate([block[at : at + 4] for at in range(0, block.shape[0], 4)], axis=1)


def reach(device, rows, lens_ref):
    return device - doc_start((device + 1) * rows - 1, lens_ref) // rows


def kept_weight(here, step, running, taps, lens_ref):
    rows = step.shape[1]
    last_begin = doc_start((here + 1) * rows - 1, lens_ref)
    row = lax.broadcasted_iota(jnp.int32, step.shape, 1)
    weight = step * jnp.exp(running[:, rows - 1 : rows] - running)
    kept = (here * rows + row >= last_begin) & ((row >= taps - 1) | (last_begin // rows >= here))
    return jnp.where(kept, weight, 0.0).T


def conv_rows(pad, raw, weight, bias, inside):
    pad[0:8] = jnp.zeros((8, raw.shape[1]), F32)
    pad[8:] = raw.astype(F32)
    return conv(pad, raw.shape[0], weight, bias.reshape(1, -1), inside)


def first_state_kernel(*refs):
    hbm_refs, out_hbm_ref = refs[:10], refs[10]
    vmem_refs = refs[11:21]
    x_edge_ref, bc_edge_ref, out_ref, b_pad_ref, pad_ref, in_sems, out_sems = refs[21:]
    x_ref, b_ref, dt_ref, wx_ref, bx_ref, wbc_ref, bbc_ref, dt_bias_ref, a_log_ref, lens_ref = vmem_refs
    rows, width = x_ref.shape
    taps = wx_ref.shape[0]

    def corner(ref, shape):
        return ref.at[tuple(pl.ds(0, extent) for extent in shape)]

    order = (9, 2, 7, 8, 1, 5, 6, 0, 3, 4)
    copies = {}
    for at in order:
        source = corner(hbm_refs[at], vmem_refs[at].shape)
        copies[at] = pltpu.make_async_copy(source, vmem_refs[at], in_sems.at[at])
        copies[at].start()
    edge_copies = []
    for at, (source, target) in enumerate(((hbm_refs[0], x_edge_ref), (hbm_refs[1], bc_edge_ref))):
        edge_copies.append(
            pltpu.make_async_copy(source.at[pl.ds(rows - EDGE, EDGE)], target, in_sems.at[10 + at])
        )
        edge_copies[-1].start()

    here = lax.axis_index("seq")
    for at in order:
        copies[at].wait()
    inside = insides(here * rows, (rows, CHUNK), taps, lens_ref)
    step, running = rates(dt_ref, dt_bias_ref, a_log_ref)
    weight = kept_weight(here, step, running, taps, lens_ref)
    narrow = [mask[:, :STATE] for mask in inside]
    inputs = conv_rows(b_pad_ref, b_ref[...], wbc_ref[...], bbc_ref[...], narrow)
    turned = inputs.astype(F32).T.astype(BF16)
    slots = pad_ref.shape[0]
    outs = []

    def send(at, view):
        copy = pltpu.make_async_copy(out_ref.at[view], out_hbm_ref.at[view], out_sems.at[at])
        copy.start()
        outs.append(copy)

    for at, start in enumerate(range(0, width, CHUNK)):
        columns = slice(start, start + CHUNK)
        pad = pad_ref.at[(at + 1) % slots]
        xc = conv_rows(pad, x_ref[:, columns], wx_ref[:, columns], bx_ref[:, columns], inside)
        weighted = (xc.astype(F32) * widen(weight, start, CHUNK)).astype(BF16)
        out_ref[:STATE, columns] = jnp.dot(turned, weighted, preferred_element_type=F32).astype(BF16)
        if at % 2:
            send(at // 2, (pl.ds(0, STATE), pl.ds(start - CHUNK, 2 * CHUNK)))
    for copy in edge_copies:
        copy.wait()
    edges = jnp.concatenate([x_edge_ref[...].astype(F32), bc_edge_ref[...].astype(F32)], axis=1)[EDGE - 4 :]
    spare = -edges.shape[1] % width
    if spare:
        edges = jnp.concatenate([edges, jnp.zeros((4, spare), F32)], axis=1)
    pieces = [edges[:, at : at + width] for at in range(0, edges.shape[1], width)]
    while len(pieces) % (EDGE // 4):
        pieces.append(jnp.zeros_like(pieces[0]))
    out_ref[STATE:] = jnp.concatenate(pieces, axis=0).astype(BF16)
    send(width // (2 * CHUNK), (pl.ds(STATE, out_ref.shape[0] - STATE), pl.ds(0, width)))
    for copy in outs:
        copy.wait()


def conv_kernel(groups, *refs):
    x_ref, bc_ref, dt_ref, wx_ref, bx_ref, wbc_ref, bbc_ref, dt_bias_ref, a_log_ref, lens_ref = refs[:10]
    keys_ref, values_ref, xc_ref, bcc_ref, kv_ref = refs[10:15]
    state_refs = refs[15:-1]
    pad_ref = refs[-1]
    rows, width = x_ref.shape
    per_group = width // groups
    heads = per_group // HDIM
    taps = wx_ref.shape[0]
    slots = pad_ref.shape[0]
    here = lax.axis_index("seq")
    kv_width = keys_ref.shape[1]
    kv_ref[:, :kv_width] = keys_ref[...]
    kv_ref[:, kv_width:] = values_ref[...]
    inside = insides(here * rows, (rows, CHUNK), taps, lens_ref)
    step, running = rates(dt_ref, dt_bias_ref, a_log_ref)
    weight = kept_weight(here, step, running, taps, lens_ref)
    for group in range(groups):
        base = slice(group * 2 * STATE, (group + 1) * 2 * STATE)
        pair = conv_rows(pad_ref.at[0], bc_ref[:, base], wbc_ref[:, base], bbc_ref[base], inside)
        bcc_ref[:, base] = pair
        turned = pair[:, :STATE].astype(F32).T.astype(BF16)
        part_weight = weight[:, group * heads : (group + 1) * heads]
        for chunk in range(0, per_group, CHUNK):
            columns = slice(group * per_group + chunk, group * per_group + chunk + CHUNK)
            pad = pad_ref.at[(chunk // CHUNK + 1) % slots]
            xc = conv_rows(pad, x_ref[:, columns], wx_ref[:, columns], bx_ref[columns], inside)
            xc_ref[:, columns] = xc
            if group:
                weighted = (xc.astype(F32) * widen(part_weight, chunk, CHUNK)).astype(BF16)
                state_refs[group - 1][:, chunk : chunk + CHUNK] = jnp.dot(
                    turned, weighted, preferred_element_type=F32
                ).astype(BF16)


def prepare_kernel(hops, *refs):
    x_ref, bc_ref, dt_ref, wx_ref, bx_ref, wbc_ref, bbc_ref, dt_bias_ref, a_log_ref, skip_ref, lens_ref = refs[:11]
    partial_ref, weight_ref, through_ref, inside_ref, flag_ref, entry_ref, wide_skip_ref, begin_ref, pad_ref = refs[11:]
    width = x_ref.shape[1]
    rows, heads = entry_ref.shape
    taps = wx_ref.shape[0]
    here = lax.axis_index("seq")
    first = here * rows
    own = reach(here, rows, lens_ref) == 0
    inside = insides(first, (8, CHUNK), taps, lens_ref)
    for lag in range(1, taps):
        inside_ref[lag - 1] = inside[lag].astype(F32)
    flag_ref[0] = jnp.broadcast_to(own.astype(F32), (8, CHUNK))
    before = reach(here - 1, rows, lens_ref)
    for hop in range(1, hops):
        flag_ref[hop] = jnp.broadcast_to((before == hop).astype(F32), (8, CHUNK))
    step, running = rates(dt_ref, dt_bias_ref, a_log_ref)
    begin = doc_start(first + lax.broadcasted_iota(jnp.int32, begin_ref.shape, 0), lens_ref)
    begin_ref[...] = begin
    turned = running.T
    entry_ref[...] = jnp.where(begin[:, :heads] < first, jnp.exp(turned), 0.0)
    row = lax.broadcasted_iota(jnp.int32, (8, heads), 0)
    total = turned[rows - 1 : rows]
    weight = step.T[:8] * jnp.exp(total - turned[:8])
    weight = jnp.where((row < taps - 1) & jnp.logical_not(own), weight, 0.0)
    through = jnp.where(own, 0.0, jnp.broadcast_to(jnp.exp(total), (8, heads)))
    skip = jnp.broadcast_to(skip_ref[...].reshape(1, -1), (8, heads))
    every = jnp.concatenate([weight, through, skip], axis=0)
    for start in range(0, width, CHUNK):
        wide = widen(every, start, CHUNK)
        weight_ref[:, start : start + CHUNK] = wide[:8]
        through_ref[:, start : start + CHUNK] = wide[8:16]
        wide_skip_ref[:, start : start + CHUNK] = wide[16:]
    pad_ref[0:8] = jnp.zeros((8, pad_ref.shape[1]), F32)
    pad_ref[8:, :width] = x_ref[...].astype(F32)[:8]
    pad_ref[8:, width:] = bc_ref[...].astype(F32)[:8]

    def some(columns, base, w_ref, b_ref):
        here_columns = slice(base + columns.start, base + columns.stop)
        total = pad_ref[8:, here_columns] * w_ref[taps - 1 : taps, columns] + b_ref[columns].reshape(1, -1)
        for lag in range(1, taps):
            term = pad_ref[8 - lag : 16 - lag, here_columns] * w_ref[taps - 1 - lag : taps - lag, columns]
            total = total + jnp.where(inside[lag], term, 0.0)
        partial_ref[:, here_columns] = total

    for start in range(0, width, CHUNK):
        some(slice(start, start + CHUNK), 0, wx_ref, bx_ref)
    for start in range(0, bc_ref.shape[1], CHUNK):
        some(slice(start, start + CHUNK), width, wbc_ref, bbc_ref)


def first_rows(lines, partial_ref, inside_ref, w_ref, pad_ref, slot, at, start):
    taps = w_ref.shape[0]
    columns = slice(start, start + CHUNK)
    pad = pad_ref.at[slot]
    pad[4:8] = lines[:, at + start : at + start + CHUNK]
    pad[8:] = jnp.zeros((8, CHUNK), F32)
    total = partial_ref[:, at + start : at + start + CHUNK]
    for lag in range(1, taps):
        term = pad[8 - lag : 16 - lag] * w_ref[taps - 1 - lag : taps - lag, columns]
        total = total + term * inside_ref[lag - 1]
    return silu(total).astype(BF16)


def relay_first_kernel(fresh, *refs):
    message_ref, state_ref, partial_ref, weight_ref, through_ref, inside_ref, flag_ref, wx_ref, wbc_ref = refs[:9]
    other_ref = refs[9] if fresh else state_ref
    out_ref, pad_ref = refs[-2:]
    width = out_ref.shape[1]
    slots = pad_ref.shape[0]
    lines = tail_lines(message_ref, STATE)
    top = functools.partial(first_rows, lines, partial_ref, inside_ref)
    inputs = top(wbc_ref, pad_ref, 0, wx_ref.shape[1], 0)[:, :STATE]
    turned = inputs.astype(F32).T.astype(BF16)
    own = flag_ref[0, 0:1] > 0.5
    for start in range(0, width, CHUNK):
        columns = slice(start, start + CHUNK)
        xc = top(wx_ref, pad_ref, (start // CHUNK + 1) % slots, 0, start)
        weighted = (xc.astype(F32) * weight_ref[:, columns]).astype(BF16)
        full = state_ref[:STATE, columns].astype(F32) + jnp.dot(
            turned, weighted, preferred_element_type=F32
        )
        full = full + through_ref[0:1, columns] * message_ref[:STATE, columns].astype(F32)
        out_ref[:, columns] = jnp.where(own, other_ref[:STATE, columns].astype(F32), full).astype(BF16)


def relay_kernel(part, fresh, *refs):
    got_ref, state_ref, through_ref, flag_ref = refs[:4]
    out_ref = refs[-1]
    width = out_ref.shape[1]
    own = flag_ref[0, 0:1] > 0.5
    for start in range(0, width, CHUNK):
        columns = slice(start, start + CHUNK)
        through = through_ref[0:1, part * width + start : part * width + start + CHUNK]
        full = state_ref[:, columns].astype(F32) + through * got_ref[:STATE, columns].astype(F32)
        if fresh:
            full = jnp.where(own, refs[4][:STATE, columns].astype(F32), full)
        out_ref[:, columns] = full.astype(BF16)


def local_kernel(groups, *refs):
    (
        message_ref, partial_ref, weight_ref, inside_ref, wx_ref, wbc_ref, dt_ref, dt_bias_ref,
        a_log_ref, wide_skip_ref, begin_ref, xc_ref, bcc_ref,
    ) = refs[:13]
    state_refs = refs[13 : 13 + groups]
    out_ref, c_ref = refs[13 + groups : 15 + groups]
    full_refs = refs[15 + groups : 15 + 2 * groups]
    pad_ref = refs[-1]
    rows, width = xc_ref.shape
    per_group = width // groups
    first = lax.axis_index("seq") * rows
    lines = tail_lines(message_ref, STATE)
    slots = pad_ref.shape[0]

    def top(w_ref, slot, at, start, below):
        new = first_rows(lines, partial_ref, inside_ref, w_ref, pad_ref, slot, at, start)
        old = below[8:EDGE].astype(F32)
        return jnp.concatenate([jnp.concatenate([new.astype(F32), old], axis=0).astype(BF16), below[EDGE:]], axis=0)

    row = lax.broadcasted_iota(jnp.int32, (rows, rows), 0)
    lane_row = lax.broadcasted_iota(jnp.int32, (rows, rows), 1)
    linked = (row >= lane_row) & (first + lane_row >= begin_ref[...])
    turned_step, turned_running = rates(dt_ref, dt_bias_ref, a_log_ref)
    running = turned_running.T
    pair_width = 2 * HDIM
    lane = lax.broadcasted_iota(jnp.int32, (rows, pair_width), 1)
    for group in range(groups):
        base = group * 2 * STATE
        pair = top(wbc_ref, group % slots, width, base, bcc_ref[:, base : base + 2 * STATE])
        inputs = pair[:, :STATE]
        outputs = pair[:, STATE:]
        c_ref[:, group * STATE : (group + 1) * STATE] = outputs
        turned = inputs[:EDGE].astype(F32).T[:, :8].astype(BF16)
        meet = lax.dot_general(
            outputs, inputs, (((1,), (1,)), ((), ())), preferred_element_type=F32
        )
        meet = jnp.where(linked, meet, 0.0)
        for chunk in range(0, per_group, CHUNK):
            at = group * per_group + chunk
            columns = slice(chunk, chunk + CHUNK)
            xc_all = top(wx_ref, (chunk // CHUNK) % slots, 0, at, xc_ref[:, at : at + CHUNK])
            weighted = xc_all[:EDGE].astype(F32)[:8] * weight_ref[:, at : at + CHUNK]
            full = state_refs[group][:STATE, columns].astype(F32) + jnp.dot(
                turned, weighted.astype(BF16), preferred_element_type=F32
            )
            full_refs[group][:, columns] = full.astype(BF16)
            wide_skip = wide_skip_ref[0:1, at : at + CHUNK]
            for start in range(0, CHUNK, pair_width):
                parts = []
                for head in ((at + start) // HDIM, (at + start) // HDIM + 1):
                    spread = running[:, head : head + 1] - turned_running[head : head + 1]
                    decay = jnp.exp(jnp.minimum(spread, 0.0))
                    parts.append((decay * (meet * turned_step[head : head + 1])).astype(BF16))
                mix = jnp.concatenate(parts, axis=1)
                xc = xc_all[:, start : start + pair_width]
                zero = jnp.zeros_like(xc)
                stacked = jnp.concatenate(
                    [jnp.where(lane < HDIM, xc, zero), jnp.where(lane < HDIM, zero, xc)], axis=0
                )
                value = jnp.dot(mix, stacked, preferred_element_type=F32)
                out_ref[:, at + start : at + start + pair_width] = (
                    value + xc.astype(F32) * wide_skip[:, start : start + pair_width]
                )


def attend_kernel(hops, *refs):
    q_ref = refs[0]
    kv_refs = refs[1 : 2 + hops]
    begin_ref, out_hbm_ref, out_ref, sems = refs[2 + hops :]
    rows = q_ref.shape[0]
    kv_heads = kv_refs[0].shape[1] // (2 * ADIM)
    share = QHEADS // KVHEADS
    count = rows * (hops + 1)
    here = lax.axis_index("seq")
    row = here * rows + lax.broadcasted_iota(jnp.int32, (rows, count), 0)
    column = (here - hops) * rows + lax.broadcasted_iota(jnp.int32, (rows, count), 1)
    begin = jnp.concatenate([begin_ref[...]] * (hops + 1), axis=1)
    allowed = (column <= row) & (column >= begin)
    scale = ADIM ** (-0.5)
    ones = jnp.ones((count, ADIM), BF16)
    allowed = jnp.concatenate([allowed] * share, axis=0)
    copies = []
    for head in range(kv_heads):
        low = head * ADIM
        keys = jnp.concatenate([ref[:, low : low + ADIM] for ref in kv_refs], axis=0)
        low = (kv_heads + head) * ADIM
        values = jnp.concatenate([ref[:, low : low + ADIM] for ref in kv_refs], axis=0)
        values = jnp.concatenate([values, ones], axis=1)
        lows = [(head * share + part) * ADIM for part in range(share)]
        asking = jnp.concatenate([q_ref[:, low : low + ADIM] for low in lows], axis=0)
        scores = lax.dot_general(asking, keys, (((1,), (1,)), ((), ())), preferred_element_type=F32)
        scores = jnp.where(allowed, scores * scale, BARRED)
        expo = jnp.exp(scores - jnp.max(scores, axis=1, keepdims=True))
        summed = jnp.dot(expo.astype(BF16), values, preferred_element_type=F32)
        result = (summed[:, :ADIM] / summed[:, ADIM:]).astype(BF16)
        for part, low in enumerate(lows):
            out_ref[:, low : low + ADIM] = result[part * rows : (part + 1) * rows]
        columns = pl.ds(head * share * ADIM, share * ADIM)
        copies.append(
            pltpu.make_async_copy(out_ref.at[:, columns], out_hbm_ref.at[:, columns], sems.at[head])
        )
        copies[-1].start()
    for copy in copies:
        copy.wait()


def norm_kernel(part, hops, *refs):
    mixed_ref, c_ref, entry_ref, z_ref, gain_ref, flag_ref = refs[:6]
    got_refs = refs[6 : 6 + hops]
    out_hbm_ref, gated_ref, out_ref, sems = refs[-4:]
    rows, width = gated_ref.shape
    heads = width // HDIM
    entry = entry_ref[:, part * heads : (part + 1) * heads]
    outputs = c_ref[:, part * STATE : (part + 1) * STATE]
    squares = jnp.zeros((rows, 1), F32)
    for start in range(0, width, CHUNK):
        columns = slice(start, start + CHUNK)
        placed = slice(part * width + start, part * width + start + CHUNK)
        state = got_refs[0][:STATE, columns].astype(F32)
        for hop in range(1, hops):
            there = flag_ref[hop, 0:1] > 0.5
            state = jnp.where(there, got_refs[hop][:STATE, columns].astype(F32), state)
        carried = jnp.dot(outputs, state.astype(BF16), preferred_element_type=F32)
        mixed = mixed_ref[:, placed] + carried * widen(entry, start, CHUNK)
        gated = mixed * silu(z_ref[:, placed].astype(F32))
        gated_ref[:, columns] = gated
        squares = squares + jnp.sum(gated * gated, axis=1, keepdims=True)
    multiplier = lax.rsqrt(squares * (1.0 / width) + EPSILON)
    copies = []
    for start in range(0, width, CHUNK):
        columns = slice(start, start + CHUNK)
        gain = gain_ref[part * width + start : part * width + start + CHUNK]
        out_ref[:, columns] = (gated_ref[:, columns] * multiplier * gain.reshape(1, -1)).astype(BF16)
        copies.append(
            pltpu.make_async_copy(
                out_ref.at[:, pl.ds(start, CHUNK)],
                out_hbm_ref.at[:, pl.ds(part * width + start, CHUNK)],
                sems.at[start // CHUNK],
            )
        )
        copies[-1].start()
    for copy in copies:
        copy.wait()


WHOLE = pl.BlockSpec(memory_space=pltpu.VMEM)
SCALARS = pl.BlockSpec(memory_space=pltpu.SMEM)
UNTOUCHED = pl.BlockSpec(memory_space=pl.ANY)


def tile(rows, columns, row, column):
    return pl.BlockSpec((rows, columns), lambda step: (row, column))


def call(kernel, name, outs, operands, specs, out_specs=None, scratch=(), flops=KERNEL_FLOPS, aliases={}, limit=VMEM_LIMIT):
    moved = sum(math.prod(a.shape) * a.dtype.itemsize for a in (*operands, *outs))
    return pl.pallas_call(
        kernel,
        name=name,
        grid=(1,),
        out_shape=outs,
        in_specs=specs,
        out_specs=[WHOLE] * len(outs) if out_specs is None else out_specs,
        scratch_shapes=list(scratch),
        input_output_aliases=aliases,
        compiler_params=pltpu.CompilerParams(vmem_limit_bytes=limit),
        cost_estimate=pl.CostEstimate(flops=flops, bytes_accessed=moved, transcendentals=0),
    )(*operands)


def onward(value, first=0):
    count = lax.axis_size("seq")
    return lax.ppermute(value, "seq", [(source, source + 1) for source in range(first, count - 1)])


def shards(
    x_raw,
    bc_raw,
    z_gate,
    dt_raw,
    conv_x_weight,
    conv_x_bias,
    conv_bc_weight,
    conv_bc_bias,
    dt_bias,
    a_log,
    skip_d,
    norm_gain,
    queries,
    keys,
    values,
    doc_lens,
):
    rows, width = x_raw.shape
    bc_width = bc_raw.shape[1]
    heads = dt_raw.shape[1]
    groups = bc_width // (2 * STATE)
    per_group = width // groups
    count = lax.axis_size("seq")
    longest = rows * count // 2
    hops = min(count - 1, -(-(longest - 1) // rows))
    assert hops * rows >= longest and (hops <= 2 or groups == 1)
    shape = jax.ShapeDtypeStruct
    dt = dt_raw.T
    params = [dt, conv_x_weight, conv_x_bias, conv_bc_weight, conv_bc_bias, dt_bias, a_log]
    pieces = -(-(width + bc_width) // per_group)
    tail_rows = EDGE * -(-4 * pieces // EDGE)

    (message,) = call(
        first_state_kernel,
        "first_state",
        [shape((STATE + tail_rows, per_group), BF16)],
        [x_raw, bc_raw, *(a if a.ndim > 1 else a[None] for a in params), doc_lens],
        [UNTOUCHED] * 10,
        out_specs=[UNTOUCHED],
        scratch=[
            pltpu.VMEM((rows, per_group), BF16),
            pltpu.VMEM((rows, STATE), BF16),
            pltpu.VMEM((per_group // HDIM, rows), F32),
            pltpu.VMEM((conv_x_weight.shape[0], per_group), F32),
            pltpu.VMEM((1, per_group), F32),
            pltpu.VMEM((conv_x_weight.shape[0], STATE), F32),
            pltpu.VMEM((1, STATE), F32),
            pltpu.VMEM((1, heads), F32),
            pltpu.VMEM((1, heads), F32),
            pltpu.SMEM(doc_lens.shape, jnp.int32),
            pltpu.VMEM((EDGE, width), BF16),
            pltpu.VMEM((EDGE, bc_width), BF16),
            pltpu.VMEM((STATE + tail_rows, per_group), BF16),
            pltpu.VMEM((rows + 8, STATE), F32),
            pltpu.VMEM((4, rows + 8, CHUNK), F32),
            pltpu.SemaphoreType.DMA((12,)),
            pltpu.SemaphoreType.DMA((per_group // (2 * CHUNK) + 1,)),
        ],
        limit=VMEM_ALL,
    )
    slots = [onward(message)]
    xc, bcc, kv, *states = call(
        functools.partial(conv_kernel, groups),
        "conv_all",
        [
            shape((rows, width), BF16),
            shape((rows, bc_width), BF16),
            shape((rows, 2 * keys.shape[1]), BF16),
            *(shape((STATE, per_group), BF16) for _ in range(groups - 1)),
        ],
        [x_raw, bc_raw, *params, doc_lens, keys, values],
        [WHOLE] * 9 + [SCALARS] + [WHOLE] * 2,
        scratch=[pltpu.VMEM((4, rows + 8, CHUNK), F32)],
    )
    states = [message, *states]
    kvs = [kv, onward(kv)]

    partial, weight, through, inside, flags, entry, wide_skip, begin = call(
        functools.partial(prepare_kernel, hops),
        "prepare",
        [
            shape((8, width + bc_width), F32),
            shape((8, width), F32),
            shape((8, width), F32),
            shape((conv_x_weight.shape[0] - 1, 8, CHUNK), F32),
            shape((hops, 8, CHUNK), F32),
            shape((rows, heads), F32),
            shape((8, width), F32),
            shape((rows, rows), jnp.int32),
        ],
        [x_raw, bc_raw, *params, skip_d, doc_lens],
        [tile(EDGE, width, 0, 0), tile(EDGE, bc_width, 0, 0)] + [WHOLE] * 8 + [SCALARS],
        scratch=[pltpu.VMEM((16, width + bc_width), F32)],
    )

    fulls = None
    for slot in range(2, hops + groups):
        part = min(slot - 1, groups) - 1
        fresh = slot <= groups
        if slot == 2:
            kernel = functools.partial(relay_first_kernel, fresh)
            operands = [slots[0], states[0], partial, weight, through, inside, flags, conv_x_weight, conv_bc_weight]
            scratch = [pltpu.VMEM((4, 16, CHUNK), F32)]
        else:
            kernel = functools.partial(relay_kernel, part, fresh)
            operands = [slots[-1], fulls[part], through, flags]
            scratch = []
        if fresh:
            operands.append(states[slot - 1])
        (passed,) = call(
            kernel,
            f"relay_slot{slot}",
            [shape((STATE, per_group), BF16)],
            operands,
            [WHOLE] * len(operands),
            scratch=scratch,
        )
        slots.append(onward(passed, max(0, slot - groups)))
        if fulls is None:
            mixed, c_out, *fulls = call(
                functools.partial(local_kernel, groups),
                "local_mix",
                [
                    shape((rows, width), F32),
                    shape((rows, groups * STATE), BF16),
                    *(shape((STATE, per_group), BF16) for _ in range(groups)),
                ],
                [
                    slots[0], partial, weight, inside, conv_x_weight, conv_bc_weight, dt, dt_bias, a_log,
                    wide_skip, begin, xc, bcc, *states,
                ],
                [WHOLE] * (13 + groups),
                scratch=[pltpu.VMEM((4, 16, CHUNK), F32)],
            )
    for hop in range(1, hops):
        kvs.append(onward(kvs[-1], hop))

    (attn_out,) = call(
        functools.partial(attend_kernel, hops),
        "attend",
        [shape(queries.shape, BF16)],
        [queries, *reversed(kvs), begin],
        [WHOLE] * (hops + 3),
        out_specs=[UNTOUCHED],
        scratch=[
            pltpu.VMEM(queries.shape, BF16),
            pltpu.SemaphoreType.DMA((keys.shape[1] // ADIM,)),
        ],
    )
    mamba_out = None
    for part in range(groups):
        operands = [mixed, c_out, entry, z_gate, norm_gain, flags, *slots[part : part + hops]]
        specs = [WHOLE] * (6 + hops)
        aliases = {}
        if mamba_out is not None:
            operands.append(mamba_out)
            specs.append(UNTOUCHED)
            aliases = {len(operands) - 1: 0}
        (mamba_out,) = call(
            functools.partial(norm_kernel, part, hops),
            f"norm_part{part}",
            [shape((rows, width), BF16)],
            operands,
            specs,
            out_specs=[UNTOUCHED],
            scratch=[
                pltpu.VMEM((rows, per_group), F32),
                pltpu.VMEM((rows, per_group), BF16),
                pltpu.SemaphoreType.DMA((per_group // CHUNK,)),
            ],
            aliases=aliases,
        )
    return (mamba_out, attn_out)


def solution(mesh):
    split = P(("groups", "seq"), "dp")
    placed = (
        split,
        split,
        split,
        split,
        P(None, "dp"),
        P("dp"),
        P(None, "dp"),
        P("dp"),
        P("dp"),
        P("dp"),
        P("dp"),
        P("dp"),
        split,
        split,
        split,
        P("groups"),
    )
    return jax.shard_map(
        shards,
        mesh=mesh,
        in_specs=placed,
        out_specs=(split, split),
        check_vma=False,
    )
```

```python
import functools
import math

import jax
import jax.numpy as jnp
from jax import lax
from jax.experimental import pallas as pl
from jax.experimental.pallas import tpu as pltpu
from jax.sharding import PartitionSpec as P

HDIM = 64
STATE = 128
QHEADS = 32
KVHEADS = 8
ADIM = 128
EPSILON = 1e-05
BARRED = -2e30
HIGHEST = lax.Precision.HIGHEST
F32 = jnp.float32
BF16 = jnp.bfloat16
CHUNK = 256
EDGE = 16
KERNEL_FLOPS = 2 * 10**9
VMEM_LIMIT = 40 * 1024 * 1024
VMEM_ALL = 62 * 1024 * 1024


def silu(value):
    return value * (0.5 * jnp.tanh(0.5 * value) + 0.5)


def softplus(value):
    return jnp.maximum(value, 0.0) + jnp.log(1.0 + jnp.exp(-jnp.abs(value)))


def doc_start(positions, lens_ref):
    begin = jnp.int32(0)
    found = positions * 0
    for doc in range(lens_ref.shape[0]):
        found = jnp.where(positions >= begin, begin, found)
        begin = begin + lens_ref[doc]
    return found


def halves(value):
    high = value.astype(BF16)
    return high, (value - high.astype(F32)).astype(BF16)


def widen(per_head, first, width):
    heads = per_head.shape[1]
    both = jnp.concatenate(halves(per_head), axis=1)
    head = lax.broadcasted_iota(jnp.int32, (2 * heads, width), 0)
    head = jnp.where(head >= heads, head - heads, head)
    channel = lax.broadcasted_iota(jnp.int32, (2 * heads, width), 1) + first
    spread = (channel // HDIM == head).astype(F32).astype(BF16)
    return jnp.dot(both, spread, preferred_element_type=F32)


def rates(dt_ref, dt_bias_ref, a_log_ref):
    heads = dt_ref.shape[0]
    step = softplus(dt_ref[...].T + dt_bias_ref[...].reshape(1, -1)[:, :heads])
    rate = -step * jnp.exp(a_log_ref[...].reshape(1, -1)[:, :heads])
    rows = step.shape[0]
    row = lax.broadcasted_iota(jnp.int32, (rows, rows), 0)
    column = lax.broadcasted_iota(jnp.int32, (rows, rows), 1)
    lower = (row >= column).astype(F32).astype(BF16)
    high = rate.astype(BF16)
    middle, low = halves(rate - high.astype(F32))
    parts = jnp.concatenate([high, middle, low], axis=0)
    lowers = jnp.concatenate([lower, lower, lower], axis=1)
    return step, jnp.dot(lowers, parts, preferred_element_type=F32)


def insides(first, shape, taps, lens_ref):
    positions = first + lax.broadcasted_iota(jnp.int32, shape, 0)
    depth = positions - doc_start(positions, lens_ref)
    return [depth >= lag for lag in range(taps)]


def conv(pad, rows, weight, bias, inside):
    taps = weight.shape[0]
    total = pad[8 : 8 + rows] * weight[taps - 1 : taps] + bias
    for lag in range(1, taps):
        term = pad[8 - lag : 8 - lag + rows] * weight[taps - 1 - lag : taps - lag]
        total = total + jnp.where(inside[lag], term, 0.0)
    return silu(total).astype(BF16)


def tail_lines(message, rows):
    block = message[rows:].astype(F32)
    return jnp.concatenate([block[at : at + 4] for at in range(0, block.shape[0], 4)], axis=1)


def reach(device, rows, lens_ref):
    return device - doc_start((device + 1) * rows - 1, lens_ref) // rows


def kept_weight(here, step, running, taps, lens_ref):
    rows = step.shape[0]
    last_begin = doc_start((here + 1) * rows - 1, lens_ref)
    row = lax.broadcasted_iota(jnp.int32, step.shape, 0)
    weight = step * jnp.exp(running[rows - 1 : rows] - running)
    kept = (here * rows + row >= last_begin) & ((row >= taps - 1) | (last_begin // rows >= here))
    return jnp.where(kept, weight, 0.0)


def conv_rows(pad, raw, weight, bias, inside):
    pad[0:8] = jnp.zeros((8, raw.shape[1]), F32)
    pad[8:] = raw.astype(F32)
    return conv(pad, raw.shape[0], weight, bias.reshape(1, -1), inside)


def first_state_kernel(*refs):
    hbm_refs, out_hbm_ref = refs[:10], refs[10]
    vmem_refs = refs[11:21]
    x_edge_ref, bc_edge_ref, out_ref, b_pad_ref, pad_ref, in_sems, out_sems = refs[21:]
    x_ref, b_ref, dt_ref, wx_ref, bx_ref, wbc_ref, bbc_ref, dt_bias_ref, a_log_ref, lens_ref = vmem_refs
    rows, width = x_ref.shape
    taps = wx_ref.shape[0]

    def corner(ref, shape):
        return ref.at[tuple(pl.ds(0, extent) for extent in shape)]

    order = (9, 2, 7, 8, 1, 5, 6, 0, 3, 4)
    copies = {}
    for at in order:
        source = corner(hbm_refs[at], vmem_refs[at].shape)
        copies[at] = pltpu.make_async_copy(source, vmem_refs[at], in_sems.at[at])
        copies[at].start()
    edge_copies = []
    for at, (source, target) in enumerate(((hbm_refs[0], x_edge_ref), (hbm_refs[1], bc_edge_ref))):
        edge_copies.append(
            pltpu.make_async_copy(source.at[pl.ds(rows - EDGE, EDGE)], target, in_sems.at[10 + at])
        )
        edge_copies[-1].start()

    here = lax.axis_index("seq")
    for at in (9, 2, 7, 8):
        copies[at].wait()
    inside = insides(here * rows, (rows, CHUNK), taps, lens_ref)
    step, running = rates(dt_ref, dt_bias_ref, a_log_ref)
    weight = kept_weight(here, step, running, taps, lens_ref)
    narrow = [mask[:, :STATE] for mask in inside]
    for at in (1, 5, 6):
        copies[at].wait()
    inputs = conv_rows(b_pad_ref, b_ref[...], wbc_ref[...], bbc_ref[...], narrow)
    turned = inputs.astype(F32).T.astype(BF16)
    for at in (0, 3, 4):
        copies[at].wait()
    slots = pad_ref.shape[0]
    outs = []

    def send(at, view):
        copy = pltpu.make_async_copy(out_ref.at[view], out_hbm_ref.at[view], out_sems.at[at])
        copy.start()
        outs.append(copy)

    for at, start in enumerate(range(0, width, CHUNK)):
        columns = slice(start, start + CHUNK)
        pad = pad_ref.at[(at + 1) % slots]
        xc = conv_rows(pad, x_ref[:, columns], wx_ref[:, columns], bx_ref[:, columns], inside)
        weighted = (xc.astype(F32) * widen(weight, start, CHUNK)).astype(BF16)
        out_ref[:STATE, columns] = jnp.dot(turned, weighted, preferred_element_type=F32).astype(BF16)
        if at % 2:
            send(at // 2, (pl.ds(0, STATE), pl.ds(start - CHUNK, 2 * CHUNK)))
    for copy in edge_copies:
        copy.wait()
    edges = jnp.concatenate([x_edge_ref[...].astype(F32), bc_edge_ref[...].astype(F32)], axis=1)[EDGE - 4 :]
    spare = -edges.shape[1] % width
    if spare:
        edges = jnp.concatenate([edges, jnp.zeros((4, spare), F32)], axis=1)
    pieces = [edges[:, at : at + width] for at in range(0, edges.shape[1], width)]
    while len(pieces) % (EDGE // 4):
        pieces.append(jnp.zeros_like(pieces[0]))
    out_ref[STATE:] = jnp.concatenate(pieces, axis=0).astype(BF16)
    send(width // (2 * CHUNK), (pl.ds(STATE, out_ref.shape[0] - STATE), pl.ds(0, width)))
    for copy in outs:
        copy.wait()


def conv_kernel(groups, *refs):
    x_ref, bc_ref, dt_ref, wx_ref, bx_ref, wbc_ref, bbc_ref, dt_bias_ref, a_log_ref, lens_ref = refs[:10]
    keys_ref, values_ref, xc_ref, bcc_ref, kv_ref = refs[10:15]
    state_refs = refs[15:-1]
    pad_ref = refs[-1]
    rows, width = x_ref.shape
    per_group = width // groups
    heads = per_group // HDIM
    taps = wx_ref.shape[0]
    slots = pad_ref.shape[0]
    here = lax.axis_index("seq")
    kv_width = keys_ref.shape[1]
    kv_ref[:, :kv_width] = keys_ref[...]
    kv_ref[:, kv_width:] = values_ref[...]
    inside = insides(here * rows, (rows, CHUNK), taps, lens_ref)
    step, running = rates(dt_ref, dt_bias_ref, a_log_ref)
    weight = kept_weight(here, step, running, taps, lens_ref)
    for group in range(groups):
        base = slice(group * 2 * STATE, (group + 1) * 2 * STATE)
        pair = conv_rows(pad_ref.at[0], bc_ref[:, base], wbc_ref[:, base], bbc_ref[base], inside)
        bcc_ref[:, base] = pair
        turned = pair[:, :STATE].astype(F32).T.astype(BF16)
        part_weight = weight[:, group * heads : (group + 1) * heads]
        for chunk in range(0, per_group, CHUNK):
            columns = slice(group * per_group + chunk, group * per_group + chunk + CHUNK)
            pad = pad_ref.at[(chunk // CHUNK + 1) % slots]
            xc = conv_rows(pad, x_ref[:, columns], wx_ref[:, columns], bx_ref[columns], inside)
            xc_ref[:, columns] = xc
            if group:
                weighted = (xc.astype(F32) * widen(part_weight, chunk, CHUNK)).astype(BF16)
                state_refs[group - 1][:, chunk : chunk + CHUNK] = jnp.dot(
                    turned, weighted, preferred_element_type=F32
                ).astype(BF16)


def prepare_kernel(hops, *refs):
    x_ref, bc_ref, dt_ref, wx_ref, bx_ref, wbc_ref, bbc_ref, dt_bias_ref, a_log_ref, skip_ref, lens_ref = refs[:11]
    partial_ref, weight_ref, through_ref, inside_ref, flag_ref, entry_ref, wide_skip_ref, begin_ref, pad_ref = refs[11:]
    width = x_ref.shape[1]
    rows, heads = entry_ref.shape
    taps = wx_ref.shape[0]
    here = lax.axis_index("seq")
    first = here * rows
    own = reach(here, rows, lens_ref) == 0
    inside = insides(first, (8, CHUNK), taps, lens_ref)
    for lag in range(1, taps):
        inside_ref[lag - 1] = inside[lag].astype(F32)
    flag_ref[0] = jnp.broadcast_to(own.astype(F32), (8, CHUNK))
    before = reach(here - 1, rows, lens_ref)
    for hop in range(1, hops):
        flag_ref[hop] = jnp.broadcast_to((before == hop).astype(F32), (8, CHUNK))
    step, running = rates(dt_ref, dt_bias_ref, a_log_ref)
    begin = doc_start(first + lax.broadcasted_iota(jnp.int32, begin_ref.shape, 0), lens_ref)
    begin_ref[...] = begin
    entry_ref[...] = jnp.where(begin[:, :heads] < first, jnp.exp(running), 0.0)
    row = lax.broadcasted_iota(jnp.int32, (8, heads), 0)
    total = running[rows - 1 : rows]
    weight = step[:8] * jnp.exp(total - running[:8])
    weight = jnp.where((row < taps - 1) & jnp.logical_not(own), weight, 0.0)
    through = jnp.where(own, 0.0, jnp.broadcast_to(jnp.exp(total), (8, heads)))
    skip = jnp.broadcast_to(skip_ref[...].reshape(1, -1), (8, heads))
    every = jnp.concatenate([weight, through, skip], axis=0)
    for start in range(0, width, CHUNK):
        wide = widen(every, start, CHUNK)
        weight_ref[:, start : start + CHUNK] = wide[:8]
        through_ref[:, start : start + CHUNK] = wide[8:16]
        wide_skip_ref[:, start : start + CHUNK] = wide[16:]
    pad_ref[0:8] = jnp.zeros((8, pad_ref.shape[1]), F32)
    pad_ref[8:, :width] = x_ref[...].astype(F32)[:8]
    pad_ref[8:, width:] = bc_ref[...].astype(F32)[:8]

    def some(columns, base, w_ref, b_ref):
        here_columns = slice(base + columns.start, base + columns.stop)
        total = pad_ref[8:, here_columns] * w_ref[taps - 1 : taps, columns] + b_ref[columns].reshape(1, -1)
        for lag in range(1, taps):
            term = pad_ref[8 - lag : 16 - lag, here_columns] * w_ref[taps - 1 - lag : taps - lag, columns]
            total = total + jnp.where(inside[lag], term, 0.0)
        partial_ref[:, here_columns] = total

    for start in range(0, width, CHUNK):
        some(slice(start, start + CHUNK), 0, wx_ref, bx_ref)
    for start in range(0, bc_ref.shape[1], CHUNK):
        some(slice(start, start + CHUNK), width, wbc_ref, bbc_ref)


def first_rows(lines, partial_ref, inside_ref, w_ref, pad_ref, slot, at, start):
    taps = w_ref.shape[0]
    columns = slice(start, start + CHUNK)
    pad = pad_ref.at[slot]
    pad[4:8] = lines[:, at + start : at + start + CHUNK]
    pad[8:] = jnp.zeros((8, CHUNK), F32)
    total = partial_ref[:, at + start : at + start + CHUNK]
    for lag in range(1, taps):
        term = pad[8 - lag : 16 - lag] * w_ref[taps - 1 - lag : taps - lag, columns]
        total = total + term * inside_ref[lag - 1]
    return silu(total).astype(BF16)


def relay_first_kernel(fresh, *refs):
    message_ref, state_ref, partial_ref, weight_ref, through_ref, inside_ref, flag_ref, wx_ref, wbc_ref = refs[:9]
    other_ref = refs[9] if fresh else state_ref
    out_ref, pad_ref = refs[-2:]
    width = out_ref.shape[1]
    slots = pad_ref.shape[0]
    lines = tail_lines(message_ref, STATE)
    top = functools.partial(first_rows, lines, partial_ref, inside_ref)
    inputs = top(wbc_ref, pad_ref, 0, wx_ref.shape[1], 0)[:, :STATE]
    turned = inputs.astype(F32).T.astype(BF16)
    own = flag_ref[0, 0:1] > 0.5
    for start in range(0, width, CHUNK):
        columns = slice(start, start + CHUNK)
        xc = top(wx_ref, pad_ref, (start // CHUNK + 1) % slots, 0, start)
        weighted = (xc.astype(F32) * weight_ref[:, columns]).astype(BF16)
        full = state_ref[:STATE, columns].astype(F32) + jnp.dot(
            turned, weighted, preferred_element_type=F32
        )
        full = full + through_ref[0:1, columns] * message_ref[:STATE, columns].astype(F32)
        out_ref[:, columns] = jnp.where(own, other_ref[:STATE, columns].astype(F32), full).astype(BF16)


def relay_kernel(part, fresh, *refs):
    got_ref, state_ref, through_ref, flag_ref = refs[:4]
    out_ref = refs[-1]
    width = out_ref.shape[1]
    own = flag_ref[0, 0:1] > 0.5
    for start in range(0, width, CHUNK):
        columns = slice(start, start + CHUNK)
        through = through_ref[0:1, part * width + start : part * width + start + CHUNK]
        full = state_ref[:, columns].astype(F32) + through * got_ref[:STATE, columns].astype(F32)
        if fresh:
            full = jnp.where(own, refs[4][:STATE, columns].astype(F32), full)
        out_ref[:, columns] = full.astype(BF16)


def local_kernel(groups, *refs):
    (
        message_ref, partial_ref, weight_ref, inside_ref, wx_ref, wbc_ref, dt_ref, dt_bias_ref,
        a_log_ref, wide_skip_ref, begin_ref, kv_ref, xc_ref, bcc_ref,
    ) = refs[:14]
    state_refs = refs[14 : 14 + groups]
    out_ref, c_ref, kv_out_ref = refs[14 + groups : 17 + groups]
    full_refs = refs[17 + groups : 17 + 2 * groups]
    kv_out_ref[...] = kv_ref[...]
    pad_ref = refs[-1]
    rows, width = xc_ref.shape
    per_group = width // groups
    first = lax.axis_index("seq") * rows
    lines = tail_lines(message_ref, STATE)
    slots = pad_ref.shape[0]

    def top(w_ref, slot, at, start, below):
        new = first_rows(lines, partial_ref, inside_ref, w_ref, pad_ref, slot, at, start)
        old = below[8:EDGE].astype(F32)
        return jnp.concatenate([jnp.concatenate([new.astype(F32), old], axis=0).astype(BF16), below[EDGE:]], axis=0)

    row = lax.broadcasted_iota(jnp.int32, (rows, rows), 0)
    lane_row = lax.broadcasted_iota(jnp.int32, (rows, rows), 1)
    linked = (row >= lane_row) & (first + lane_row >= begin_ref[...])
    step, running = rates(dt_ref, dt_bias_ref, a_log_ref)
    turned_running = running.T
    turned_step = step.T
    pair_width = 2 * HDIM
    lane = lax.broadcasted_iota(jnp.int32, (rows, pair_width), 1)
    for group in range(groups):
        base = group * 2 * STATE
        pair = top(wbc_ref, group % slots, width, base, bcc_ref[:, base : base + 2 * STATE])
        inputs = pair[:, :STATE]
        outputs = pair[:, STATE:]
        c_ref[:, group * STATE : (group + 1) * STATE] = outputs
        turned = inputs[:EDGE].astype(F32).T[:, :8].astype(BF16)
        meet = lax.dot_general(
            outputs, inputs, (((1,), (1,)), ((), ())), preferred_element_type=F32
        )
        meet = jnp.where(linked, meet, 0.0)
        for chunk in range(0, per_group, CHUNK):
            at = group * per_group + chunk
            columns = slice(chunk, chunk + CHUNK)
            xc_all = top(wx_ref, (chunk // CHUNK) % slots, 0, at, xc_ref[:, at : at + CHUNK])
            weighted = xc_all[:EDGE].astype(F32)[:8] * weight_ref[:, at : at + CHUNK]
            full = state_refs[group][:STATE, columns].astype(F32) + jnp.dot(
                turned, weighted.astype(BF16), preferred_element_type=F32
            )
            full_refs[group][:, columns] = full.astype(BF16)
            wide_skip = wide_skip_ref[0:1, at : at + CHUNK]
            for start in range(0, CHUNK, pair_width):
                parts = []
                for head in ((at + start) // HDIM, (at + start) // HDIM + 1):
                    spread = running[:, head : head + 1] - turned_running[head : head + 1]
                    decay = jnp.exp(jnp.minimum(spread, 0.0))
                    parts.append((decay * (meet * turned_step[head : head + 1])).astype(BF16))
                mix = jnp.concatenate(parts, axis=1)
                xc = xc_all[:, start : start + pair_width]
                zero = jnp.zeros_like(xc)
                stacked = jnp.concatenate(
                    [jnp.where(lane < HDIM, xc, zero), jnp.where(lane < HDIM, zero, xc)], axis=0
                )
                value = jnp.dot(mix, stacked, preferred_element_type=F32)
                out_ref[:, at + start : at + start + pair_width] = (
                    value + xc.astype(F32) * wide_skip[:, start : start + pair_width]
                )


def attend_kernel(hops, *refs):
    q_ref = refs[0]
    kv_refs = refs[1 : 2 + hops]
    begin_ref, out_hbm_ref, out_ref, sems = refs[2 + hops :]
    rows = q_ref.shape[0]
    kv_heads = kv_refs[0].shape[1] // (2 * ADIM)
    share = QHEADS // KVHEADS
    count = rows * (hops + 1)
    here = lax.axis_index("seq")
    row = here * rows + lax.broadcasted_iota(jnp.int32, (rows, count), 0)
    column = (here - hops) * rows + lax.broadcasted_iota(jnp.int32, (rows, count), 1)
    begin = jnp.concatenate([begin_ref[...]] * (hops + 1), axis=1)
    allowed = (column <= row) & (column >= begin)
    scale = ADIM ** (-0.5)
    ones = jnp.ones((count, ADIM), BF16)
    allowed = jnp.concatenate([allowed] * share, axis=0)
    copies = []
    for head in range(kv_heads):
        low = head * ADIM
        keys = jnp.concatenate([ref[:, low : low + ADIM] for ref in kv_refs], axis=0)
        low = (kv_heads + head) * ADIM
        values = jnp.concatenate([ref[:, low : low + ADIM] for ref in kv_refs], axis=0)
        values = jnp.concatenate([values, ones], axis=1)
        lows = [(head * share + part) * ADIM for part in range(share)]
        asking = jnp.concatenate([q_ref[:, low : low + ADIM] for low in lows], axis=0)
        scores = lax.dot_general(asking, keys, (((1,), (1,)), ((), ())), preferred_element_type=F32)
        scores = jnp.where(allowed, scores * scale, BARRED)
        expo = jnp.exp(scores - jnp.max(scores, axis=1, keepdims=True))
        summed = jnp.dot(expo.astype(BF16), values, preferred_element_type=F32)
        result = (summed[:, :ADIM] / summed[:, ADIM:]).astype(BF16)
        for part, low in enumerate(lows):
            out_ref[:, low : low + ADIM] = result[part * rows : (part + 1) * rows]
        columns = pl.ds(head * share * ADIM, share * ADIM)
        copies.append(
            pltpu.make_async_copy(out_ref.at[:, columns], out_hbm_ref.at[:, columns], sems.at[head])
        )
        copies[-1].start()
    for copy in copies:
        copy.wait()


def norm_kernel(part, hops, *refs):
    mixed_ref, c_ref, entry_ref, z_ref, gain_ref, flag_ref = refs[:6]
    got_refs = refs[6 : 6 + hops]
    out_hbm_ref, gated_ref, out_ref, sems = refs[-4:]
    rows, width = gated_ref.shape
    heads = width // HDIM
    entry = entry_ref[:, part * heads : (part + 1) * heads]
    outputs = c_ref[:, part * STATE : (part + 1) * STATE]
    squares = jnp.zeros((rows, 128), F32)
    for start in range(0, width, CHUNK):
        columns = slice(start, start + CHUNK)
        placed = slice(part * width + start, part * width + start + CHUNK)
        state = got_refs[0][:STATE, columns]
        for hop in range(1, hops):
            there = flag_ref[hop, 0:1] > 0.5
            state = jnp.where(there, got_refs[hop][:STATE, columns].astype(F32), state.astype(F32))
        carried = jnp.dot(outputs, state.astype(BF16), preferred_element_type=F32)
        mixed = mixed_ref[:, placed] + carried * widen(entry, start, CHUNK)
        gated = mixed * silu(z_ref[:, placed].astype(F32))
        gated_ref[:, columns] = gated
        for lane in range(0, CHUNK, 128):
            squares = squares + gated[:, lane : lane + 128] * gated[:, lane : lane + 128]
    squares = jnp.sum(squares, axis=1, keepdims=True)
    multiplier = lax.rsqrt(squares * (1.0 / width) + EPSILON)
    copies = []
    for start in range(0, width, CHUNK):
        columns = slice(start, start + CHUNK)
        gain = gain_ref[part * width + start : part * width + start + CHUNK]
        out_ref[:, columns] = (gated_ref[:, columns] * multiplier * gain.reshape(1, -1)).astype(BF16)
        copies.append(
            pltpu.make_async_copy(
                out_ref.at[:, pl.ds(start, CHUNK)],
                out_hbm_ref.at[:, pl.ds(part * width + start, CHUNK)],
                sems.at[start // CHUNK],
            )
        )
        copies[-1].start()
    for copy in copies:
        copy.wait()


WHOLE = pl.BlockSpec(memory_space=pltpu.VMEM)
SCALARS = pl.BlockSpec(memory_space=pltpu.SMEM)
UNTOUCHED = pl.BlockSpec(memory_space=pl.ANY)


def tile(rows, columns, row, column):
    return pl.BlockSpec((rows, columns), lambda step: (row, column))


def call(kernel, name, outs, operands, specs, out_specs=None, scratch=(), flops=KERNEL_FLOPS, aliases={}, limit=VMEM_LIMIT):
    moved = sum(math.prod(a.shape) * a.dtype.itemsize for a in (*operands, *outs))
    return pl.pallas_call(
        kernel,
        name=name,
        grid=(1,),
        out_shape=outs,
        in_specs=specs,
        out_specs=[WHOLE] * len(outs) if out_specs is None else out_specs,
        scratch_shapes=list(scratch),
        input_output_aliases=aliases,
        compiler_params=pltpu.CompilerParams(vmem_limit_bytes=limit),
        cost_estimate=pl.CostEstimate(flops=flops, bytes_accessed=moved, transcendentals=0),
    )(*operands)


def onward(value, first=0):
    count = lax.axis_size("seq")
    return lax.ppermute(value, "seq", [(source, source + 1) for source in range(first, count - 1)])


def shards(
    x_raw,
    bc_raw,
    z_gate,
    dt_raw,
    conv_x_weight,
    conv_x_bias,
    conv_bc_weight,
    conv_bc_bias,
    dt_bias,
    a_log,
    skip_d,
    norm_gain,
    queries,
    keys,
    values,
    doc_lens,
):
    rows, width = x_raw.shape
    bc_width = bc_raw.shape[1]
    heads = dt_raw.shape[1]
    groups = bc_width // (2 * STATE)
    per_group = width // groups
    count = lax.axis_size("seq")
    longest = rows * count // 2
    hops = min(count - 1, -(-(longest - 1) // rows))
    assert hops * rows >= longest and (hops <= 2 or groups == 1)
    shape = jax.ShapeDtypeStruct
    dt = dt_raw.T
    params = [dt, conv_x_weight, conv_x_bias, conv_bc_weight, conv_bc_bias, dt_bias, a_log]
    pieces = -(-(width + bc_width) // per_group)
    tail_rows = EDGE * -(-4 * pieces // EDGE)

    (message,) = call(
        first_state_kernel,
        "first_state",
        [shape((STATE + tail_rows, per_group), BF16)],
        [x_raw, bc_raw, *(a if a.ndim > 1 else a[None] for a in params), doc_lens],
        [UNTOUCHED] * 10,
        out_specs=[UNTOUCHED],
        scratch=[
            pltpu.VMEM((rows, per_group), BF16),
            pltpu.VMEM((rows, STATE), BF16),
            pltpu.VMEM((per_group // HDIM, rows), F32),
            pltpu.VMEM((conv_x_weight.shape[0], per_group), F32),
            pltpu.VMEM((1, per_group), F32),
            pltpu.VMEM((conv_x_weight.shape[0], STATE), F32),
            pltpu.VMEM((1, STATE), F32),
            pltpu.VMEM((1, heads), F32),
            pltpu.VMEM((1, heads), F32),
            pltpu.SMEM(doc_lens.shape, jnp.int32),
            pltpu.VMEM((EDGE, width), BF16),
            pltpu.VMEM((EDGE, bc_width), BF16),
            pltpu.VMEM((STATE + tail_rows, per_group), BF16),
            pltpu.VMEM((rows + 8, STATE), F32),
            pltpu.VMEM((4, rows + 8, CHUNK), F32),
            pltpu.SemaphoreType.DMA((12,)),
            pltpu.SemaphoreType.DMA((per_group // (2 * CHUNK) + 1,)),
        ],
        limit=VMEM_ALL,
    )
    slots = [onward(message)]
    xc, bcc, kv, *states = call(
        functools.partial(conv_kernel, groups),
        "conv_all",
        [
            shape((rows, width), BF16),
            shape((rows, bc_width), BF16),
            shape((rows, 2 * keys.shape[1]), BF16),
            *(shape((STATE, per_group), BF16) for _ in range(groups - 1)),
        ],
        [x_raw, bc_raw, *params, doc_lens, keys, values],
        [WHOLE] * 9 + [SCALARS] + [WHOLE] * 2,
        scratch=[pltpu.VMEM((4, rows + 8, CHUNK), F32)],
    )
    states = [message, *states]
    kvs = [kv, onward(kv)]

    partial, weight, through, inside, flags, entry, wide_skip, begin = call(
        functools.partial(prepare_kernel, hops),
        "prepare",
        [
            shape((8, width + bc_width), F32),
            shape((8, width), F32),
            shape((8, width), F32),
            shape((conv_x_weight.shape[0] - 1, 8, CHUNK), F32),
            shape((hops, 8, CHUNK), F32),
            shape((rows, heads), F32),
            shape((8, width), F32),
            shape((rows, rows), jnp.int32),
        ],
        [x_raw, bc_raw, *params, skip_d, doc_lens],
        [tile(EDGE, width, 0, 0), tile(EDGE, bc_width, 0, 0)] + [WHOLE] * 8 + [SCALARS],
        scratch=[pltpu.VMEM((16, width + bc_width), F32)],
    )

    fulls = None
    for slot in range(2, hops + groups):
        part = min(slot - 1, groups) - 1
        fresh = slot <= groups
        if slot == 2:
            kernel = functools.partial(relay_first_kernel, fresh)
            operands = [slots[0], states[0], partial, weight, through, inside, flags, conv_x_weight, conv_bc_weight]
            scratch = [pltpu.VMEM((4, 16, CHUNK), F32)]
        else:
            kernel = functools.partial(relay_kernel, part, fresh)
            operands = [slots[-1], fulls[part], through, flags]
            scratch = []
        if fresh:
            operands.append(states[slot - 1])
        (passed,) = call(
            kernel,
            f"relay_slot{slot}",
            [shape((STATE, per_group), BF16)],
            operands,
            [WHOLE] * len(operands),
            scratch=scratch,
        )
        slots.append(onward(passed))
        if fulls is None:
            mixed, c_out, kv_on, *fulls = call(
                functools.partial(local_kernel, groups),
                "local_mix",
                [
                    shape((rows, width), F32),
                    shape((rows, groups * STATE), BF16),
                    shape(kv.shape, BF16),
                    *(shape((STATE, per_group), BF16) for _ in range(groups)),
                ],
                [
                    slots[0], partial, weight, inside, conv_x_weight, conv_bc_weight, dt, dt_bias, a_log,
                    wide_skip, begin, kvs[1], xc, bcc, *states,
                ],
                [WHOLE] * (14 + groups),
                scratch=[pltpu.VMEM((4, 16, CHUNK), F32)],
            )
    for hop in range(1, hops):
        kvs.append(onward(kv_on if hop == 1 else kvs[-1], hop))

    (attn_out,) = call(
        functools.partial(attend_kernel, hops),
        "attend",
        [shape(queries.shape, BF16)],
        [queries, *reversed(kvs), begin],
        [WHOLE] * (hops + 3),
        out_specs=[UNTOUCHED],
        scratch=[
            pltpu.VMEM(queries.shape, BF16),
            pltpu.SemaphoreType.DMA((keys.shape[1] // ADIM,)),
        ],
    )
    mamba_out = None
    for part in range(groups):
        got = slots[-1:] if part == groups - 1 else slots[part : part + hops]
        operands = [mixed, c_out, entry, z_gate, norm_gain, flags, *got]
        specs = [WHOLE] * (6 + len(got))
        aliases = {}
        if mamba_out is not None:
            operands.append(mamba_out)
            specs.append(UNTOUCHED)
            aliases = {len(operands) - 1: 0}
        (mamba_out,) = call(
            functools.partial(norm_kernel, part, len(got)),
            f"norm_part{part}",
            [shape((rows, width), BF16)],
            operands,
            specs,
            out_specs=[UNTOUCHED],
            scratch=[
                pltpu.VMEM((rows, per_group), F32),
                pltpu.VMEM((rows, per_group), BF16),
                pltpu.SemaphoreType.DMA((per_group // CHUNK,)),
            ],
            aliases=aliases,
        )
    return (mamba_out, attn_out)


def solution(mesh):
    split = P(("groups", "seq"), "dp")
    placed = (
        split,
        split,
        split,
        split,
        P(None, "dp"),
        P("dp"),
        P(None, "dp"),
        P("dp"),
        P("dp"),
        P("dp"),
        P("dp"),
        P("dp"),
        split,
        split,
        split,
        P("groups"),
    )
    return jax.shard_map(
        shards,
        mesh=mesh,
        in_specs=placed,
        out_specs=(split, split),
        check_vma=False,
    )
```

```python
import functools
import math

import jax
import jax.numpy as jnp
from jax import lax
from jax.experimental import pallas as pl
from jax.experimental.pallas import tpu as pltpu
from jax.sharding import PartitionSpec as P

HDIM = 64
STATE = 128
QHEADS = 32
KVHEADS = 8
ADIM = 128
EPSILON = 1e-05
BARRED = -2e30
HIGHEST = lax.Precision.HIGHEST
F32 = jnp.float32
BF16 = jnp.bfloat16
CHUNK = 256
EDGE = 16
KERNEL_FLOPS = 2 * 10**9
VMEM_LIMIT = 40 * 1024 * 1024
VMEM_ALL = 62 * 1024 * 1024


def silu(value):
    return value * (0.5 * jnp.tanh(0.5 * value) + 0.5)


def softplus(value):
    return jnp.maximum(value, 0.0) + jnp.log(1.0 + jnp.exp(-jnp.abs(value)))


def doc_start(positions, lens_ref):
    begin = jnp.int32(0)
    found = positions * 0
    for doc in range(lens_ref.shape[0]):
        found = jnp.where(positions >= begin, begin, found)
        begin = begin + lens_ref[doc]
    return found


def halves(value):
    high = value.astype(BF16)
    return high, (value - high.astype(F32)).astype(BF16)


def widen(per_head, first, width):
    heads = per_head.shape[1]
    both = jnp.concatenate(halves(per_head), axis=1)
    head = lax.broadcasted_iota(jnp.int32, (2 * heads, width), 0)
    head = jnp.where(head >= heads, head - heads, head)
    channel = lax.broadcasted_iota(jnp.int32, (2 * heads, width), 1) + first
    spread = (channel // HDIM == head).astype(F32).astype(BF16)
    return jnp.dot(both, spread, preferred_element_type=F32)


def rates(dt_ref, dt_bias_ref, a_log_ref):
    heads = dt_ref.shape[0]
    step = softplus(dt_ref[...].T + dt_bias_ref[...].reshape(1, -1)[:, :heads])
    rate = -step * jnp.exp(a_log_ref[...].reshape(1, -1)[:, :heads])
    rows = step.shape[0]
    row = lax.broadcasted_iota(jnp.int32, (rows, rows), 0)
    column = lax.broadcasted_iota(jnp.int32, (rows, rows), 1)
    lower = (row >= column).astype(F32).astype(BF16)
    high = rate.astype(BF16)
    middle, low = halves(rate - high.astype(F32))
    parts = jnp.concatenate([high, middle, low], axis=0)
    lowers = jnp.concatenate([lower, lower, lower], axis=1)
    return step, jnp.dot(lowers, parts, preferred_element_type=F32)


def insides(first, shape, taps, lens_ref):
    positions = first + lax.broadcasted_iota(jnp.int32, shape, 0)
    depth = positions - doc_start(positions, lens_ref)
    return [depth >= lag for lag in range(taps)]


def conv(pad, rows, weight, bias, inside):
    taps = weight.shape[0]
    total = pad[8 : 8 + rows] * weight[taps - 1 : taps] + bias
    for lag in range(1, taps):
        term = pad[8 - lag : 8 - lag + rows] * weight[taps - 1 - lag : taps - lag]
        total = total + jnp.where(inside[lag], term, 0.0)
    return silu(total).astype(BF16)


def tail_lines(message, rows):
    block = message[rows:].astype(F32)
    return jnp.concatenate([block[at : at + 4] for at in range(0, block.shape[0], 4)], axis=1)


def reach(device, rows, lens_ref):
    return device - doc_start((device + 1) * rows - 1, lens_ref) // rows


def kept_weight(here, step, running, taps, lens_ref):
    rows = step.shape[0]
    last_begin = doc_start((here + 1) * rows - 1, lens_ref)
    row = lax.broadcasted_iota(jnp.int32, step.shape, 0)
    weight = step * jnp.exp(running[rows - 1 : rows] - running)
    kept = (here * rows + row >= last_begin) & ((row >= taps - 1) | (last_begin // rows >= here))
    return jnp.where(kept, weight, 0.0)


def conv_rows(pad, raw, weight, bias, inside):
    pad[0:8] = jnp.zeros((8, raw.shape[1]), F32)
    pad[8:] = raw.astype(F32)
    return conv(pad, raw.shape[0], weight, bias.reshape(1, -1), inside)


def first_state_kernel(*refs):
    hbm_refs, out_hbm_ref = refs[:10], refs[10]
    vmem_refs = refs[11:21]
    x_edge_ref, bc_edge_ref, out_ref, b_pad_ref, pad_ref, in_sems, out_sems = refs[21:]
    x_ref, b_ref, dt_ref, wx_ref, bx_ref, wbc_ref, bbc_ref, dt_bias_ref, a_log_ref, lens_ref = vmem_refs
    rows, width = x_ref.shape
    taps = wx_ref.shape[0]

    def corner(ref, shape):
        return ref.at[tuple(pl.ds(0, extent) for extent in shape)]

    order = (9, 2, 7, 8, 1, 5, 6, 0, 3, 4)
    copies = {}
    for at in order:
        source = corner(hbm_refs[at], vmem_refs[at].shape)
        copies[at] = pltpu.make_async_copy(source, vmem_refs[at], in_sems.at[at])
        copies[at].start()
    edge_copies = []
    for at, (source, target) in enumerate(((hbm_refs[0], x_edge_ref), (hbm_refs[1], bc_edge_ref))):
        edge_copies.append(
            pltpu.make_async_copy(source.at[pl.ds(rows - EDGE, EDGE)], target, in_sems.at[10 + at])
        )
        edge_copies[-1].start()

    here = lax.axis_index("seq")
    for at in (9, 2, 7, 8):
        copies[at].wait()
    inside = insides(here * rows, (rows, CHUNK), taps, lens_ref)
    step, running = rates(dt_ref, dt_bias_ref, a_log_ref)
    weight = kept_weight(here, step, running, taps, lens_ref)
    narrow = [mask[:, :STATE] for mask in inside]
    for at in (1, 5, 6):
        copies[at].wait()
    inputs = conv_rows(b_pad_ref, b_ref[...], wbc_ref[...], bbc_ref[...], narrow)
    turned = inputs.astype(F32).T.astype(BF16)
    for at in (0, 3, 4):
        copies[at].wait()
    slots = pad_ref.shape[0]
    outs = []

    def send(at, view):
        copy = pltpu.make_async_copy(out_ref.at[view], out_hbm_ref.at[view], out_sems.at[at])
        copy.start()
        outs.append(copy)

    for at, start in enumerate(range(0, width, CHUNK)):
        columns = slice(start, start + CHUNK)
        pad = pad_ref.at[(at + 1) % slots]
        xc = conv_rows(pad, x_ref[:, columns], wx_ref[:, columns], bx_ref[:, columns], inside)
        weighted = (xc.astype(F32) * widen(weight, start, CHUNK)).astype(BF16)
        out_ref[:STATE, columns] = jnp.dot(turned, weighted, preferred_element_type=F32).astype(BF16)
        if at % 2:
            send(at // 2, (pl.ds(0, STATE), pl.ds(start - CHUNK, 2 * CHUNK)))
    for copy in edge_copies:
        copy.wait()
    edges = jnp.concatenate([x_edge_ref[...].astype(F32), bc_edge_ref[...].astype(F32)], axis=1)[EDGE - 4 :]
    spare = -edges.shape[1] % width
    if spare:
        edges = jnp.concatenate([edges, jnp.zeros((4, spare), F32)], axis=1)
    pieces = [edges[:, at : at + width] for at in range(0, edges.shape[1], width)]
    while len(pieces) % (EDGE // 4):
        pieces.append(jnp.zeros_like(pieces[0]))
    out_ref[STATE:] = jnp.concatenate(pieces, axis=0).astype(BF16)
    send(width // (2 * CHUNK), (pl.ds(STATE, out_ref.shape[0] - STATE), pl.ds(0, width)))
    for copy in outs:
        copy.wait()


def prepare_kernel(hops, groups, *refs):
    x_ref, bc_ref, dt_ref, wx_ref, bx_ref, wbc_ref, bbc_ref, dt_bias_ref, a_log_ref, skip_ref, lens_ref = refs[:11]
    keys_ref, values_ref = refs[11:13]
    xc_ref, bcc_ref, kv_ref, partial_ref, weight_ref, through_ref, inside_ref, flag_ref, entry_ref = refs[13:22]
    wide_skip_ref, begin_ref = refs[22:24]
    state_refs = refs[24:-2]
    top_ref, pad_ref = refs[-2:]
    rows, width = x_ref.shape
    per_group = width // groups
    taps = wx_ref.shape[0]
    slots = pad_ref.shape[0]
    here = lax.axis_index("seq")
    first = here * rows
    kv_width = keys_ref.shape[1]
    kv_ref[:, :kv_width] = keys_ref[...]
    kv_ref[:, kv_width:] = values_ref[...]
    inside = insides(first, (rows, CHUNK), taps, lens_ref)
    step, running = rates(dt_ref, dt_bias_ref, a_log_ref)
    heads = step.shape[1]
    group_heads = heads // groups
    kept = kept_weight(here, step, running, taps, lens_ref)
    for group in range(groups):
        base = slice(group * 2 * STATE, (group + 1) * 2 * STATE)
        pair = conv_rows(pad_ref.at[0], bc_ref[:, base], wbc_ref[:, base], bbc_ref[base], inside)
        bcc_ref[:, base] = pair
        turned = pair[:, :STATE].astype(F32).T.astype(BF16)
        part_weight = kept[:, group * group_heads : (group + 1) * group_heads]
        for chunk in range(0, per_group, CHUNK):
            columns = slice(group * per_group + chunk, group * per_group + chunk + CHUNK)
            pad = pad_ref.at[(chunk // CHUNK + 1) % slots]
            xc = conv_rows(pad, x_ref[:, columns], wx_ref[:, columns], bx_ref[columns], inside)
            xc_ref[:, columns] = xc
            if group:
                weighted = (xc.astype(F32) * widen(part_weight, chunk, CHUNK)).astype(BF16)
                state_refs[group - 1][:, chunk : chunk + CHUNK] = jnp.dot(
                    turned, weighted, preferred_element_type=F32
                ).astype(BF16)

    own = reach(here, rows, lens_ref) == 0
    inside = [mask[:8] for mask in inside]
    for lag in range(1, taps):
        inside_ref[lag - 1] = inside[lag].astype(F32)
    flag_ref[0] = jnp.broadcast_to(own.astype(F32), (8, CHUNK))
    before = reach(here - 1, rows, lens_ref)
    for hop in range(1, hops):
        flag_ref[hop] = jnp.broadcast_to((before == hop).astype(F32), (8, CHUNK))
    begin = doc_start(first + lax.broadcasted_iota(jnp.int32, begin_ref.shape, 0), lens_ref)
    begin_ref[...] = begin
    entry_ref[...] = jnp.where(begin[:, :heads] < first, jnp.exp(running), 0.0)
    row = lax.broadcasted_iota(jnp.int32, (8, heads), 0)
    total = running[rows - 1 : rows]
    weight = step[:8] * jnp.exp(total - running[:8])
    weight = jnp.where((row < taps - 1) & jnp.logical_not(own), weight, 0.0)
    through = jnp.where(own, 0.0, jnp.broadcast_to(jnp.exp(total), (8, heads)))
    skip = jnp.broadcast_to(skip_ref[...].reshape(1, -1), (8, heads))
    every = jnp.concatenate([weight, through, skip], axis=0)
    for start in range(0, width, CHUNK):
        wide = widen(every, start, CHUNK)
        weight_ref[:, start : start + CHUNK] = wide[:8]
        through_ref[:, start : start + CHUNK] = wide[8:16]
        wide_skip_ref[:, start : start + CHUNK] = wide[16:]
    top_ref[0:8] = jnp.zeros((8, top_ref.shape[1]), F32)
    top_ref[8:, :width] = x_ref[:EDGE].astype(F32)[:8]
    top_ref[8:, width:] = bc_ref[:EDGE].astype(F32)[:8]

    def some(columns, base, w_ref, b_ref):
        here_columns = slice(base + columns.start, base + columns.stop)
        total = top_ref[8:, here_columns] * w_ref[taps - 1 : taps, columns] + b_ref[columns].reshape(1, -1)
        for lag in range(1, taps):
            term = top_ref[8 - lag : 16 - lag, here_columns] * w_ref[taps - 1 - lag : taps - lag, columns]
            total = total + jnp.where(inside[lag], term, 0.0)
        partial_ref[:, here_columns] = total

    for start in range(0, width, CHUNK):
        some(slice(start, start + CHUNK), 0, wx_ref, bx_ref)
    for start in range(0, bc_ref.shape[1], CHUNK):
        some(slice(start, start + CHUNK), width, wbc_ref, bbc_ref)


def first_rows(lines, partial_ref, inside_ref, w_ref, pad_ref, slot, at, start):
    taps = w_ref.shape[0]
    columns = slice(start, start + CHUNK)
    pad = pad_ref.at[slot]
    pad[4:8] = lines[:, at + start : at + start + CHUNK]
    pad[8:] = jnp.zeros((8, CHUNK), F32)
    total = partial_ref[:, at + start : at + start + CHUNK]
    for lag in range(1, taps):
        term = pad[8 - lag : 16 - lag] * w_ref[taps - 1 - lag : taps - lag, columns]
        total = total + term * inside_ref[lag - 1]
    return silu(total).astype(BF16)


def relay_first_kernel(fresh, *refs):
    message_ref, state_ref, partial_ref, weight_ref, through_ref, inside_ref, flag_ref, wx_ref, wbc_ref = refs[:9]
    other_ref = refs[9] if fresh else state_ref
    out_ref, pad_ref = refs[-2:]
    width = out_ref.shape[1]
    slots = pad_ref.shape[0]
    lines = tail_lines(message_ref, STATE)
    top = functools.partial(first_rows, lines, partial_ref, inside_ref)
    inputs = top(wbc_ref, pad_ref, 0, wx_ref.shape[1], 0)[:, :STATE]
    turned = inputs.astype(F32).T.astype(BF16)
    own = flag_ref[0, 0:1] > 0.5
    for start in range(0, width, CHUNK):
        columns = slice(start, start + CHUNK)
        xc = top(wx_ref, pad_ref, (start // CHUNK + 1) % slots, 0, start)
        weighted = (xc.astype(F32) * weight_ref[:, columns]).astype(BF16)
        full = state_ref[:STATE, columns].astype(F32) + jnp.dot(
            turned, weighted, preferred_element_type=F32
        )
        full = full + through_ref[0:1, columns] * message_ref[:STATE, columns].astype(F32)
        out_ref[:, columns] = jnp.where(own, other_ref[:STATE, columns].astype(F32), full).astype(BF16)


def relay_kernel(part, fresh, *refs):
    got_ref, state_ref, through_ref, flag_ref = refs[:4]
    out_ref = refs[-1]
    width = out_ref.shape[1]
    own = flag_ref[0, 0:1] > 0.5
    for start in range(0, width, CHUNK):
        columns = slice(start, start + CHUNK)
        through = through_ref[0:1, part * width + start : part * width + start + CHUNK]
        full = state_ref[:, columns].astype(F32) + through * got_ref[:STATE, columns].astype(F32)
        if fresh:
            full = jnp.where(own, refs[4][:STATE, columns].astype(F32), full)
        out_ref[:, columns] = full.astype(BF16)


def local_kernel(groups, *refs):
    (
        message_ref, partial_ref, weight_ref, inside_ref, wx_ref, wbc_ref, dt_ref, dt_bias_ref,
        a_log_ref, wide_skip_ref, begin_ref, kv_ref, entry_ref, z_ref, xc_ref, bcc_ref,
    ) = refs[:16]
    state_refs = refs[16 : 16 + groups]
    out_ref, decay_ref, c_ref, kv_out_ref = refs[16 + groups : 20 + groups]
    full_refs = refs[20 + groups : 20 + 2 * groups]
    kv_out_ref[...] = kv_ref[...]
    pad_ref = refs[-1]
    rows, width = xc_ref.shape
    per_group = width // groups
    heads = per_group // HDIM
    first = lax.axis_index("seq") * rows
    lines = tail_lines(message_ref, STATE)
    slots = pad_ref.shape[0]

    def top(w_ref, slot, at, start, below):
        new = first_rows(lines, partial_ref, inside_ref, w_ref, pad_ref, slot, at, start)
        old = below[8:EDGE].astype(F32)
        return jnp.concatenate([jnp.concatenate([new.astype(F32), old], axis=0).astype(BF16), below[EDGE:]], axis=0)

    row = lax.broadcasted_iota(jnp.int32, (rows, rows), 0)
    lane_row = lax.broadcasted_iota(jnp.int32, (rows, rows), 1)
    linked = (row >= lane_row) & (first + lane_row >= begin_ref[...])
    step, running = rates(dt_ref, dt_bias_ref, a_log_ref)
    turned_running = running.T
    turned_step = step.T
    pair_width = 2 * HDIM
    lane = lax.broadcasted_iota(jnp.int32, (rows, pair_width), 1)
    for group in range(groups):
        base = group * 2 * STATE
        pair = top(wbc_ref, group % slots, width, base, bcc_ref[:, base : base + 2 * STATE])
        inputs = pair[:, :STATE]
        outputs = pair[:, STATE:]
        c_ref[:, group * STATE : (group + 1) * STATE] = outputs
        turned = inputs[:EDGE].astype(F32).T[:, :8].astype(BF16)
        meet = lax.dot_general(
            outputs, inputs, (((1,), (1,)), ((), ())), preferred_element_type=F32
        )
        meet = jnp.where(linked, meet, 0.0)
        for chunk in range(0, per_group, CHUNK):
            at = group * per_group + chunk
            columns = slice(chunk, chunk + CHUNK)
            xc_all = top(wx_ref, (chunk // CHUNK) % slots, 0, at, xc_ref[:, at : at + CHUNK])
            weighted = xc_all[:EDGE].astype(F32)[:8] * weight_ref[:, at : at + CHUNK]
            full = state_refs[group][:STATE, columns].astype(F32) + jnp.dot(
                turned, weighted.astype(BF16), preferred_element_type=F32
            )
            full_refs[group][:, columns] = full.astype(BF16)
            wide_skip = wide_skip_ref[0:1, at : at + CHUNK]
            gate = silu(z_ref[:, at : at + CHUNK].astype(F32))
            entry = entry_ref[:, group * heads : (group + 1) * heads]
            decay_ref[:, at : at + CHUNK] = widen(entry, chunk, CHUNK) * gate
            for start in range(0, CHUNK, pair_width):
                parts = []
                for head in ((at + start) // HDIM, (at + start) // HDIM + 1):
                    spread = running[:, head : head + 1] - turned_running[head : head + 1]
                    decay = jnp.exp(jnp.minimum(spread, 0.0))
                    parts.append((decay * (meet * turned_step[head : head + 1])).astype(BF16))
                mix = jnp.concatenate(parts, axis=1)
                xc = xc_all[:, start : start + pair_width]
                zero = jnp.zeros_like(xc)
                stacked = jnp.concatenate(
                    [jnp.where(lane < HDIM, xc, zero), jnp.where(lane < HDIM, zero, xc)], axis=0
                )
                value = jnp.dot(mix, stacked, preferred_element_type=F32)
                value = value + xc.astype(F32) * wide_skip[:, start : start + pair_width]
                out_ref[:, at + start : at + start + pair_width] = value * gate[:, start : start + pair_width]


def attend_kernel(hops, *refs):
    q_ref = refs[0]
    kv_refs = refs[1 : 2 + hops]
    begin_ref, out_hbm_ref, out_ref, sems = refs[2 + hops :]
    rows = q_ref.shape[0]
    kv_heads = kv_refs[0].shape[1] // (2 * ADIM)
    share = QHEADS // KVHEADS
    count = rows * (hops + 1)
    here = lax.axis_index("seq")
    row = here * rows + lax.broadcasted_iota(jnp.int32, (rows, count), 0)
    column = (here - hops) * rows + lax.broadcasted_iota(jnp.int32, (rows, count), 1)
    begin = jnp.concatenate([begin_ref[...]] * (hops + 1), axis=1)
    allowed = (column <= row) & (column >= begin)
    scale = ADIM ** (-0.5)
    ones = jnp.ones((count, ADIM), BF16)
    allowed = jnp.concatenate([allowed] * share, axis=0)
    copies = []
    for head in range(kv_heads):
        low = head * ADIM
        keys = jnp.concatenate([ref[:, low : low + ADIM] for ref in kv_refs], axis=0)
        low = (kv_heads + head) * ADIM
        values = jnp.concatenate([ref[:, low : low + ADIM] for ref in kv_refs], axis=0)
        values = jnp.concatenate([values, ones], axis=1)
        lows = [(head * share + part) * ADIM for part in range(share)]
        asking = jnp.concatenate([q_ref[:, low : low + ADIM] for low in lows], axis=0)
        scores = lax.dot_general(asking, keys, (((1,), (1,)), ((), ())), preferred_element_type=F32)
        scores = jnp.where(allowed, scores * scale, BARRED)
        expo = jnp.exp(scores - jnp.max(scores, axis=1, keepdims=True))
        summed = jnp.dot(expo.astype(BF16), values, preferred_element_type=F32)
        result = (summed[:, :ADIM] / summed[:, ADIM:]).astype(BF16)
        for part, low in enumerate(lows):
            out_ref[:, low : low + ADIM] = result[part * rows : (part + 1) * rows]
        columns = pl.ds(head * share * ADIM, share * ADIM)
        copies.append(
            pltpu.make_async_copy(out_ref.at[:, columns], out_hbm_ref.at[:, columns], sems.at[head])
        )
        copies[-1].start()
    for copy in copies:
        copy.wait()


def norm_kernel(part, hops, *refs):
    local_ref, decay_ref, c_ref, gain_ref, flag_ref = refs[:5]
    got_refs = refs[5 : 5 + hops]
    out_hbm_ref, gated_ref, out_ref, sems = refs[-4:]
    rows, width = gated_ref.shape
    outputs = c_ref[:, part * STATE : (part + 1) * STATE]
    squares = jnp.zeros((rows, 128), F32)
    for start in range(0, width, CHUNK):
        columns = slice(start, start + CHUNK)
        placed = slice(part * width + start, part * width + start + CHUNK)
        state = got_refs[0][:STATE, columns]
        for hop in range(1, hops):
            there = flag_ref[hop, 0:1] > 0.5
            state = jnp.where(there, got_refs[hop][:STATE, columns].astype(F32), state.astype(F32))
        carried = jnp.dot(outputs, state.astype(BF16), preferred_element_type=F32)
        gated = local_ref[:, placed] + carried * decay_ref[:, placed]
        gated_ref[:, columns] = gated
        for lane in range(0, CHUNK, 128):
            squares = squares + gated[:, lane : lane + 128] * gated[:, lane : lane + 128]
    squares = jnp.sum(squares, axis=1, keepdims=True)
    multiplier = lax.rsqrt(squares * (1.0 / width) + EPSILON)
    copies = []
    for start in range(0, width, CHUNK):
        columns = slice(start, start + CHUNK)
        gain = gain_ref[part * width + start : part * width + start + CHUNK]
        out_ref[:, columns] = (gated_ref[:, columns] * multiplier * gain.reshape(1, -1)).astype(BF16)
        copies.append(
            pltpu.make_async_copy(
                out_ref.at[:, pl.ds(start, CHUNK)],
                out_hbm_ref.at[:, pl.ds(part * width + start, CHUNK)],
                sems.at[start // CHUNK],
            )
        )
        copies[-1].start()
    for copy in copies:
        copy.wait()


WHOLE = pl.BlockSpec(memory_space=pltpu.VMEM)
SCALARS = pl.BlockSpec(memory_space=pltpu.SMEM)
UNTOUCHED = pl.BlockSpec(memory_space=pl.ANY)


def tile(rows, columns, row, column):
    return pl.BlockSpec((rows, columns), lambda step: (row, column))


def call(kernel, name, outs, operands, specs, out_specs=None, scratch=(), flops=KERNEL_FLOPS, aliases={}, limit=VMEM_LIMIT):
    moved = sum(math.prod(a.shape) * a.dtype.itemsize for a in (*operands, *outs))
    return pl.pallas_call(
        kernel,
        name=name,
        grid=(1,),
        out_shape=outs,
        in_specs=specs,
        out_specs=[WHOLE] * len(outs) if out_specs is None else out_specs,
        scratch_shapes=list(scratch),
        input_output_aliases=aliases,
        compiler_params=pltpu.CompilerParams(vmem_limit_bytes=limit),
        cost_estimate=pl.CostEstimate(flops=flops, bytes_accessed=moved, transcendentals=0),
    )(*operands)


def onward(value, first=0):
    count = lax.axis_size("seq")
    return lax.ppermute(value, "seq", [(source, source + 1) for source in range(first, count - 1)])


def shards(
    x_raw,
    bc_raw,
    z_gate,
    dt_raw,
    conv_x_weight,
    conv_x_bias,
    conv_bc_weight,
    conv_bc_bias,
    dt_bias,
    a_log,
    skip_d,
    norm_gain,
    queries,
    keys,
    values,
    doc_lens,
):
    rows, width = x_raw.shape
    bc_width = bc_raw.shape[1]
    heads = dt_raw.shape[1]
    groups = bc_width // (2 * STATE)
    per_group = width // groups
    count = lax.axis_size("seq")
    longest = rows * count // 2
    hops = min(count - 1, -(-(longest - 1) // rows))
    assert hops * rows >= longest and (hops <= 2 or groups == 1)
    shape = jax.ShapeDtypeStruct
    dt = dt_raw.T
    params = [dt, conv_x_weight, conv_x_bias, conv_bc_weight, conv_bc_bias, dt_bias, a_log]
    pieces = -(-(width + bc_width) // per_group)
    tail_rows = EDGE * -(-4 * pieces // EDGE)

    (message,) = call(
        first_state_kernel,
        "first_state",
        [shape((STATE + tail_rows, per_group), BF16)],
        [x_raw, bc_raw, *(a if a.ndim > 1 else a[None] for a in params), doc_lens],
        [UNTOUCHED] * 10,
        out_specs=[UNTOUCHED],
        scratch=[
            pltpu.VMEM((rows, per_group), BF16),
            pltpu.VMEM((rows, STATE), BF16),
            pltpu.VMEM((per_group // HDIM, rows), F32),
            pltpu.VMEM((conv_x_weight.shape[0], per_group), F32),
            pltpu.VMEM((1, per_group), F32),
            pltpu.VMEM((conv_x_weight.shape[0], STATE), F32),
            pltpu.VMEM((1, STATE), F32),
            pltpu.VMEM((1, heads), F32),
            pltpu.VMEM((1, heads), F32),
            pltpu.SMEM(doc_lens.shape, jnp.int32),
            pltpu.VMEM((EDGE, width), BF16),
            pltpu.VMEM((EDGE, bc_width), BF16),
            pltpu.VMEM((STATE + tail_rows, per_group), BF16),
            pltpu.VMEM((rows + 8, STATE), F32),
            pltpu.VMEM((4, rows + 8, CHUNK), F32),
            pltpu.SemaphoreType.DMA((12,)),
            pltpu.SemaphoreType.DMA((per_group // (2 * CHUNK) + 1,)),
        ],
        limit=VMEM_ALL,
    )
    slots = [onward(message)]
    prepared = call(
        functools.partial(prepare_kernel, hops, groups),
        "prepare",
        [
            shape((rows, width), BF16),
            shape((rows, bc_width), BF16),
            shape((rows, 2 * keys.shape[1]), BF16),
            shape((8, width + bc_width), F32),
            shape((8, width), F32),
            shape((8, width), F32),
            shape((conv_x_weight.shape[0] - 1, 8, CHUNK), F32),
            shape((hops, 8, CHUNK), F32),
            shape((rows, heads), F32),
            shape((8, width), F32),
            shape((rows, rows), jnp.int32),
            *(shape((STATE, per_group), BF16) for _ in range(groups - 1)),
        ],
        [x_raw, bc_raw, *params, skip_d, doc_lens, keys, values],
        [WHOLE] * 10 + [SCALARS] + [WHOLE] * 2,
        scratch=[
            pltpu.VMEM((16, width + bc_width), F32),
            pltpu.VMEM((4, rows + 8, CHUNK), F32),
        ],
    )
    xc, bcc, kv, partial, weight, through, inside, flags, entry, wide_skip, begin, *states = prepared
    states = [message, *states]
    kvs = [kv, onward(kv)]
    fulls = None
    for slot in range(2, hops + groups):
        part = min(slot - 1, groups) - 1
        fresh = slot <= groups
        if slot == 2:
            kernel = functools.partial(relay_first_kernel, fresh)
            operands = [slots[0], states[0], partial, weight, through, inside, flags, conv_x_weight, conv_bc_weight]
            scratch = [pltpu.VMEM((4, 16, CHUNK), F32)]
        else:
            kernel = functools.partial(relay_kernel, part, fresh)
            operands = [slots[-1], fulls[part], through, flags]
            scratch = []
        if fresh:
            operands.append(states[slot - 1])
        (passed,) = call(
            kernel,
            f"relay_slot{slot}",
            [shape((STATE, per_group), BF16)],
            operands,
            [WHOLE] * len(operands),
            scratch=scratch,
        )
        slots.append(onward(passed))
        if fulls is None:
            gated, decay, c_out, kv_on, *fulls = call(
                functools.partial(local_kernel, groups),
                "local_mix",
                [
                    shape((rows, width), F32),
                    shape((rows, width), F32),
                    shape((rows, groups * STATE), BF16),
                    shape(kv.shape, BF16),
                    *(shape((STATE, per_group), BF16) for _ in range(groups)),
                ],
                [
                    slots[0], partial, weight, inside, conv_x_weight, conv_bc_weight, dt, dt_bias, a_log,
                    wide_skip, begin, kvs[1], entry, z_gate, xc, bcc, *states,
                ],
                [WHOLE] * (16 + groups),
                scratch=[pltpu.VMEM((4, 16, CHUNK), F32)],
            )
    for hop in range(1, hops):
        kvs.append(onward(kv_on if hop == 1 else kvs[-1], hop))

    (attn_out,) = call(
        functools.partial(attend_kernel, hops),
        "attend",
        [shape(queries.shape, BF16)],
        [queries, *reversed(kvs), begin],
        [WHOLE] * (hops + 3),
        out_specs=[UNTOUCHED],
        scratch=[
            pltpu.VMEM(queries.shape, BF16),
            pltpu.SemaphoreType.DMA((keys.shape[1] // ADIM,)),
        ],
    )
    mamba_out = None
    for part in range(groups):
        got = slots[-1:] if part == groups - 1 else slots[part : part + hops]
        operands = [gated, decay, c_out, norm_gain, flags, *got]
        specs = [WHOLE] * (5 + len(got))
        aliases = {}
        if mamba_out is not None:
            operands.append(mamba_out)
            specs.append(UNTOUCHED)
            aliases = {len(operands) - 1: 0}
        (mamba_out,) = call(
            functools.partial(norm_kernel, part, len(got)),
            f"norm_part{part}",
            [shape((rows, width), BF16)],
            operands,
            specs,
            out_specs=[UNTOUCHED],
            scratch=[
                pltpu.VMEM((rows, per_group), F32),
                pltpu.VMEM((rows, per_group), BF16),
                pltpu.SemaphoreType.DMA((per_group // CHUNK,)),
            ],
            aliases=aliases,
        )
    return (mamba_out, attn_out)


def solution(mesh):
    split = P(("groups", "seq"), "dp")
    placed = (
        split,
        split,
        split,
        split,
        P(None, "dp"),
        P("dp"),
        P(None, "dp"),
        P("dp"),
        P("dp"),
        P("dp"),
        P("dp"),
        P("dp"),
        split,
        split,
        split,
        P("groups"),
    )
    return jax.shard_map(
        shards,
        mesh=mesh,
        in_specs=placed,
        out_specs=(split, split),
        check_vma=False,
    )
```

```python
import functools
import math
from typing import NamedTuple

import jax
import jax.numpy as jnp
from jax import lax
from jax.experimental import pallas as pl
from jax.experimental.pallas import tpu as pltpu
from jax.sharding import PartitionSpec as P

HDIM = 64
STATE = 128
QHEADS = 32
KVHEADS = 8
ADIM = 128
EPSILON = 1e-05
BARRED = -2e30
HIGHEST = lax.Precision.HIGHEST
F32 = jnp.float32
BF16 = jnp.bfloat16
CHUNK = 256
EDGE = 16
KERNEL_FLOPS = 2 * 10**9
VMEM_LIMIT = 40 * 1024 * 1024
VMEM_ALL = 62 * 1024 * 1024


def silu(value):
    return value * (0.5 * jnp.tanh(0.5 * value) + 0.5)


def softplus(value):
    return jnp.maximum(value, 0.0) + jnp.log(1.0 + jnp.exp(-jnp.abs(value)))


def doc_start(positions, lens_ref):
    begin = jnp.int32(0)
    found = positions * 0
    for doc in range(lens_ref.shape[0]):
        found = jnp.where(positions >= begin, begin, found)
        begin = begin + lens_ref[doc]
    return found


def halves(value):
    high = value.astype(BF16)
    return high, (value - high.astype(F32)).astype(BF16)


def widen(per_head, first, width):
    heads = per_head.shape[1]
    both = jnp.concatenate(halves(per_head), axis=1)
    head = lax.broadcasted_iota(jnp.int32, (2 * heads, width), 0)
    head = jnp.where(head >= heads, head - heads, head)
    channel = lax.broadcasted_iota(jnp.int32, (2 * heads, width), 1) + first
    spread = (channel // HDIM == head).astype(F32).astype(BF16)
    return jnp.dot(both, spread, preferred_element_type=F32)


def rates(dt_ref, dt_bias_ref, a_log_ref):
    heads = dt_ref.shape[0]
    step = softplus(dt_ref[...].T + dt_bias_ref[...].reshape(1, -1)[:, :heads])
    rate = -step * jnp.exp(a_log_ref[...].reshape(1, -1)[:, :heads])
    rows = step.shape[0]
    row = lax.broadcasted_iota(jnp.int32, (rows, rows), 0)
    column = lax.broadcasted_iota(jnp.int32, (rows, rows), 1)
    lower = (row >= column).astype(F32).astype(BF16)
    high = rate.astype(BF16)
    middle, low = halves(rate - high.astype(F32))
    parts = jnp.concatenate([high, middle, low], axis=0)
    lowers = jnp.concatenate([lower, lower, lower], axis=1)
    return step, jnp.dot(lowers, parts, preferred_element_type=F32)


def insides(first, shape, taps, lens_ref):
    positions = first + lax.broadcasted_iota(jnp.int32, shape, 0)
    depth = positions - doc_start(positions, lens_ref)
    return [depth >= lag for lag in range(taps)]


def conv(pad, rows, weight, bias, inside):
    taps = weight.shape[0]
    total = pad[8 : 8 + rows] * weight[taps - 1 : taps] + bias
    for lag in range(1, taps):
        term = pad[8 - lag : 8 - lag + rows] * weight[taps - 1 - lag : taps - lag]
        total = total + jnp.where(inside[lag], term, 0.0)
    return silu(total).astype(BF16)


def tail_lines(message, rows):
    block = message[rows:].astype(F32)
    return jnp.concatenate([block[at : at + 4] for at in range(0, block.shape[0], 4)], axis=1)


def reach(device, rows, lens_ref):
    return device - doc_start((device + 1) * rows - 1, lens_ref) // rows


def kept_weight(here, step, running, taps, lens_ref):
    rows = step.shape[0]
    last_begin = doc_start((here + 1) * rows - 1, lens_ref)
    row = lax.broadcasted_iota(jnp.int32, step.shape, 0)
    weight = step * jnp.exp(running[rows - 1 : rows] - running)
    kept = (here * rows + row >= last_begin) & ((row >= taps - 1) | (last_begin // rows >= here))
    return jnp.where(kept, weight, 0.0)


def conv_rows(pad, raw, weight, bias, inside):
    pad[0:8] = jnp.zeros((8, raw.shape[1]), F32)
    pad[8:] = raw.astype(F32)
    return conv(pad, raw.shape[0], weight, bias.reshape(1, -1), inside)


def first_state_kernel(*refs):
    hbm_refs, out_hbm_ref = refs[:10], refs[10]
    vmem_refs = refs[11:21]
    x_edge_ref, bc_edge_ref, out_ref, b_pad_ref, pad_ref, in_sems, out_sems = refs[21:]
    x_ref, b_ref, dt_ref, wx_ref, bx_ref, wbc_ref, bbc_ref, dt_bias_ref, a_log_ref, lens_ref = vmem_refs
    rows, width = x_ref.shape
    taps = wx_ref.shape[0]

    def corner(ref, shape):
        return ref.at[tuple(pl.ds(0, extent) for extent in shape)]

    order = (9, 2, 7, 8, 1, 5, 6, 0, 3, 4)
    copies = {}
    for at in order:
        source = corner(hbm_refs[at], vmem_refs[at].shape)
        copies[at] = pltpu.make_async_copy(source, vmem_refs[at], in_sems.at[at])
        copies[at].start()
    edge_copies = []
    for at, (source, target) in enumerate(((hbm_refs[0], x_edge_ref), (hbm_refs[1], bc_edge_ref))):
        edge_copies.append(
            pltpu.make_async_copy(source.at[pl.ds(rows - EDGE, EDGE)], target, in_sems.at[10 + at])
        )
        edge_copies[-1].start()

    here = lax.axis_index("seq")
    for at in (9, 2, 7, 8):
        copies[at].wait()
    inside = insides(here * rows, (rows, CHUNK), taps, lens_ref)
    step, running = rates(dt_ref, dt_bias_ref, a_log_ref)
    weight = kept_weight(here, step, running, taps, lens_ref)
    narrow = [mask[:, :STATE] for mask in inside]
    for at in (1, 5, 6):
        copies[at].wait()
    inputs = conv_rows(b_pad_ref, b_ref[...], wbc_ref[...], bbc_ref[...], narrow)
    turned = inputs.astype(F32).T.astype(BF16)
    for at in (0, 3, 4):
        copies[at].wait()
    slots = pad_ref.shape[0]
    outs = []

    def send(at, view):
        copy = pltpu.make_async_copy(out_ref.at[view], out_hbm_ref.at[view], out_sems.at[at])
        copy.start()
        outs.append(copy)

    for at, start in enumerate(range(0, width, CHUNK)):
        columns = slice(start, start + CHUNK)
        pad = pad_ref.at[(at + 1) % slots]
        xc = conv_rows(pad, x_ref[:, columns], wx_ref[:, columns], bx_ref[:, columns], inside)
        weighted = (xc.astype(F32) * widen(weight, start, CHUNK)).astype(BF16)
        out_ref[:STATE, columns] = jnp.dot(turned, weighted, preferred_element_type=F32).astype(BF16)
        if at % 2:
            send(at // 2, (pl.ds(0, STATE), pl.ds(start - CHUNK, 2 * CHUNK)))
    for copy in edge_copies:
        copy.wait()
    edges = jnp.concatenate([x_edge_ref[...].astype(F32), bc_edge_ref[...].astype(F32)], axis=1)[EDGE - 4 :]
    spare = -edges.shape[1] % width
    if spare:
        edges = jnp.concatenate([edges, jnp.zeros((4, spare), F32)], axis=1)
    pieces = [edges[:, at : at + width] for at in range(0, edges.shape[1], width)]
    while len(pieces) % (EDGE // 4):
        pieces.append(jnp.zeros_like(pieces[0]))
    out_ref[STATE:] = jnp.concatenate(pieces, axis=0).astype(BF16)
    send(width // (2 * CHUNK), (pl.ds(STATE, out_ref.shape[0] - STATE), pl.ds(0, width)))
    for copy in outs:
        copy.wait()


def prepare_kernel(hops, groups, *refs):
    x_ref, bc_ref, dt_ref, wx_ref, bx_ref, wbc_ref, bbc_ref, dt_bias_ref, a_log_ref, skip_ref, lens_ref = refs[:11]
    keys_ref, values_ref = refs[11:13]
    xc_ref, bcc_ref, kv_ref, partial_ref, weight_ref, through_ref, inside_ref, flag_ref, entry_ref = refs[13:22]
    wide_skip_ref, begin_ref = refs[22:24]
    state_refs = refs[24:-2]
    top_ref, pad_ref = refs[-2:]
    rows, width = x_ref.shape
    per_group = width // groups
    taps = wx_ref.shape[0]
    slots = pad_ref.shape[0]
    here = lax.axis_index("seq")
    first = here * rows
    kv_width = keys_ref.shape[1]
    kv_ref[:, :kv_width] = keys_ref[...]
    kv_ref[:, kv_width:] = values_ref[...]
    inside = insides(first, (rows, CHUNK), taps, lens_ref)
    step, running = rates(dt_ref, dt_bias_ref, a_log_ref)
    heads = step.shape[1]
    group_heads = heads // groups
    kept = kept_weight(here, step, running, taps, lens_ref)
    for group in range(groups):
        base = slice(group * 2 * STATE, (group + 1) * 2 * STATE)
        pair = conv_rows(pad_ref.at[0], bc_ref[:, base], wbc_ref[:, base], bbc_ref[base], inside)
        bcc_ref[:, base] = pair
        turned = pair[:, :STATE].astype(F32).T.astype(BF16)
        part_weight = kept[:, group * group_heads : (group + 1) * group_heads]
        for chunk in range(0, per_group, CHUNK):
            columns = slice(group * per_group + chunk, group * per_group + chunk + CHUNK)
            pad = pad_ref.at[(chunk // CHUNK + 1) % slots]
            xc = conv_rows(pad, x_ref[:, columns], wx_ref[:, columns], bx_ref[columns], inside)
            xc_ref[:, columns] = xc
            if group:
                weighted = (xc.astype(F32) * widen(part_weight, chunk, CHUNK)).astype(BF16)
                state_refs[group - 1][:, chunk : chunk + CHUNK] = jnp.dot(
                    turned, weighted, preferred_element_type=F32
                ).astype(BF16)

    own = reach(here, rows, lens_ref) == 0
    inside = [mask[:8] for mask in inside]
    for lag in range(1, taps):
        inside_ref[lag - 1] = inside[lag].astype(F32)
    flag_ref[0] = jnp.broadcast_to(own.astype(F32), (8, CHUNK))
    before = reach(here - 1, rows, lens_ref)
    for hop in range(1, hops):
        flag_ref[hop] = jnp.broadcast_to((before == hop).astype(F32), (8, CHUNK))
    begin = doc_start(first + lax.broadcasted_iota(jnp.int32, begin_ref.shape, 0), lens_ref)
    begin_ref[...] = begin
    entry_ref[...] = jnp.where(begin[:, :heads] < first, jnp.exp(running), 0.0)
    row = lax.broadcasted_iota(jnp.int32, (8, heads), 0)
    total = running[rows - 1 : rows]
    weight = step[:8] * jnp.exp(total - running[:8])
    weight = jnp.where((row < taps - 1) & jnp.logical_not(own), weight, 0.0)
    through = jnp.where(own, 0.0, jnp.broadcast_to(jnp.exp(total), (8, heads)))
    skip = jnp.broadcast_to(skip_ref[...].reshape(1, -1), (8, heads))
    every = jnp.concatenate([weight, through, skip], axis=0)
    for start in range(0, width, CHUNK):
        wide = widen(every, start, CHUNK)
        weight_ref[:, start : start + CHUNK] = wide[:8]
        through_ref[:, start : start + CHUNK] = wide[8:16]
        wide_skip_ref[:, start : start + CHUNK] = wide[16:]
    top_ref[0:8] = jnp.zeros((8, top_ref.shape[1]), F32)
    top_ref[8:, :width] = x_ref[:EDGE].astype(F32)[:8]
    top_ref[8:, width:] = bc_ref[:EDGE].astype(F32)[:8]

    def some(columns, base, w_ref, b_ref):
        here_columns = slice(base + columns.start, base + columns.stop)
        total = top_ref[8:, here_columns] * w_ref[taps - 1 : taps, columns] + b_ref[columns].reshape(1, -1)
        for lag in range(1, taps):
            term = top_ref[8 - lag : 16 - lag, here_columns] * w_ref[taps - 1 - lag : taps - lag, columns]
            total = total + jnp.where(inside[lag], term, 0.0)
        partial_ref[:, here_columns] = total

    for start in range(0, width, CHUNK):
        some(slice(start, start + CHUNK), 0, wx_ref, bx_ref)
    for start in range(0, bc_ref.shape[1], CHUNK):
        some(slice(start, start + CHUNK), width, wbc_ref, bbc_ref)


def first_rows(lines, partial_ref, inside_ref, w_ref, pad_ref, slot, at, start):
    taps = w_ref.shape[0]
    columns = slice(start, start + CHUNK)
    pad = pad_ref.at[slot]
    pad[4:8] = lines[:, at + start : at + start + CHUNK]
    pad[8:] = jnp.zeros((8, CHUNK), F32)
    total = partial_ref[:, at + start : at + start + CHUNK]
    for lag in range(1, taps):
        term = pad[8 - lag : 16 - lag] * w_ref[taps - 1 - lag : taps - lag, columns]
        total = total + term * inside_ref[lag - 1]
    return silu(total).astype(BF16)


def relay_first_kernel(fresh, *refs):
    message_ref, state_ref, partial_ref, weight_ref, through_ref, inside_ref, flag_ref, wx_ref, wbc_ref = refs[:9]
    other_ref = refs[9] if fresh else state_ref
    out_ref, pad_ref = refs[-2:]
    width = out_ref.shape[1]
    slots = pad_ref.shape[0]
    lines = tail_lines(message_ref, STATE)
    top = functools.partial(first_rows, lines, partial_ref, inside_ref)
    inputs = top(wbc_ref, pad_ref, 0, wx_ref.shape[1], 0)[:, :STATE]
    turned = inputs.astype(F32).T.astype(BF16)
    own = flag_ref[0, 0:1] > 0.5
    for start in range(0, width, CHUNK):
        columns = slice(start, start + CHUNK)
        xc = top(wx_ref, pad_ref, (start // CHUNK + 1) % slots, 0, start)
        weighted = (xc.astype(F32) * weight_ref[:, columns]).astype(BF16)
        full = state_ref[:STATE, columns].astype(F32) + jnp.dot(
            turned, weighted, preferred_element_type=F32
        )
        full = full + through_ref[0:1, columns] * message_ref[:STATE, columns].astype(F32)
        out_ref[:, columns] = jnp.where(own, other_ref[:STATE, columns].astype(F32), full).astype(BF16)


def relay_kernel(part, fresh, *refs):
    got_ref, state_ref, through_ref, flag_ref = refs[:4]
    out_ref = refs[-1]
    width = out_ref.shape[1]
    own = flag_ref[0, 0:1] > 0.5
    for start in range(0, width, CHUNK):
        columns = slice(start, start + CHUNK)
        through = through_ref[0:1, part * width + start : part * width + start + CHUNK]
        full = state_ref[:, columns].astype(F32) + through * got_ref[:STATE, columns].astype(F32)
        if fresh:
            full = jnp.where(own, refs[4][:STATE, columns].astype(F32), full)
        out_ref[:, columns] = full.astype(BF16)


def local_kernel(groups, *refs):
    (
        message_ref, partial_ref, weight_ref, inside_ref, wx_ref, wbc_ref, dt_ref, dt_bias_ref,
        a_log_ref, wide_skip_ref, begin_ref, entry_ref, z_ref, xc_ref, bcc_ref,
    ) = refs[:15]
    state_refs = refs[15 : 15 + groups]
    out_ref, decay_ref, c_ref = refs[15 + groups : 18 + groups]
    full_refs = refs[18 + groups : 18 + 2 * groups]

    pad_ref = refs[-1]
    rows, width = xc_ref.shape
    per_group = width // groups
    heads = per_group // HDIM
    first = lax.axis_index("seq") * rows
    lines = tail_lines(message_ref, STATE)
    slots = pad_ref.shape[0]

    def top(w_ref, slot, at, start, below):
        new = first_rows(lines, partial_ref, inside_ref, w_ref, pad_ref, slot, at, start)
        old = below[8:EDGE].astype(F32)
        return jnp.concatenate([jnp.concatenate([new.astype(F32), old], axis=0).astype(BF16), below[EDGE:]], axis=0)

    row = lax.broadcasted_iota(jnp.int32, (rows, rows), 0)
    lane_row = lax.broadcasted_iota(jnp.int32, (rows, rows), 1)
    linked = (row >= lane_row) & (first + lane_row >= begin_ref[...])
    step, running = rates(dt_ref, dt_bias_ref, a_log_ref)
    turned_running = running.T
    turned_step = step.T
    pair_width = 2 * HDIM
    lane = lax.broadcasted_iota(jnp.int32, (rows, pair_width), 1)
    for group in range(groups):
        base = group * 2 * STATE
        pair = top(wbc_ref, group % slots, width, base, bcc_ref[:, base : base + 2 * STATE])
        inputs = pair[:, :STATE]
        outputs = pair[:, STATE:]
        c_ref[:, group * STATE : (group + 1) * STATE] = outputs
        turned = inputs[:EDGE].astype(F32).T[:, :8].astype(BF16)
        meet = lax.dot_general(
            outputs, inputs, (((1,), (1,)), ((), ())), preferred_element_type=F32
        )
        meet = jnp.where(linked, meet, 0.0)
        for chunk in range(0, per_group, CHUNK):
            at = group * per_group + chunk
            columns = slice(chunk, chunk + CHUNK)
            xc_all = top(wx_ref, (chunk // CHUNK) % slots, 0, at, xc_ref[:, at : at + CHUNK])
            weighted = xc_all[:EDGE].astype(F32)[:8] * weight_ref[:, at : at + CHUNK]
            full = state_refs[group][:STATE, columns].astype(F32) + jnp.dot(
                turned, weighted.astype(BF16), preferred_element_type=F32
            )
            full_refs[group][:, columns] = full.astype(BF16)
            wide_skip = wide_skip_ref[0:1, at : at + CHUNK]
            gate = silu(z_ref[:, at : at + CHUNK].astype(F32))
            entry = entry_ref[:, group * heads : (group + 1) * heads]
            decay_ref[:, at : at + CHUNK] = widen(entry, chunk, CHUNK) * gate
            for start in range(0, CHUNK, pair_width):
                parts = []
                for head in ((at + start) // HDIM, (at + start) // HDIM + 1):
                    spread = running[:, head : head + 1] - turned_running[head : head + 1]
                    decay = jnp.exp(jnp.minimum(spread, 0.0))
                    parts.append((decay * (meet * turned_step[head : head + 1])).astype(BF16))
                mix = jnp.concatenate(parts, axis=1)
                xc = xc_all[:, start : start + pair_width]
                zero = jnp.zeros_like(xc)
                stacked = jnp.concatenate(
                    [jnp.where(lane < HDIM, xc, zero), jnp.where(lane < HDIM, zero, xc)], axis=0
                )
                value = jnp.dot(mix, stacked, preferred_element_type=F32)
                value = value + xc.astype(F32) * wide_skip[:, start : start + pair_width]
                out_ref[:, at + start : at + start + pair_width] = value * gate[:, start : start + pair_width]


def attend(q_ref, kv_refs, begin_ref, blocks, share, head):
    rows = q_ref.shape[0]
    kv_heads = kv_refs[0].shape[1] // (2 * ADIM)
    count = rows * blocks.count
    here = lax.axis_index("seq")
    row = here * rows + lax.broadcasted_iota(jnp.int32, (rows, count), 0)
    lane = (here - blocks.farthest) * rows + lax.broadcasted_iota(jnp.int32, (rows, count), 1)
    begin = jnp.concatenate([begin_ref[...]] * blocks.count, axis=1)
    allowed = jnp.concatenate([(lane <= row) & (lane >= begin)] * share, axis=0)
    low = head * ADIM
    keys = jnp.concatenate([ref[:, low : low + ADIM] for ref in kv_refs], axis=0)
    low = (kv_heads + head) * ADIM
    values = jnp.concatenate([ref[:, low : low + ADIM] for ref in kv_refs], axis=0)
    values = jnp.concatenate([values, jnp.ones((count, ADIM), BF16)], axis=1)
    lows = [(head * share + part) * ADIM for part in range(share)]
    asking = jnp.concatenate([q_ref[:, low : low + ADIM] for low in lows], axis=0)
    scores = lax.dot_general(asking, keys, (((1,), (1,)), ((), ())), preferred_element_type=F32)
    return jnp.where(allowed, scores * ADIM ** (-0.5), BARRED), values


class Blocks(NamedTuple):
    farthest: int
    count: int


def near_kernel(*refs):
    q_ref, before_ref, own_ref, begin_ref, _, sum_ref, total_ref, peak_ref, kv_ref = refs
    kv_ref[...] = before_ref[...]
    rows = q_ref.shape[0]
    share = QHEADS // KVHEADS
    for head in range(own_ref.shape[1] // (2 * ADIM)):
        scores, values = attend(q_ref, (before_ref, own_ref), begin_ref, Blocks(1, 2), share, head)
        peak = jnp.max(scores, axis=1, keepdims=True)
        summed = jnp.dot(jnp.exp(scores - peak).astype(BF16), values, preferred_element_type=F32)
        peak = jnp.broadcast_to(peak, (peak.shape[0], ADIM))
        for part in range(share):
            low = (head * share + part) * ADIM
            these = slice(part * rows, (part + 1) * rows)
            sum_ref[:, low : low + ADIM] = summed[these, :ADIM]
            total_ref[:, low : low + ADIM] = summed[these, ADIM:]
            peak_ref[:, low : low + ADIM] = peak[these]


def far_kernel(hops, *refs):
    q_ref, begin_ref, sum_ref, total_ref, peak_ref = refs[:5]
    kv_refs = refs[5 : 4 + hops]
    out_hbm_ref, out_ref, sems = refs[4 + hops :]
    rows = q_ref.shape[0]
    share = QHEADS // KVHEADS
    copies = []
    for head in range(kv_refs[0].shape[1] // (2 * ADIM)):
        lows = [(head * share + part) * ADIM for part in range(share)]

        def stacked(ref):
            return jnp.concatenate([ref[:, low : low + ADIM] for low in lows], axis=0)

        scores, values = attend(q_ref, kv_refs, begin_ref, Blocks(hops, hops - 1), share, head)
        near = stacked(peak_ref)
        peak = jnp.maximum(near, jnp.max(scores, axis=1, keepdims=True))
        expo = jnp.exp(scores - jnp.concatenate([peak] * (scores.shape[1] // ADIM), axis=1))
        summed = jnp.dot(expo.astype(BF16), values, preferred_element_type=F32)
        factor = jnp.exp(near - peak)
        total = stacked(total_ref) * factor + summed[:, ADIM:]
        result = ((stacked(sum_ref) * factor + summed[:, :ADIM]) / total).astype(BF16)
        for part, low in enumerate(lows):
            out_ref[:, low : low + ADIM] = result[part * rows : (part + 1) * rows]
        columns = pl.ds(head * share * ADIM, share * ADIM)
        copies.append(
            pltpu.make_async_copy(out_ref.at[:, columns], out_hbm_ref.at[:, columns], sems.at[head])
        )
        copies[-1].start()
    for copy in copies:
        copy.wait()


def norm_kernel(part, hops, *refs):
    local_ref, decay_ref, c_ref, gain_ref, flag_ref = refs[:5]
    got_refs = refs[5 : 5 + hops]
    out_hbm_ref, gated_ref, out_ref, sems = refs[-4:]
    rows, width = gated_ref.shape
    outputs = c_ref[:, part * STATE : (part + 1) * STATE]
    squares = jnp.zeros((rows, 128), F32)
    for start in range(0, width, CHUNK):
        columns = slice(start, start + CHUNK)
        placed = slice(part * width + start, part * width + start + CHUNK)
        state = got_refs[0][:STATE, columns]
        for hop in range(1, hops):
            there = flag_ref[hop, 0:1] > 0.5
            state = jnp.where(there, got_refs[hop][:STATE, columns].astype(F32), state.astype(F32))
        carried = jnp.dot(outputs, state.astype(BF16), preferred_element_type=F32)
        gated = local_ref[:, placed] + carried * decay_ref[:, placed]
        gated_ref[:, columns] = gated
        for lane in range(0, CHUNK, 128):
            squares = squares + gated[:, lane : lane + 128] * gated[:, lane : lane + 128]
    squares = jnp.sum(squares, axis=1, keepdims=True)
    multiplier = lax.rsqrt(squares * (1.0 / width) + EPSILON)
    copies = []
    for start in range(0, width, CHUNK):
        columns = slice(start, start + CHUNK)
        gain = gain_ref[part * width + start : part * width + start + CHUNK]
        out_ref[:, columns] = (gated_ref[:, columns] * multiplier * gain.reshape(1, -1)).astype(BF16)
        copies.append(
            pltpu.make_async_copy(
                out_ref.at[:, pl.ds(start, CHUNK)],
                out_hbm_ref.at[:, pl.ds(part * width + start, CHUNK)],
                sems.at[start // CHUNK],
            )
        )
        copies[-1].start()
    for copy in copies:
        copy.wait()


WHOLE = pl.BlockSpec(memory_space=pltpu.VMEM)
SCALARS = pl.BlockSpec(memory_space=pltpu.SMEM)
UNTOUCHED = pl.BlockSpec(memory_space=pl.ANY)


def tile(rows, columns, row, column):
    return pl.BlockSpec((rows, columns), lambda step: (row, column))


def call(kernel, name, outs, operands, specs, out_specs=None, scratch=(), flops=KERNEL_FLOPS, aliases={}, limit=VMEM_LIMIT):
    moved = sum(math.prod(a.shape) * a.dtype.itemsize for a in (*operands, *outs))
    return pl.pallas_call(
        kernel,
        name=name,
        grid=(1,),
        out_shape=outs,
        in_specs=specs,
        out_specs=[WHOLE] * len(outs) if out_specs is None else out_specs,
        scratch_shapes=list(scratch),
        input_output_aliases=aliases,
        compiler_params=pltpu.CompilerParams(vmem_limit_bytes=limit),
        cost_estimate=pl.CostEstimate(flops=flops, bytes_accessed=moved, transcendentals=0),
    )(*operands)


def onward(value, first=0):
    count = lax.axis_size("seq")
    return lax.ppermute(value, "seq", [(source, source + 1) for source in range(first, count - 1)])


def shards(
    x_raw,
    bc_raw,
    z_gate,
    dt_raw,
    conv_x_weight,
    conv_x_bias,
    conv_bc_weight,
    conv_bc_bias,
    dt_bias,
    a_log,
    skip_d,
    norm_gain,
    queries,
    keys,
    values,
    doc_lens,
):
    rows, width = x_raw.shape
    bc_width = bc_raw.shape[1]
    heads = dt_raw.shape[1]
    groups = bc_width // (2 * STATE)
    per_group = width // groups
    count = lax.axis_size("seq")
    longest = rows * count // 2
    hops = min(count - 1, -(-(longest - 1) // rows))
    assert hops * rows >= longest and (hops == 2 or hops > 2 and groups == 1)
    shape = jax.ShapeDtypeStruct
    dt = dt_raw.T
    params = [dt, conv_x_weight, conv_x_bias, conv_bc_weight, conv_bc_bias, dt_bias, a_log]
    pieces = -(-(width + bc_width) // per_group)
    tail_rows = EDGE * -(-4 * pieces // EDGE)

    (message,) = call(
        first_state_kernel,
        "first_state",
        [shape((STATE + tail_rows, per_group), BF16)],
        [x_raw, bc_raw, *(a if a.ndim > 1 else a[None] for a in params), doc_lens],
        [UNTOUCHED] * 10,
        out_specs=[UNTOUCHED],
        scratch=[
            pltpu.VMEM((rows, per_group), BF16),
            pltpu.VMEM((rows, STATE), BF16),
            pltpu.VMEM((per_group // HDIM, rows), F32),
            pltpu.VMEM((conv_x_weight.shape[0], per_group), F32),
            pltpu.VMEM((1, per_group), F32),
            pltpu.VMEM((conv_x_weight.shape[0], STATE), F32),
            pltpu.VMEM((1, STATE), F32),
            pltpu.VMEM((1, heads), F32),
            pltpu.VMEM((1, heads), F32),
            pltpu.SMEM(doc_lens.shape, jnp.int32),
            pltpu.VMEM((EDGE, width), BF16),
            pltpu.VMEM((EDGE, bc_width), BF16),
            pltpu.VMEM((STATE + tail_rows, per_group), BF16),
            pltpu.VMEM((rows + 8, STATE), F32),
            pltpu.VMEM((4, rows + 8, CHUNK), F32),
            pltpu.SemaphoreType.DMA((12,)),
            pltpu.SemaphoreType.DMA((per_group // (2 * CHUNK) + 1,)),
        ],
        limit=VMEM_ALL,
    )
    slots = [onward(message)]
    prepared = call(
        functools.partial(prepare_kernel, hops, groups),
        "prepare",
        [
            shape((rows, width), BF16),
            shape((rows, bc_width), BF16),
            shape((rows, 2 * keys.shape[1]), BF16),
            shape((8, width + bc_width), F32),
            shape((8, width), F32),
            shape((8, width), F32),
            shape((conv_x_weight.shape[0] - 1, 8, CHUNK), F32),
            shape((hops, 8, CHUNK), F32),
            shape((rows, heads), F32),
            shape((8, width), F32),
            shape((rows, rows), jnp.int32),
            *(shape((STATE, per_group), BF16) for _ in range(groups - 1)),
        ],
        [x_raw, bc_raw, *params, skip_d, doc_lens, keys, values],
        [WHOLE] * 10 + [SCALARS] + [WHOLE] * 2,
        scratch=[
            pltpu.VMEM((16, width + bc_width), F32),
            pltpu.VMEM((4, rows + 8, CHUNK), F32),
        ],
    )
    xc, bcc, kv, partial, weight, through, inside, flags, entry, wide_skip, begin, *states = prepared
    states = [message, *states]
    kvs = [kv, onward(kv)]
    fulls = None
    for slot in range(2, hops + groups):
        part = min(slot - 1, groups) - 1
        fresh = slot <= groups
        if slot == 2:
            kernel = functools.partial(relay_first_kernel, fresh)
            operands = [slots[0], states[0], partial, weight, through, inside, flags, conv_x_weight, conv_bc_weight]
            scratch = [pltpu.VMEM((4, 16, CHUNK), F32)]
        else:
            kernel = functools.partial(relay_kernel, part, fresh)
            operands = [slots[-1], fulls[part], through, flags]
            scratch = []
        if fresh:
            operands.append(states[slot - 1])
        (passed,) = call(
            kernel,
            f"relay_slot{slot}",
            [shape((STATE, per_group), BF16)],
            operands,
            [WHOLE] * len(operands),
            scratch=scratch,
        )
        slots.append(onward(passed))
        if fulls is None:
            gated, decay, c_out, *fulls = call(
                functools.partial(local_kernel, groups),
                "local_mix",
                [
                    shape((rows, width), F32),
                    shape((rows, width), F32),
                    shape((rows, groups * STATE), BF16),
                    *(shape((STATE, per_group), BF16) for _ in range(groups)),
                ],
                [
                    slots[0], partial, weight, inside, conv_x_weight, conv_bc_weight, dt, dt_bias, a_log,
                    wide_skip, begin, entry, z_gate, xc, bcc, *states,
                ],
                [WHOLE] * (15 + groups),
                scratch=[pltpu.VMEM((4, 16, CHUNK), F32)],
            )
    parts = shape(queries.shape, F32)
    *near, kv_on = call(
        near_kernel,
        "attend_near",
        [parts, parts, parts, shape(kv.shape, BF16)],
        [queries, kvs[1], kv, begin, c_out],
        [WHOLE] * 4 + [UNTOUCHED],
    )
    for hop in range(1, hops):
        kvs.append(onward(kv_on if hop == 1 else kvs[-1], hop))
    (attn_out,) = call(
        functools.partial(far_kernel, hops),
        "attend_far",
        [shape(queries.shape, BF16)],
        [queries, begin, *near, *reversed(kvs[2:])],
        [WHOLE] * (4 + hops),
        out_specs=[UNTOUCHED],
        scratch=[
            pltpu.VMEM(queries.shape, BF16),
            pltpu.SemaphoreType.DMA((keys.shape[1] // ADIM,)),
        ],
    )
    mamba_out = None
    for part in range(groups):
        got = slots[-1:] if part == groups - 1 else slots[part : part + hops]
        operands = [gated, decay, c_out, norm_gain, flags, *got]
        specs = [WHOLE] * (5 + len(got))
        aliases = {}
        if mamba_out is not None:
            operands.append(mamba_out)
            specs.append(UNTOUCHED)
            aliases = {len(operands) - 1: 0}
        (mamba_out,) = call(
            functools.partial(norm_kernel, part, len(got)),
            f"norm_part{part}",
            [shape((rows, width), BF16)],
            operands,
            specs,
            out_specs=[UNTOUCHED],
            scratch=[
                pltpu.VMEM((rows, per_group), F32),
                pltpu.VMEM((rows, per_group), BF16),
                pltpu.SemaphoreType.DMA((per_group // CHUNK,)),
            ],
            aliases=aliases,
        )
    return (mamba_out, attn_out)


def solution(mesh):
    split = P(("groups", "seq"), "dp")
    placed = (
        split,
        split,
        split,
        split,
        P(None, "dp"),
        P("dp"),
        P(None, "dp"),
        P("dp"),
        P("dp"),
        P("dp"),
        P("dp"),
        P("dp"),
        split,
        split,
        split,
        P("groups"),
    )
    return jax.shard_map(
        shards,
        mesh=mesh,
        in_specs=placed,
        out_specs=(split, split),
        check_vma=False,
    )
```

```python
import functools
import math
from typing import NamedTuple

import jax
import jax.numpy as jnp
from jax import lax
from jax.experimental import pallas as pl
from jax.experimental.pallas import tpu as pltpu
from jax.sharding import PartitionSpec as P

HDIM = 64
STATE = 128
QHEADS = 32
KVHEADS = 8
ADIM = 128
EPSILON = 1e-05
BARRED = -2e30
HIGHEST = lax.Precision.HIGHEST
F32 = jnp.float32
BF16 = jnp.bfloat16
CHUNK = 256
EDGE = 16
KERNEL_FLOPS = 2 * 10**9
VMEM_LIMIT = 40 * 1024 * 1024
VMEM_ALL = 62 * 1024 * 1024


def silu(value):
    return value * (0.5 * jnp.tanh(0.5 * value) + 0.5)


def softplus(value):
    return jnp.maximum(value, 0.0) + jnp.log(1.0 + jnp.exp(-jnp.abs(value)))


def doc_start(positions, lens_ref):
    begin = jnp.int32(0)
    found = positions * 0
    for doc in range(lens_ref.shape[0]):
        found = jnp.where(positions >= begin, begin, found)
        begin = begin + lens_ref[doc]
    return found


def halves(value):
    high = value.astype(BF16)
    return high, (value - high.astype(F32)).astype(BF16)


def widen(per_head, first, width):
    heads = per_head.shape[1]
    both = jnp.concatenate(halves(per_head), axis=1)
    head = lax.broadcasted_iota(jnp.int32, (2 * heads, width), 0)
    head = jnp.where(head >= heads, head - heads, head)
    channel = lax.broadcasted_iota(jnp.int32, (2 * heads, width), 1) + first
    spread = (channel // HDIM == head).astype(F32).astype(BF16)
    return jnp.dot(both, spread, preferred_element_type=F32)


def rates(dt_ref, dt_bias_ref, a_log_ref):
    heads = dt_ref.shape[0]
    step = softplus(dt_ref[...].T + dt_bias_ref[...].reshape(1, -1)[:, :heads])
    rate = -step * jnp.exp(a_log_ref[...].reshape(1, -1)[:, :heads])
    rows = step.shape[0]
    row = lax.broadcasted_iota(jnp.int32, (rows, rows), 0)
    column = lax.broadcasted_iota(jnp.int32, (rows, rows), 1)
    lower = (row >= column).astype(F32).astype(BF16)
    high = rate.astype(BF16)
    middle, low = halves(rate - high.astype(F32))
    parts = jnp.concatenate([high, middle, low], axis=0)
    lowers = jnp.concatenate([lower, lower, lower], axis=1)
    return step, jnp.dot(lowers, parts, preferred_element_type=F32)


def insides(first, shape, taps, lens_ref):
    positions = first + lax.broadcasted_iota(jnp.int32, shape, 0)
    depth = positions - doc_start(positions, lens_ref)
    return [depth >= lag for lag in range(taps)]


def conv(pad, rows, weight, bias, inside):
    taps = weight.shape[0]
    total = pad[8 : 8 + rows] * weight[taps - 1 : taps] + bias
    for lag in range(1, taps):
        term = pad[8 - lag : 8 - lag + rows] * weight[taps - 1 - lag : taps - lag]
        total = total + jnp.where(inside[lag], term, 0.0)
    return silu(total).astype(BF16)


def tail_lines(message, rows):
    block = message[rows:].astype(F32)
    return jnp.concatenate([block[at : at + 4] for at in range(0, block.shape[0], 4)], axis=1)


def reach(device, rows, lens_ref):
    return device - doc_start((device + 1) * rows - 1, lens_ref) // rows


def kept_weight(here, step, running, taps, lens_ref):
    rows = step.shape[0]
    last_begin = doc_start((here + 1) * rows - 1, lens_ref)
    row = lax.broadcasted_iota(jnp.int32, step.shape, 0)
    weight = step * jnp.exp(running[rows - 1 : rows] - running)
    kept = (here * rows + row >= last_begin) & ((row >= taps - 1) | (last_begin // rows >= here))
    return jnp.where(kept, weight, 0.0)


def conv_rows(pad, raw, weight, bias, inside):
    pad[0:8] = jnp.zeros((8, raw.shape[1]), F32)
    pad[8:] = raw.astype(F32)
    return conv(pad, raw.shape[0], weight, bias.reshape(1, -1), inside)


def first_state_kernel(*refs):
    hbm_refs, out_hbm_ref = refs[:10], refs[10]
    vmem_refs = refs[11:21]
    x_edge_ref, bc_edge_ref, out_ref, b_pad_ref, pad_ref, in_sems, out_sems = refs[21:]
    x_ref, b_ref, dt_ref, wx_ref, bx_ref, wbc_ref, bbc_ref, dt_bias_ref, a_log_ref, lens_ref = vmem_refs
    rows, width = x_ref.shape
    taps = wx_ref.shape[0]

    def corner(ref, shape):
        return ref.at[tuple(pl.ds(0, extent) for extent in shape)]

    order = (9, 2, 7, 8, 1, 5, 6, 0, 3, 4)
    copies = {}
    for at in order:
        source = corner(hbm_refs[at], vmem_refs[at].shape)
        copies[at] = pltpu.make_async_copy(source, vmem_refs[at], in_sems.at[at])
        copies[at].start()
    edge_copies = []
    for at, (source, target) in enumerate(((hbm_refs[0], x_edge_ref), (hbm_refs[1], bc_edge_ref))):
        edge_copies.append(
            pltpu.make_async_copy(source.at[pl.ds(rows - EDGE, EDGE)], target, in_sems.at[10 + at])
        )
        edge_copies[-1].start()

    here = lax.axis_index("seq")
    for at in (9, 2, 7, 8):
        copies[at].wait()
    inside = insides(here * rows, (rows, CHUNK), taps, lens_ref)
    step, running = rates(dt_ref, dt_bias_ref, a_log_ref)
    weight = kept_weight(here, step, running, taps, lens_ref)
    narrow = [mask[:, :STATE] for mask in inside]
    for at in (1, 5, 6):
        copies[at].wait()
    inputs = conv_rows(b_pad_ref, b_ref[...], wbc_ref[...], bbc_ref[...], narrow)
    turned = inputs.astype(F32).T.astype(BF16)
    for at in (0, 3, 4):
        copies[at].wait()
    slots = pad_ref.shape[0]
    outs = []

    def send(at, view):
        copy = pltpu.make_async_copy(out_ref.at[view], out_hbm_ref.at[view], out_sems.at[at])
        copy.start()
        outs.append(copy)

    for at, start in enumerate(range(0, width, CHUNK)):
        columns = slice(start, start + CHUNK)
        pad = pad_ref.at[(at + 1) % slots]
        xc = conv_rows(pad, x_ref[:, columns], wx_ref[:, columns], bx_ref[:, columns], inside)
        weighted = (xc.astype(F32) * widen(weight, start, CHUNK)).astype(BF16)
        out_ref[:STATE, columns] = jnp.dot(turned, weighted, preferred_element_type=F32).astype(BF16)
        if at % 2:
            send(at // 2, (pl.ds(0, STATE), pl.ds(start - CHUNK, 2 * CHUNK)))
    for copy in edge_copies:
        copy.wait()
    edges = jnp.concatenate([x_edge_ref[...].astype(F32), bc_edge_ref[...].astype(F32)], axis=1)[EDGE - 4 :]
    spare = -edges.shape[1] % width
    if spare:
        edges = jnp.concatenate([edges, jnp.zeros((4, spare), F32)], axis=1)
    pieces = [edges[:, at : at + width] for at in range(0, edges.shape[1], width)]
    while len(pieces) % (EDGE // 4):
        pieces.append(jnp.zeros_like(pieces[0]))
    out_ref[STATE:] = jnp.concatenate(pieces, axis=0).astype(BF16)
    send(width // (2 * CHUNK), (pl.ds(STATE, out_ref.shape[0] - STATE), pl.ds(0, width)))
    for copy in outs:
        copy.wait()


def prepare_kernel(hops, groups, *refs):
    x_ref, bc_ref, dt_ref, wx_ref, bx_ref, wbc_ref, bbc_ref, dt_bias_ref, a_log_ref, skip_ref, lens_ref = refs[:11]
    keys_ref, values_ref, z_ref = refs[11:14]
    xc_ref, bcc_ref, kv_ref, partial_ref, weight_ref, through_ref, inside_ref, flag_ref = refs[14:22]
    wide_skip_ref, begin_ref, step_ref, running_ref, out_ref, gate_ref, decay_ref = refs[22:29]
    state_refs = refs[29:-2]
    top_ref, pad_ref = refs[-2:]
    rows, width = x_ref.shape
    per_group = width // groups
    taps = wx_ref.shape[0]
    slots = pad_ref.shape[0]
    here = lax.axis_index("seq")
    first = here * rows
    kv_width = keys_ref.shape[1]
    kv_ref[:, :kv_width] = keys_ref[...]
    kv_ref[:, kv_width:] = values_ref[...]
    inside = insides(first, (rows, CHUNK), taps, lens_ref)
    step, running = rates(dt_ref, dt_bias_ref, a_log_ref)
    heads = step.shape[1]
    group_heads = heads // groups
    kept = kept_weight(here, step, running, taps, lens_ref)
    for group in range(groups):
        base = slice(group * 2 * STATE, (group + 1) * 2 * STATE)
        pair = conv_rows(pad_ref.at[0], bc_ref[:, base], wbc_ref[:, base], bbc_ref[base], inside)
        bcc_ref[:, base] = pair
        turned = pair[:, :STATE].astype(F32).T.astype(BF16)
        part_weight = kept[:, group * group_heads : (group + 1) * group_heads]
        for chunk in range(0, per_group, CHUNK):
            columns = slice(group * per_group + chunk, group * per_group + chunk + CHUNK)
            pad = pad_ref.at[(chunk // CHUNK + 1) % slots]
            xc = conv_rows(pad, x_ref[:, columns], wx_ref[:, columns], bx_ref[columns], inside)
            xc_ref[:, columns] = xc
            if group:
                weighted = (xc.astype(F32) * widen(part_weight, chunk, CHUNK)).astype(BF16)
                state_refs[group - 1][:, chunk : chunk + CHUNK] = jnp.dot(
                    turned, weighted, preferred_element_type=F32
                ).astype(BF16)

    own = reach(here, rows, lens_ref) == 0
    inside = [mask[:8] for mask in inside]
    for lag in range(1, taps):
        inside_ref[lag - 1] = inside[lag].astype(F32)
    flag_ref[0] = jnp.broadcast_to(own.astype(F32), (8, CHUNK))
    before = reach(here - 1, rows, lens_ref)
    for hop in range(1, hops):
        flag_ref[hop] = jnp.broadcast_to((before == hop).astype(F32), (8, CHUNK))
    begin = doc_start(first + lax.broadcasted_iota(jnp.int32, begin_ref.shape, 0), lens_ref)
    begin_ref[...] = begin
    entry = jnp.where(begin[:, :heads] < first, jnp.exp(running), 0.0)
    step_ref[...] = step
    running_ref[...] = running
    row = lax.broadcasted_iota(jnp.int32, (8, heads), 0)
    total = running[rows - 1 : rows]
    weight = step[:8] * jnp.exp(total - running[:8])
    weight = jnp.where((row < taps - 1) & jnp.logical_not(own), weight, 0.0)
    through = jnp.where(own, 0.0, jnp.broadcast_to(jnp.exp(total), (8, heads)))
    skip = jnp.broadcast_to(skip_ref[...].reshape(1, -1), (8, heads))
    every = jnp.concatenate([weight, through, skip], axis=0)
    for start in range(0, width, CHUNK):
        wide = widen(every, start, CHUNK)
        weight_ref[:, start : start + CHUNK] = wide[:8]
        through_ref[:, start : start + CHUNK] = wide[8:16]
        wide_skip_ref[:, start : start + CHUNK] = wide[16:]
    top_ref[0:8] = jnp.zeros((8, top_ref.shape[1]), F32)
    top_ref[8:, :width] = x_ref[:EDGE].astype(F32)[:8]
    top_ref[8:, width:] = bc_ref[:EDGE].astype(F32)[:8]

    def some(columns, base, w_ref, b_ref):
        here_columns = slice(base + columns.start, base + columns.stop)
        total = top_ref[8:, here_columns] * w_ref[taps - 1 : taps, columns] + b_ref[columns].reshape(1, -1)
        for lag in range(1, taps):
            term = top_ref[8 - lag : 16 - lag, here_columns] * w_ref[taps - 1 - lag : taps - lag, columns]
            total = total + jnp.where(inside[lag], term, 0.0)
        partial_ref[:, here_columns] = total

    for start in range(0, width, CHUNK):
        some(slice(start, start + CHUNK), 0, wx_ref, bx_ref)
    for start in range(0, bc_ref.shape[1], CHUNK):
        some(slice(start, start + CHUNK), width, wbc_ref, bbc_ref)

    row = lax.broadcasted_iota(jnp.int32, (rows, rows), 0)
    lane = lax.broadcasted_iota(jnp.int32, (rows, rows), 1)
    linked = (row >= lane) & (first + lane >= begin) & (lane >= 8)
    turned_running = running.T
    turned_step = step.T
    pair_width = 2 * HDIM
    channel = lax.broadcasted_iota(jnp.int32, (rows, pair_width), 1)
    below = lax.broadcasted_iota(jnp.int32, (rows, CHUNK), 0) >= 8
    for group in range(groups):
        base = group * 2 * STATE
        meet = lax.dot_general(
            bcc_ref[:, base + STATE : base + 2 * STATE],
            bcc_ref[:, base : base + STATE],
            (((1,), (1,)), ((), ())),
            preferred_element_type=F32,
        )
        meet = jnp.where(linked, meet, 0.0)
        group_entry = entry[:, group * group_heads : (group + 1) * group_heads]
        for chunk in range(0, per_group, CHUNK):
            at = group * per_group + chunk
            columns = slice(at, at + CHUNK)
            gate = silu(z_ref[:, columns].astype(F32))
            gate_ref[:, columns] = gate
            decay_ref[:, columns] = widen(group_entry, chunk, CHUNK) * gate
            xc_all = xc_ref[:, columns]
            skipped = jnp.where(below, xc_all.astype(F32) * wide_skip_ref[0:1, columns], 0.0)
            for start in range(0, CHUNK, pair_width):
                parts = []
                for head in ((at + start) // HDIM, (at + start) // HDIM + 1):
                    spread = running[:, head : head + 1] - turned_running[head : head + 1]
                    decay = jnp.exp(jnp.minimum(spread, 0.0))
                    parts.append((decay * (meet * turned_step[head : head + 1])).astype(BF16))
                mix = jnp.concatenate(parts, axis=1)
                here_columns = slice(start, start + pair_width)
                xc = xc_all[:, here_columns]
                zero = jnp.zeros_like(xc)
                stacked = jnp.concatenate(
                    [jnp.where(channel < HDIM, xc, zero), jnp.where(channel < HDIM, zero, xc)], axis=0
                )
                value = jnp.dot(mix, stacked, preferred_element_type=F32) + skipped[:, here_columns]
                out_ref[:, at + start : at + start + pair_width] = value * gate[:, here_columns]


def first_rows(lines, partial_ref, inside_ref, w_ref, pad_ref, slot, at, start):
    taps = w_ref.shape[0]
    columns = slice(start, start + CHUNK)
    pad = pad_ref.at[slot]
    pad[4:8] = lines[:, at + start : at + start + CHUNK]
    pad[8:] = jnp.zeros((8, CHUNK), F32)
    total = partial_ref[:, at + start : at + start + CHUNK]
    for lag in range(1, taps):
        term = pad[8 - lag : 16 - lag] * w_ref[taps - 1 - lag : taps - lag, columns]
        total = total + term * inside_ref[lag - 1]
    return silu(total).astype(BF16)


def relay_first_kernel(fresh, *refs):
    message_ref, state_ref, partial_ref, weight_ref, through_ref, inside_ref, flag_ref, wx_ref, wbc_ref = refs[:9]
    other_ref = refs[9] if fresh else state_ref
    out_ref, pad_ref = refs[-2:]
    width = out_ref.shape[1]
    slots = pad_ref.shape[0]
    lines = tail_lines(message_ref, STATE)
    top = functools.partial(first_rows, lines, partial_ref, inside_ref)
    inputs = top(wbc_ref, pad_ref, 0, wx_ref.shape[1], 0)[:, :STATE]
    turned = inputs.astype(F32).T.astype(BF16)
    own = flag_ref[0, 0:1] > 0.5
    for start in range(0, width, CHUNK):
        columns = slice(start, start + CHUNK)
        xc = top(wx_ref, pad_ref, (start // CHUNK + 1) % slots, 0, start)
        weighted = (xc.astype(F32) * weight_ref[:, columns]).astype(BF16)
        full = state_ref[:STATE, columns].astype(F32) + jnp.dot(
            turned, weighted, preferred_element_type=F32
        )
        full = full + through_ref[0:1, columns] * message_ref[:STATE, columns].astype(F32)
        out_ref[:, columns] = jnp.where(own, other_ref[:STATE, columns].astype(F32), full).astype(BF16)


def relay_kernel(part, fresh, *refs):
    got_ref, state_ref, through_ref, flag_ref = refs[:4]
    out_ref = refs[-1]
    width = out_ref.shape[1]
    own = flag_ref[0, 0:1] > 0.5
    for start in range(0, width, CHUNK):
        columns = slice(start, start + CHUNK)
        through = through_ref[0:1, part * width + start : part * width + start + CHUNK]
        full = state_ref[:, columns].astype(F32) + through * got_ref[:STATE, columns].astype(F32)
        if fresh:
            full = jnp.where(own, refs[4][:STATE, columns].astype(F32), full)
        out_ref[:, columns] = full.astype(BF16)


def first_rows_kernel(groups, *refs):
    (
        message_ref, partial_ref, weight_ref, inside_ref, wx_ref, wbc_ref, step_ref, running_ref,
        wide_skip_ref, begin_ref, bcc_ref, main_ref, gate_ref,
    ) = refs[:13]
    state_refs = refs[13 : 13 + groups]
    out_ref, c_ref = refs[13 + groups : 15 + groups]
    full_refs = refs[15 + groups : 15 + 2 * groups]
    pad_ref = refs[-1]
    rows, width = main_ref.shape
    per_group = width // groups
    heads = per_group // HDIM
    lanes = 8 * heads
    first = lax.axis_index("seq") * rows
    lines = tail_lines(message_ref, STATE)
    slots = pad_ref.shape[0]
    top = functools.partial(first_rows, lines, partial_ref, inside_ref)
    lane = lax.broadcasted_iota(jnp.int32, (rows, lanes), 1)
    line = lane & 7
    row = lax.broadcasted_iota(jnp.int32, (rows, lanes), 0)
    begin = jnp.concatenate([begin_ref[...]] * -(-lanes // rows), axis=1)[:, :lanes]
    linked = (row >= line) & (first + line >= begin)
    head = lax.broadcasted_iota(jnp.int32, (3 * heads, lanes), 0)
    for _ in range(2):
        head = jnp.where(head >= heads, head - heads, head)
    spread = (lax.broadcasted_iota(jnp.int32, (3 * heads, lanes), 1) >> 3 == head).astype(F32).astype(BF16)
    own_line = lax.broadcasted_iota(jnp.int32, (8, lanes), 0) == line[:8]

    def to_lanes(value):
        high = value.astype(BF16)
        middle, low = halves(value - high.astype(F32))
        return jnp.dot(jnp.concatenate([high, middle, low], axis=1), spread, preferred_element_type=F32)

    def by_line(value):
        return jnp.sum(jnp.where(own_line, value, 0.0), axis=0, keepdims=True)

    channel = lax.broadcasted_iota(jnp.int32, (8, CHUNK), 1)
    for group in range(groups):
        base = group * 2 * STATE
        these = slice(group * heads, (group + 1) * heads)
        new = top(wbc_ref, pad_ref, group % slots, width, base).astype(F32)
        old = bcc_ref[:, base + STATE : base + 2 * STATE]
        outputs = jnp.concatenate([new[:, STATE:], old[:EDGE].astype(F32)[8:]], axis=0).astype(BF16)
        outputs = jnp.concatenate([outputs, old[EDGE:]], axis=0)
        c_ref[:, group * STATE : (group + 1) * STATE] = outputs
        inputs = jnp.concatenate([new[:, :STATE]] * heads, axis=0).astype(BF16)
        meet = lax.dot_general(
            outputs, inputs, (((1,), (1,)), ((), ())), preferred_element_type=F32
        )
        running = to_lanes(running_ref[:, these])
        decay = jnp.exp(jnp.minimum(running - by_line(running[:8]), 0.0))
        mix = decay * (meet * by_line(to_lanes(step_ref[:8, these])))
        mix = jnp.where(linked, mix, 0.0).astype(BF16)
        turned = inputs[:EDGE].astype(F32).T[:, :8].astype(BF16)
        for chunk in range(0, per_group, CHUNK):
            at = group * per_group + chunk
            columns = slice(at, at + CHUNK)
            xc = top(wx_ref, pad_ref, (chunk // CHUNK + 1) % slots, 0, at).astype(F32)
            full = state_refs[group][:STATE, chunk : chunk + CHUNK].astype(F32) + jnp.dot(
                turned, (xc * weight_ref[:, columns]).astype(BF16), preferred_element_type=F32
            )
            full_refs[group][:, chunk : chunk + CHUNK] = full.astype(BF16)
            blocks = []
            for at_head in range(heads):
                low = at_head * HDIM - chunk
                if 0 <= low < CHUNK:
                    blocks.append(jnp.where((channel >= low) & (channel < low + HDIM), xc, 0.0))
                else:
                    blocks.append(jnp.zeros_like(xc))
            spread_xc = jnp.concatenate(blocks, axis=0).astype(BF16)
            gate = gate_ref[:, columns]
            value = main_ref[:, columns] + gate * jnp.dot(mix, spread_xc, preferred_element_type=F32)
            out_ref[:, columns] = value
            out_ref[0:8, columns] = value[:8] + gate[:8] * (xc * wide_skip_ref[:, columns])


def attend(q_ref, kv_refs, begin_ref, blocks, share, head):
    rows = q_ref.shape[0]
    kv_heads = kv_refs[0].shape[1] // (2 * ADIM)
    count = rows * blocks.count
    here = lax.axis_index("seq")
    row = here * rows + lax.broadcasted_iota(jnp.int32, (rows, count), 0)
    lane = (here - blocks.farthest) * rows + lax.broadcasted_iota(jnp.int32, (rows, count), 1)
    begin = jnp.concatenate([begin_ref[...]] * blocks.count, axis=1)
    allowed = jnp.concatenate([(lane <= row) & (lane >= begin)] * share, axis=0)
    low = head * ADIM
    keys = jnp.concatenate([ref[:, low : low + ADIM] for ref in kv_refs], axis=0)
    low = (kv_heads + head) * ADIM
    values = jnp.concatenate([ref[:, low : low + ADIM] for ref in kv_refs], axis=0)
    values = jnp.concatenate([values, jnp.ones((count, ADIM), BF16)], axis=1)
    lows = [(head * share + part) * ADIM for part in range(share)]
    asking = jnp.concatenate([q_ref[:, low : low + ADIM] for low in lows], axis=0)
    scores = lax.dot_general(asking, keys, (((1,), (1,)), ((), ())), preferred_element_type=F32)
    return jnp.where(allowed, scores * ADIM ** (-0.5), BARRED), values


class Blocks(NamedTuple):
    farthest: int
    count: int


def near_kernel(*refs):
    q_ref, before_ref, own_ref, begin_ref, _, sum_ref, total_ref, peak_ref, kv_ref = refs
    kv_ref[...] = before_ref[...]
    rows = q_ref.shape[0]
    share = QHEADS // KVHEADS
    for head in range(own_ref.shape[1] // (2 * ADIM)):
        scores, values = attend(q_ref, (before_ref, own_ref), begin_ref, Blocks(1, 2), share, head)
        peak = jnp.max(scores, axis=1, keepdims=True)
        summed = jnp.dot(jnp.exp(scores - peak).astype(BF16), values, preferred_element_type=F32)
        peak = jnp.broadcast_to(peak, (peak.shape[0], ADIM))
        for part in range(share):
            low = (head * share + part) * ADIM
            these = slice(part * rows, (part + 1) * rows)
            sum_ref[:, low : low + ADIM] = summed[these, :ADIM]
            total_ref[:, low : low + ADIM] = summed[these, ADIM:]
            peak_ref[:, low : low + ADIM] = peak[these]


def far_kernel(hops, *refs):
    q_ref, begin_ref, sum_ref, total_ref, peak_ref = refs[:5]
    kv_refs = refs[5 : 4 + hops]
    out_hbm_ref, out_ref, sems = refs[4 + hops :]
    rows = q_ref.shape[0]
    share = QHEADS // KVHEADS
    copies = []
    for head in range(kv_refs[0].shape[1] // (2 * ADIM)):
        lows = [(head * share + part) * ADIM for part in range(share)]

        def stacked(ref):
            return jnp.concatenate([ref[:, low : low + ADIM] for low in lows], axis=0)

        scores, values = attend(q_ref, kv_refs, begin_ref, Blocks(hops, hops - 1), share, head)
        near = stacked(peak_ref)
        peak = jnp.maximum(near, jnp.max(scores, axis=1, keepdims=True))
        expo = jnp.exp(scores - jnp.concatenate([peak] * (scores.shape[1] // ADIM), axis=1))
        summed = jnp.dot(expo.astype(BF16), values, preferred_element_type=F32)
        factor = jnp.exp(near - peak)
        total = stacked(total_ref) * factor + summed[:, ADIM:]
        result = ((stacked(sum_ref) * factor + summed[:, :ADIM]) / total).astype(BF16)
        for part, low in enumerate(lows):
            out_ref[:, low : low + ADIM] = result[part * rows : (part + 1) * rows]
        columns = pl.ds(head * share * ADIM, share * ADIM)
        copies.append(
            pltpu.make_async_copy(out_ref.at[:, columns], out_hbm_ref.at[:, columns], sems.at[head])
        )
        copies[-1].start()
    for copy in copies:
        copy.wait()


def norm_kernel(part, hops, *refs):
    local_ref, decay_ref, c_ref, gain_ref, flag_ref = refs[:5]
    got_refs = refs[5 : 5 + hops]
    out_hbm_ref, gated_ref, out_ref, sems = refs[-4:]
    rows, width = gated_ref.shape
    outputs = c_ref[:, part * STATE : (part + 1) * STATE]
    squares = jnp.zeros((rows, 128), F32)
    for start in range(0, width, CHUNK):
        columns = slice(start, start + CHUNK)
        placed = slice(part * width + start, part * width + start + CHUNK)
        state = got_refs[0][:STATE, columns]
        for hop in range(1, hops):
            there = flag_ref[hop, 0:1] > 0.5
            state = jnp.where(there, got_refs[hop][:STATE, columns].astype(F32), state.astype(F32))
        carried = jnp.dot(outputs, state.astype(BF16), preferred_element_type=F32)
        gated = local_ref[:, placed] + carried * decay_ref[:, placed]
        gated_ref[:, columns] = gated
        for lane in range(0, CHUNK, 128):
            squares = squares + gated[:, lane : lane + 128] * gated[:, lane : lane + 128]
    squares = jnp.sum(squares, axis=1, keepdims=True)
    multiplier = lax.rsqrt(squares * (1.0 / width) + EPSILON)
    copies = []
    for start in range(0, width, CHUNK):
        columns = slice(start, start + CHUNK)
        gain = gain_ref[part * width + start : part * width + start + CHUNK]
        out_ref[:, columns] = (gated_ref[:, columns] * multiplier * gain.reshape(1, -1)).astype(BF16)
        copies.append(
            pltpu.make_async_copy(
                out_ref.at[:, pl.ds(start, CHUNK)],
                out_hbm_ref.at[:, pl.ds(part * width + start, CHUNK)],
                sems.at[start // CHUNK],
            )
        )
        copies[-1].start()
    for copy in copies:
        copy.wait()


WHOLE = pl.BlockSpec(memory_space=pltpu.VMEM)
SCALARS = pl.BlockSpec(memory_space=pltpu.SMEM)
UNTOUCHED = pl.BlockSpec(memory_space=pl.ANY)


def tile(rows, columns, row, column):
    return pl.BlockSpec((rows, columns), lambda step: (row, column))


def call(kernel, name, outs, operands, specs, out_specs=None, scratch=(), flops=KERNEL_FLOPS, aliases={}, limit=VMEM_LIMIT):
    moved = sum(math.prod(a.shape) * a.dtype.itemsize for a in (*operands, *outs))
    return pl.pallas_call(
        kernel,
        name=name,
        grid=(1,),
        out_shape=outs,
        in_specs=specs,
        out_specs=[WHOLE] * len(outs) if out_specs is None else out_specs,
        scratch_shapes=list(scratch),
        input_output_aliases=aliases,
        compiler_params=pltpu.CompilerParams(vmem_limit_bytes=limit),
        cost_estimate=pl.CostEstimate(flops=flops, bytes_accessed=moved, transcendentals=0),
    )(*operands)


def onward(value, first=0):
    count = lax.axis_size("seq")
    return lax.ppermute(value, "seq", [(source, source + 1) for source in range(first, count - 1)])


def shards(
    x_raw,
    bc_raw,
    z_gate,
    dt_raw,
    conv_x_weight,
    conv_x_bias,
    conv_bc_weight,
    conv_bc_bias,
    dt_bias,
    a_log,
    skip_d,
    norm_gain,
    queries,
    keys,
    values,
    doc_lens,
):
    rows, width = x_raw.shape
    bc_width = bc_raw.shape[1]
    heads = dt_raw.shape[1]
    groups = bc_width // (2 * STATE)
    per_group = width // groups
    count = lax.axis_size("seq")
    longest = rows * count // 2
    hops = min(count - 1, -(-(longest - 1) // rows))
    assert hops * rows >= longest and (hops == 2 or hops > 2 and groups == 1)
    shape = jax.ShapeDtypeStruct
    dt = dt_raw.T
    params = [dt, conv_x_weight, conv_x_bias, conv_bc_weight, conv_bc_bias, dt_bias, a_log]
    pieces = -(-(width + bc_width) // per_group)
    tail_rows = EDGE * -(-4 * pieces // EDGE)

    (message,) = call(
        first_state_kernel,
        "first_state",
        [shape((STATE + tail_rows, per_group), BF16)],
        [x_raw, bc_raw, *(a if a.ndim > 1 else a[None] for a in params), doc_lens],
        [UNTOUCHED] * 10,
        out_specs=[UNTOUCHED],
        scratch=[
            pltpu.VMEM((rows, per_group), BF16),
            pltpu.VMEM((rows, STATE), BF16),
            pltpu.VMEM((per_group // HDIM, rows), F32),
            pltpu.VMEM((conv_x_weight.shape[0], per_group), F32),
            pltpu.VMEM((1, per_group), F32),
            pltpu.VMEM((conv_x_weight.shape[0], STATE), F32),
            pltpu.VMEM((1, STATE), F32),
            pltpu.VMEM((1, heads), F32),
            pltpu.VMEM((1, heads), F32),
            pltpu.SMEM(doc_lens.shape, jnp.int32),
            pltpu.VMEM((EDGE, width), BF16),
            pltpu.VMEM((EDGE, bc_width), BF16),
            pltpu.VMEM((STATE + tail_rows, per_group), BF16),
            pltpu.VMEM((rows + 8, STATE), F32),
            pltpu.VMEM((4, rows + 8, CHUNK), F32),
            pltpu.SemaphoreType.DMA((12,)),
            pltpu.SemaphoreType.DMA((per_group // (2 * CHUNK) + 1,)),
        ],
        limit=VMEM_ALL,
    )
    slots = [onward(message)]
    prepared = call(
        functools.partial(prepare_kernel, hops, groups),
        "prepare",
        [
            shape((rows, width), BF16),
            shape((rows, bc_width), BF16),
            shape((rows, 2 * keys.shape[1]), BF16),
            shape((8, width + bc_width), F32),
            shape((8, width), F32),
            shape((8, width), F32),
            shape((conv_x_weight.shape[0] - 1, 8, CHUNK), F32),
            shape((hops, 8, CHUNK), F32),
            shape((8, width), F32),
            shape((rows, rows), jnp.int32),
            shape((rows, heads), F32),
            shape((rows, heads), F32),
            shape((rows, width), F32),
            shape((rows, width), F32),
            shape((rows, width), F32),
            *(shape((STATE, per_group), BF16) for _ in range(groups - 1)),
        ],
        [x_raw, bc_raw, *params, skip_d, doc_lens, keys, values, z_gate],
        [WHOLE] * 10 + [SCALARS] + [WHOLE] * 3,
        scratch=[
            pltpu.VMEM((16, width + bc_width), F32),
            pltpu.VMEM((4, rows + 8, CHUNK), F32),
        ],
    )
    _, bcc, kv, partial, weight, through, inside, flags, wide_skip, begin, *prepared = prepared
    step, running, main, gate, decay, *states = prepared
    states = [message, *states]
    kvs = [kv, onward(kv)]
    fulls = None
    for slot in range(2, hops + groups):
        part = min(slot - 1, groups) - 1
        fresh = slot <= groups
        if slot == 2:
            kernel = functools.partial(relay_first_kernel, fresh)
            operands = [slots[0], states[0], partial, weight, through, inside, flags, conv_x_weight, conv_bc_weight]
            scratch = [pltpu.VMEM((4, 16, CHUNK), F32)]
        else:
            kernel = functools.partial(relay_kernel, part, fresh)
            operands = [slots[-1], fulls[part], through, flags]
            scratch = []
        if fresh:
            operands.append(states[slot - 1])
        (passed,) = call(
            kernel,
            f"relay_slot{slot}",
            [shape((STATE, per_group), BF16)],
            operands,
            [WHOLE] * len(operands),
            scratch=scratch,
        )
        slots.append(onward(passed))
        if fulls is None:
            gated, c_out, *fulls = call(
                functools.partial(first_rows_kernel, groups),
                "first_rows",
                [
                    shape((rows, width), F32),
                    shape((rows, groups * STATE), BF16),
                    *(shape((STATE, per_group), BF16) for _ in range(groups)),
                ],
                [
                    slots[0], partial, weight, inside, conv_x_weight, conv_bc_weight, step, running,
                    wide_skip, begin, bcc, main, gate, *states,
                ],
                [WHOLE] * (13 + groups),
                scratch=[pltpu.VMEM((4, 16, CHUNK), F32)],
            )
    parts = shape(queries.shape, F32)
    *near, kv_on = call(
        near_kernel,
        "attend_near",
        [parts, parts, parts, shape(kv.shape, BF16)],
        [queries, kvs[1], kv, begin, c_out],
        [WHOLE] * 4 + [UNTOUCHED],
    )
    for hop in range(1, hops):
        kvs.append(onward(kv_on if hop == 1 else kvs[-1], hop))
    (attn_out,) = call(
        functools.partial(far_kernel, hops),
        "attend_far",
        [shape(queries.shape, BF16)],
        [queries, begin, *near, *reversed(kvs[2:])],
        [WHOLE] * (4 + hops),
        out_specs=[UNTOUCHED],
        scratch=[
            pltpu.VMEM(queries.shape, BF16),
            pltpu.SemaphoreType.DMA((keys.shape[1] // ADIM,)),
        ],
    )
    mamba_out = None
    for part in range(groups):
        got = slots[-1:] if part == groups - 1 else slots[part : part + hops]
        operands = [gated, decay, c_out, norm_gain, flags, *got]
        specs = [WHOLE] * (5 + len(got))
        aliases = {}
        if mamba_out is not None:
            operands.append(mamba_out)
            specs.append(UNTOUCHED)
            aliases = {len(operands) - 1: 0}
        (mamba_out,) = call(
            functools.partial(norm_kernel, part, len(got)),
            f"norm_part{part}",
            [shape((rows, width), BF16)],
            operands,
            specs,
            out_specs=[UNTOUCHED],
            scratch=[
                pltpu.VMEM((rows, per_group), F32),
                pltpu.VMEM((rows, per_group), BF16),
                pltpu.SemaphoreType.DMA((per_group // CHUNK,)),
            ],
            aliases=aliases,
        )
    return (mamba_out, attn_out)


def solution(mesh):
    split = P(("groups", "seq"), "dp")
    placed = (
        split,
        split,
        split,
        split,
        P(None, "dp"),
        P("dp"),
        P(None, "dp"),
        P("dp"),
        P("dp"),
        P("dp"),
        P("dp"),
        P("dp"),
        split,
        split,
        split,
        P("groups"),
    )
    return jax.shard_map(
        shards,
        mesh=mesh,
        in_specs=placed,
        out_specs=(split, split),
        check_vma=False,
    )
```

```python
import functools
import math
from typing import NamedTuple

import jax
import jax.numpy as jnp
from jax import lax
from jax.experimental import pallas as pl
from jax.experimental.pallas import tpu as pltpu
from jax.sharding import PartitionSpec as P

HDIM = 64
STATE = 128
QHEADS = 32
KVHEADS = 8
ADIM = 128
EPSILON = 1e-05
BARRED = -2e30
HIGHEST = lax.Precision.HIGHEST
F32 = jnp.float32
BF16 = jnp.bfloat16
CHUNK = 256
EDGE = 16
KERNEL_FLOPS = 2 * 10**9
VMEM_LIMIT = 40 * 1024 * 1024
VMEM_ALL = 62 * 1024 * 1024


def silu(value):
    return value * (0.5 * jnp.tanh(0.5 * value) + 0.5)


def softplus(value):
    return jnp.maximum(value, 0.0) + jnp.log(1.0 + jnp.exp(-jnp.abs(value)))


def doc_start(positions, lens_ref):
    begin = jnp.int32(0)
    found = positions * 0
    for doc in range(lens_ref.shape[0]):
        found = jnp.where(positions >= begin, begin, found)
        begin = begin + lens_ref[doc]
    return found


def halves(value):
    high = value.astype(BF16)
    return high, (value - high.astype(F32)).astype(BF16)


def widen(per_head, first, width):
    heads = per_head.shape[1]
    both = jnp.concatenate(halves(per_head), axis=1)
    head = lax.broadcasted_iota(jnp.int32, (2 * heads, width), 0)
    head = jnp.where(head >= heads, head - heads, head)
    channel = lax.broadcasted_iota(jnp.int32, (2 * heads, width), 1) + first
    spread = (channel // HDIM == head).astype(F32).astype(BF16)
    return jnp.dot(both, spread, preferred_element_type=F32)


def rates(dt_ref, dt_bias_ref, a_log_ref):
    heads = dt_ref.shape[0]
    step = softplus(dt_ref[...].T + dt_bias_ref[...].reshape(1, -1)[:, :heads])
    rate = -step * jnp.exp(a_log_ref[...].reshape(1, -1)[:, :heads])
    rows = step.shape[0]
    row = lax.broadcasted_iota(jnp.int32, (rows, rows), 0)
    column = lax.broadcasted_iota(jnp.int32, (rows, rows), 1)
    lower = (row >= column).astype(F32).astype(BF16)
    high = rate.astype(BF16)
    middle, low = halves(rate - high.astype(F32))
    parts = jnp.concatenate([high, middle, low], axis=0)
    lowers = jnp.concatenate([lower, lower, lower], axis=1)
    return step, jnp.dot(lowers, parts, preferred_element_type=F32)


def insides(first, shape, taps, lens_ref):
    positions = first + lax.broadcasted_iota(jnp.int32, shape, 0)
    depth = positions - doc_start(positions, lens_ref)
    return [depth >= lag for lag in range(taps)]


def conv(pad, rows, weight, bias, inside):
    taps = weight.shape[0]
    total = pad[8 : 8 + rows] * weight[taps - 1 : taps] + bias
    for lag in range(1, taps):
        term = pad[8 - lag : 8 - lag + rows] * weight[taps - 1 - lag : taps - lag]
        total = total + jnp.where(inside[lag], term, 0.0)
    return silu(total).astype(BF16)


def tail_lines(message, rows):
    block = message[rows:].astype(F32)
    return jnp.concatenate([block[at : at + 4] for at in range(0, block.shape[0], 4)], axis=1)


def reach(device, rows, lens_ref):
    return device - doc_start((device + 1) * rows - 1, lens_ref) // rows


def kept_weight(here, step, running, taps, lens_ref):
    rows = step.shape[0]
    last_begin = doc_start((here + 1) * rows - 1, lens_ref)
    row = lax.broadcasted_iota(jnp.int32, step.shape, 0)
    weight = step * jnp.exp(running[rows - 1 : rows] - running)
    kept = (here * rows + row >= last_begin) & ((row >= taps - 1) | (last_begin // rows >= here))
    return jnp.where(kept, weight, 0.0)


def conv_rows(pad, raw, weight, bias, inside):
    pad[0:8] = jnp.zeros((8, raw.shape[1]), F32)
    pad[8:] = raw.astype(F32)
    return conv(pad, raw.shape[0], weight, bias.reshape(1, -1), inside)


def first_state_kernel(*refs):
    hbm_refs, out_hbm_ref = refs[:10], refs[10]
    vmem_refs = refs[11:21]
    x_edge_ref, bc_edge_ref, out_ref, b_pad_ref, pad_ref, in_sems, out_sems = refs[21:]
    x_ref, b_ref, dt_ref, wx_ref, bx_ref, wbc_ref, bbc_ref, dt_bias_ref, a_log_ref, lens_ref = vmem_refs
    rows, width = x_ref.shape
    taps = wx_ref.shape[0]

    def corner(ref, shape):
        return ref.at[tuple(pl.ds(0, extent) for extent in shape)]

    order = (9, 2, 7, 8, 1, 5, 6, 0, 3, 4)
    copies = {}
    for at in order:
        source = corner(hbm_refs[at], vmem_refs[at].shape)
        copies[at] = pltpu.make_async_copy(source, vmem_refs[at], in_sems.at[at])
        copies[at].start()
    edge_copies = []
    for at, (source, target) in enumerate(((hbm_refs[0], x_edge_ref), (hbm_refs[1], bc_edge_ref))):
        edge_copies.append(
            pltpu.make_async_copy(source.at[pl.ds(rows - EDGE, EDGE)], target, in_sems.at[10 + at])
        )
        edge_copies[-1].start()

    here = lax.axis_index("seq")
    for at in (9, 2, 7, 8):
        copies[at].wait()
    inside = insides(here * rows, (rows, CHUNK), taps, lens_ref)
    step, running = rates(dt_ref, dt_bias_ref, a_log_ref)
    weight = kept_weight(here, step, running, taps, lens_ref)
    narrow = [mask[:, :STATE] for mask in inside]
    for at in (1, 5, 6):
        copies[at].wait()
    inputs = conv_rows(b_pad_ref, b_ref[...], wbc_ref[...], bbc_ref[...], narrow)
    turned = inputs.astype(F32).T.astype(BF16)
    for at in (0, 3, 4):
        copies[at].wait()
    slots = pad_ref.shape[0]
    outs = []

    def send(at, view):
        copy = pltpu.make_async_copy(out_ref.at[view], out_hbm_ref.at[view], out_sems.at[at])
        copy.start()
        outs.append(copy)

    for at, start in enumerate(range(0, width, CHUNK)):
        columns = slice(start, start + CHUNK)
        pad = pad_ref.at[(at + 1) % slots]
        xc = conv_rows(pad, x_ref[:, columns], wx_ref[:, columns], bx_ref[:, columns], inside)
        weighted = (xc.astype(F32) * widen(weight, start, CHUNK)).astype(BF16)
        out_ref[:STATE, columns] = jnp.dot(turned, weighted, preferred_element_type=F32).astype(BF16)
        if at % 2:
            send(at // 2, (pl.ds(0, STATE), pl.ds(start - CHUNK, 2 * CHUNK)))
    for copy in edge_copies:
        copy.wait()
    edges = jnp.concatenate([x_edge_ref[...].astype(F32), bc_edge_ref[...].astype(F32)], axis=1)[EDGE - 4 :]
    spare = -edges.shape[1] % width
    if spare:
        edges = jnp.concatenate([edges, jnp.zeros((4, spare), F32)], axis=1)
    pieces = [edges[:, at : at + width] for at in range(0, edges.shape[1], width)]
    while len(pieces) % (EDGE // 4):
        pieces.append(jnp.zeros_like(pieces[0]))
    out_ref[STATE:] = jnp.concatenate(pieces, axis=0).astype(BF16)
    send(width // (2 * CHUNK), (pl.ds(STATE, out_ref.shape[0] - STATE), pl.ds(0, width)))
    for copy in outs:
        copy.wait()


def prepare_kernel(hops, groups, *refs):
    x_ref, bc_ref, dt_ref, wx_ref, bx_ref, wbc_ref, bbc_ref, dt_bias_ref, a_log_ref, skip_ref, lens_ref = refs[:11]
    z_ref = refs[11]
    xc_ref, bcc_ref, partial_ref, weight_ref, through_ref, inside_ref, flag_ref = refs[12:19]
    wide_skip_ref, begin_ref, step_ref, running_ref, out_ref, gate_ref, decay_ref = refs[19:26]
    state_refs = refs[26:-2]
    top_ref, pad_ref = refs[-2:]
    rows, width = x_ref.shape
    per_group = width // groups
    taps = wx_ref.shape[0]
    slots = pad_ref.shape[0]
    here = lax.axis_index("seq")
    first = here * rows
    inside = insides(first, (rows, CHUNK), taps, lens_ref)
    step, running = rates(dt_ref, dt_bias_ref, a_log_ref)
    heads = step.shape[1]
    group_heads = heads // groups
    kept = kept_weight(here, step, running, taps, lens_ref)
    for group in range(groups):
        base = slice(group * 2 * STATE, (group + 1) * 2 * STATE)
        pair = conv_rows(pad_ref.at[0], bc_ref[:, base], wbc_ref[:, base], bbc_ref[base], inside)
        bcc_ref[:, base] = pair
        turned = pair[:, :STATE].astype(F32).T.astype(BF16)
        part_weight = kept[:, group * group_heads : (group + 1) * group_heads]
        for chunk in range(0, per_group, CHUNK):
            columns = slice(group * per_group + chunk, group * per_group + chunk + CHUNK)
            pad = pad_ref.at[(chunk // CHUNK + 1) % slots]
            xc = conv_rows(pad, x_ref[:, columns], wx_ref[:, columns], bx_ref[columns], inside)
            xc_ref[:, columns] = xc
            if group:
                weighted = (xc.astype(F32) * widen(part_weight, chunk, CHUNK)).astype(BF16)
                state_refs[group - 1][:, chunk : chunk + CHUNK] = jnp.dot(
                    turned, weighted, preferred_element_type=F32
                ).astype(BF16)

    own = reach(here, rows, lens_ref) == 0
    inside = [mask[:8] for mask in inside]
    for lag in range(1, taps):
        inside_ref[lag - 1] = inside[lag].astype(F32)
    flag_ref[0] = jnp.broadcast_to(own.astype(F32), (8, CHUNK))
    before = reach(here - 1, rows, lens_ref)
    for hop in range(1, hops):
        flag_ref[hop] = jnp.broadcast_to((before == hop).astype(F32), (8, CHUNK))
    begin = doc_start(first + lax.broadcasted_iota(jnp.int32, begin_ref.shape, 0), lens_ref)
    begin_ref[...] = begin
    entry = jnp.where(begin[:, :heads] < first, jnp.exp(running), 0.0)
    step_ref[...] = step
    running_ref[...] = running
    row = lax.broadcasted_iota(jnp.int32, (8, heads), 0)
    total = running[rows - 1 : rows]
    weight = step[:8] * jnp.exp(total - running[:8])
    weight = jnp.where((row < taps - 1) & jnp.logical_not(own), weight, 0.0)
    through = jnp.where(own, 0.0, jnp.broadcast_to(jnp.exp(total), (8, heads)))
    skip = jnp.broadcast_to(skip_ref[...].reshape(1, -1), (8, heads))
    every = jnp.concatenate([weight, through, skip], axis=0)
    for start in range(0, width, CHUNK):
        wide = widen(every, start, CHUNK)
        weight_ref[:, start : start + CHUNK] = wide[:8]
        through_ref[:, start : start + CHUNK] = wide[8:16]
        wide_skip_ref[:, start : start + CHUNK] = wide[16:]
    top_ref[0:8] = jnp.zeros((8, top_ref.shape[1]), F32)
    top_ref[8:, :width] = x_ref[:EDGE].astype(F32)[:8]
    top_ref[8:, width:] = bc_ref[:EDGE].astype(F32)[:8]

    def some(columns, base, w_ref, b_ref):
        here_columns = slice(base + columns.start, base + columns.stop)
        total = top_ref[8:, here_columns] * w_ref[taps - 1 : taps, columns] + b_ref[columns].reshape(1, -1)
        for lag in range(1, taps):
            term = top_ref[8 - lag : 16 - lag, here_columns] * w_ref[taps - 1 - lag : taps - lag, columns]
            total = total + jnp.where(inside[lag], term, 0.0)
        partial_ref[:, here_columns] = total

    for start in range(0, width, CHUNK):
        some(slice(start, start + CHUNK), 0, wx_ref, bx_ref)
    for start in range(0, bc_ref.shape[1], CHUNK):
        some(slice(start, start + CHUNK), width, wbc_ref, bbc_ref)

    row = lax.broadcasted_iota(jnp.int32, (rows, rows), 0)
    lane = lax.broadcasted_iota(jnp.int32, (rows, rows), 1)
    linked = (row >= lane) & (first + lane >= begin) & (lane >= 8)
    turned_running = running.T
    turned_step = step.T
    pair_width = 2 * HDIM
    channel = lax.broadcasted_iota(jnp.int32, (rows, pair_width), 1)
    below = lax.broadcasted_iota(jnp.int32, (rows, CHUNK), 0) >= 8
    for group in range(groups):
        base = group * 2 * STATE
        meet = lax.dot_general(
            bcc_ref[:, base + STATE : base + 2 * STATE],
            bcc_ref[:, base : base + STATE],
            (((1,), (1,)), ((), ())),
            preferred_element_type=F32,
        )
        meet = jnp.where(linked, meet, 0.0)
        group_entry = entry[:, group * group_heads : (group + 1) * group_heads]
        for chunk in range(0, per_group, CHUNK):
            at = group * per_group + chunk
            columns = slice(at, at + CHUNK)
            gate = silu(z_ref[:, columns].astype(F32))
            gate_ref[:, columns] = gate
            decay_ref[:, columns] = widen(group_entry, chunk, CHUNK) * gate
            xc_all = xc_ref[:, columns]
            skipped = jnp.where(below, xc_all.astype(F32) * wide_skip_ref[0:1, columns], 0.0)
            for start in range(0, CHUNK, pair_width):
                parts = []
                for head in ((at + start) // HDIM, (at + start) // HDIM + 1):
                    spread = running[:, head : head + 1] - turned_running[head : head + 1]
                    decay = jnp.exp(jnp.minimum(spread, 0.0))
                    parts.append((decay * (meet * turned_step[head : head + 1])).astype(BF16))
                mix = jnp.concatenate(parts, axis=1)
                here_columns = slice(start, start + pair_width)
                xc = xc_all[:, here_columns]
                zero = jnp.zeros_like(xc)
                stacked = jnp.concatenate(
                    [jnp.where(channel < HDIM, xc, zero), jnp.where(channel < HDIM, zero, xc)], axis=0
                )
                value = jnp.dot(mix, stacked, preferred_element_type=F32) + skipped[:, here_columns]
                out_ref[:, at + start : at + start + pair_width] = value * gate[:, here_columns]


def first_rows(lines, partial_ref, inside_ref, w_ref, pad_ref, slot, at, start):
    taps = w_ref.shape[0]
    columns = slice(start, start + CHUNK)
    pad = pad_ref.at[slot]
    pad[4:8] = lines[:, at + start : at + start + CHUNK]
    pad[8:] = jnp.zeros((8, CHUNK), F32)
    total = partial_ref[:, at + start : at + start + CHUNK]
    for lag in range(1, taps):
        term = pad[8 - lag : 16 - lag] * w_ref[taps - 1 - lag : taps - lag, columns]
        total = total + term * inside_ref[lag - 1]
    return silu(total).astype(BF16)


def relay_first_kernel(fresh, *refs):
    message_ref, state_ref, partial_ref, weight_ref, through_ref, inside_ref, flag_ref, wx_ref, wbc_ref = refs[:9]
    other_ref = refs[9] if fresh else state_ref
    out_ref, pad_ref = refs[-2:]
    width = out_ref.shape[1]
    slots = pad_ref.shape[0]
    lines = tail_lines(message_ref, STATE)
    top = functools.partial(first_rows, lines, partial_ref, inside_ref)
    inputs = top(wbc_ref, pad_ref, 0, wx_ref.shape[1], 0)[:, :STATE]
    turned = inputs.astype(F32).T.astype(BF16)
    own = flag_ref[0, 0:1] > 0.5
    for start in range(0, width, CHUNK):
        columns = slice(start, start + CHUNK)
        xc = top(wx_ref, pad_ref, (start // CHUNK + 1) % slots, 0, start)
        weighted = (xc.astype(F32) * weight_ref[:, columns]).astype(BF16)
        full = state_ref[:STATE, columns].astype(F32) + jnp.dot(
            turned, weighted, preferred_element_type=F32
        )
        full = full + through_ref[0:1, columns] * message_ref[:STATE, columns].astype(F32)
        out_ref[:, columns] = jnp.where(own, other_ref[:STATE, columns].astype(F32), full).astype(BF16)


def relay_kernel(part, fresh, *refs):
    got_ref, state_ref, through_ref, flag_ref = refs[:4]
    out_ref = refs[-1]
    width = out_ref.shape[1]
    own = flag_ref[0, 0:1] > 0.5
    for start in range(0, width, CHUNK):
        columns = slice(start, start + CHUNK)
        through = through_ref[0:1, part * width + start : part * width + start + CHUNK]
        full = state_ref[:, columns].astype(F32) + through * got_ref[:STATE, columns].astype(F32)
        if fresh:
            full = jnp.where(own, refs[4][:STATE, columns].astype(F32), full)
        out_ref[:, columns] = full.astype(BF16)


def first_rows_kernel(groups, *refs):
    (
        message_ref, partial_ref, weight_ref, inside_ref, wx_ref, wbc_ref, step_ref, running_ref,
        wide_skip_ref, begin_ref, bcc_ref, main_ref, gate_ref,
    ) = refs[:13]
    state_refs = refs[13 : 13 + groups]
    out_ref, c_ref = refs[13 + groups : 15 + groups]
    full_refs = refs[15 + groups : 15 + 2 * groups]
    pad_ref = refs[-1]
    rows, width = main_ref.shape
    per_group = width // groups
    heads = per_group // HDIM
    lanes = 8 * heads
    first = lax.axis_index("seq") * rows
    lines = tail_lines(message_ref, STATE)
    slots = pad_ref.shape[0]
    top = functools.partial(first_rows, lines, partial_ref, inside_ref)
    lane = lax.broadcasted_iota(jnp.int32, (rows, lanes), 1)
    line = lane & 7
    row = lax.broadcasted_iota(jnp.int32, (rows, lanes), 0)
    begin = jnp.concatenate([begin_ref[...]] * -(-lanes // rows), axis=1)[:, :lanes]
    linked = (row >= line) & (first + line >= begin)
    head = lax.broadcasted_iota(jnp.int32, (3 * heads, lanes), 0)
    for _ in range(2):
        head = jnp.where(head >= heads, head - heads, head)
    spread = (lax.broadcasted_iota(jnp.int32, (3 * heads, lanes), 1) >> 3 == head).astype(F32).astype(BF16)
    own_line = lax.broadcasted_iota(jnp.int32, (8, lanes), 0) == line[:8]

    def to_lanes(value):
        high = value.astype(BF16)
        middle, low = halves(value - high.astype(F32))
        return jnp.dot(jnp.concatenate([high, middle, low], axis=1), spread, preferred_element_type=F32)

    def by_line(value):
        return jnp.sum(jnp.where(own_line, value, 0.0), axis=0, keepdims=True)

    channel = lax.broadcasted_iota(jnp.int32, (8, CHUNK), 1)
    for group in range(groups):
        base = group * 2 * STATE
        these = slice(group * heads, (group + 1) * heads)
        new = top(wbc_ref, pad_ref, group % slots, width, base).astype(F32)
        old = bcc_ref[:, base + STATE : base + 2 * STATE]
        outputs = jnp.concatenate([new[:, STATE:], old[:EDGE].astype(F32)[8:]], axis=0).astype(BF16)
        outputs = jnp.concatenate([outputs, old[EDGE:]], axis=0)
        c_ref[:, group * STATE : (group + 1) * STATE] = outputs
        inputs = jnp.concatenate([new[:, :STATE]] * heads, axis=0).astype(BF16)
        meet = lax.dot_general(
            outputs, inputs, (((1,), (1,)), ((), ())), preferred_element_type=F32
        )
        running = to_lanes(running_ref[:, these])
        decay = jnp.exp(jnp.minimum(running - by_line(running[:8]), 0.0))
        mix = decay * (meet * by_line(to_lanes(step_ref[:8, these])))
        mix = jnp.where(linked, mix, 0.0).astype(BF16)
        turned = inputs[:EDGE].astype(F32).T[:, :8].astype(BF16)
        for chunk in range(0, per_group, CHUNK):
            at = group * per_group + chunk
            columns = slice(at, at + CHUNK)
            xc = top(wx_ref, pad_ref, (chunk // CHUNK + 1) % slots, 0, at).astype(F32)
            full = state_refs[group][:STATE, chunk : chunk + CHUNK].astype(F32) + jnp.dot(
                turned, (xc * weight_ref[:, columns]).astype(BF16), preferred_element_type=F32
            )
            full_refs[group][:, chunk : chunk + CHUNK] = full.astype(BF16)
            blocks = []
            for at_head in range(heads):
                low = at_head * HDIM - chunk
                if 0 <= low < CHUNK:
                    blocks.append(jnp.where((channel >= low) & (channel < low + HDIM), xc, 0.0))
                else:
                    blocks.append(jnp.zeros_like(xc))
            spread_xc = jnp.concatenate(blocks, axis=0).astype(BF16)
            gate = gate_ref[:, columns]
            value = main_ref[:, columns] + gate * jnp.dot(mix, spread_xc, preferred_element_type=F32)
            out_ref[:, columns] = value
            out_ref[0:8, columns] = value[:8] + gate[:8] * (xc * wide_skip_ref[:, columns])


def attend(q_ref, kv_refs, begin_ref, blocks, share, head):
    rows = q_ref.shape[0]
    kv_heads = kv_refs[0].shape[1] // (2 * ADIM)
    count = rows * blocks.count
    here = lax.axis_index("seq")
    row = here * rows + lax.broadcasted_iota(jnp.int32, (rows, count), 0)
    lane = (here - blocks.farthest) * rows + lax.broadcasted_iota(jnp.int32, (rows, count), 1)
    begin = jnp.concatenate([begin_ref[...]] * blocks.count, axis=1)
    allowed = jnp.concatenate([(lane <= row) & (lane >= begin)] * share, axis=0)
    low = head * ADIM
    keys = jnp.concatenate([ref[:, low : low + ADIM] for ref in kv_refs], axis=0)
    low = (kv_heads + head) * ADIM
    values = jnp.concatenate([ref[:, low : low + ADIM] for ref in kv_refs], axis=0)
    values = jnp.concatenate([values, jnp.ones((count, ADIM), BF16)], axis=1)
    lows = [(head * share + part) * ADIM for part in range(share)]
    asking = jnp.concatenate([q_ref[:, low : low + ADIM] for low in lows], axis=0)
    scores = lax.dot_general(asking, keys, (((1,), (1,)), ((), ())), preferred_element_type=F32)
    return jnp.where(allowed, scores * ADIM ** (-0.5), BARRED), values


class Blocks(NamedTuple):
    farthest: int
    count: int


def fold(q_ref, kv_refs, begin_ref, blocks, share, head, carry):
    lows = [(head * share + part) * ADIM for part in range(share)]
    scores, values = attend(q_ref, kv_refs, begin_ref, blocks, share, head)
    peak = jnp.max(scores, axis=1, keepdims=True)
    peak = jnp.broadcast_to(peak, (peak.shape[0], ADIM))
    if carry is not None:
        sums, totals, before = (
            jnp.concatenate([ref[:, low : low + ADIM] for low in lows], axis=0) for ref in carry
        )
        peak = jnp.maximum(peak, before)
    expo = jnp.exp(scores - jnp.concatenate([peak] * (scores.shape[1] // ADIM), axis=1))
    summed = jnp.dot(expo.astype(BF16), values, preferred_element_type=F32)
    if carry is None:
        return lows, summed[:, :ADIM], summed[:, ADIM:], peak
    factor = jnp.exp(before - peak)
    return lows, sums * factor + summed[:, :ADIM], totals * factor + summed[:, ADIM:], peak


def own_kernel(q_ref, keys_ref, values_ref, begin_ref, *outs):
    kv_ref = outs[3]
    kv_width = keys_ref.shape[1]
    kv_ref[:, :kv_width] = keys_ref[...]
    kv_ref[:, kv_width:] = values_ref[...]
    rows = q_ref.shape[0]
    share = QHEADS // KVHEADS
    for head in range(kv_width // ADIM):
        lows, *results = fold(q_ref, (kv_ref,), begin_ref, Blocks(0, 1), share, head, None)
        for ref, result in zip(outs, results):
            for part, low in enumerate(lows):
                ref[:, low : low + ADIM] = result[part * rows : (part + 1) * rows]


def near_kernel(q_ref, before_ref, begin_ref, *refs):
    carry, outs = refs[:3], refs[4:]
    outs[3][...] = before_ref[...]
    rows = q_ref.shape[0]
    share = QHEADS // KVHEADS
    for head in range(before_ref.shape[1] // (2 * ADIM)):
        lows, *results = fold(q_ref, (before_ref,), begin_ref, Blocks(1, 1), share, head, carry)
        for ref, result in zip(outs, results):
            for part, low in enumerate(lows):
                ref[:, low : low + ADIM] = result[part * rows : (part + 1) * rows]


def far_kernel(hops, *refs):
    q_ref, begin_ref = refs[:2]
    kv_refs = refs[5 : 4 + hops]
    out_hbm_ref, out_ref, sems = refs[4 + hops :]
    rows = q_ref.shape[0]
    share = QHEADS // KVHEADS
    copies = []
    for head in range(kv_refs[0].shape[1] // (2 * ADIM)):
        blocks = Blocks(hops, hops - 1)
        lows, sums, totals, _ = fold(q_ref, kv_refs, begin_ref, blocks, share, head, refs[2:5])
        result = (sums / totals).astype(BF16)
        for part, low in enumerate(lows):
            out_ref[:, low : low + ADIM] = result[part * rows : (part + 1) * rows]
        columns = pl.ds(head * share * ADIM, share * ADIM)
        copies.append(
            pltpu.make_async_copy(out_ref.at[:, columns], out_hbm_ref.at[:, columns], sems.at[head])
        )
        copies[-1].start()
    for copy in copies:
        copy.wait()


def norm_kernel(part, hops, first, given, *refs):
    local_ref, decay_ref, c_ref, gain_ref, flag_ref = refs[:5]
    got_refs = refs[5 : 5 + hops]
    out_hbm_ref, *token_refs = refs[5 + hops + given : -3]
    gated_ref, out_ref, sems = refs[-3:]
    for ref in token_refs:
        ref[...] = jnp.zeros_like(ref)

    def work():
        rows, width = gated_ref.shape
        outputs = c_ref[:, part * STATE : (part + 1) * STATE]
        squares = jnp.zeros((rows, 128), F32)
        for start in range(0, width, CHUNK):
            columns = slice(start, start + CHUNK)
            placed = slice(part * width + start, part * width + start + CHUNK)
            state = got_refs[0][:STATE, columns]
            for hop in range(1, hops):
                there = flag_ref[first + hop, 0:1] > 0.5
                state = jnp.where(there, got_refs[hop][:STATE, columns].astype(F32), state.astype(F32))
            carried = jnp.dot(outputs, state.astype(BF16), preferred_element_type=F32)
            gated = local_ref[:, placed] + carried * decay_ref[:, placed]
            gated_ref[:, columns] = gated
            for lane in range(0, CHUNK, 128):
                squares = squares + gated[:, lane : lane + 128] * gated[:, lane : lane + 128]
        squares = jnp.sum(squares, axis=1, keepdims=True)
        multiplier = lax.rsqrt(squares * (1.0 / width) + EPSILON)
        copies = []
        for start in range(0, width, CHUNK):
            columns = slice(start, start + CHUNK)
            gain = gain_ref[part * width + start : part * width + start + CHUNK]
            out_ref[:, columns] = (gated_ref[:, columns] * multiplier * gain.reshape(1, -1)).astype(BF16)
            copies.append(
                pltpu.make_async_copy(
                    out_ref.at[:, pl.ds(start, CHUNK)],
                    out_hbm_ref.at[:, pl.ds(part * width + start, CHUNK)],
                    sems.at[start // CHUNK],
                )
            )
            copies[-1].start()
        for copy in copies:
            copy.wait()

    if first:
        pl.when(jnp.max(flag_ref[first:]) > 0.5)(work)
    else:
        work()


WHOLE = pl.BlockSpec(memory_space=pltpu.VMEM)
SCALARS = pl.BlockSpec(memory_space=pltpu.SMEM)
UNTOUCHED = pl.BlockSpec(memory_space=pl.ANY)


def tile(rows, columns, row, column):
    return pl.BlockSpec((rows, columns), lambda step: (row, column))


def call(kernel, name, outs, operands, specs, out_specs=None, scratch=(), flops=KERNEL_FLOPS, aliases={}, limit=VMEM_LIMIT):
    moved = sum(math.prod(a.shape) * a.dtype.itemsize for a in (*operands, *outs))
    return pl.pallas_call(
        kernel,
        name=name,
        grid=(1,),
        out_shape=outs,
        in_specs=specs,
        out_specs=[WHOLE] * len(outs) if out_specs is None else out_specs,
        scratch_shapes=list(scratch),
        input_output_aliases=aliases,
        compiler_params=pltpu.CompilerParams(vmem_limit_bytes=limit),
        cost_estimate=pl.CostEstimate(flops=flops, bytes_accessed=moved, transcendentals=0),
    )(*operands)


def onward(value, first=0):
    count = lax.axis_size("seq")
    return lax.ppermute(value, "seq", [(source, source + 1) for source in range(first, count - 1)])


def shards(
    x_raw,
    bc_raw,
    z_gate,
    dt_raw,
    conv_x_weight,
    conv_x_bias,
    conv_bc_weight,
    conv_bc_bias,
    dt_bias,
    a_log,
    skip_d,
    norm_gain,
    queries,
    keys,
    values,
    doc_lens,
):
    rows, width = x_raw.shape
    bc_width = bc_raw.shape[1]
    heads = dt_raw.shape[1]
    groups = bc_width // (2 * STATE)
    per_group = width // groups
    count = lax.axis_size("seq")
    longest = rows * count // 2
    hops = min(count - 1, -(-(longest - 1) // rows))
    assert hops * rows >= longest and (hops == 2 or hops > 2 and groups == 1)
    shape = jax.ShapeDtypeStruct
    dt = dt_raw.T
    params = [dt, conv_x_weight, conv_x_bias, conv_bc_weight, conv_bc_bias, dt_bias, a_log]
    pieces = -(-(width + bc_width) // per_group)
    tail_rows = EDGE * -(-4 * pieces // EDGE)

    (message,) = call(
        first_state_kernel,
        "first_state",
        [shape((STATE + tail_rows, per_group), BF16)],
        [x_raw, bc_raw, *(a if a.ndim > 1 else a[None] for a in params), doc_lens],
        [UNTOUCHED] * 10,
        out_specs=[UNTOUCHED],
        scratch=[
            pltpu.VMEM((rows, per_group), BF16),
            pltpu.VMEM((rows, STATE), BF16),
            pltpu.VMEM((per_group // HDIM, rows), F32),
            pltpu.VMEM((conv_x_weight.shape[0], per_group), F32),
            pltpu.VMEM((1, per_group), F32),
            pltpu.VMEM((conv_x_weight.shape[0], STATE), F32),
            pltpu.VMEM((1, STATE), F32),
            pltpu.VMEM((1, heads), F32),
            pltpu.VMEM((1, heads), F32),
            pltpu.SMEM(doc_lens.shape, jnp.int32),
            pltpu.VMEM((EDGE, width), BF16),
            pltpu.VMEM((EDGE, bc_width), BF16),
            pltpu.VMEM((STATE + tail_rows, per_group), BF16),
            pltpu.VMEM((rows + 8, STATE), F32),
            pltpu.VMEM((4, rows + 8, CHUNK), F32),
            pltpu.SemaphoreType.DMA((12,)),
            pltpu.SemaphoreType.DMA((per_group // (2 * CHUNK) + 1,)),
        ],
        limit=VMEM_ALL,
    )
    slots = [onward(message)]
    prepared = call(
        functools.partial(prepare_kernel, hops, groups),
        "prepare",
        [
            shape((rows, width), BF16),
            shape((rows, bc_width), BF16),
            shape((8, width + bc_width), F32),
            shape((8, width), F32),
            shape((8, width), F32),
            shape((conv_x_weight.shape[0] - 1, 8, CHUNK), F32),
            shape((hops, 8, CHUNK), F32),
            shape((8, width), F32),
            shape((rows, rows), jnp.int32),
            shape((rows, heads), F32),
            shape((rows, heads), F32),
            shape((rows, width), F32),
            shape((rows, width), F32),
            shape((rows, width), F32),
            *(shape((STATE, per_group), BF16) for _ in range(groups - 1)),
        ],
        [x_raw, bc_raw, *params, skip_d, doc_lens, z_gate],
        [WHOLE] * 10 + [SCALARS] + [WHOLE],
        scratch=[
            pltpu.VMEM((16, width + bc_width), F32),
            pltpu.VMEM((4, rows + 8, CHUNK), F32),
        ],
    )
    _, bcc, partial, weight, through, inside, flags, wide_skip, begin, *prepared = prepared
    step, running, main, gate, decay, *states = prepared
    states = [message, *states]
    carried = [shape(queries.shape, F32)] * 3 + [shape((rows, 2 * keys.shape[1]), BF16)]
    *carry, kv = call(own_kernel, "attend_own", carried, [queries, keys, values, begin], [WHOLE] * 4)
    kvs = [kv, onward(kv)]
    fulls = None
    for slot in range(2, hops + groups):
        part = min(slot - 1, groups) - 1
        fresh = slot <= groups
        if slot == 2:
            kernel = functools.partial(relay_first_kernel, fresh)
            operands = [slots[0], states[0], partial, weight, through, inside, flags, conv_x_weight, conv_bc_weight]
            scratch = [pltpu.VMEM((4, 16, CHUNK), F32)]
        else:
            kernel = functools.partial(relay_kernel, part, fresh)
            operands = [slots[-1], fulls[part], through, flags]
            scratch = []
        if fresh:
            operands.append(states[slot - 1])
        (passed,) = call(
            kernel,
            f"relay_slot{slot}",
            [shape((STATE, per_group), BF16)],
            operands,
            [WHOLE] * len(operands),
            scratch=scratch,
        )
        slots.append(onward(passed))
        if fulls is None:
            gated, c_out, *fulls = call(
                functools.partial(first_rows_kernel, groups),
                "first_rows",
                [
                    shape((rows, width), F32),
                    shape((rows, groups * STATE), BF16),
                    *(shape((STATE, per_group), BF16) for _ in range(groups)),
                ],
                [
                    slots[0], partial, weight, inside, conv_x_weight, conv_bc_weight, step, running,
                    wide_skip, begin, bcc, main, gate, *states,
                ],
                [WHOLE] * (13 + groups),
                scratch=[pltpu.VMEM((4, 16, CHUNK), F32)],
            )
    def norm(part, first, got, out=None, token=False):
        operands = [gated, decay, c_out, norm_gain, flags, *got]
        specs = [WHOLE] * len(operands)
        outs = [shape((rows, width), BF16)] + [shape((8, 128), F32)] * token
        aliases = {}
        if out is not None:
            aliases = {len(operands): 0}
            operands.append(out)
            specs.append(UNTOUCHED)
        return call(
            functools.partial(norm_kernel, part, len(got), first, out is not None),
            f"norm_part{part}_{first}",
            outs,
            operands,
            specs,
            out_specs=[UNTOUCHED] + [WHOLE] * token,
            scratch=[
                pltpu.VMEM((rows, per_group), F32),
                pltpu.VMEM((rows, per_group), BF16),
                pltpu.SemaphoreType.DMA((per_group // CHUNK,)),
            ],
            aliases=aliases,
        )

    mamba_out, token = None, c_out
    for part in range(groups - 1):
        mamba_out, token = norm(part, 0, slots[part : part + 1], mamba_out, True)
    *carry, kv_on = call(
        near_kernel,
        "attend_near",
        carried,
        [queries, kvs[1], begin, *carry, token],
        [WHOLE] * 6 + [UNTOUCHED],
    )
    for hop in range(1, hops):
        kvs.append(onward(kv_on if hop == 1 else kvs[-1], hop))
    (attn_out,) = call(
        functools.partial(far_kernel, hops),
        "attend_far",
        [shape(queries.shape, BF16)],
        [queries, begin, *carry, *reversed(kvs[2:])],
        [WHOLE] * (4 + hops),
        out_specs=[UNTOUCHED],
        scratch=[
            pltpu.VMEM(queries.shape, BF16),
            pltpu.SemaphoreType.DMA((keys.shape[1] // ADIM,)),
        ],
    )
    for part in range(groups - 1):
        (mamba_out,) = norm(part, 1, slots[part + 1 : part + hops], mamba_out)
    (mamba_out,) = norm(groups - 1, 0, slots[-1:], mamba_out)
    return (mamba_out, attn_out)


def solution(mesh):
    split = P(("groups", "seq"), "dp")
    placed = (
        split,
        split,
        split,
        split,
        P(None, "dp"),
        P("dp"),
        P(None, "dp"),
        P("dp"),
        P("dp"),
        P("dp"),
        P("dp"),
        P("dp"),
        split,
        split,
        split,
        P("groups"),
    )
    return jax.shard_map(
        shards,
        mesh=mesh,
        in_specs=placed,
        out_specs=(split, split),
        check_vma=False,
    )
```

```python
import functools
import math
from typing import NamedTuple

import jax
import jax.numpy as jnp
from jax import lax
from jax.experimental import pallas as pl
from jax.experimental.pallas import tpu as pltpu
from jax.sharding import PartitionSpec as P

HDIM = 64
STATE = 128
QHEADS = 32
KVHEADS = 8
ADIM = 128
EPSILON = 1e-05
BARRED = -2e30
HIGHEST = lax.Precision.HIGHEST
F32 = jnp.float32
BF16 = jnp.bfloat16
CHUNK = 256
EDGE = 16
KERNEL_FLOPS = 2 * 10**9
VMEM_LIMIT = 40 * 1024 * 1024
VMEM_ALL = 62 * 1024 * 1024


def silu(value):
    return value * (0.5 * jnp.tanh(0.5 * value) + 0.5)


def softplus(value):
    return jnp.maximum(value, 0.0) + jnp.log(1.0 + jnp.exp(-jnp.abs(value)))


def doc_start(positions, lens_ref):
    begin = jnp.int32(0)
    found = positions * 0
    for doc in range(lens_ref.shape[0]):
        found = jnp.where(positions >= begin, begin, found)
        begin = begin + lens_ref[doc]
    return found


def halves(value):
    high = value.astype(BF16)
    return high, (value - high.astype(F32)).astype(BF16)


def widen(per_head, first, width):
    heads = per_head.shape[1]
    both = jnp.concatenate(halves(per_head), axis=1)
    head = lax.broadcasted_iota(jnp.int32, (2 * heads, width), 0)
    head = jnp.where(head >= heads, head - heads, head)
    channel = lax.broadcasted_iota(jnp.int32, (2 * heads, width), 1) + first
    spread = (channel // HDIM == head).astype(F32).astype(BF16)
    return jnp.dot(both, spread, preferred_element_type=F32)


def rates(dt_ref, dt_bias_ref, a_log_ref):
    heads = dt_ref.shape[0]
    step = softplus(dt_ref[...].T + dt_bias_ref[...].reshape(1, -1)[:, :heads])
    rate = -step * jnp.exp(a_log_ref[...].reshape(1, -1)[:, :heads])
    rows = step.shape[0]
    row = lax.broadcasted_iota(jnp.int32, (rows, rows), 0)
    column = lax.broadcasted_iota(jnp.int32, (rows, rows), 1)
    lower = (row >= column).astype(F32).astype(BF16)
    high = rate.astype(BF16)
    middle, low = halves(rate - high.astype(F32))
    parts = jnp.concatenate([high, middle, low], axis=0)
    lowers = jnp.concatenate([lower, lower, lower], axis=1)
    return step, jnp.dot(lowers, parts, preferred_element_type=F32)


def insides(first, shape, taps, lens_ref):
    positions = first + lax.broadcasted_iota(jnp.int32, shape, 0)
    depth = positions - doc_start(positions, lens_ref)
    return [depth >= lag for lag in range(taps)]


def conv(pad, rows, weight, bias, inside):
    taps = weight.shape[0]
    total = pad[8 : 8 + rows] * weight[taps - 1 : taps] + bias
    for lag in range(1, taps):
        term = pad[8 - lag : 8 - lag + rows] * weight[taps - 1 - lag : taps - lag]
        total = total + jnp.where(inside[lag], term, 0.0)
    return silu(total)


def tail_lines(message, rows):
    block = message[rows:].astype(F32)
    return jnp.concatenate([block[at : at + 4] for at in range(0, block.shape[0], 4)], axis=1)


def reach(device, rows, lens_ref):
    return device - doc_start((device + 1) * rows - 1, lens_ref) // rows


def kept_weight(here, step, running, taps, lens_ref):
    rows = step.shape[0]
    last_begin = doc_start((here + 1) * rows - 1, lens_ref)
    row = lax.broadcasted_iota(jnp.int32, step.shape, 0)
    weight = step * jnp.exp(running[rows - 1 : rows] - running)
    kept = (here * rows + row >= last_begin) & ((row >= taps - 1) | (last_begin // rows >= here))
    return jnp.where(kept, weight, 0.0)


def conv_rows(pad, raw, weight, bias, inside):
    pad[0:8] = jnp.zeros((8, raw.shape[1]), F32)
    pad[8:] = raw.astype(F32)
    return conv(pad, raw.shape[0], weight, bias.reshape(1, -1), inside)


def first_state_kernel(*refs):
    hbm_refs, out_hbm_ref = refs[:10], refs[10]
    vmem_refs = refs[11:21]
    x_edge_ref, bc_edge_ref, out_ref, b_pad_ref, pad_ref, in_sems, out_sems = refs[21:]
    x_ref, b_ref, dt_ref, wx_ref, bx_ref, wbc_ref, bbc_ref, dt_bias_ref, a_log_ref, lens_ref = vmem_refs
    rows, width = x_ref.shape
    taps = wx_ref.shape[0]

    def corner(ref, shape):
        return ref.at[tuple(pl.ds(0, extent) for extent in shape)]

    order = (9, 2, 7, 8, 1, 5, 6, 0, 3, 4)
    copies = {}
    for at in order:
        source = corner(hbm_refs[at], vmem_refs[at].shape)
        copies[at] = pltpu.make_async_copy(source, vmem_refs[at], in_sems.at[at])
        copies[at].start()
    edge_copies = []
    for at, (source, target) in enumerate(((hbm_refs[0], x_edge_ref), (hbm_refs[1], bc_edge_ref))):
        edge_copies.append(
            pltpu.make_async_copy(source.at[pl.ds(rows - EDGE, EDGE)], target, in_sems.at[10 + at])
        )
        edge_copies[-1].start()

    here = lax.axis_index("seq")
    for at in (9, 2, 7, 8):
        copies[at].wait()
    inside = insides(here * rows, (rows, CHUNK), taps, lens_ref)
    step, running = rates(dt_ref, dt_bias_ref, a_log_ref)
    weight = kept_weight(here, step, running, taps, lens_ref)
    narrow = [mask[:, :STATE] for mask in inside]
    for at in (1, 5, 6):
        copies[at].wait()
    inputs = conv_rows(b_pad_ref, b_ref[...], wbc_ref[...], bbc_ref[...], narrow)
    turned = inputs.T.astype(BF16)
    for at in (0, 3, 4):
        copies[at].wait()
    slots = pad_ref.shape[0]
    outs = []

    def send(at, view):
        copy = pltpu.make_async_copy(out_ref.at[view], out_hbm_ref.at[view], out_sems.at[at])
        copy.start()
        outs.append(copy)

    for at, start in enumerate(range(0, width, CHUNK)):
        columns = slice(start, start + CHUNK)
        pad = pad_ref.at[(at + 1) % slots]
        xc = conv_rows(pad, x_ref[:, columns], wx_ref[:, columns], bx_ref[:, columns], inside)
        weighted = (xc * widen(weight, start, CHUNK)).astype(BF16)
        out_ref[:STATE, columns] = jnp.dot(turned, weighted, preferred_element_type=F32).astype(BF16)
        if at % 2:
            send(at // 2, (pl.ds(0, STATE), pl.ds(start - CHUNK, 2 * CHUNK)))
    for copy in edge_copies:
        copy.wait()
    edges = jnp.concatenate([x_edge_ref[...].astype(F32), bc_edge_ref[...].astype(F32)], axis=1)[EDGE - 4 :]
    spare = -edges.shape[1] % width
    if spare:
        edges = jnp.concatenate([edges, jnp.zeros((4, spare), F32)], axis=1)
    pieces = [edges[:, at : at + width] for at in range(0, edges.shape[1], width)]
    while len(pieces) % (EDGE // 4):
        pieces.append(jnp.zeros_like(pieces[0]))
    out_ref[STATE:] = jnp.concatenate(pieces, axis=0).astype(BF16)
    send(width // (2 * CHUNK), (pl.ds(STATE, out_ref.shape[0] - STATE), pl.ds(0, width)))
    for copy in outs:
        copy.wait()


def prepare_kernel(hops, groups, *refs):
    x_ref, bc_ref, dt_ref, wx_ref, bx_ref, wbc_ref, bbc_ref, dt_bias_ref, a_log_ref, skip_ref, lens_ref = refs[:11]
    z_ref = refs[11]
    xc_ref, bcc_ref, partial_ref, weight_ref, through_ref, inside_ref, flag_ref = refs[12:19]
    wide_skip_ref, begin_ref, step_ref, running_ref, out_ref, gate_ref, decay_ref = refs[19:26]
    state_refs = refs[26:-2]
    top_ref, pad_ref = refs[-2:]
    rows, width = x_ref.shape
    per_group = width // groups
    taps = wx_ref.shape[0]
    slots = pad_ref.shape[0]
    here = lax.axis_index("seq")
    first = here * rows
    inside = insides(first, (rows, CHUNK), taps, lens_ref)
    step, running = rates(dt_ref, dt_bias_ref, a_log_ref)
    heads = step.shape[1]
    group_heads = heads // groups
    kept = kept_weight(here, step, running, taps, lens_ref)
    for group in range(groups):
        base = slice(group * 2 * STATE, (group + 1) * 2 * STATE)
        pair = conv_rows(pad_ref.at[0], bc_ref[:, base], wbc_ref[:, base], bbc_ref[base], inside)
        bcc_ref[:, base] = pair.astype(BF16)
        turned = pair[:, :STATE].T.astype(BF16)
        part_weight = kept[:, group * group_heads : (group + 1) * group_heads]
        for chunk in range(0, per_group, CHUNK):
            columns = slice(group * per_group + chunk, group * per_group + chunk + CHUNK)
            pad = pad_ref.at[(chunk // CHUNK + 1) % slots]
            xc = conv_rows(pad, x_ref[:, columns], wx_ref[:, columns], bx_ref[columns], inside)
            xc_ref[:, columns] = xc.astype(BF16)
            if group:
                weighted = (xc * widen(part_weight, chunk, CHUNK)).astype(BF16)
                state_refs[group - 1][:, chunk : chunk + CHUNK] = jnp.dot(
                    turned, weighted, preferred_element_type=F32
                ).astype(BF16)

    own = reach(here, rows, lens_ref) == 0
    inside = [mask[:8] for mask in inside]
    for lag in range(1, taps):
        inside_ref[lag - 1] = inside[lag].astype(F32)
    flag_ref[0] = jnp.broadcast_to(own.astype(F32), (8, CHUNK))
    before = reach(here - 1, rows, lens_ref)
    for hop in range(1, hops):
        flag_ref[hop] = jnp.broadcast_to((before == hop).astype(F32), (8, CHUNK))
    begin = doc_start(first + lax.broadcasted_iota(jnp.int32, begin_ref.shape, 0), lens_ref)
    begin_ref[...] = begin
    entry = jnp.where(begin[:, :heads] < first, jnp.exp(running), 0.0)
    step_ref[...] = step
    running_ref[...] = running
    row = lax.broadcasted_iota(jnp.int32, (8, heads), 0)
    total = running[rows - 1 : rows]
    weight = step[:8] * jnp.exp(total - running[:8])
    weight = jnp.where((row < taps - 1) & jnp.logical_not(own), weight, 0.0)
    through = jnp.where(own, 0.0, jnp.broadcast_to(jnp.exp(total), (8, heads)))
    skip = jnp.broadcast_to(skip_ref[...].reshape(1, -1), (8, heads))
    every = jnp.concatenate([weight, through, skip], axis=0)
    for start in range(0, width, CHUNK):
        wide = widen(every, start, CHUNK)
        weight_ref[:, start : start + CHUNK] = wide[:8]
        through_ref[:, start : start + CHUNK] = wide[8:16]
        wide_skip_ref[:, start : start + CHUNK] = wide[16:]
    top_ref[0:8] = jnp.zeros((8, top_ref.shape[1]), F32)
    top_ref[8:, :width] = x_ref[:EDGE].astype(F32)[:8]
    top_ref[8:, width:] = bc_ref[:EDGE].astype(F32)[:8]

    def some(columns, base, w_ref, b_ref):
        here_columns = slice(base + columns.start, base + columns.stop)
        total = top_ref[8:, here_columns] * w_ref[taps - 1 : taps, columns] + b_ref[columns].reshape(1, -1)
        for lag in range(1, taps):
            term = top_ref[8 - lag : 16 - lag, here_columns] * w_ref[taps - 1 - lag : taps - lag, columns]
            total = total + jnp.where(inside[lag], term, 0.0)
        partial_ref[:, here_columns] = total

    for start in range(0, width, CHUNK):
        some(slice(start, start + CHUNK), 0, wx_ref, bx_ref)
    for start in range(0, bc_ref.shape[1], CHUNK):
        some(slice(start, start + CHUNK), width, wbc_ref, bbc_ref)

    row = lax.broadcasted_iota(jnp.int32, (rows, rows), 0)
    lane = lax.broadcasted_iota(jnp.int32, (rows, rows), 1)
    linked = (row >= lane) & (first + lane >= begin) & (lane >= 8)
    turned_running = running.T
    turned_step = step.T
    pair_width = 2 * HDIM
    channel = lax.broadcasted_iota(jnp.int32, (rows, pair_width), 1)
    below = lax.broadcasted_iota(jnp.int32, (rows, CHUNK), 0) >= 8
    for group in range(groups):
        base = group * 2 * STATE
        meet = lax.dot_general(
            bcc_ref[:, base + STATE : base + 2 * STATE],
            bcc_ref[:, base : base + STATE],
            (((1,), (1,)), ((), ())),
            preferred_element_type=F32,
        )
        meet = jnp.where(linked, meet, 0.0)
        group_entry = entry[:, group * group_heads : (group + 1) * group_heads]
        for chunk in range(0, per_group, CHUNK):
            at = group * per_group + chunk
            columns = slice(at, at + CHUNK)
            gate = silu(z_ref[:, columns].astype(F32))
            gate_ref[:, columns] = gate
            decay_ref[:, columns] = widen(group_entry, chunk, CHUNK) * gate
            xc_all = xc_ref[:, columns]
            skipped = jnp.where(below, xc_all.astype(F32) * wide_skip_ref[0:1, columns], 0.0)
            for start in range(0, CHUNK, pair_width):
                parts = []
                for head in ((at + start) // HDIM, (at + start) // HDIM + 1):
                    spread = running[:, head : head + 1] - turned_running[head : head + 1]
                    decay = jnp.exp(jnp.minimum(spread, 0.0))
                    parts.append((decay * (meet * turned_step[head : head + 1])).astype(BF16))
                mix = jnp.concatenate(parts, axis=1)
                here_columns = slice(start, start + pair_width)
                xc = xc_all[:, here_columns]
                zero = jnp.zeros_like(xc)
                stacked = jnp.concatenate(
                    [jnp.where(channel < HDIM, xc, zero), jnp.where(channel < HDIM, zero, xc)], axis=0
                )
                value = jnp.dot(mix, stacked, preferred_element_type=F32) + skipped[:, here_columns]
                out_ref[:, at + start : at + start + pair_width] = value * gate[:, here_columns]


def first_rows(lines, partial_ref, inside_ref, w_ref, pad_ref, slot, at, start):
    taps = w_ref.shape[0]
    columns = slice(start, start + CHUNK)
    pad = pad_ref.at[slot]
    pad[4:8] = lines[:, at + start : at + start + CHUNK]
    pad[8:] = jnp.zeros((8, CHUNK), F32)
    total = partial_ref[:, at + start : at + start + CHUNK]
    for lag in range(1, taps):
        term = pad[8 - lag : 16 - lag] * w_ref[taps - 1 - lag : taps - lag, columns]
        total = total + term * inside_ref[lag - 1]
    return silu(total).astype(BF16)


def relay_first_kernel(fresh, *refs):
    message_ref, state_ref, partial_ref, weight_ref, through_ref, inside_ref, flag_ref, wx_ref, wbc_ref = refs[:9]
    other_ref = refs[9] if fresh else state_ref
    out_ref, pad_ref = refs[-2:]
    width = out_ref.shape[1]
    slots = pad_ref.shape[0]
    lines = tail_lines(message_ref, STATE)
    top = functools.partial(first_rows, lines, partial_ref, inside_ref)
    inputs = top(wbc_ref, pad_ref, 0, wx_ref.shape[1], 0)[:, :STATE]
    turned = inputs.astype(F32).T.astype(BF16)
    own = flag_ref[0, 0:1] > 0.5
    for start in range(0, width, CHUNK):
        columns = slice(start, start + CHUNK)
        xc = top(wx_ref, pad_ref, (start // CHUNK + 1) % slots, 0, start)
        weighted = (xc.astype(F32) * weight_ref[:, columns]).astype(BF16)
        full = state_ref[:STATE, columns].astype(F32) + jnp.dot(
            turned, weighted, preferred_element_type=F32
        )
        full = full + through_ref[0:1, columns] * message_ref[:STATE, columns].astype(F32)
        out_ref[:, columns] = jnp.where(own, other_ref[:STATE, columns].astype(F32), full).astype(BF16)


def relay_kernel(part, fresh, *refs):
    got_ref, state_ref, through_ref, flag_ref = refs[:4]
    out_ref = refs[-1]
    width = out_ref.shape[1]
    own = flag_ref[0, 0:1] > 0.5
    for start in range(0, width, CHUNK):
        columns = slice(start, start + CHUNK)
        through = through_ref[0:1, part * width + start : part * width + start + CHUNK]
        full = state_ref[:, columns].astype(F32) + through * got_ref[:STATE, columns].astype(F32)
        if fresh:
            full = jnp.where(own, refs[4][:STATE, columns].astype(F32), full)
        out_ref[:, columns] = full.astype(BF16)


def first_rows_kernel(groups, *refs):
    (
        message_ref, partial_ref, weight_ref, inside_ref, wx_ref, wbc_ref, step_ref, running_ref,
        wide_skip_ref, begin_ref, bcc_ref, main_ref, gate_ref,
    ) = refs[:13]
    state_refs = refs[13 : 13 + groups]
    out_ref, c_ref = refs[13 + groups : 15 + groups]
    full_refs = refs[15 + groups : 15 + 2 * groups]
    pad_ref = refs[-1]
    rows, width = main_ref.shape
    per_group = width // groups
    heads = per_group // HDIM
    lanes = 8 * heads
    first = lax.axis_index("seq") * rows
    lines = tail_lines(message_ref, STATE)
    slots = pad_ref.shape[0]
    top = functools.partial(first_rows, lines, partial_ref, inside_ref)
    lane = lax.broadcasted_iota(jnp.int32, (rows, lanes), 1)
    line = lane & 7
    row = lax.broadcasted_iota(jnp.int32, (rows, lanes), 0)
    begin = jnp.concatenate([begin_ref[...]] * -(-lanes // rows), axis=1)[:, :lanes]
    linked = (row >= line) & (first + line >= begin)
    head = lax.broadcasted_iota(jnp.int32, (3 * heads, lanes), 0)
    for _ in range(2):
        head = jnp.where(head >= heads, head - heads, head)
    spread = (lax.broadcasted_iota(jnp.int32, (3 * heads, lanes), 1) >> 3 == head).astype(F32).astype(BF16)
    own_line = lax.broadcasted_iota(jnp.int32, (8, lanes), 0) == line[:8]

    def to_lanes(value):
        high = value.astype(BF16)
        middle, low = halves(value - high.astype(F32))
        return jnp.dot(jnp.concatenate([high, middle, low], axis=1), spread, preferred_element_type=F32)

    def by_line(value):
        return jnp.sum(jnp.where(own_line, value, 0.0), axis=0, keepdims=True)

    channel = lax.broadcasted_iota(jnp.int32, (8, CHUNK), 1)
    for group in range(groups):
        base = group * 2 * STATE
        these = slice(group * heads, (group + 1) * heads)
        new = top(wbc_ref, pad_ref, group % slots, width, base).astype(F32)
        old = bcc_ref[:, base + STATE : base + 2 * STATE]
        outputs = jnp.concatenate([new[:, STATE:], old[:EDGE].astype(F32)[8:]], axis=0).astype(BF16)
        outputs = jnp.concatenate([outputs, old[EDGE:]], axis=0)
        c_ref[:, group * STATE : (group + 1) * STATE] = outputs
        inputs = jnp.concatenate([new[:, :STATE]] * heads, axis=0).astype(BF16)
        meet = lax.dot_general(
            outputs, inputs, (((1,), (1,)), ((), ())), preferred_element_type=F32
        )
        running = to_lanes(running_ref[:, these])
        decay = jnp.exp(jnp.minimum(running - by_line(running[:8]), 0.0))
        mix = decay * (meet * by_line(to_lanes(step_ref[:8, these])))
        mix = jnp.where(linked, mix, 0.0).astype(BF16)
        turned = inputs[:EDGE].astype(F32).T[:, :8].astype(BF16)
        for chunk in range(0, per_group, CHUNK):
            at = group * per_group + chunk
            columns = slice(at, at + CHUNK)
            xc = top(wx_ref, pad_ref, (chunk // CHUNK + 1) % slots, 0, at).astype(F32)
            full = state_refs[group][:STATE, chunk : chunk + CHUNK].astype(F32) + jnp.dot(
                turned, (xc * weight_ref[:, columns]).astype(BF16), preferred_element_type=F32
            )
            full_refs[group][:, chunk : chunk + CHUNK] = full.astype(BF16)
            blocks = []
            for at_head in range(heads):
                low = at_head * HDIM - chunk
                if 0 <= low < CHUNK:
                    blocks.append(jnp.where((channel >= low) & (channel < low + HDIM), xc, 0.0))
                else:
                    blocks.append(jnp.zeros_like(xc))
            spread_xc = jnp.concatenate(blocks, axis=0).astype(BF16)
            gate = gate_ref[:, columns]
            value = main_ref[:, columns] + gate * jnp.dot(mix, spread_xc, preferred_element_type=F32)
            out_ref[:, columns] = value
            out_ref[0:8, columns] = value[:8] + gate[:8] * (xc * wide_skip_ref[:, columns])


def attend(q_ref, kv_refs, begin_ref, blocks, share, head):
    rows = q_ref.shape[0]
    kv_heads = kv_refs[0].shape[1] // (2 * ADIM)
    count = rows * blocks.count
    here = lax.axis_index("seq")
    row = here * rows + lax.broadcasted_iota(jnp.int32, (rows, count), 0)
    lane = (here - blocks.farthest) * rows + lax.broadcasted_iota(jnp.int32, (rows, count), 1)
    begin = jnp.concatenate([begin_ref[...]] * blocks.count, axis=1)
    allowed = jnp.concatenate([(lane <= row) & (lane >= begin)] * share, axis=0)
    low = head * ADIM
    keys = jnp.concatenate([ref[:, low : low + ADIM] for ref in kv_refs], axis=0)
    low = (kv_heads + head) * ADIM
    values = jnp.concatenate([ref[:, low : low + ADIM] for ref in kv_refs], axis=0)
    values = jnp.concatenate([values, jnp.ones((count, ADIM), BF16)], axis=1)
    lows = [(head * share + part) * ADIM for part in range(share)]
    asking = jnp.concatenate([q_ref[:, low : low + ADIM] for low in lows], axis=0)
    scores = lax.dot_general(asking, keys, (((1,), (1,)), ((), ())), preferred_element_type=F32)
    return jnp.where(allowed, scores * ADIM ** (-0.5), BARRED), values


class Blocks(NamedTuple):
    farthest: int
    count: int


def fold(q_ref, kv_refs, begin_ref, blocks, share, head, carry):
    lows = [(head * share + part) * ADIM for part in range(share)]
    scores, values = attend(q_ref, kv_refs, begin_ref, blocks, share, head)
    peak = jnp.max(scores, axis=1, keepdims=True)
    peak = jnp.broadcast_to(peak, (peak.shape[0], ADIM))
    if carry is not None:
        sums, totals, before = (
            jnp.concatenate([ref[:, low : low + ADIM] for low in lows], axis=0) for ref in carry
        )
        peak = jnp.maximum(peak, before)
    expo = jnp.exp(scores - jnp.concatenate([peak] * (scores.shape[1] // ADIM), axis=1))
    summed = jnp.dot(expo.astype(BF16), values, preferred_element_type=F32)
    if carry is None:
        return lows, summed[:, :ADIM], summed[:, ADIM:], peak
    factor = jnp.exp(before - peak)
    return lows, sums * factor + summed[:, :ADIM], totals * factor + summed[:, ADIM:], peak


def own_kernel(q_ref, keys_ref, values_ref, begin_ref, *outs):
    kv_ref = outs[3]
    kv_width = keys_ref.shape[1]
    kv_ref[:, :kv_width] = keys_ref[...]
    kv_ref[:, kv_width:] = values_ref[...]
    rows = q_ref.shape[0]
    share = QHEADS // KVHEADS
    for head in range(kv_width // ADIM):
        lows, *results = fold(q_ref, (kv_ref,), begin_ref, Blocks(0, 1), share, head, None)
        for ref, result in zip(outs, results):
            for part, low in enumerate(lows):
                ref[:, low : low + ADIM] = result[part * rows : (part + 1) * rows]


def near_kernel(q_ref, before_ref, begin_ref, *refs):
    carry, outs = refs[:3], refs[4:]
    outs[3][...] = before_ref[...]
    rows = q_ref.shape[0]
    share = QHEADS // KVHEADS
    for head in range(before_ref.shape[1] // (2 * ADIM)):
        lows, *results = fold(q_ref, (before_ref,), begin_ref, Blocks(1, 1), share, head, carry)
        for ref, result in zip(outs, results):
            for part, low in enumerate(lows):
                ref[:, low : low + ADIM] = result[part * rows : (part + 1) * rows]


def far_kernel(hops, *refs):
    q_ref, begin_ref = refs[:2]
    kv_refs = refs[5 : 4 + hops]
    out_hbm_ref, out_ref, sems = refs[4 + hops :]
    rows = q_ref.shape[0]
    share = QHEADS // KVHEADS
    copies = []
    for head in range(kv_refs[0].shape[1] // (2 * ADIM)):
        blocks = Blocks(hops, hops - 1)
        lows, sums, totals, _ = fold(q_ref, kv_refs, begin_ref, blocks, share, head, refs[2:5])
        result = (sums / totals).astype(BF16)
        for part, low in enumerate(lows):
            out_ref[:, low : low + ADIM] = result[part * rows : (part + 1) * rows]
        columns = pl.ds(head * share * ADIM, share * ADIM)
        copies.append(
            pltpu.make_async_copy(out_ref.at[:, columns], out_hbm_ref.at[:, columns], sems.at[head])
        )
        copies[-1].start()
    for copy in copies:
        copy.wait()


def norm_kernel(part, hops, *refs):
    local_ref, decay_ref, c_ref, gain_ref, flag_ref = refs[:5]
    got_refs = refs[5 : 5 + hops]
    out_hbm_ref, gated_ref, out_ref, sems = refs[-4:]
    rows, width = gated_ref.shape
    outputs = c_ref[:, part * STATE : (part + 1) * STATE]
    squares = jnp.zeros((rows, 128), F32)
    for start in range(0, width, CHUNK):
        columns = slice(start, start + CHUNK)
        placed = slice(part * width + start, part * width + start + CHUNK)
        state = got_refs[0][:STATE, columns]
        for hop in range(1, hops):
            there = flag_ref[hop, 0:1] > 0.5
            state = jnp.where(there, got_refs[hop][:STATE, columns].astype(F32), state.astype(F32))
        carried = jnp.dot(outputs, state.astype(BF16), preferred_element_type=F32)
        gated = local_ref[:, placed] + carried * decay_ref[:, placed]
        gated_ref[:, columns] = gated
        for lane in range(0, CHUNK, 128):
            squares = squares + gated[:, lane : lane + 128] * gated[:, lane : lane + 128]
    squares = jnp.sum(squares, axis=1, keepdims=True)
    multiplier = lax.rsqrt(squares * (1.0 / width) + EPSILON)
    copies = []
    for start in range(0, width, CHUNK):
        columns = slice(start, start + CHUNK)
        gain = gain_ref[part * width + start : part * width + start + CHUNK]
        out_ref[:, columns] = (gated_ref[:, columns] * multiplier * gain.reshape(1, -1)).astype(BF16)
        copies.append(
            pltpu.make_async_copy(
                out_ref.at[:, pl.ds(start, CHUNK)],
                out_hbm_ref.at[:, pl.ds(part * width + start, CHUNK)],
                sems.at[start // CHUNK],
            )
        )
        copies[-1].start()
    for copy in copies:
        copy.wait()


WHOLE = pl.BlockSpec(memory_space=pltpu.VMEM)
SCALARS = pl.BlockSpec(memory_space=pltpu.SMEM)
UNTOUCHED = pl.BlockSpec(memory_space=pl.ANY)


def tile(rows, columns, row, column):
    return pl.BlockSpec((rows, columns), lambda step: (row, column))


def call(kernel, name, outs, operands, specs, out_specs=None, scratch=(), flops=KERNEL_FLOPS, aliases={}, limit=VMEM_LIMIT):
    moved = sum(math.prod(a.shape) * a.dtype.itemsize for a in (*operands, *outs))
    return pl.pallas_call(
        kernel,
        name=name,
        grid=(1,),
        out_shape=outs,
        in_specs=specs,
        out_specs=[WHOLE] * len(outs) if out_specs is None else out_specs,
        scratch_shapes=list(scratch),
        input_output_aliases=aliases,
        compiler_params=pltpu.CompilerParams(vmem_limit_bytes=limit),
        cost_estimate=pl.CostEstimate(flops=flops, bytes_accessed=moved, transcendentals=0),
    )(*operands)


def onward(value, first=0):
    count = lax.axis_size("seq")
    return lax.ppermute(value, "seq", [(source, source + 1) for source in range(first, count - 1)])


def shards(
    x_raw,
    bc_raw,
    z_gate,
    dt_raw,
    conv_x_weight,
    conv_x_bias,
    conv_bc_weight,
    conv_bc_bias,
    dt_bias,
    a_log,
    skip_d,
    norm_gain,
    queries,
    keys,
    values,
    doc_lens,
):
    rows, width = x_raw.shape
    bc_width = bc_raw.shape[1]
    heads = dt_raw.shape[1]
    groups = bc_width // (2 * STATE)
    per_group = width // groups
    count = lax.axis_size("seq")
    longest = rows * count // 2
    hops = min(count - 1, -(-(longest - 1) // rows))
    assert hops * rows >= longest and (hops == 2 or hops > 2 and groups == 1)
    shape = jax.ShapeDtypeStruct
    dt = dt_raw.T
    params = [dt, conv_x_weight, conv_x_bias, conv_bc_weight, conv_bc_bias, dt_bias, a_log]
    pieces = -(-(width + bc_width) // per_group)
    tail_rows = EDGE * -(-4 * pieces // EDGE)

    (message,) = call(
        first_state_kernel,
        "first_state",
        [shape((STATE + tail_rows, per_group), BF16)],
        [x_raw, bc_raw, *(a if a.ndim > 1 else a[None] for a in params), doc_lens],
        [UNTOUCHED] * 10,
        out_specs=[UNTOUCHED],
        scratch=[
            pltpu.VMEM((rows, per_group), BF16),
            pltpu.VMEM((rows, STATE), BF16),
            pltpu.VMEM((per_group // HDIM, rows), F32),
            pltpu.VMEM((conv_x_weight.shape[0], per_group), F32),
            pltpu.VMEM((1, per_group), F32),
            pltpu.VMEM((conv_x_weight.shape[0], STATE), F32),
            pltpu.VMEM((1, STATE), F32),
            pltpu.VMEM((1, heads), F32),
            pltpu.VMEM((1, heads), F32),
            pltpu.SMEM(doc_lens.shape, jnp.int32),
            pltpu.VMEM((EDGE, width), BF16),
            pltpu.VMEM((EDGE, bc_width), BF16),
            pltpu.VMEM((STATE + tail_rows, per_group), BF16),
            pltpu.VMEM((rows + 8, STATE), F32),
            pltpu.VMEM((4, rows + 8, CHUNK), F32),
            pltpu.SemaphoreType.DMA((12,)),
            pltpu.SemaphoreType.DMA((per_group // (2 * CHUNK) + 1,)),
        ],
        limit=VMEM_ALL,
    )
    slots = [onward(message)]
    prepared = call(
        functools.partial(prepare_kernel, hops, groups),
        "prepare",
        [
            shape((rows, width), BF16),
            shape((rows, bc_width), BF16),
            shape((8, width + bc_width), F32),
            shape((8, width), F32),
            shape((8, width), F32),
            shape((conv_x_weight.shape[0] - 1, 8, CHUNK), F32),
            shape((hops, 8, CHUNK), F32),
            shape((8, width), F32),
            shape((rows, rows), jnp.int32),
            shape((rows, heads), F32),
            shape((rows, heads), F32),
            shape((rows, width), F32),
            shape((rows, width), F32),
            shape((rows, width), F32),
            *(shape((STATE, per_group), BF16) for _ in range(groups - 1)),
        ],
        [x_raw, bc_raw, *params, skip_d, doc_lens, z_gate],
        [WHOLE] * 10 + [SCALARS] + [WHOLE],
        scratch=[
            pltpu.VMEM((16, width + bc_width), F32),
            pltpu.VMEM((4, rows + 8, CHUNK), F32),
        ],
    )
    _, bcc, partial, weight, through, inside, flags, wide_skip, begin, *prepared = prepared
    step, running, main, gate, decay, *states = prepared
    states = [message, *states]
    carried = [shape(queries.shape, F32)] * 3 + [shape((rows, 2 * keys.shape[1]), BF16)]
    *carry, kv = call(own_kernel, "attend_own", carried, [queries, keys, values, begin], [WHOLE] * 4)
    kvs = [kv, onward(kv)]
    fulls = None
    for slot in range(2, hops + groups):
        part = min(slot - 1, groups) - 1
        fresh = slot <= groups
        if slot == 2:
            kernel = functools.partial(relay_first_kernel, fresh)
            operands = [slots[0], states[0], partial, weight, through, inside, flags, conv_x_weight, conv_bc_weight]
            scratch = [pltpu.VMEM((4, 16, CHUNK), F32)]
        else:
            kernel = functools.partial(relay_kernel, part, fresh)
            operands = [slots[-1], fulls[part], through, flags]
            scratch = []
        if fresh:
            operands.append(states[slot - 1])
        (passed,) = call(
            kernel,
            f"relay_slot{slot}",
            [shape((STATE, per_group), BF16)],
            operands,
            [WHOLE] * len(operands),
            scratch=scratch,
        )
        slots.append(onward(passed))
        if fulls is None:
            gated, c_out, *fulls = call(
                functools.partial(first_rows_kernel, groups),
                "first_rows",
                [
                    shape((rows, width), F32),
                    shape((rows, groups * STATE), BF16),
                    *(shape((STATE, per_group), BF16) for _ in range(groups)),
                ],
                [
                    slots[0], partial, weight, inside, conv_x_weight, conv_bc_weight, step, running,
                    wide_skip, begin, bcc, main, gate, *states,
                ],
                [WHOLE] * (13 + groups),
                scratch=[pltpu.VMEM((4, 16, CHUNK), F32)],
            )
    *carry, kv_on = call(
        near_kernel,
        "attend_near",
        carried,
        [queries, kvs[1], begin, *carry, c_out],
        [WHOLE] * 6 + [UNTOUCHED],
    )
    for hop in range(1, hops):
        kvs.append(onward(kv_on if hop == 1 else kvs[-1], hop))
    (attn_out,) = call(
        functools.partial(far_kernel, hops),
        "attend_far",
        [shape(queries.shape, BF16)],
        [queries, begin, *carry, *reversed(kvs[2:])],
        [WHOLE] * (4 + hops),
        out_specs=[UNTOUCHED],
        scratch=[
            pltpu.VMEM(queries.shape, BF16),
            pltpu.SemaphoreType.DMA((keys.shape[1] // ADIM,)),
        ],
    )
    mamba_out = None
    for part in range(groups):
        got = slots[-1:] if part == groups - 1 else slots[part : part + hops]
        operands = [gated, decay, c_out, norm_gain, flags, *got]
        specs = [WHOLE] * (5 + len(got))
        aliases = {}
        if mamba_out is not None:
            operands.append(mamba_out)
            specs.append(UNTOUCHED)
            aliases = {len(operands) - 1: 0}
        (mamba_out,) = call(
            functools.partial(norm_kernel, part, len(got)),
            f"norm_part{part}",
            [shape((rows, width), BF16)],
            operands,
            specs,
            out_specs=[UNTOUCHED],
            scratch=[
                pltpu.VMEM((rows, per_group), F32),
                pltpu.VMEM((rows, per_group), BF16),
                pltpu.SemaphoreType.DMA((per_group // CHUNK,)),
            ],
            aliases=aliases,
        )
    return (mamba_out, attn_out)


def solution(mesh):
    split = P(("groups", "seq"), "dp")
    placed = (
        split,
        split,
        split,
        split,
        P(None, "dp"),
        P("dp"),
        P(None, "dp"),
        P("dp"),
        P("dp"),
        P("dp"),
        P("dp"),
        P("dp"),
        split,
        split,
        split,
        P("groups"),
    )
    return jax.shard_map(
        shards,
        mesh=mesh,
        in_specs=placed,
        out_specs=(split, split),
        check_vma=False,
    )
```

```python
import functools
import math
from typing import NamedTuple

import jax
import jax.numpy as jnp
from jax import lax
from jax.experimental import pallas as pl
from jax.experimental.pallas import tpu as pltpu
from jax.sharding import PartitionSpec as P

HDIM = 64
STATE = 128
QHEADS = 32
KVHEADS = 8
ADIM = 128
EPSILON = 1e-05
BARRED = -2e30
HIGHEST = lax.Precision.HIGHEST
F32 = jnp.float32
BF16 = jnp.bfloat16
CHUNK = 256
EDGE = 16
KERNEL_FLOPS = 2 * 10**9
VMEM_LIMIT = 40 * 1024 * 1024
VMEM_ALL = 62 * 1024 * 1024


def silu(value):
    return value * (0.5 * jnp.tanh(0.5 * value) + 0.5)


def softplus(value):
    return jnp.maximum(value, 0.0) + jnp.log(1.0 + jnp.exp(-jnp.abs(value)))


def doc_start(positions, lens_ref):
    begin = jnp.int32(0)
    found = positions * 0
    for doc in range(lens_ref.shape[0]):
        found = jnp.where(positions >= begin, begin, found)
        begin = begin + lens_ref[doc]
    return found


def halves(value):
    high = value.astype(BF16)
    return high, (value - high.astype(F32)).astype(BF16)


def widen(per_head, first, width):
    heads = per_head.shape[1]
    both = jnp.concatenate(halves(per_head), axis=1)
    head = lax.broadcasted_iota(jnp.int32, (2 * heads, width), 0)
    head = jnp.where(head >= heads, head - heads, head)
    channel = lax.broadcasted_iota(jnp.int32, (2 * heads, width), 1) + first
    spread = (channel // HDIM == head).astype(F32).astype(BF16)
    return jnp.dot(both, spread, preferred_element_type=F32)


def rates(dt_ref, dt_bias_ref, a_log_ref):
    heads = dt_ref.shape[0]
    step = softplus(dt_ref[...].T + dt_bias_ref[...].reshape(1, -1)[:, :heads])
    rate = -step * jnp.exp(a_log_ref[...].reshape(1, -1)[:, :heads])
    rows = step.shape[0]
    row = lax.broadcasted_iota(jnp.int32, (rows, rows), 0)
    column = lax.broadcasted_iota(jnp.int32, (rows, rows), 1)
    lower = (row >= column).astype(F32).astype(BF16)
    high = rate.astype(BF16)
    middle, low = halves(rate - high.astype(F32))
    parts = jnp.concatenate([high, middle, low], axis=0)
    lowers = jnp.concatenate([lower, lower, lower], axis=1)
    return step, jnp.dot(lowers, parts, preferred_element_type=F32)


def insides(first, shape, taps, lens_ref):
    positions = first + lax.broadcasted_iota(jnp.int32, shape, 0)
    depth = positions - doc_start(positions, lens_ref)
    return [depth >= lag for lag in range(taps)]


def conv(pad, rows, weight, bias, inside):
    taps = weight.shape[0]
    total = pad[8 : 8 + rows] * weight[taps - 1 : taps] + bias
    for lag in range(1, taps):
        term = pad[8 - lag : 8 - lag + rows] * weight[taps - 1 - lag : taps - lag]
        total = total + jnp.where(inside[lag], term, 0.0)
    return silu(total)


def tail_lines(message, rows):
    block = message[rows:].astype(F32)
    return jnp.concatenate([block[at : at + 4] for at in range(0, block.shape[0], 4)], axis=1)


def reach(device, rows, lens_ref):
    return device - doc_start((device + 1) * rows - 1, lens_ref) // rows


def kept_weight(here, step, running, taps, lens_ref):
    rows = step.shape[0]
    last_begin = doc_start((here + 1) * rows - 1, lens_ref)
    row = lax.broadcasted_iota(jnp.int32, step.shape, 0)
    weight = step * jnp.exp(running[rows - 1 : rows] - running)
    kept = (here * rows + row >= last_begin) & ((row >= taps - 1) | (last_begin // rows >= here))
    return jnp.where(kept, weight, 0.0)


def conv_rows(pad, raw, weight, bias, inside):
    pad[0:8] = jnp.zeros((8, raw.shape[1]), F32)
    pad[8:] = raw.astype(F32)
    return conv(pad, raw.shape[0], weight, bias.reshape(1, -1), inside)


def first_state_kernel(*refs):
    hbm_refs, out_hbm_ref = refs[:10], refs[10]
    vmem_refs = refs[11:21]
    x_edge_ref, bc_edge_ref, out_ref, b_pad_ref, pad_ref, in_sems, out_sems = refs[21:]
    x_ref, b_ref, dt_ref, wx_ref, bx_ref, wbc_ref, bbc_ref, dt_bias_ref, a_log_ref, lens_ref = vmem_refs
    rows, width = x_ref.shape
    taps = wx_ref.shape[0]

    def corner(ref, shape):
        return ref.at[tuple(pl.ds(0, extent) for extent in shape)]

    order = (9, 2, 7, 8, 1, 5, 6, 0, 3, 4)
    copies = {}
    for at in order:
        source = corner(hbm_refs[at], vmem_refs[at].shape)
        copies[at] = pltpu.make_async_copy(source, vmem_refs[at], in_sems.at[at])
        copies[at].start()
    edge_copies = []
    for at, (source, target) in enumerate(((hbm_refs[0], x_edge_ref), (hbm_refs[1], bc_edge_ref))):
        edge_copies.append(
            pltpu.make_async_copy(source.at[pl.ds(rows - EDGE, EDGE)], target, in_sems.at[10 + at])
        )
        edge_copies[-1].start()

    here = lax.axis_index("seq")
    for at in (9, 2, 7, 8):
        copies[at].wait()
    inside = insides(here * rows, (rows, CHUNK), taps, lens_ref)
    step, running = rates(dt_ref, dt_bias_ref, a_log_ref)
    weight = kept_weight(here, step, running, taps, lens_ref)
    narrow = [mask[:, :STATE] for mask in inside]
    for at in (1, 5, 6):
        copies[at].wait()
    inputs = conv_rows(b_pad_ref, b_ref[...], wbc_ref[...], bbc_ref[...], narrow)
    turned = inputs.T.astype(BF16)
    for at in (0, 3, 4):
        copies[at].wait()
    slots = pad_ref.shape[0]
    outs = []

    def send(at, view):
        copy = pltpu.make_async_copy(out_ref.at[view], out_hbm_ref.at[view], out_sems.at[at])
        copy.start()
        outs.append(copy)

    for at, start in enumerate(range(0, width, CHUNK)):
        columns = slice(start, start + CHUNK)
        pad = pad_ref.at[(at + 1) % slots]
        xc = conv_rows(pad, x_ref[:, columns], wx_ref[:, columns], bx_ref[:, columns], inside)
        weighted = (xc * widen(weight, start, CHUNK)).astype(BF16)
        out_ref[:STATE, columns] = jnp.dot(turned, weighted, preferred_element_type=F32).astype(BF16)
        if at % 2:
            send(at // 2, (pl.ds(0, STATE), pl.ds(start - CHUNK, 2 * CHUNK)))
    for copy in edge_copies:
        copy.wait()
    edges = jnp.concatenate([x_edge_ref[...].astype(F32), bc_edge_ref[...].astype(F32)], axis=1)[EDGE - 4 :]
    spare = -edges.shape[1] % width
    if spare:
        edges = jnp.concatenate([edges, jnp.zeros((4, spare), F32)], axis=1)
    pieces = [edges[:, at : at + width] for at in range(0, edges.shape[1], width)]
    while len(pieces) % (EDGE // 4):
        pieces.append(jnp.zeros_like(pieces[0]))
    out_ref[STATE:] = jnp.concatenate(pieces, axis=0).astype(BF16)
    send(width // (2 * CHUNK), (pl.ds(STATE, out_ref.shape[0] - STATE), pl.ds(0, width)))
    for copy in outs:
        copy.wait()


def prepare_kernel(hops, groups, *refs):
    x_ref, bc_ref, dt_ref, wx_ref, bx_ref, wbc_ref, bbc_ref, dt_bias_ref, a_log_ref, skip_ref, lens_ref = refs[:11]
    z_ref = refs[11]
    xc_ref, bcc_ref, partial_ref, weight_ref, through_ref, inside_ref, flag_ref = refs[12:19]
    wide_skip_ref, begin_ref, step_ref, running_ref, out_ref, gate_ref, decay_ref = refs[19:26]
    state_refs = refs[26:-2]
    top_ref, pad_ref = refs[-2:]
    rows, width = x_ref.shape
    per_group = width // groups
    taps = wx_ref.shape[0]
    slots = pad_ref.shape[0]
    here = lax.axis_index("seq")
    first = here * rows
    inside = insides(first, (rows, CHUNK), taps, lens_ref)
    step, running = rates(dt_ref, dt_bias_ref, a_log_ref)
    heads = step.shape[1]
    group_heads = heads // groups
    kept = kept_weight(here, step, running, taps, lens_ref)
    for group in range(groups):
        base = slice(group * 2 * STATE, (group + 1) * 2 * STATE)
        pair = conv_rows(pad_ref.at[0], bc_ref[:, base], wbc_ref[:, base], bbc_ref[base], inside)
        bcc_ref[:, base] = pair.astype(BF16)
        turned = pair[:, :STATE].T.astype(BF16)
        part_weight = kept[:, group * group_heads : (group + 1) * group_heads]
        for chunk in range(0, per_group, CHUNK):
            columns = slice(group * per_group + chunk, group * per_group + chunk + CHUNK)
            pad = pad_ref.at[(chunk // CHUNK + 1) % slots]
            xc = conv_rows(pad, x_ref[:, columns], wx_ref[:, columns], bx_ref[columns], inside)
            xc_ref[:, columns] = xc.astype(BF16)
            if group:
                weighted = (xc * widen(part_weight, chunk, CHUNK)).astype(BF16)
                state_refs[group - 1][:, chunk : chunk + CHUNK] = jnp.dot(
                    turned, weighted, preferred_element_type=F32
                ).astype(BF16)

    own = reach(here, rows, lens_ref) == 0
    inside = [mask[:8] for mask in inside]
    for lag in range(1, taps):
        inside_ref[lag - 1] = inside[lag].astype(F32)
    flag_ref[0] = jnp.broadcast_to(own.astype(F32), (8, CHUNK))
    before = reach(here - 1, rows, lens_ref)
    for hop in range(1, hops):
        flag_ref[hop] = jnp.broadcast_to((before == hop).astype(F32), (8, CHUNK))
    begin = doc_start(first + lax.broadcasted_iota(jnp.int32, begin_ref.shape, 0), lens_ref)
    begin_ref[...] = begin
    entry = jnp.where(begin[:, :heads] < first, jnp.exp(running), 0.0)
    step_ref[...] = step
    running_ref[...] = running
    row = lax.broadcasted_iota(jnp.int32, (8, heads), 0)
    total = running[rows - 1 : rows]
    weight = step[:8] * jnp.exp(total - running[:8])
    weight = jnp.where((row < taps - 1) & jnp.logical_not(own), weight, 0.0)
    through = jnp.where(own, 0.0, jnp.broadcast_to(jnp.exp(total), (8, heads)))
    skip = jnp.broadcast_to(skip_ref[...].reshape(1, -1), (8, heads))
    every = jnp.concatenate([weight, through, skip], axis=0)
    for start in range(0, width, CHUNK):
        wide = widen(every, start, CHUNK)
        weight_ref[:, start : start + CHUNK] = wide[:8]
        through_ref[:, start : start + CHUNK] = wide[8:16]
        wide_skip_ref[:, start : start + CHUNK] = wide[16:]
    top_ref[0:8] = jnp.zeros((8, top_ref.shape[1]), F32)
    top_ref[8:, :width] = x_ref[:EDGE].astype(F32)[:8]
    top_ref[8:, width:] = bc_ref[:EDGE].astype(F32)[:8]

    def some(columns, base, w_ref, b_ref):
        here_columns = slice(base + columns.start, base + columns.stop)
        total = top_ref[8:, here_columns] * w_ref[taps - 1 : taps, columns] + b_ref[columns].reshape(1, -1)
        for lag in range(1, taps):
            term = top_ref[8 - lag : 16 - lag, here_columns] * w_ref[taps - 1 - lag : taps - lag, columns]
            total = total + jnp.where(inside[lag], term, 0.0)
        partial_ref[:, here_columns] = total

    for start in range(0, width, CHUNK):
        some(slice(start, start + CHUNK), 0, wx_ref, bx_ref)
    for start in range(0, bc_ref.shape[1], CHUNK):
        some(slice(start, start + CHUNK), width, wbc_ref, bbc_ref)

    row = lax.broadcasted_iota(jnp.int32, (rows, rows), 0)
    lane = lax.broadcasted_iota(jnp.int32, (rows, rows), 1)
    linked = (row >= lane) & (first + lane >= begin) & (lane >= 8)
    turned_running = running.T
    turned_step = step.T
    pair_width = 2 * HDIM
    channel = lax.broadcasted_iota(jnp.int32, (rows, pair_width), 1)
    below = lax.broadcasted_iota(jnp.int32, (rows, CHUNK), 0) >= 8
    for group in range(groups):
        base = group * 2 * STATE
        meet = lax.dot_general(
            bcc_ref[:, base + STATE : base + 2 * STATE],
            bcc_ref[:, base : base + STATE],
            (((1,), (1,)), ((), ())),
            preferred_element_type=F32,
        )
        meet = jnp.where(linked, meet, 0.0)
        group_entry = entry[:, group * group_heads : (group + 1) * group_heads]
        for chunk in range(0, per_group, CHUNK):
            at = group * per_group + chunk
            columns = slice(at, at + CHUNK)
            gate = silu(z_ref[:, columns].astype(F32))
            gate_ref[:, columns] = gate
            decay_ref[:, columns] = widen(group_entry, chunk, CHUNK) * gate
            xc_all = xc_ref[:, columns]
            skipped = jnp.where(below, xc_all.astype(F32) * wide_skip_ref[0:1, columns], 0.0)
            for start in range(0, CHUNK, pair_width):
                parts = []
                for head in ((at + start) // HDIM, (at + start) // HDIM + 1):
                    spread = running[:, head : head + 1] - turned_running[head : head + 1]
                    decay = jnp.exp(jnp.minimum(spread, 0.0))
                    parts.append((decay * (meet * turned_step[head : head + 1])).astype(BF16))
                mix = jnp.concatenate(parts, axis=1)
                here_columns = slice(start, start + pair_width)
                xc = xc_all[:, here_columns]
                zero = jnp.zeros_like(xc)
                stacked = jnp.concatenate(
                    [jnp.where(channel < HDIM, xc, zero), jnp.where(channel < HDIM, zero, xc)], axis=0
                )
                value = jnp.dot(mix, stacked, preferred_element_type=F32) + skipped[:, here_columns]
                out_ref[:, at + start : at + start + pair_width] = value * gate[:, here_columns]


def first_rows(lines, partial_ref, inside_ref, w_ref, pad_ref, slot, at, start):
    taps = w_ref.shape[0]
    columns = slice(start, start + CHUNK)
    pad = pad_ref.at[slot]
    pad[4:8] = lines[:, at + start : at + start + CHUNK]
    pad[8:] = jnp.zeros((8, CHUNK), F32)
    total = partial_ref[:, at + start : at + start + CHUNK]
    for lag in range(1, taps):
        term = pad[8 - lag : 16 - lag] * w_ref[taps - 1 - lag : taps - lag, columns]
        total = total + term * inside_ref[lag - 1]
    return silu(total).astype(BF16)


def relay_first_kernel(fresh, *refs):
    message_ref, state_ref, partial_ref, weight_ref, through_ref, inside_ref, flag_ref, wx_ref, wbc_ref = refs[:9]
    other_ref = refs[9] if fresh else state_ref
    out_ref, pad_ref = refs[-2:]
    width = out_ref.shape[1]
    slots = pad_ref.shape[0]
    lines = tail_lines(message_ref, STATE)
    top = functools.partial(first_rows, lines, partial_ref, inside_ref)
    inputs = top(wbc_ref, pad_ref, 0, wx_ref.shape[1], 0)[:, :STATE]
    turned = inputs.astype(F32).T.astype(BF16)
    own = flag_ref[0, 0:1] > 0.5
    for start in range(0, width, CHUNK):
        columns = slice(start, start + CHUNK)
        xc = top(wx_ref, pad_ref, (start // CHUNK + 1) % slots, 0, start)
        weighted = (xc.astype(F32) * weight_ref[:, columns]).astype(BF16)
        full = state_ref[:STATE, columns].astype(F32) + jnp.dot(
            turned, weighted, preferred_element_type=F32
        )
        full = full + through_ref[0:1, columns] * message_ref[:STATE, columns].astype(F32)
        out_ref[:, columns] = jnp.where(own, other_ref[:STATE, columns].astype(F32), full).astype(BF16)


def relay_kernel(part, fresh, *refs):
    got_ref, state_ref, through_ref, flag_ref = refs[:4]
    out_ref = refs[-1]
    width = out_ref.shape[1]
    own = flag_ref[0, 0:1] > 0.5
    for start in range(0, width, CHUNK):
        columns = slice(start, start + CHUNK)
        through = through_ref[0:1, part * width + start : part * width + start + CHUNK]
        full = state_ref[:, columns].astype(F32) + through * got_ref[:STATE, columns].astype(F32)
        if fresh:
            full = jnp.where(own, refs[4][:STATE, columns].astype(F32), full)
        out_ref[:, columns] = full.astype(BF16)


def first_rows_kernel(groups, *refs):
    (
        message_ref, partial_ref, weight_ref, inside_ref, wx_ref, wbc_ref, step_ref, running_ref,
        wide_skip_ref, begin_ref, bcc_ref, main_ref, gate_ref,
    ) = refs[:13]
    state_refs = refs[13 : 13 + groups]
    out_ref, c_ref = refs[13 + groups : 15 + groups]
    full_refs = refs[15 + groups : 15 + 2 * groups]
    pad_ref = refs[-1]
    rows, width = main_ref.shape
    per_group = width // groups
    heads = per_group // HDIM
    lanes = 8 * heads
    first = lax.axis_index("seq") * rows
    lines = tail_lines(message_ref, STATE)
    slots = pad_ref.shape[0]
    top = functools.partial(first_rows, lines, partial_ref, inside_ref)
    lane = lax.broadcasted_iota(jnp.int32, (rows, lanes), 1)
    line = lane & 7
    row = lax.broadcasted_iota(jnp.int32, (rows, lanes), 0)
    begin = jnp.concatenate([begin_ref[...]] * -(-lanes // rows), axis=1)[:, :lanes]
    linked = (row >= line) & (first + line >= begin)
    head = lax.broadcasted_iota(jnp.int32, (3 * heads, lanes), 0)
    for _ in range(2):
        head = jnp.where(head >= heads, head - heads, head)
    spread = (lax.broadcasted_iota(jnp.int32, (3 * heads, lanes), 1) >> 3 == head).astype(F32).astype(BF16)
    own_line = lax.broadcasted_iota(jnp.int32, (8, lanes), 0) == line[:8]

    def to_lanes(value):
        high = value.astype(BF16)
        middle, low = halves(value - high.astype(F32))
        return jnp.dot(jnp.concatenate([high, middle, low], axis=1), spread, preferred_element_type=F32)

    def by_line(value):
        return jnp.sum(jnp.where(own_line, value, 0.0), axis=0, keepdims=True)

    channel = lax.broadcasted_iota(jnp.int32, (8, CHUNK), 1)
    for group in range(groups):
        base = group * 2 * STATE
        these = slice(group * heads, (group + 1) * heads)
        new = top(wbc_ref, pad_ref, group % slots, width, base).astype(F32)
        old = bcc_ref[:, base + STATE : base + 2 * STATE]
        outputs = jnp.concatenate([new[:, STATE:], old[:EDGE].astype(F32)[8:]], axis=0).astype(BF16)
        outputs = jnp.concatenate([outputs, old[EDGE:]], axis=0)
        c_ref[:, group * STATE : (group + 1) * STATE] = outputs
        inputs = jnp.concatenate([new[:, :STATE]] * heads, axis=0).astype(BF16)
        meet = lax.dot_general(
            outputs, inputs, (((1,), (1,)), ((), ())), preferred_element_type=F32
        )
        running = to_lanes(running_ref[:, these])
        decay = jnp.exp(jnp.minimum(running - by_line(running[:8]), 0.0))
        mix = decay * (meet * by_line(to_lanes(step_ref[:8, these])))
        mix = jnp.where(linked, mix, 0.0).astype(BF16)
        turned = inputs[:EDGE].astype(F32).T[:, :8].astype(BF16)
        for chunk in range(0, per_group, CHUNK):
            at = group * per_group + chunk
            columns = slice(at, at + CHUNK)
            xc = top(wx_ref, pad_ref, (chunk // CHUNK + 1) % slots, 0, at).astype(F32)
            full = state_refs[group][:STATE, chunk : chunk + CHUNK].astype(F32) + jnp.dot(
                turned, (xc * weight_ref[:, columns]).astype(BF16), preferred_element_type=F32
            )
            full_refs[group][:, chunk : chunk + CHUNK] = full.astype(BF16)
            blocks = []
            for at_head in range(heads):
                low = at_head * HDIM - chunk
                if 0 <= low < CHUNK:
                    blocks.append(jnp.where((channel >= low) & (channel < low + HDIM), xc, 0.0))
                else:
                    blocks.append(jnp.zeros_like(xc))
            spread_xc = jnp.concatenate(blocks, axis=0).astype(BF16)
            gate = gate_ref[:, columns]
            value = main_ref[:, columns] + gate * jnp.dot(mix, spread_xc, preferred_element_type=F32)
            out_ref[:, columns] = value
            out_ref[0:8, columns] = value[:8] + gate[:8] * (xc * wide_skip_ref[:, columns])


def attend(q_ref, kv_refs, begin_ref, blocks, share, head):
    rows = q_ref.shape[0]
    kv_heads = kv_refs[0].shape[1] // (2 * ADIM)
    count = rows * blocks.count
    here = lax.axis_index("seq")
    row = here * rows + lax.broadcasted_iota(jnp.int32, (rows, count), 0)
    lane = (here - blocks.farthest) * rows + lax.broadcasted_iota(jnp.int32, (rows, count), 1)
    begin = jnp.concatenate([begin_ref[...]] * blocks.count, axis=1)
    allowed = jnp.concatenate([(lane <= row) & (lane >= begin)] * share, axis=0)
    low = head * ADIM
    keys = jnp.concatenate([ref[:, low : low + ADIM] for ref in kv_refs], axis=0)
    low = (kv_heads + head) * ADIM
    values = jnp.concatenate([ref[:, low : low + ADIM] for ref in kv_refs], axis=0)
    values = jnp.concatenate([values, jnp.ones((count, ADIM), BF16)], axis=1)
    lows = [(head * share + part) * ADIM for part in range(share)]
    asking = jnp.concatenate([q_ref[:, low : low + ADIM] for low in lows], axis=0)
    scores = lax.dot_general(asking, keys, (((1,), (1,)), ((), ())), preferred_element_type=F32)
    return jnp.where(allowed, scores * ADIM ** (-0.5), BARRED), values


class Blocks(NamedTuple):
    farthest: int
    count: int


def fold(q_ref, kv_refs, begin_ref, blocks, share, head, carry):
    lows = [(head * share + part) * ADIM for part in range(share)]
    scores, values = attend(q_ref, kv_refs, begin_ref, blocks, share, head)
    peak = jnp.max(scores, axis=1, keepdims=True)
    peak = jnp.broadcast_to(peak, (peak.shape[0], ADIM))
    if carry is not None:
        sums, totals, before = (
            jnp.concatenate([ref[:, low : low + ADIM] for low in lows], axis=0) for ref in carry
        )
        peak = jnp.maximum(peak, before)
    expo = jnp.exp(scores - jnp.concatenate([peak] * (scores.shape[1] // ADIM), axis=1))
    summed = jnp.dot(expo.astype(BF16), values, preferred_element_type=F32)
    if carry is None:
        return lows, summed[:, :ADIM], summed[:, ADIM:], peak
    factor = jnp.exp(before - peak)
    return lows, sums * factor + summed[:, :ADIM], totals * factor + summed[:, ADIM:], peak


def own_kernel(q_ref, keys_ref, values_ref, begin_ref, *outs):
    kv_ref = outs[3]
    kv_width = keys_ref.shape[1]
    kv_ref[:, :kv_width] = keys_ref[...]
    kv_ref[:, kv_width:] = values_ref[...]
    rows = q_ref.shape[0]
    share = QHEADS // KVHEADS
    for head in range(kv_width // ADIM):
        lows, *results = fold(q_ref, (kv_ref,), begin_ref, Blocks(0, 1), share, head, None)
        for ref, result in zip(outs, results):
            for part, low in enumerate(lows):
                ref[:, low : low + ADIM] = result[part * rows : (part + 1) * rows]


def near_kernel(q_ref, before_ref, begin_ref, *refs):
    carry, outs = refs[:3], refs[4:]
    outs[3][...] = before_ref[...]
    rows = q_ref.shape[0]
    share = QHEADS // KVHEADS
    for head in range(before_ref.shape[1] // (2 * ADIM)):
        lows, *results = fold(q_ref, (before_ref,), begin_ref, Blocks(1, 1), share, head, carry)
        for ref, result in zip(outs, results):
            for part, low in enumerate(lows):
                ref[:, low : low + ADIM] = result[part * rows : (part + 1) * rows]


def far_kernel(hops, *refs):
    q_ref, begin_ref = refs[:2]
    kv_refs = refs[5 : 4 + hops]
    out_hbm_ref, out_ref, sems = refs[4 + hops :]
    rows = q_ref.shape[0]
    share = QHEADS // KVHEADS
    copies = []
    for head in range(kv_refs[0].shape[1] // (2 * ADIM)):
        blocks = Blocks(hops, hops - 1)
        lows, sums, totals, _ = fold(q_ref, kv_refs, begin_ref, blocks, share, head, refs[2:5])
        result = (sums / totals).astype(BF16)
        for part, low in enumerate(lows):
            out_ref[:, low : low + ADIM] = result[part * rows : (part + 1) * rows]
        columns = pl.ds(head * share * ADIM, share * ADIM)
        copies.append(
            pltpu.make_async_copy(out_ref.at[:, columns], out_hbm_ref.at[:, columns], sems.at[head])
        )
        copies[-1].start()
    for copy in copies:
        copy.wait()


def norm_kernel(part, hops, turn, given, *refs):
    local_ref, decay_ref, c_ref, gain_ref, flag_ref = refs[:5]
    got_refs = refs[5 : 5 + hops]
    out_hbm_ref, *token_refs = refs[5 + hops + given : -3]
    gated_ref, out_ref, sems = refs[-3:]
    for ref in token_refs:
        ref[...] = jnp.zeros_like(ref)

    def work():
        rows, width = gated_ref.shape
        outputs = c_ref[:, part * STATE : (part + 1) * STATE]
        squares = jnp.zeros((rows, 128), F32)
        for start in range(0, width, CHUNK):
            columns = slice(start, start + CHUNK)
            placed = slice(part * width + start, part * width + start + CHUNK)
            state = got_refs[0][:STATE, columns]
            for hop in range(1, hops):
                there = flag_ref[hop, 0:1] > 0.5
                state = jnp.where(there, got_refs[hop][:STATE, columns].astype(F32), state.astype(F32))
            carried = jnp.dot(outputs, state.astype(BF16), preferred_element_type=F32)
            gated = local_ref[:, placed] + carried * decay_ref[:, placed]
            gated_ref[:, columns] = gated
            for lane in range(0, CHUNK, 128):
                squares = squares + gated[:, lane : lane + 128] * gated[:, lane : lane + 128]
        squares = jnp.sum(squares, axis=1, keepdims=True)
        multiplier = lax.rsqrt(squares * (1.0 / width) + EPSILON)
        copies = []
        for start in range(0, width, CHUNK):
            columns = slice(start, start + CHUNK)
            gain = gain_ref[part * width + start : part * width + start + CHUNK]
            out_ref[:, columns] = (gated_ref[:, columns] * multiplier * gain.reshape(1, -1)).astype(BF16)
            copies.append(
                pltpu.make_async_copy(
                    out_ref.at[:, pl.ds(start, CHUNK)],
                    out_hbm_ref.at[:, pl.ds(part * width + start, CHUNK)],
                    sems.at[start // CHUNK],
                )
            )
            copies[-1].start()
        for copy in copies:
            copy.wait()

    odd = lax.axis_index("dp") % 2 == 1
    if turn == 0:
        pl.when(odd)(work)
    elif turn == 1:
        pl.when(jnp.logical_not(odd) | (jnp.max(flag_ref[1:]) > 0.5))(work)
    else:
        work()


WHOLE = pl.BlockSpec(memory_space=pltpu.VMEM)
SCALARS = pl.BlockSpec(memory_space=pltpu.SMEM)
UNTOUCHED = pl.BlockSpec(memory_space=pl.ANY)


def tile(rows, columns, row, column):
    return pl.BlockSpec((rows, columns), lambda step: (row, column))


def call(kernel, name, outs, operands, specs, out_specs=None, scratch=(), flops=KERNEL_FLOPS, aliases={}, limit=VMEM_LIMIT):
    moved = sum(math.prod(a.shape) * a.dtype.itemsize for a in (*operands, *outs))
    return pl.pallas_call(
        kernel,
        name=name,
        grid=(1,),
        out_shape=outs,
        in_specs=specs,
        out_specs=[WHOLE] * len(outs) if out_specs is None else out_specs,
        scratch_shapes=list(scratch),
        input_output_aliases=aliases,
        compiler_params=pltpu.CompilerParams(vmem_limit_bytes=limit),
        cost_estimate=pl.CostEstimate(flops=flops, bytes_accessed=moved, transcendentals=0),
    )(*operands)


def onward(value, first=0):
    count = lax.axis_size("seq")
    return lax.ppermute(value, "seq", [(source, source + 1) for source in range(first, count - 1)])


def shards(
    x_raw,
    bc_raw,
    z_gate,
    dt_raw,
    conv_x_weight,
    conv_x_bias,
    conv_bc_weight,
    conv_bc_bias,
    dt_bias,
    a_log,
    skip_d,
    norm_gain,
    queries,
    keys,
    values,
    doc_lens,
):
    rows, width = x_raw.shape
    bc_width = bc_raw.shape[1]
    heads = dt_raw.shape[1]
    groups = bc_width // (2 * STATE)
    per_group = width // groups
    count = lax.axis_size("seq")
    longest = rows * count // 2
    hops = min(count - 1, -(-(longest - 1) // rows))
    assert hops * rows >= longest and (hops == 2 or hops > 2 and groups == 1)
    shape = jax.ShapeDtypeStruct
    dt = dt_raw.T
    params = [dt, conv_x_weight, conv_x_bias, conv_bc_weight, conv_bc_bias, dt_bias, a_log]
    pieces = -(-(width + bc_width) // per_group)
    tail_rows = EDGE * -(-4 * pieces // EDGE)

    (message,) = call(
        first_state_kernel,
        "first_state",
        [shape((STATE + tail_rows, per_group), BF16)],
        [x_raw, bc_raw, *(a if a.ndim > 1 else a[None] for a in params), doc_lens],
        [UNTOUCHED] * 10,
        out_specs=[UNTOUCHED],
        scratch=[
            pltpu.VMEM((rows, per_group), BF16),
            pltpu.VMEM((rows, STATE), BF16),
            pltpu.VMEM((per_group // HDIM, rows), F32),
            pltpu.VMEM((conv_x_weight.shape[0], per_group), F32),
            pltpu.VMEM((1, per_group), F32),
            pltpu.VMEM((conv_x_weight.shape[0], STATE), F32),
            pltpu.VMEM((1, STATE), F32),
            pltpu.VMEM((1, heads), F32),
            pltpu.VMEM((1, heads), F32),
            pltpu.SMEM(doc_lens.shape, jnp.int32),
            pltpu.VMEM((EDGE, width), BF16),
            pltpu.VMEM((EDGE, bc_width), BF16),
            pltpu.VMEM((STATE + tail_rows, per_group), BF16),
            pltpu.VMEM((rows + 8, STATE), F32),
            pltpu.VMEM((4, rows + 8, CHUNK), F32),
            pltpu.SemaphoreType.DMA((12,)),
            pltpu.SemaphoreType.DMA((per_group // (2 * CHUNK) + 1,)),
        ],
        limit=VMEM_ALL,
    )
    slots = [onward(message)]
    prepared = call(
        functools.partial(prepare_kernel, hops, groups),
        "prepare",
        [
            shape((rows, width), BF16),
            shape((rows, bc_width), BF16),
            shape((8, width + bc_width), F32),
            shape((8, width), F32),
            shape((8, width), F32),
            shape((conv_x_weight.shape[0] - 1, 8, CHUNK), F32),
            shape((hops, 8, CHUNK), F32),
            shape((8, width), F32),
            shape((rows, rows), jnp.int32),
            shape((rows, heads), F32),
            shape((rows, heads), F32),
            shape((rows, width), F32),
            shape((rows, width), F32),
            shape((rows, width), F32),
            *(shape((STATE, per_group), BF16) for _ in range(groups - 1)),
        ],
        [x_raw, bc_raw, *params, skip_d, doc_lens, z_gate],
        [WHOLE] * 10 + [SCALARS] + [WHOLE],
        scratch=[
            pltpu.VMEM((16, width + bc_width), F32),
            pltpu.VMEM((4, rows + 8, CHUNK), F32),
        ],
    )
    _, bcc, partial, weight, through, inside, flags, wide_skip, begin, *prepared = prepared
    step, running, main, gate, decay, *states = prepared
    states = [message, *states]
    carried = [shape(queries.shape, F32)] * 3 + [shape((rows, 2 * keys.shape[1]), BF16)]
    *carry, kv = call(own_kernel, "attend_own", carried, [queries, keys, values, begin], [WHOLE] * 4)
    kvs = [kv, onward(kv)]
    fulls = None
    for slot in range(2, hops + groups):
        part = min(slot - 1, groups) - 1
        fresh = slot <= groups
        if slot == 2:
            kernel = functools.partial(relay_first_kernel, fresh)
            operands = [slots[0], states[0], partial, weight, through, inside, flags, conv_x_weight, conv_bc_weight]
            scratch = [pltpu.VMEM((4, 16, CHUNK), F32)]
        else:
            kernel = functools.partial(relay_kernel, part, fresh)
            operands = [slots[-1], fulls[part], through, flags]
            scratch = []
        if fresh:
            operands.append(states[slot - 1])
        (passed,) = call(
            kernel,
            f"relay_slot{slot}",
            [shape((STATE, per_group), BF16)],
            operands,
            [WHOLE] * len(operands),
            scratch=scratch,
        )
        slots.append(onward(passed, max(0, slot - groups)))
        if fulls is None:
            gated, c_out, *fulls = call(
                functools.partial(first_rows_kernel, groups),
                "first_rows",
                [
                    shape((rows, width), F32),
                    shape((rows, groups * STATE), BF16),
                    *(shape((STATE, per_group), BF16) for _ in range(groups)),
                ],
                [
                    slots[0], partial, weight, inside, conv_x_weight, conv_bc_weight, step, running,
                    wide_skip, begin, bcc, main, gate, *states,
                ],
                [WHOLE] * (13 + groups),
                scratch=[pltpu.VMEM((4, 16, CHUNK), F32)],
            )
    def norm(part, turn, got, out=None, token=False):
        operands = [gated, decay, c_out, norm_gain, flags, *got]
        specs = [WHOLE] * len(operands)
        outs = [shape((rows, width), BF16)] + [shape((8, 128), F32)] * token
        aliases = {}
        if out is not None:
            aliases = {len(operands): 0}
            operands.append(out)
            specs.append(UNTOUCHED)
        return call(
            functools.partial(norm_kernel, part, len(got), turn, out is not None),
            f"norm_part{part}_{turn}",
            outs,
            operands,
            specs,
            out_specs=[UNTOUCHED] + [WHOLE] * token,
            scratch=[
                pltpu.VMEM((rows, per_group), F32),
                pltpu.VMEM((rows, per_group), BF16),
                pltpu.SemaphoreType.DMA((per_group // CHUNK,)),
            ],
            aliases=aliases,
        )

    mamba_out, token = None, c_out
    for part in range(groups - 1):
        mamba_out, token = norm(part, 0, slots[part : part + 1], mamba_out, True)
    *carry, kv_on = call(
        near_kernel,
        "attend_near",
        carried,
        [queries, kvs[1], begin, *carry, token],
        [WHOLE] * 6 + [UNTOUCHED],
    )
    for hop in range(1, hops):
        kvs.append(onward(kv_on if hop == 1 else kvs[-1], hop))
    (attn_out,) = call(
        functools.partial(far_kernel, hops),
        "attend_far",
        [shape(queries.shape, BF16)],
        [queries, begin, *carry, *reversed(kvs[2:])],
        [WHOLE] * (4 + hops),
        out_specs=[UNTOUCHED],
        scratch=[
            pltpu.VMEM(queries.shape, BF16),
            pltpu.SemaphoreType.DMA((keys.shape[1] // ADIM,)),
        ],
    )
    for part in range(groups):
        last = part == groups - 1
        (mamba_out,) = norm(part, 1 + last, slots[part : part + hops], mamba_out)
    return (mamba_out, attn_out)


def solution(mesh):
    split = P(("groups", "seq"), "dp")
    placed = (
        split,
        split,
        split,
        split,
        P(None, "dp"),
        P("dp"),
        P(None, "dp"),
        P("dp"),
        P("dp"),
        P("dp"),
        P("dp"),
        P("dp"),
        split,
        split,
        split,
        P("groups"),
    )
    return jax.shard_map(
        shards,
        mesh=mesh,
        in_specs=placed,
        out_specs=(split, split),
        check_vma=False,
    )
```

```python
import functools
import math
from typing import NamedTuple

import jax
import jax.numpy as jnp
from jax import lax
from jax.experimental import pallas as pl
from jax.experimental.pallas import tpu as pltpu
from jax.sharding import PartitionSpec as P

HDIM = 64
STATE = 128
QHEADS = 32
KVHEADS = 8
ADIM = 128
EPSILON = 1e-05
BARRED = -2e30
HIGHEST = lax.Precision.HIGHEST
F32 = jnp.float32
BF16 = jnp.bfloat16
CHUNK = 256
EDGE = 16
KERNEL_FLOPS = 2 * 10**9
VMEM_LIMIT = 40 * 1024 * 1024
VMEM_ALL = 62 * 1024 * 1024


def silu(value):
    return value * (0.5 * jnp.tanh(0.5 * value) + 0.5)


def softplus(value):
    return jnp.maximum(value, 0.0) + jnp.log(1.0 + jnp.exp(-jnp.abs(value)))


def doc_start(positions, lens_ref):
    begin = jnp.int32(0)
    found = positions * 0
    for doc in range(lens_ref.shape[0]):
        found = jnp.where(positions >= begin, begin, found)
        begin = begin + lens_ref[doc]
    return found


def halves(value):
    high = value.astype(BF16)
    return high, (value - high.astype(F32)).astype(BF16)


def widen(per_head, first, width):
    heads = per_head.shape[1]
    both = jnp.concatenate(halves(per_head), axis=1)
    head = lax.broadcasted_iota(jnp.int32, (2 * heads, width), 0)
    head = jnp.where(head >= heads, head - heads, head)
    channel = lax.broadcasted_iota(jnp.int32, (2 * heads, width), 1) + first
    spread = (channel // HDIM == head).astype(F32).astype(BF16)
    return jnp.dot(both, spread, preferred_element_type=F32)


def rates(dt_ref, dt_bias_ref, a_log_ref):
    heads = dt_ref.shape[0]
    step = softplus(dt_ref[...].T + dt_bias_ref[...].reshape(1, -1)[:, :heads])
    rate = -step * jnp.exp(a_log_ref[...].reshape(1, -1)[:, :heads])
    rows = step.shape[0]
    row = lax.broadcasted_iota(jnp.int32, (rows, rows), 0)
    column = lax.broadcasted_iota(jnp.int32, (rows, rows), 1)
    lower = (row >= column).astype(F32).astype(BF16)
    high = rate.astype(BF16)
    middle, low = halves(rate - high.astype(F32))
    parts = jnp.concatenate([high, middle, low], axis=0)
    lowers = jnp.concatenate([lower, lower, lower], axis=1)
    return step, jnp.dot(lowers, parts, preferred_element_type=F32)


def insides(first, shape, taps, lens_ref):
    positions = first + lax.broadcasted_iota(jnp.int32, shape, 0)
    depth = positions - doc_start(positions, lens_ref)
    return [depth >= lag for lag in range(taps)]


def conv(pad, rows, weight, bias, inside):
    taps = weight.shape[0]
    total = pad[8 : 8 + rows] * weight[taps - 1 : taps] + bias
    for lag in range(1, taps):
        term = pad[8 - lag : 8 - lag + rows] * weight[taps - 1 - lag : taps - lag]
        total = total + jnp.where(inside[lag], term, 0.0)
    return silu(total)


def tail_lines(message, rows):
    block = message[rows:].astype(F32)
    return jnp.concatenate([block[at : at + 4] for at in range(0, block.shape[0], 4)], axis=1)


def reach(device, rows, lens_ref):
    return device - doc_start((device + 1) * rows - 1, lens_ref) // rows


def kept_weight(here, step, running, taps, lens_ref):
    rows = step.shape[0]
    last_begin = doc_start((here + 1) * rows - 1, lens_ref)
    row = lax.broadcasted_iota(jnp.int32, step.shape, 0)
    weight = step * jnp.exp(running[rows - 1 : rows] - running)
    kept = (here * rows + row >= last_begin) & ((row >= taps - 1) | (last_begin // rows >= here))
    return jnp.where(kept, weight, 0.0)


def conv_rows(pad, raw, weight, bias, inside):
    pad[0:8] = jnp.zeros((8, raw.shape[1]), F32)
    pad[8:] = raw.astype(F32)
    return conv(pad, raw.shape[0], weight, bias.reshape(1, -1), inside)


def first_state_kernel(*refs):
    hbm_refs, out_hbm_ref = refs[:10], refs[10]
    vmem_refs = refs[11:21]
    x_edge_ref, bc_edge_ref, out_ref, b_pad_ref, pad_ref, in_sems, out_sems = refs[21:]
    x_ref, b_ref, dt_ref, wx_ref, bx_ref, wbc_ref, bbc_ref, dt_bias_ref, a_log_ref, lens_ref = vmem_refs
    rows, width = x_ref.shape
    taps = wx_ref.shape[0]

    def corner(ref, shape):
        return ref.at[tuple(pl.ds(0, extent) for extent in shape)]

    order = (9, 2, 7, 8, 1, 5, 6, 0, 3, 4)
    copies = {}
    for at in order:
        source = corner(hbm_refs[at], vmem_refs[at].shape)
        copies[at] = pltpu.make_async_copy(source, vmem_refs[at], in_sems.at[at])
        copies[at].start()
    edge_copies = []
    for at, (source, target) in enumerate(((hbm_refs[0], x_edge_ref), (hbm_refs[1], bc_edge_ref))):
        edge_copies.append(
            pltpu.make_async_copy(source.at[pl.ds(rows - EDGE, EDGE)], target, in_sems.at[10 + at])
        )
        edge_copies[-1].start()

    here = lax.axis_index("seq")
    for at in (9, 2, 7, 8):
        copies[at].wait()
    inside = insides(here * rows, (rows, CHUNK), taps, lens_ref)
    step, running = rates(dt_ref, dt_bias_ref, a_log_ref)
    weight = kept_weight(here, step, running, taps, lens_ref)
    narrow = [mask[:, :STATE] for mask in inside]
    for at in (1, 5, 6):
        copies[at].wait()
    inputs = conv_rows(b_pad_ref, b_ref[...], wbc_ref[...], bbc_ref[...], narrow)
    turned = inputs.T.astype(BF16)
    for at in (0, 3, 4):
        copies[at].wait()
    slots = pad_ref.shape[0]
    outs = []

    def send(at, view):
        copy = pltpu.make_async_copy(out_ref.at[view], out_hbm_ref.at[view], out_sems.at[at])
        copy.start()
        outs.append(copy)

    for at, start in enumerate(range(0, width, CHUNK)):
        columns = slice(start, start + CHUNK)
        pad = pad_ref.at[(at + 1) % slots]
        xc = conv_rows(pad, x_ref[:, columns], wx_ref[:, columns], bx_ref[:, columns], inside)
        weighted = (xc * widen(weight, start, CHUNK)).astype(BF16)
        out_ref[:STATE, columns] = jnp.dot(turned, weighted, preferred_element_type=F32).astype(BF16)
        if at % 2:
            send(at // 2, (pl.ds(0, STATE), pl.ds(start - CHUNK, 2 * CHUNK)))
    for copy in edge_copies:
        copy.wait()
    edges = jnp.concatenate([x_edge_ref[...].astype(F32), bc_edge_ref[...].astype(F32)], axis=1)[EDGE - 4 :]
    spare = -edges.shape[1] % width
    if spare:
        edges = jnp.concatenate([edges, jnp.zeros((4, spare), F32)], axis=1)
    pieces = [edges[:, at : at + width] for at in range(0, edges.shape[1], width)]
    while len(pieces) % (EDGE // 4):
        pieces.append(jnp.zeros_like(pieces[0]))
    out_ref[STATE:] = jnp.concatenate(pieces, axis=0).astype(BF16)
    send(width // (2 * CHUNK), (pl.ds(STATE, out_ref.shape[0] - STATE), pl.ds(0, width)))
    for copy in outs:
        copy.wait()


def prepare_kernel(hops, groups, *refs):
    x_ref, bc_ref, dt_ref, wx_ref, bx_ref, wbc_ref, bbc_ref, dt_bias_ref, a_log_ref, skip_ref, lens_ref = refs[:11]
    z_ref = refs[11]
    xc_ref, bcc_ref, partial_ref, weight_ref, through_ref, inside_ref, flag_ref = refs[12:19]
    wide_skip_ref, begin_ref, step_ref, running_ref, out_ref, gate_ref, decay_ref = refs[19:26]
    state_refs = refs[26:-2]
    top_ref, pad_ref = refs[-2:]
    rows, width = x_ref.shape
    per_group = width // groups
    taps = wx_ref.shape[0]
    slots = pad_ref.shape[0]
    here = lax.axis_index("seq")
    first = here * rows
    inside = insides(first, (rows, CHUNK), taps, lens_ref)
    step, running = rates(dt_ref, dt_bias_ref, a_log_ref)
    heads = step.shape[1]
    group_heads = heads // groups
    kept = kept_weight(here, step, running, taps, lens_ref)
    for group in range(groups):
        base = slice(group * 2 * STATE, (group + 1) * 2 * STATE)
        pair = conv_rows(pad_ref.at[0], bc_ref[:, base], wbc_ref[:, base], bbc_ref[base], inside)
        bcc_ref[:, base] = pair.astype(BF16)
        turned = pair[:, :STATE].T.astype(BF16)
        part_weight = kept[:, group * group_heads : (group + 1) * group_heads]
        for chunk in range(0, per_group, CHUNK):
            columns = slice(group * per_group + chunk, group * per_group + chunk + CHUNK)
            pad = pad_ref.at[(chunk // CHUNK + 1) % slots]
            xc = conv_rows(pad, x_ref[:, columns], wx_ref[:, columns], bx_ref[columns], inside)
            xc_ref[:, columns] = xc.astype(BF16)
            if group:
                weighted = (xc * widen(part_weight, chunk, CHUNK)).astype(BF16)
                state_refs[group - 1][:, chunk : chunk + CHUNK] = jnp.dot(
                    turned, weighted, preferred_element_type=F32
                ).astype(BF16)

    own = reach(here, rows, lens_ref) == 0
    inside = [mask[:8] for mask in inside]
    for lag in range(1, taps):
        inside_ref[lag - 1] = inside[lag].astype(F32)
    flag_ref[0] = jnp.broadcast_to(own.astype(F32), (8, CHUNK))
    before = reach(here - 1, rows, lens_ref)
    for hop in range(1, hops):
        flag_ref[hop] = jnp.broadcast_to((before == hop).astype(F32), (8, CHUNK))
    begin = doc_start(first + lax.broadcasted_iota(jnp.int32, begin_ref.shape, 0), lens_ref)
    begin_ref[...] = begin
    entry = jnp.where(begin[:, :heads] < first, jnp.exp(running), 0.0)
    step_ref[...] = step
    running_ref[...] = running
    row = lax.broadcasted_iota(jnp.int32, (8, heads), 0)
    total = running[rows - 1 : rows]
    weight = step[:8] * jnp.exp(total - running[:8])
    weight = jnp.where((row < taps - 1) & jnp.logical_not(own), weight, 0.0)
    through = jnp.where(own, 0.0, jnp.broadcast_to(jnp.exp(total), (8, heads)))
    skip = jnp.broadcast_to(skip_ref[...].reshape(1, -1), (8, heads))
    every = jnp.concatenate([weight, through, skip], axis=0)
    for start in range(0, width, CHUNK):
        wide = widen(every, start, CHUNK)
        weight_ref[:, start : start + CHUNK] = wide[:8]
        through_ref[:, start : start + CHUNK] = wide[8:16]
        wide_skip_ref[:, start : start + CHUNK] = wide[16:]
    top_ref[0:8] = jnp.zeros((8, top_ref.shape[1]), F32)
    top_ref[8:, :width] = x_ref[:EDGE].astype(F32)[:8]
    top_ref[8:, width:] = bc_ref[:EDGE].astype(F32)[:8]

    def some(columns, base, w_ref, b_ref):
        here_columns = slice(base + columns.start, base + columns.stop)
        total = top_ref[8:, here_columns] * w_ref[taps - 1 : taps, columns] + b_ref[columns].reshape(1, -1)
        for lag in range(1, taps):
            term = top_ref[8 - lag : 16 - lag, here_columns] * w_ref[taps - 1 - lag : taps - lag, columns]
            total = total + jnp.where(inside[lag], term, 0.0)
        partial_ref[:, here_columns] = total

    for start in range(0, width, CHUNK):
        some(slice(start, start + CHUNK), 0, wx_ref, bx_ref)
    for start in range(0, bc_ref.shape[1], CHUNK):
        some(slice(start, start + CHUNK), width, wbc_ref, bbc_ref)

    row = lax.broadcasted_iota(jnp.int32, (rows, rows), 0)
    lane = lax.broadcasted_iota(jnp.int32, (rows, rows), 1)
    linked = (row >= lane) & (first + lane >= begin) & (lane >= 8)
    turned_running = running.T
    turned_step = step.T
    pair_width = 2 * HDIM
    channel = lax.broadcasted_iota(jnp.int32, (rows, pair_width), 1)
    below = lax.broadcasted_iota(jnp.int32, (rows, CHUNK), 0) >= 8
    for group in range(groups):
        base = group * 2 * STATE
        meet = lax.dot_general(
            bcc_ref[:, base + STATE : base + 2 * STATE],
            bcc_ref[:, base : base + STATE],
            (((1,), (1,)), ((), ())),
            preferred_element_type=F32,
        )
        meet = jnp.where(linked, meet, 0.0)
        group_entry = entry[:, group * group_heads : (group + 1) * group_heads]
        for chunk in range(0, per_group, CHUNK):
            at = group * per_group + chunk
            columns = slice(at, at + CHUNK)
            gate = silu(z_ref[:, columns].astype(F32))
            gate_ref[:, columns] = gate
            decay_ref[:, columns] = widen(group_entry, chunk, CHUNK) * gate
            xc_all = xc_ref[:, columns]
            skipped = jnp.where(below, xc_all.astype(F32) * wide_skip_ref[0:1, columns], 0.0)
            for start in range(0, CHUNK, pair_width):
                parts = []
                for head in ((at + start) // HDIM, (at + start) // HDIM + 1):
                    spread = running[:, head : head + 1] - turned_running[head : head + 1]
                    decay = jnp.exp(jnp.minimum(spread, 0.0))
                    parts.append((decay * (meet * turned_step[head : head + 1])).astype(BF16))
                mix = jnp.concatenate(parts, axis=1)
                here_columns = slice(start, start + pair_width)
                xc = xc_all[:, here_columns]
                zero = jnp.zeros_like(xc)
                stacked = jnp.concatenate(
                    [jnp.where(channel < HDIM, xc, zero), jnp.where(channel < HDIM, zero, xc)], axis=0
                )
                value = jnp.dot(mix, stacked, preferred_element_type=F32) + skipped[:, here_columns]
                out_ref[:, at + start : at + start + pair_width] = value * gate[:, here_columns]


def first_rows(lines, partial_ref, inside_ref, w_ref, pad_ref, slot, at, start):
    taps = w_ref.shape[0]
    columns = slice(start, start + CHUNK)
    pad = pad_ref.at[slot]
    pad[4:8] = lines[:, at + start : at + start + CHUNK]
    pad[8:] = jnp.zeros((8, CHUNK), F32)
    total = partial_ref[:, at + start : at + start + CHUNK]
    for lag in range(1, taps):
        term = pad[8 - lag : 16 - lag] * w_ref[taps - 1 - lag : taps - lag, columns]
        total = total + term * inside_ref[lag - 1]
    return silu(total)


def sixteen(value):
    return jnp.concatenate([value, jnp.zeros_like(value)], axis=0).astype(BF16)


def relay_first_kernel(fresh, *refs):
    message_ref, state_ref, partial_ref, weight_ref, through_ref, inside_ref, flag_ref, wx_ref, wbc_ref = refs[:9]
    other_ref = refs[9] if fresh else state_ref
    out_ref, pad_ref = refs[-2:]
    width = out_ref.shape[1]
    slots = pad_ref.shape[0]
    lines = tail_lines(message_ref, STATE)
    top = functools.partial(first_rows, lines, partial_ref, inside_ref)
    inputs = top(wbc_ref, pad_ref, 0, wx_ref.shape[1], 0)[:, :STATE]
    turned = jnp.concatenate([inputs, inputs], axis=0).T.astype(BF16)
    own = flag_ref[0, 0:1] > 0.5
    for start in range(0, width, CHUNK):
        columns = slice(start, start + CHUNK)
        xc = top(wx_ref, pad_ref, (start // CHUNK + 1) % slots, 0, start)
        weighted = sixteen(xc * weight_ref[:, columns])
        full = state_ref[:STATE, columns].astype(F32) + jnp.dot(
            turned, weighted, preferred_element_type=F32
        )
        full = full + through_ref[0:1, columns] * message_ref[:STATE, columns].astype(F32)
        out_ref[:, columns] = jnp.where(own, other_ref[:STATE, columns].astype(F32), full).astype(BF16)


def relay_kernel(part, fresh, *refs):
    got_ref, state_ref, through_ref, flag_ref = refs[:4]
    out_ref = refs[-1]
    width = out_ref.shape[1]
    own = flag_ref[0, 0:1] > 0.5
    for start in range(0, width, CHUNK):
        columns = slice(start, start + CHUNK)
        through = through_ref[0:1, part * width + start : part * width + start + CHUNK]
        full = state_ref[:, columns].astype(F32) + through * got_ref[:STATE, columns].astype(F32)
        if fresh:
            full = jnp.where(own, refs[4][:STATE, columns].astype(F32), full)
        out_ref[:, columns] = full.astype(BF16)


def first_rows_kernel(groups, *refs):
    (
        message_ref, partial_ref, weight_ref, inside_ref, wx_ref, wbc_ref, step_ref, running_ref,
        wide_skip_ref, begin_ref, bcc_ref, main_ref, gate_ref,
    ) = refs[:13]
    state_refs = refs[13 : 13 + groups]
    out_ref, c_ref = refs[13 + groups : 15 + groups]
    full_refs = refs[15 + groups : 15 + 2 * groups]
    pad_ref = refs[-1]
    rows, width = main_ref.shape
    per_group = width // groups
    heads = per_group // HDIM
    lanes = 8 * heads
    first = lax.axis_index("seq") * rows
    lines = tail_lines(message_ref, STATE)
    slots = pad_ref.shape[0]
    top = functools.partial(first_rows, lines, partial_ref, inside_ref)
    lane = lax.broadcasted_iota(jnp.int32, (rows, lanes), 1)
    line = lane & 7
    row = lax.broadcasted_iota(jnp.int32, (rows, lanes), 0)
    begin = jnp.concatenate([begin_ref[...]] * -(-lanes // rows), axis=1)[:, :lanes]
    linked = (row >= line) & (first + line >= begin)
    head = lax.broadcasted_iota(jnp.int32, (3 * heads, lanes), 0)
    for _ in range(2):
        head = jnp.where(head >= heads, head - heads, head)
    spread = (lax.broadcasted_iota(jnp.int32, (3 * heads, lanes), 1) >> 3 == head).astype(F32).astype(BF16)
    own_line = lax.broadcasted_iota(jnp.int32, (8, lanes), 0) == line[:8]

    def to_lanes(value):
        high = value.astype(BF16)
        middle, low = halves(value - high.astype(F32))
        return jnp.dot(jnp.concatenate([high, middle, low], axis=1), spread, preferred_element_type=F32)

    def by_line(value):
        return jnp.sum(jnp.where(own_line, value, 0.0), axis=0, keepdims=True)

    channel = lax.broadcasted_iota(jnp.int32, (8, CHUNK), 1)
    for group in range(groups):
        base = group * 2 * STATE
        these = slice(group * heads, (group + 1) * heads)
        new = top(wbc_ref, pad_ref, group % slots, width, base)
        old = bcc_ref[:, base + STATE : base + 2 * STATE]
        outputs = jnp.concatenate([new[:, STATE:], old[:EDGE].astype(F32)[8:]], axis=0).astype(BF16)
        outputs = jnp.concatenate([outputs, old[EDGE:]], axis=0)
        c_ref[:, group * STATE : (group + 1) * STATE] = outputs
        inputs = jnp.concatenate([new[:, :STATE]] * heads, axis=0).astype(BF16)
        meet = lax.dot_general(
            outputs, inputs, (((1,), (1,)), ((), ())), preferred_element_type=F32
        )
        running = to_lanes(running_ref[:, these])
        decay = jnp.exp(jnp.minimum(running - by_line(running[:8]), 0.0))
        mix = decay * (meet * by_line(to_lanes(step_ref[:8, these])))
        mix = jnp.where(linked, mix, 0.0).astype(BF16)
        turned = inputs[:EDGE].astype(F32).T.astype(BF16)
        for chunk in range(0, per_group, CHUNK):
            at = group * per_group + chunk
            columns = slice(at, at + CHUNK)
            xc = top(wx_ref, pad_ref, (chunk // CHUNK + 1) % slots, 0, at)
            full = state_refs[group][:STATE, chunk : chunk + CHUNK].astype(F32) + jnp.dot(
                turned, sixteen(xc * weight_ref[:, columns]), preferred_element_type=F32
            )
            full_refs[group][:, chunk : chunk + CHUNK] = full.astype(BF16)
            blocks = []
            for at_head in range(heads):
                low = at_head * HDIM - chunk
                if 0 <= low < CHUNK:
                    blocks.append(jnp.where((channel >= low) & (channel < low + HDIM), xc, 0.0))
                else:
                    blocks.append(jnp.zeros_like(xc))
            spread_xc = jnp.concatenate(blocks, axis=0).astype(BF16)
            gate = gate_ref[:, columns]
            value = main_ref[:, columns] + gate * jnp.dot(mix, spread_xc, preferred_element_type=F32)
            out_ref[:, columns] = value
            out_ref[0:8, columns] = value[:8] + gate[:8] * (xc * wide_skip_ref[:, columns])


def attend(q_ref, kv_refs, begin_ref, blocks, share, head):
    rows = q_ref.shape[0]
    kv_heads = kv_refs[0].shape[1] // (2 * ADIM)
    count = rows * blocks.count
    here = lax.axis_index("seq")
    row = here * rows + lax.broadcasted_iota(jnp.int32, (rows, count), 0)
    lane = (here - blocks.farthest) * rows + lax.broadcasted_iota(jnp.int32, (rows, count), 1)
    begin = jnp.concatenate([begin_ref[...]] * blocks.count, axis=1)
    allowed = jnp.concatenate([(lane <= row) & (lane >= begin)] * share, axis=0)
    low = head * ADIM
    keys = jnp.concatenate([ref[:, low : low + ADIM] for ref in kv_refs], axis=0)
    low = (kv_heads + head) * ADIM
    values = jnp.concatenate([ref[:, low : low + ADIM] for ref in kv_refs], axis=0)
    values = jnp.concatenate([values, jnp.ones((count, ADIM), BF16)], axis=1)
    lows = [(head * share + part) * ADIM for part in range(share)]
    asking = jnp.concatenate([q_ref[:, low : low + ADIM] for low in lows], axis=0)
    scores = lax.dot_general(asking, keys, (((1,), (1,)), ((), ())), preferred_element_type=F32)
    return jnp.where(allowed, scores * ADIM ** (-0.5), BARRED), values


class Blocks(NamedTuple):
    farthest: int
    count: int


def fold(q_ref, kv_refs, begin_ref, blocks, share, head, carry):
    lows = [(head * share + part) * ADIM for part in range(share)]
    scores, values = attend(q_ref, kv_refs, begin_ref, blocks, share, head)
    peak = jnp.max(scores, axis=1, keepdims=True)
    peak = jnp.broadcast_to(peak, (peak.shape[0], ADIM))
    if carry is not None:
        sums, totals, before = (
            jnp.concatenate([ref[:, low : low + ADIM] for low in lows], axis=0) for ref in carry
        )
        peak = jnp.maximum(peak, before)
    expo = jnp.exp(scores - jnp.concatenate([peak] * (scores.shape[1] // ADIM), axis=1))
    summed = jnp.dot(expo.astype(BF16), values, preferred_element_type=F32)
    if carry is None:
        return lows, summed[:, :ADIM], summed[:, ADIM:], peak
    factor = jnp.exp(before - peak)
    return lows, sums * factor + summed[:, :ADIM], totals * factor + summed[:, ADIM:], peak


def own_kernel(q_ref, keys_ref, values_ref, begin_ref, *outs):
    kv_ref = outs[3]
    kv_width = keys_ref.shape[1]
    kv_ref[:, :kv_width] = keys_ref[...]
    kv_ref[:, kv_width:] = values_ref[...]
    rows = q_ref.shape[0]
    share = QHEADS // KVHEADS
    for head in range(kv_width // ADIM):
        lows, *results = fold(q_ref, (kv_ref,), begin_ref, Blocks(0, 1), share, head, None)
        for ref, result in zip(outs, results):
            for part, low in enumerate(lows):
                ref[:, low : low + ADIM] = result[part * rows : (part + 1) * rows]


def near_kernel(q_ref, before_ref, begin_ref, *refs):
    carry, outs = refs[:3], refs[4:]
    outs[3][...] = before_ref[...]
    rows = q_ref.shape[0]
    share = QHEADS // KVHEADS
    for head in range(before_ref.shape[1] // (2 * ADIM)):
        lows, *results = fold(q_ref, (before_ref,), begin_ref, Blocks(1, 1), share, head, carry)
        for ref, result in zip(outs, results):
            for part, low in enumerate(lows):
                ref[:, low : low + ADIM] = result[part * rows : (part + 1) * rows]


def far_kernel(hops, *refs):
    q_ref, begin_ref = refs[:2]
    kv_refs = refs[5 : 4 + hops]
    out_hbm_ref, out_ref, sems = refs[4 + hops :]
    rows = q_ref.shape[0]
    share = QHEADS // KVHEADS
    copies = []
    for head in range(kv_refs[0].shape[1] // (2 * ADIM)):
        blocks = Blocks(hops, hops - 1)
        lows, sums, totals, _ = fold(q_ref, kv_refs, begin_ref, blocks, share, head, refs[2:5])
        result = (sums / totals).astype(BF16)
        for part, low in enumerate(lows):
            out_ref[:, low : low + ADIM] = result[part * rows : (part + 1) * rows]
        columns = pl.ds(head * share * ADIM, share * ADIM)
        copies.append(
            pltpu.make_async_copy(out_ref.at[:, columns], out_hbm_ref.at[:, columns], sems.at[head])
        )
        copies[-1].start()
    for copy in copies:
        copy.wait()


def norm_kernel(part, hops, first, where, given, *refs):
    local_ref, decay_ref, c_ref, gain_ref, flag_ref = refs[:5]
    got_refs = refs[5 : 5 + hops]
    out_hbm_ref, *token_refs = refs[5 + hops + given : -3]
    gated_ref, out_ref, sems = refs[-3:]
    for ref in token_refs:
        ref[...] = jnp.zeros_like(ref)

    def work():
        rows, width = gated_ref.shape
        outputs = c_ref[:, part * STATE : (part + 1) * STATE]
        squares = jnp.zeros((rows, 128), F32)
        for start in range(0, width, CHUNK):
            columns = slice(start, start + CHUNK)
            placed = slice(part * width + start, part * width + start + CHUNK)
            state = got_refs[0][:STATE, columns]
            for hop in range(1, hops):
                there = flag_ref[first + hop, 0:1] > 0.5
                state = jnp.where(there, got_refs[hop][:STATE, columns].astype(F32), state.astype(F32))
            carried = jnp.dot(outputs, state.astype(BF16), preferred_element_type=F32)
            gated = local_ref[:, placed] + carried * decay_ref[:, placed]
            gated_ref[:, columns] = gated
            for lane in range(0, CHUNK, 128):
                squares = squares + gated[:, lane : lane + 128] * gated[:, lane : lane + 128]
        squares = jnp.sum(squares, axis=1, keepdims=True)
        multiplier = lax.rsqrt(squares * (1.0 / width) + EPSILON)
        copies = []
        for start in range(0, width, CHUNK):
            columns = slice(start, start + CHUNK)
            gain = gain_ref[part * width + start : part * width + start + CHUNK]
            out_ref[:, columns] = (gated_ref[:, columns] * multiplier * gain.reshape(1, -1)).astype(BF16)
            copies.append(
                pltpu.make_async_copy(
                    out_ref.at[:, pl.ds(start, CHUNK)],
                    out_hbm_ref.at[:, pl.ds(part * width + start, CHUNK)],
                    sems.at[start // CHUNK],
                )
            )
            copies[-1].start()
        for copy in copies:
            copy.wait()

    odd = lax.axis_index("dp") % 2 == 1
    later = jnp.max(flag_ref[1:]) > 0.5
    here = {"odd": odd, "rest": jnp.logical_not(odd) | later, "first": jnp.logical_not(later), "later": later}
    pl.when(here[where])(work)


WHOLE = pl.BlockSpec(memory_space=pltpu.VMEM)
SCALARS = pl.BlockSpec(memory_space=pltpu.SMEM)
UNTOUCHED = pl.BlockSpec(memory_space=pl.ANY)


def tile(rows, columns, row, column):
    return pl.BlockSpec((rows, columns), lambda step: (row, column))


def call(kernel, name, outs, operands, specs, out_specs=None, scratch=(), flops=KERNEL_FLOPS, aliases={}, limit=VMEM_LIMIT):
    moved = sum(math.prod(a.shape) * a.dtype.itemsize for a in (*operands, *outs))
    return pl.pallas_call(
        kernel,
        name=name,
        grid=(1,),
        out_shape=outs,
        in_specs=specs,
        out_specs=[WHOLE] * len(outs) if out_specs is None else out_specs,
        scratch_shapes=list(scratch),
        input_output_aliases=aliases,
        compiler_params=pltpu.CompilerParams(vmem_limit_bytes=limit),
        cost_estimate=pl.CostEstimate(flops=flops, bytes_accessed=moved, transcendentals=0),
    )(*operands)


def onward(value, first=0):
    count = lax.axis_size("seq")
    return lax.ppermute(value, "seq", [(source, source + 1) for source in range(first, count - 1)])


def shards(
    x_raw,
    bc_raw,
    z_gate,
    dt_raw,
    conv_x_weight,
    conv_x_bias,
    conv_bc_weight,
    conv_bc_bias,
    dt_bias,
    a_log,
    skip_d,
    norm_gain,
    queries,
    keys,
    values,
    doc_lens,
):
    rows, width = x_raw.shape
    bc_width = bc_raw.shape[1]
    heads = dt_raw.shape[1]
    groups = bc_width // (2 * STATE)
    per_group = width // groups
    count = lax.axis_size("seq")
    longest = rows * count // 2
    hops = min(count - 1, -(-(longest - 1) // rows))
    assert hops * rows >= longest and (hops == 2 or hops > 2 and groups == 1)
    shape = jax.ShapeDtypeStruct
    dt = dt_raw.T
    params = [dt, conv_x_weight, conv_x_bias, conv_bc_weight, conv_bc_bias, dt_bias, a_log]
    pieces = -(-(width + bc_width) // per_group)
    tail_rows = EDGE * -(-4 * pieces // EDGE)

    (message,) = call(
        first_state_kernel,
        "first_state",
        [shape((STATE + tail_rows, per_group), BF16)],
        [x_raw, bc_raw, *(a if a.ndim > 1 else a[None] for a in params), doc_lens],
        [UNTOUCHED] * 10,
        out_specs=[UNTOUCHED],
        scratch=[
            pltpu.VMEM((rows, per_group), BF16),
            pltpu.VMEM((rows, STATE), BF16),
            pltpu.VMEM((per_group // HDIM, rows), F32),
            pltpu.VMEM((conv_x_weight.shape[0], per_group), F32),
            pltpu.VMEM((1, per_group), F32),
            pltpu.VMEM((conv_x_weight.shape[0], STATE), F32),
            pltpu.VMEM((1, STATE), F32),
            pltpu.VMEM((1, heads), F32),
            pltpu.VMEM((1, heads), F32),
            pltpu.SMEM(doc_lens.shape, jnp.int32),
            pltpu.VMEM((EDGE, width), BF16),
            pltpu.VMEM((EDGE, bc_width), BF16),
            pltpu.VMEM((STATE + tail_rows, per_group), BF16),
            pltpu.VMEM((rows + 8, STATE), F32),
            pltpu.VMEM((4, rows + 8, CHUNK), F32),
            pltpu.SemaphoreType.DMA((12,)),
            pltpu.SemaphoreType.DMA((per_group // (2 * CHUNK) + 1,)),
        ],
        limit=VMEM_ALL,
    )
    slots = [onward(message)]
    prepared = call(
        functools.partial(prepare_kernel, hops, groups),
        "prepare",
        [
            shape((rows, width), BF16),
            shape((rows, bc_width), BF16),
            shape((8, width + bc_width), F32),
            shape((8, width), F32),
            shape((8, width), F32),
            shape((conv_x_weight.shape[0] - 1, 8, CHUNK), F32),
            shape((hops, 8, CHUNK), F32),
            shape((8, width), F32),
            shape((rows, rows), jnp.int32),
            shape((rows, heads), F32),
            shape((rows, heads), F32),
            shape((rows, width), F32),
            shape((rows, width), F32),
            shape((rows, width), F32),
            *(shape((STATE, per_group), BF16) for _ in range(groups - 1)),
        ],
        [x_raw, bc_raw, *params, skip_d, doc_lens, z_gate],
        [WHOLE] * 10 + [SCALARS] + [WHOLE],
        scratch=[
            pltpu.VMEM((16, width + bc_width), F32),
            pltpu.VMEM((4, rows + 8, CHUNK), F32),
        ],
    )
    _, bcc, partial, weight, through, inside, flags, wide_skip, begin, *prepared = prepared
    step, running, main, gate, decay, *states = prepared
    states = [message, *states]
    carried = [shape(queries.shape, F32)] * 3 + [shape((rows, 2 * keys.shape[1]), BF16)]
    *carry, kv = call(own_kernel, "attend_own", carried, [queries, keys, values, begin], [WHOLE] * 4)
    kvs = [kv, onward(kv)]
    fulls = None
    for slot in range(2, hops + groups):
        part = min(slot - 1, groups) - 1
        fresh = slot <= groups
        if slot == 2:
            kernel = functools.partial(relay_first_kernel, fresh)
            operands = [slots[0], states[0], partial, weight, through, inside, flags, conv_x_weight, conv_bc_weight]
            scratch = [pltpu.VMEM((4, 16, CHUNK), F32)]
        else:
            kernel = functools.partial(relay_kernel, part, fresh)
            operands = [slots[-1], fulls[part], through, flags]
            scratch = []
        if fresh:
            operands.append(states[slot - 1])
        (passed,) = call(
            kernel,
            f"relay_slot{slot}",
            [shape((STATE, per_group), BF16)],
            operands,
            [WHOLE] * len(operands),
            scratch=scratch,
        )
        slots.append(onward(passed, max(0, slot - groups)))
        if fulls is None:
            gated, c_out, *fulls = call(
                functools.partial(first_rows_kernel, groups),
                "first_rows",
                [
                    shape((rows, width), F32),
                    shape((rows, groups * STATE), BF16),
                    *(shape((STATE, per_group), BF16) for _ in range(groups)),
                ],
                [
                    slots[0], partial, weight, inside, conv_x_weight, conv_bc_weight, step, running,
                    wide_skip, begin, bcc, main, gate, *states,
                ],
                [WHOLE] * (13 + groups),
                scratch=[pltpu.VMEM((4, 16, CHUNK), F32)],
            )
    def norm(part, first, stop, where, out=None, token=False):
        got = slots[part + first : part + stop]
        operands = [gated, decay, c_out, norm_gain, flags, *got]
        specs = [WHOLE] * len(operands)
        outs = [shape((rows, width), BF16)] + [shape((8, 128), F32)] * token
        aliases = {}
        if out is not None:
            aliases = {len(operands): 0}
            operands.append(out)
            specs.append(UNTOUCHED)
        return call(
            functools.partial(norm_kernel, part, len(got), first, where, out is not None),
            f"norm_part{part}_{where}",
            outs,
            operands,
            specs,
            out_specs=[UNTOUCHED] + [WHOLE] * token,
            scratch=[
                pltpu.VMEM((rows, per_group), F32),
                pltpu.VMEM((rows, per_group), BF16),
                pltpu.SemaphoreType.DMA((per_group // CHUNK,)),
            ],
            aliases=aliases,
            flops=KERNEL_FLOPS // 2,
        )

    mamba_out, token = None, c_out
    for part in range(groups - 1):
        mamba_out, token = norm(part, 0, 1, "odd", mamba_out, True)
    *carry, kv_on = call(
        near_kernel,
        "attend_near",
        carried,
        [queries, kvs[1], begin, *carry, token],
        [WHOLE] * 6 + [UNTOUCHED],
    )
    for hop in range(1, hops):
        kvs.append(onward(kv_on if hop == 1 else kvs[-1], hop))
    (attn_out,) = call(
        functools.partial(far_kernel, hops),
        "attend_far",
        [shape(queries.shape, BF16)],
        [queries, begin, *carry, *reversed(kvs[2:])],
        [WHOLE] * (4 + hops),
        out_specs=[UNTOUCHED],
        scratch=[
            pltpu.VMEM(queries.shape, BF16),
            pltpu.SemaphoreType.DMA((keys.shape[1] // ADIM,)),
        ],
    )
    for part in range(groups - 1):
        (mamba_out,) = norm(part, 0, hops, "rest", mamba_out)
    (mamba_out,) = norm(groups - 1, 0, 1, "first", mamba_out)
    (mamba_out,) = norm(groups - 1, 1, hops, "later", mamba_out)
    return (mamba_out, attn_out)


def solution(mesh):
    split = P(("groups", "seq"), "dp")
    placed = (
        split,
        split,
        split,
        split,
        P(None, "dp"),
        P("dp"),
        P(None, "dp"),
        P("dp"),
        P("dp"),
        P("dp"),
        P("dp"),
        P("dp"),
        split,
        split,
        split,
        P("groups"),
    )
    return jax.shard_map(
        shards,
        mesh=mesh,
        in_specs=placed,
        out_specs=(split, split),
        check_vma=False,
    )
```

```python
import functools
import math
from typing import NamedTuple

import jax
import jax.numpy as jnp
from jax import lax
from jax.experimental import pallas as pl
from jax.experimental.pallas import tpu as pltpu
from jax.sharding import PartitionSpec as P

HDIM = 64
STATE = 128
QHEADS = 32
KVHEADS = 8
ADIM = 128
EPSILON = 1e-05
BARRED = -2e30
HIGHEST = lax.Precision.HIGHEST
F32 = jnp.float32
BF16 = jnp.bfloat16
CHUNK = 256
EDGE = 16
KERNEL_FLOPS = 2 * 10**9
VMEM_LIMIT = 40 * 1024 * 1024
VMEM_ALL = 62 * 1024 * 1024


def silu(value):
    return value * (0.5 * jnp.tanh(0.5 * value) + 0.5)


def softplus(value):
    return jnp.maximum(value, 0.0) + jnp.log(1.0 + jnp.exp(-jnp.abs(value)))


def doc_start(positions, lens_ref):
    begin = jnp.int32(0)
    found = positions * 0
    for doc in range(lens_ref.shape[0]):
        found = jnp.where(positions >= begin, begin, found)
        begin = begin + lens_ref[doc]
    return found


def halves(value):
    high = value.astype(BF16)
    return high, (value - high.astype(F32)).astype(BF16)


def widen(per_head, first, width):
    heads = per_head.shape[1]
    both = jnp.concatenate(halves(per_head), axis=1)
    head = lax.broadcasted_iota(jnp.int32, (2 * heads, width), 0)
    head = jnp.where(head >= heads, head - heads, head)
    channel = lax.broadcasted_iota(jnp.int32, (2 * heads, width), 1) + first
    spread = (channel // HDIM == head).astype(F32).astype(BF16)
    return jnp.dot(both, spread, preferred_element_type=F32)


def rates(dt_ref, dt_bias_ref, a_log_ref):
    heads = dt_ref.shape[0]
    step = softplus(dt_ref[...].T + dt_bias_ref[...].reshape(1, -1)[:, :heads])
    rate = -step * jnp.exp(a_log_ref[...].reshape(1, -1)[:, :heads])
    rows = step.shape[0]
    row = lax.broadcasted_iota(jnp.int32, (rows, rows), 0)
    column = lax.broadcasted_iota(jnp.int32, (rows, rows), 1)
    lower = (row >= column).astype(F32).astype(BF16)
    high = rate.astype(BF16)
    middle, low = halves(rate - high.astype(F32))
    parts = jnp.concatenate([high, middle, low], axis=0)
    lowers = jnp.concatenate([lower, lower, lower], axis=1)
    return step, jnp.dot(lowers, parts, preferred_element_type=F32)


def insides(first, shape, taps, lens_ref):
    positions = first + lax.broadcasted_iota(jnp.int32, shape, 0)
    depth = positions - doc_start(positions, lens_ref)
    return [depth >= lag for lag in range(taps)]


def conv(pad, rows, weight, bias, inside):
    taps = weight.shape[0]
    total = pad[8 : 8 + rows] * weight[taps - 1 : taps] + bias
    for lag in range(1, taps):
        term = pad[8 - lag : 8 - lag + rows] * weight[taps - 1 - lag : taps - lag]
        total = total + jnp.where(inside[lag], term, 0.0)
    return silu(total)


def tail_lines(message, rows):
    block = message[rows:].astype(F32)
    return jnp.concatenate([block[at : at + 4] for at in range(0, block.shape[0], 4)], axis=1)


def reach(device, rows, lens_ref):
    return device - doc_start((device + 1) * rows - 1, lens_ref) // rows


def kept_weight(here, step, running, taps, lens_ref):
    rows = step.shape[0]
    last_begin = doc_start((here + 1) * rows - 1, lens_ref)
    row = lax.broadcasted_iota(jnp.int32, step.shape, 0)
    weight = step * jnp.exp(running[rows - 1 : rows] - running)
    kept = (here * rows + row >= last_begin) & ((row >= taps - 1) | (last_begin // rows >= here))
    return jnp.where(kept, weight, 0.0)


def conv_rows(pad, raw, weight, bias, inside):
    pad[0:8] = jnp.zeros((8, raw.shape[1]), F32)
    pad[8:] = raw.astype(F32)
    return conv(pad, raw.shape[0], weight, bias.reshape(1, -1), inside)


def first_state_kernel(*refs):
    hbm_refs, out_hbm_ref = refs[:10], refs[10]
    vmem_refs = refs[11:21]
    x_edge_ref, bc_edge_ref, out_ref, b_pad_ref, pad_ref, in_sems, out_sems = refs[21:]
    x_ref, b_ref, dt_ref, wx_ref, bx_ref, wbc_ref, bbc_ref, dt_bias_ref, a_log_ref, lens_ref = vmem_refs
    rows, width = x_ref.shape
    taps = wx_ref.shape[0]

    def corner(ref, shape):
        return ref.at[tuple(pl.ds(0, extent) for extent in shape)]

    order = (0, 9, 2, 7, 8, 1, 5, 6, 3, 4)
    copies = {}
    for at in order:
        source = corner(hbm_refs[at], vmem_refs[at].shape)
        copies[at] = pltpu.make_async_copy(source, vmem_refs[at], in_sems.at[at])
        copies[at].start()
    edge_copies = []
    for at, (source, target) in enumerate(((hbm_refs[0], x_edge_ref), (hbm_refs[1], bc_edge_ref))):
        edge_copies.append(
            pltpu.make_async_copy(source.at[pl.ds(rows - EDGE, EDGE)], target, in_sems.at[10 + at])
        )
        edge_copies[-1].start()

    here = lax.axis_index("seq")
    for at in (9, 2, 7, 8):
        copies[at].wait()
    inside = insides(here * rows, (rows, CHUNK), taps, lens_ref)
    step, running = rates(dt_ref, dt_bias_ref, a_log_ref)
    weight = kept_weight(here, step, running, taps, lens_ref)
    narrow = [mask[:, :STATE] for mask in inside]
    for at in (1, 5, 6):
        copies[at].wait()
    inputs = conv_rows(b_pad_ref, b_ref[...], wbc_ref[...], bbc_ref[...], narrow)
    turned = inputs.T.astype(BF16)
    for at in (0, 3, 4):
        copies[at].wait()
    slots = pad_ref.shape[0]
    outs = []

    def send(at, view):
        copy = pltpu.make_async_copy(out_ref.at[view], out_hbm_ref.at[view], out_sems.at[at])
        copy.start()
        outs.append(copy)

    for at, start in enumerate(range(0, width, CHUNK)):
        columns = slice(start, start + CHUNK)
        pad = pad_ref.at[(at + 1) % slots]
        xc = conv_rows(pad, x_ref[:, columns], wx_ref[:, columns], bx_ref[:, columns], inside)
        weighted = (xc * widen(weight, start, CHUNK)).astype(BF16)
        out_ref[:STATE, columns] = jnp.dot(turned, weighted, preferred_element_type=F32).astype(BF16)
        if at % 2:
            send(at // 2, (pl.ds(0, STATE), pl.ds(start - CHUNK, 2 * CHUNK)))
    for copy in edge_copies:
        copy.wait()
    edges = jnp.concatenate([x_edge_ref[...].astype(F32), bc_edge_ref[...].astype(F32)], axis=1)[EDGE - 4 :]
    spare = -edges.shape[1] % width
    if spare:
        edges = jnp.concatenate([edges, jnp.zeros((4, spare), F32)], axis=1)
    pieces = [edges[:, at : at + width] for at in range(0, edges.shape[1], width)]
    while len(pieces) % (EDGE // 4):
        pieces.append(jnp.zeros_like(pieces[0]))
    out_ref[STATE:] = jnp.concatenate(pieces, axis=0).astype(BF16)
    send(width // (2 * CHUNK), (pl.ds(STATE, out_ref.shape[0] - STATE), pl.ds(0, width)))
    for copy in outs:
        copy.wait()


def prepare_kernel(hops, groups, *refs):
    x_ref, bc_ref, dt_ref, wx_ref, bx_ref, wbc_ref, bbc_ref, dt_bias_ref, a_log_ref, skip_ref, lens_ref = refs[:11]
    z_ref = refs[11]
    xc_ref, bcc_ref, partial_ref, weight_ref, through_ref, inside_ref, flag_ref = refs[12:19]
    wide_skip_ref, begin_ref, step_ref, running_ref, out_ref, gate_ref, decay_ref = refs[19:26]
    state_refs = refs[26:-2]
    top_ref, pad_ref = refs[-2:]
    rows, width = x_ref.shape
    per_group = width // groups
    taps = wx_ref.shape[0]
    slots = pad_ref.shape[0]
    here = lax.axis_index("seq")
    first = here * rows
    inside = insides(first, (rows, CHUNK), taps, lens_ref)
    step, running = rates(dt_ref, dt_bias_ref, a_log_ref)
    heads = step.shape[1]
    group_heads = heads // groups
    kept = kept_weight(here, step, running, taps, lens_ref)
    for group in range(groups):
        base = slice(group * 2 * STATE, (group + 1) * 2 * STATE)
        pair = conv_rows(pad_ref.at[0], bc_ref[:, base], wbc_ref[:, base], bbc_ref[base], inside)
        bcc_ref[:, base] = pair.astype(BF16)
        turned = pair[:, :STATE].T.astype(BF16)
        part_weight = kept[:, group * group_heads : (group + 1) * group_heads]
        for chunk in range(0, per_group, CHUNK):
            columns = slice(group * per_group + chunk, group * per_group + chunk + CHUNK)
            pad = pad_ref.at[(chunk // CHUNK + 1) % slots]
            xc = conv_rows(pad, x_ref[:, columns], wx_ref[:, columns], bx_ref[columns], inside)
            xc_ref[:, columns] = xc.astype(BF16)
            if group:
                weighted = (xc * widen(part_weight, chunk, CHUNK)).astype(BF16)
                state_refs[group - 1][:, chunk : chunk + CHUNK] = jnp.dot(
                    turned, weighted, preferred_element_type=F32
                ).astype(BF16)

    own = reach(here, rows, lens_ref) == 0
    inside = [mask[:8] for mask in inside]
    for lag in range(1, taps):
        inside_ref[lag - 1] = inside[lag].astype(F32)
    flag_ref[0] = jnp.broadcast_to(own.astype(F32), (8, CHUNK))
    before = reach(here - 1, rows, lens_ref)
    for hop in range(1, hops):
        flag_ref[hop] = jnp.broadcast_to((before == hop).astype(F32), (8, CHUNK))
    begin = doc_start(first + lax.broadcasted_iota(jnp.int32, begin_ref.shape, 0), lens_ref)
    begin_ref[...] = begin
    entry = jnp.where(begin[:, :heads] < first, jnp.exp(running), 0.0)
    step_ref[...] = step
    running_ref[...] = running
    row = lax.broadcasted_iota(jnp.int32, (8, heads), 0)
    total = running[rows - 1 : rows]
    weight = step[:8] * jnp.exp(total - running[:8])
    weight = jnp.where((row < taps - 1) & jnp.logical_not(own), weight, 0.0)
    through = jnp.where(own, 0.0, jnp.broadcast_to(jnp.exp(total), (8, heads)))
    skip = jnp.broadcast_to(skip_ref[...].reshape(1, -1), (8, heads))
    every = jnp.concatenate([weight, through, skip], axis=0)
    for start in range(0, width, CHUNK):
        wide = widen(every, start, CHUNK)
        weight_ref[:, start : start + CHUNK] = wide[:8]
        through_ref[:, start : start + CHUNK] = wide[8:16]
        wide_skip_ref[:, start : start + CHUNK] = wide[16:]
    top_ref[0:8] = jnp.zeros((8, top_ref.shape[1]), F32)
    top_ref[8:, :width] = x_ref[:EDGE].astype(F32)[:8]
    top_ref[8:, width:] = bc_ref[:EDGE].astype(F32)[:8]

    def some(columns, base, w_ref, b_ref):
        here_columns = slice(base + columns.start, base + columns.stop)
        total = top_ref[8:, here_columns] * w_ref[taps - 1 : taps, columns] + b_ref[columns].reshape(1, -1)
        for lag in range(1, taps):
            term = top_ref[8 - lag : 16 - lag, here_columns] * w_ref[taps - 1 - lag : taps - lag, columns]
            total = total + jnp.where(inside[lag], term, 0.0)
        partial_ref[:, here_columns] = total

    for start in range(0, width, CHUNK):
        some(slice(start, start + CHUNK), 0, wx_ref, bx_ref)
    for start in range(0, bc_ref.shape[1], CHUNK):
        some(slice(start, start + CHUNK), width, wbc_ref, bbc_ref)

    row = lax.broadcasted_iota(jnp.int32, (rows, rows), 0)
    lane = lax.broadcasted_iota(jnp.int32, (rows, rows), 1)
    linked = (row >= lane) & (first + lane >= begin) & (lane >= 8)
    turned_running = running.T
    turned_step = step.T
    pair_width = 2 * HDIM
    channel = lax.broadcasted_iota(jnp.int32, (rows, pair_width), 1)
    below = lax.broadcasted_iota(jnp.int32, (rows, CHUNK), 0) >= 8
    for group in range(groups):
        base = group * 2 * STATE
        meet = lax.dot_general(
            bcc_ref[:, base + STATE : base + 2 * STATE],
            bcc_ref[:, base : base + STATE],
            (((1,), (1,)), ((), ())),
            preferred_element_type=F32,
        )
        meet = jnp.where(linked, meet, 0.0)
        group_entry = entry[:, group * group_heads : (group + 1) * group_heads]
        for chunk in range(0, per_group, CHUNK):
            at = group * per_group + chunk
            columns = slice(at, at + CHUNK)
            gate = silu(z_ref[:, columns].astype(F32))
            gate_ref[:, columns] = gate
            decay_ref[:, columns] = widen(group_entry, chunk, CHUNK) * gate
            xc_all = xc_ref[:, columns]
            skipped = jnp.where(below, xc_all.astype(F32) * wide_skip_ref[0:1, columns], 0.0)
            for start in range(0, CHUNK, pair_width):
                parts = []
                for head in ((at + start) // HDIM, (at + start) // HDIM + 1):
                    spread = running[:, head : head + 1] - turned_running[head : head + 1]
                    decay = jnp.exp(jnp.minimum(spread, 0.0))
                    parts.append((decay * (meet * turned_step[head : head + 1])).astype(BF16))
                mix = jnp.concatenate(parts, axis=1)
                here_columns = slice(start, start + pair_width)
                xc = xc_all[:, here_columns]
                zero = jnp.zeros_like(xc)
                stacked = jnp.concatenate(
                    [jnp.where(channel < HDIM, xc, zero), jnp.where(channel < HDIM, zero, xc)], axis=0
                )
                value = jnp.dot(mix, stacked, preferred_element_type=F32) + skipped[:, here_columns]
                out_ref[:, at + start : at + start + pair_width] = value * gate[:, here_columns]


def first_rows(lines, partial_ref, inside_ref, w_ref, pad_ref, slot, at, start):
    taps = w_ref.shape[0]
    columns = slice(start, start + CHUNK)
    pad = pad_ref.at[slot]
    pad[4:8] = lines[:, at + start : at + start + CHUNK]
    pad[8:] = jnp.zeros((8, CHUNK), F32)
    total = partial_ref[:, at + start : at + start + CHUNK]
    for lag in range(1, taps):
        term = pad[8 - lag : 16 - lag] * w_ref[taps - 1 - lag : taps - lag, columns]
        total = total + term * inside_ref[lag - 1]
    return silu(total)


def sixteen(value):
    return jnp.concatenate([value, jnp.zeros_like(value)], axis=0).astype(BF16)


def relay_first_kernel(fresh, *refs):
    message_ref, state_ref, partial_ref, weight_ref, through_ref, inside_ref, flag_ref, wx_ref, wbc_ref = refs[:9]
    other_ref = refs[9] if fresh else state_ref
    out_ref, pad_ref = refs[-2:]
    width = out_ref.shape[1]
    slots = pad_ref.shape[0]
    lines = tail_lines(message_ref, STATE)
    top = functools.partial(first_rows, lines, partial_ref, inside_ref)
    inputs = top(wbc_ref, pad_ref, 0, wx_ref.shape[1], 0)[:, :STATE]
    turned = jnp.concatenate([inputs, inputs], axis=0).T.astype(BF16)
    own = flag_ref[0, 0:1] > 0.5
    for start in range(0, width, CHUNK):
        columns = slice(start, start + CHUNK)
        xc = top(wx_ref, pad_ref, (start // CHUNK + 1) % slots, 0, start)
        weighted = sixteen(xc * weight_ref[:, columns])
        full = state_ref[:STATE, columns].astype(F32) + jnp.dot(
            turned, weighted, preferred_element_type=F32
        )
        full = full + through_ref[0:1, columns] * message_ref[:STATE, columns].astype(F32)
        out_ref[:, columns] = jnp.where(own, other_ref[:STATE, columns].astype(F32), full).astype(BF16)


def relay_kernel(part, fresh, *refs):
    got_ref, state_ref, through_ref, flag_ref = refs[:4]
    out_ref = refs[-1]
    width = out_ref.shape[1]
    own = flag_ref[0, 0:1] > 0.5
    for start in range(0, width, CHUNK):
        columns = slice(start, start + CHUNK)
        through = through_ref[0:1, part * width + start : part * width + start + CHUNK]
        full = state_ref[:, columns].astype(F32) + through * got_ref[:STATE, columns].astype(F32)
        if fresh:
            full = jnp.where(own, refs[4][:STATE, columns].astype(F32), full)
        out_ref[:, columns] = full.astype(BF16)


def first_rows_kernel(groups, *refs):
    (
        message_ref, partial_ref, weight_ref, inside_ref, wx_ref, wbc_ref, step_ref, running_ref,
        wide_skip_ref, begin_ref, bcc_ref, main_ref, gate_ref,
    ) = refs[:13]
    state_refs = refs[13 : 13 + groups]
    out_ref, c_ref = refs[13 + groups : 15 + groups]
    full_refs = refs[15 + groups : 15 + 2 * groups]
    pad_ref = refs[-1]
    rows, width = main_ref.shape
    per_group = width // groups
    heads = per_group // HDIM
    lanes = 8 * heads
    first = lax.axis_index("seq") * rows
    lines = tail_lines(message_ref, STATE)
    slots = pad_ref.shape[0]
    top = functools.partial(first_rows, lines, partial_ref, inside_ref)
    lane = lax.broadcasted_iota(jnp.int32, (rows, lanes), 1)
    line = lane & 7
    row = lax.broadcasted_iota(jnp.int32, (rows, lanes), 0)
    begin = jnp.concatenate([begin_ref[...]] * -(-lanes // rows), axis=1)[:, :lanes]
    linked = (row >= line) & (first + line >= begin)
    head = lax.broadcasted_iota(jnp.int32, (3 * heads, lanes), 0)
    for _ in range(2):
        head = jnp.where(head >= heads, head - heads, head)
    spread = (lax.broadcasted_iota(jnp.int32, (3 * heads, lanes), 1) >> 3 == head).astype(F32).astype(BF16)
    own_line = lax.broadcasted_iota(jnp.int32, (8, lanes), 0) == line[:8]

    def to_lanes(value):
        high = value.astype(BF16)
        middle, low = halves(value - high.astype(F32))
        return jnp.dot(jnp.concatenate([high, middle, low], axis=1), spread, preferred_element_type=F32)

    def by_line(value):
        return jnp.sum(jnp.where(own_line, value, 0.0), axis=0, keepdims=True)

    channel = lax.broadcasted_iota(jnp.int32, (8, CHUNK), 1)
    for group in range(groups):
        base = group * 2 * STATE
        these = slice(group * heads, (group + 1) * heads)
        new = top(wbc_ref, pad_ref, group % slots, width, base)
        old = bcc_ref[:, base + STATE : base + 2 * STATE]
        outputs = jnp.concatenate([new[:, STATE:], old[:EDGE].astype(F32)[8:]], axis=0).astype(BF16)
        outputs = jnp.concatenate([outputs, old[EDGE:]], axis=0)
        c_ref[:, group * STATE : (group + 1) * STATE] = outputs
        inputs = jnp.concatenate([new[:, :STATE]] * heads, axis=0).astype(BF16)
        meet = lax.dot_general(
            outputs, inputs, (((1,), (1,)), ((), ())), preferred_element_type=F32
        )
        running = to_lanes(running_ref[:, these])
        decay = jnp.exp(jnp.minimum(running - by_line(running[:8]), 0.0))
        mix = decay * (meet * by_line(to_lanes(step_ref[:8, these])))
        mix = jnp.where(linked, mix, 0.0).astype(BF16)
        turned = inputs[:EDGE].astype(F32).T.astype(BF16)
        for chunk in range(0, per_group, CHUNK):
            at = group * per_group + chunk
            columns = slice(at, at + CHUNK)
            xc = top(wx_ref, pad_ref, (chunk // CHUNK + 1) % slots, 0, at)
            full = state_refs[group][:STATE, chunk : chunk + CHUNK].astype(F32) + jnp.dot(
                turned, sixteen(xc * weight_ref[:, columns]), preferred_element_type=F32
            )
            full_refs[group][:, chunk : chunk + CHUNK] = full.astype(BF16)
            blocks = []
            for at_head in range(heads):
                low = at_head * HDIM - chunk
                if 0 <= low < CHUNK:
                    blocks.append(jnp.where((channel >= low) & (channel < low + HDIM), xc, 0.0))
                else:
                    blocks.append(jnp.zeros_like(xc))
            spread_xc = jnp.concatenate(blocks, axis=0).astype(BF16)
            gate = gate_ref[:, columns]
            value = main_ref[:, columns] + gate * jnp.dot(mix, spread_xc, preferred_element_type=F32)
            out_ref[:, columns] = value
            out_ref[0:8, columns] = value[:8] + gate[:8] * (xc * wide_skip_ref[:, columns])


def attend(q_ref, kv_refs, begin_ref, blocks, share, head):
    rows = q_ref.shape[0]
    kv_heads = kv_refs[0].shape[1] // (2 * ADIM)
    count = rows * blocks.count
    here = lax.axis_index("seq")
    row = here * rows + lax.broadcasted_iota(jnp.int32, (rows, count), 0)
    lane = (here - blocks.farthest) * rows + lax.broadcasted_iota(jnp.int32, (rows, count), 1)
    begin = jnp.concatenate([begin_ref[...]] * blocks.count, axis=1)
    allowed = jnp.concatenate([(lane <= row) & (lane >= begin)] * share, axis=0)
    low = head * ADIM
    keys = jnp.concatenate([ref[:, low : low + ADIM] for ref in kv_refs], axis=0)
    low = (kv_heads + head) * ADIM
    values = jnp.concatenate([ref[:, low : low + ADIM] for ref in kv_refs], axis=0)
    values = jnp.concatenate([values, jnp.ones((count, ADIM), BF16)], axis=1)
    lows = [(head * share + part) * ADIM for part in range(share)]
    asking = jnp.concatenate([q_ref[:, low : low + ADIM] for low in lows], axis=0)
    scores = lax.dot_general(asking, keys, (((1,), (1,)), ((), ())), preferred_element_type=F32)
    return jnp.where(allowed, scores * ADIM ** (-0.5), BARRED), values


class Blocks(NamedTuple):
    farthest: int
    count: int


def fold(q_ref, kv_refs, begin_ref, blocks, share, head, carry):
    lows = [(head * share + part) * ADIM for part in range(share)]
    scores, values = attend(q_ref, kv_refs, begin_ref, blocks, share, head)
    peak = jnp.max(scores, axis=1, keepdims=True)
    peak = jnp.broadcast_to(peak, (peak.shape[0], ADIM))
    if carry is not None:
        sums, totals, before = (
            jnp.concatenate([ref[:, low : low + ADIM] for low in lows], axis=0) for ref in carry
        )
        peak = jnp.maximum(peak, before)
    expo = jnp.exp(scores - jnp.concatenate([peak] * (scores.shape[1] // ADIM), axis=1))
    summed = jnp.dot(expo.astype(BF16), values, preferred_element_type=F32)
    if carry is None:
        return lows, summed[:, :ADIM], summed[:, ADIM:], peak
    factor = jnp.exp(before - peak)
    return lows, sums * factor + summed[:, :ADIM], totals * factor + summed[:, ADIM:], peak


def own_kernel(q_ref, keys_ref, values_ref, begin_ref, *outs):
    kv_ref = outs[3]
    kv_width = keys_ref.shape[1]
    kv_ref[:, :kv_width] = keys_ref[...]
    kv_ref[:, kv_width:] = values_ref[...]
    rows = q_ref.shape[0]
    share = QHEADS // KVHEADS
    for head in range(kv_width // ADIM):
        lows, *results = fold(q_ref, (kv_ref,), begin_ref, Blocks(0, 1), share, head, None)
        for ref, result in zip(outs, results):
            for part, low in enumerate(lows):
                ref[:, low : low + ADIM] = result[part * rows : (part + 1) * rows]


def near_kernel(q_ref, before_ref, begin_ref, *refs):
    carry, outs = refs[:3], refs[4:]
    outs[3][...] = before_ref[...]
    rows = q_ref.shape[0]
    share = QHEADS // KVHEADS
    for head in range(before_ref.shape[1] // (2 * ADIM)):
        lows, *results = fold(q_ref, (before_ref,), begin_ref, Blocks(1, 1), share, head, carry)
        for ref, result in zip(outs, results):
            for part, low in enumerate(lows):
                ref[:, low : low + ADIM] = result[part * rows : (part + 1) * rows]


def far_kernel(hops, *refs):
    q_ref, begin_ref = refs[:2]
    kv_refs = refs[5 : 4 + hops]
    out_hbm_ref, out_ref, sems = refs[4 + hops :]
    rows = q_ref.shape[0]
    share = QHEADS // KVHEADS
    copies = []
    for head in range(kv_refs[0].shape[1] // (2 * ADIM)):
        blocks = Blocks(hops, hops - 1)
        lows, sums, totals, _ = fold(q_ref, kv_refs, begin_ref, blocks, share, head, refs[2:5])
        result = (sums / totals).astype(BF16)
        for part, low in enumerate(lows):
            out_ref[:, low : low + ADIM] = result[part * rows : (part + 1) * rows]
        columns = pl.ds(head * share * ADIM, share * ADIM)
        copies.append(
            pltpu.make_async_copy(out_ref.at[:, columns], out_hbm_ref.at[:, columns], sems.at[head])
        )
        copies[-1].start()
    for copy in copies:
        copy.wait()


def norm_kernel(part, hops, first, where, given, *refs):
    local_ref, decay_ref, c_ref, gain_ref, flag_ref = refs[:5]
    got_refs = refs[5 : 5 + hops]
    out_hbm_ref, *token_refs = refs[5 + hops + given : -3]
    gated_ref, out_ref, sems = refs[-3:]
    for ref in token_refs:
        ref[...] = jnp.zeros_like(ref)

    def work():
        rows, width = gated_ref.shape
        outputs = c_ref[:, part * STATE : (part + 1) * STATE]
        squares = jnp.zeros((rows, 128), F32)
        for start in range(0, width, CHUNK):
            columns = slice(start, start + CHUNK)
            placed = slice(part * width + start, part * width + start + CHUNK)
            state = got_refs[0][:STATE, columns]
            for hop in range(1, hops):
                there = flag_ref[first + hop, 0:1] > 0.5
                state = jnp.where(there, got_refs[hop][:STATE, columns].astype(F32), state.astype(F32))
            carried = jnp.dot(outputs, state.astype(BF16), preferred_element_type=F32)
            gated = local_ref[:, placed] + carried * decay_ref[:, placed]
            gated_ref[:, columns] = gated
            for lane in range(0, CHUNK, 128):
                squares = squares + gated[:, lane : lane + 128] * gated[:, lane : lane + 128]
        squares = jnp.sum(squares, axis=1, keepdims=True)
        multiplier = lax.rsqrt(squares * (1.0 / width) + EPSILON)
        copies = []
        for start in range(0, width, CHUNK):
            columns = slice(start, start + CHUNK)
            gain = gain_ref[part * width + start : part * width + start + CHUNK]
            out_ref[:, columns] = (gated_ref[:, columns] * multiplier * gain.reshape(1, -1)).astype(BF16)
            copies.append(
                pltpu.make_async_copy(
                    out_ref.at[:, pl.ds(start, CHUNK)],
                    out_hbm_ref.at[:, pl.ds(part * width + start, CHUNK)],
                    sems.at[start // CHUNK],
                )
            )
            copies[-1].start()
        for copy in copies:
            copy.wait()

    odd = lax.axis_index("dp") % 2 == 1
    later = sum(flag_ref[hop, 0, 0] for hop in range(1, flag_ref.shape[0])) > 0.5
    here = {"odd": odd, "rest": jnp.logical_not(odd) | later, "first": jnp.logical_not(later), "later": later}
    pl.when(here[where])(work)


WHOLE = pl.BlockSpec(memory_space=pltpu.VMEM)
SCALARS = pl.BlockSpec(memory_space=pltpu.SMEM)
UNTOUCHED = pl.BlockSpec(memory_space=pl.ANY)


def tile(rows, columns, row, column):
    return pl.BlockSpec((rows, columns), lambda step: (row, column))


def call(kernel, name, outs, operands, specs, out_specs=None, scratch=(), flops=KERNEL_FLOPS, aliases={}, limit=VMEM_LIMIT):
    moved = sum(math.prod(a.shape) * a.dtype.itemsize for a in (*operands, *outs))
    return pl.pallas_call(
        kernel,
        name=name,
        grid=(1,),
        out_shape=outs,
        in_specs=specs,
        out_specs=[WHOLE] * len(outs) if out_specs is None else out_specs,
        scratch_shapes=list(scratch),
        input_output_aliases=aliases,
        compiler_params=pltpu.CompilerParams(vmem_limit_bytes=limit),
        cost_estimate=pl.CostEstimate(flops=flops, bytes_accessed=moved, transcendentals=0),
    )(*operands)


def onward(value, first=0):
    count = lax.axis_size("seq")
    return lax.ppermute(value, "seq", [(source, source + 1) for source in range(first, count - 1)])


def shards(
    x_raw,
    bc_raw,
    z_gate,
    dt_raw,
    conv_x_weight,
    conv_x_bias,
    conv_bc_weight,
    conv_bc_bias,
    dt_bias,
    a_log,
    skip_d,
    norm_gain,
    queries,
    keys,
    values,
    doc_lens,
):
    rows, width = x_raw.shape
    bc_width = bc_raw.shape[1]
    heads = dt_raw.shape[1]
    groups = bc_width // (2 * STATE)
    per_group = width // groups
    count = lax.axis_size("seq")
    longest = rows * count // 2
    hops = min(count - 1, -(-(longest - 1) // rows))
    assert hops * rows >= longest and (hops == 2 or hops > 2 and groups == 1)
    shape = jax.ShapeDtypeStruct
    dt = dt_raw.T
    params = [dt, conv_x_weight, conv_x_bias, conv_bc_weight, conv_bc_bias, dt_bias, a_log]
    pieces = -(-(width + bc_width) // per_group)
    tail_rows = EDGE * -(-4 * pieces // EDGE)

    (message,) = call(
        first_state_kernel,
        "first_state",
        [shape((STATE + tail_rows, per_group), BF16)],
        [x_raw, bc_raw, *(a if a.ndim > 1 else a[None] for a in params), doc_lens],
        [UNTOUCHED] * 10,
        out_specs=[UNTOUCHED],
        scratch=[
            pltpu.VMEM((rows, per_group), BF16),
            pltpu.VMEM((rows, STATE), BF16),
            pltpu.VMEM((per_group // HDIM, rows), F32),
            pltpu.VMEM((conv_x_weight.shape[0], per_group), F32),
            pltpu.VMEM((1, per_group), F32),
            pltpu.VMEM((conv_x_weight.shape[0], STATE), F32),
            pltpu.VMEM((1, STATE), F32),
            pltpu.VMEM((1, heads), F32),
            pltpu.VMEM((1, heads), F32),
            pltpu.SMEM(doc_lens.shape, jnp.int32),
            pltpu.VMEM((EDGE, width), BF16),
            pltpu.VMEM((EDGE, bc_width), BF16),
            pltpu.VMEM((STATE + tail_rows, per_group), BF16),
            pltpu.VMEM((rows + 8, STATE), F32),
            pltpu.VMEM((4, rows + 8, CHUNK), F32),
            pltpu.SemaphoreType.DMA((12,)),
            pltpu.SemaphoreType.DMA((per_group // (2 * CHUNK) + 1,)),
        ],
        limit=VMEM_ALL,
    )
    slots = [onward(message)]
    prepared = call(
        functools.partial(prepare_kernel, hops, groups),
        "prepare",
        [
            shape((rows, width), BF16),
            shape((rows, bc_width), BF16),
            shape((8, width + bc_width), F32),
            shape((8, width), F32),
            shape((8, width), F32),
            shape((conv_x_weight.shape[0] - 1, 8, CHUNK), F32),
            shape((hops, 8, CHUNK), F32),
            shape((8, width), F32),
            shape((rows, rows), jnp.int32),
            shape((rows, heads), F32),
            shape((rows, heads), F32),
            shape((rows, width), F32),
            shape((rows, width), F32),
            shape((rows, width), F32),
            *(shape((STATE, per_group), BF16) for _ in range(groups - 1)),
        ],
        [x_raw, bc_raw, *params, skip_d, doc_lens, z_gate],
        [WHOLE] * 10 + [SCALARS] + [WHOLE],
        scratch=[
            pltpu.VMEM((16, width + bc_width), F32),
            pltpu.VMEM((4, rows + 8, CHUNK), F32),
        ],
    )
    _, bcc, partial, weight, through, inside, flags, wide_skip, begin, *prepared = prepared
    step, running, main, gate, decay, *states = prepared
    states = [message, *states]
    carried = [shape(queries.shape, F32)] * 3 + [shape((rows, 2 * keys.shape[1]), BF16)]
    *carry, kv = call(own_kernel, "attend_own", carried, [queries, keys, values, begin], [WHOLE] * 4)
    kvs = [kv, onward(kv)]
    fulls = None
    for slot in range(2, hops + groups):
        part = min(slot - 1, groups) - 1
        fresh = slot <= groups
        if slot == 2:
            kernel = functools.partial(relay_first_kernel, fresh)
            operands = [slots[0], states[0], partial, weight, through, inside, flags, conv_x_weight, conv_bc_weight]
            scratch = [pltpu.VMEM((4, 16, CHUNK), F32)]
        else:
            kernel = functools.partial(relay_kernel, part, fresh)
            operands = [slots[-1], fulls[part], through, flags]
            scratch = []
        if fresh:
            operands.append(states[slot - 1])
        (passed,) = call(
            kernel,
            f"relay_slot{slot}",
            [shape((STATE, per_group), BF16)],
            operands,
            [WHOLE] * len(operands),
            scratch=scratch,
        )
        slots.append(onward(passed, max(0, slot - groups)))
        if fulls is None:
            gated, c_out, *fulls = call(
                functools.partial(first_rows_kernel, groups),
                "first_rows",
                [
                    shape((rows, width), F32),
                    shape((rows, groups * STATE), BF16),
                    *(shape((STATE, per_group), BF16) for _ in range(groups)),
                ],
                [
                    slots[0], partial, weight, inside, conv_x_weight, conv_bc_weight, step, running,
                    wide_skip, begin, bcc, main, gate, *states,
                ],
                [WHOLE] * (13 + groups),
                scratch=[pltpu.VMEM((4, 16, CHUNK), F32)],
            )
    def norm(part, first, stop, where, out=None, token=False):
        got = slots[part + first : part + stop]
        operands = [gated, decay, c_out, norm_gain, flags, *got]
        specs = [WHOLE] * len(operands)
        outs = [shape((rows, width), BF16)] + [shape((8, 128), F32)] * token
        aliases = {}
        if out is not None:
            aliases = {len(operands): 0}
            operands.append(out)
            specs.append(UNTOUCHED)
        return call(
            functools.partial(norm_kernel, part, len(got), first, where, out is not None),
            f"norm_part{part}_{where}",
            outs,
            operands,
            specs,
            out_specs=[UNTOUCHED] + [WHOLE] * token,
            scratch=[
                pltpu.VMEM((rows, per_group), F32),
                pltpu.VMEM((rows, per_group), BF16),
                pltpu.SemaphoreType.DMA((per_group // CHUNK,)),
            ],
            aliases=aliases,
            flops=KERNEL_FLOPS // 2,
        )

    mamba_out, token = None, c_out
    for part in range(groups - 1):
        mamba_out, token = norm(part, 0, 1, "odd", mamba_out, True)
    *carry, kv_on = call(
        near_kernel,
        "attend_near",
        carried,
        [queries, kvs[1], begin, *carry, token],
        [WHOLE] * 6 + [UNTOUCHED],
    )
    for hop in range(1, hops):
        kvs.append(onward(kv_on if hop == 1 else kvs[-1], hop))
    (attn_out,) = call(
        functools.partial(far_kernel, hops),
        "attend_far",
        [shape(queries.shape, BF16)],
        [queries, begin, *carry, *reversed(kvs[2:])],
        [WHOLE] * (4 + hops),
        out_specs=[UNTOUCHED],
        scratch=[
            pltpu.VMEM(queries.shape, BF16),
            pltpu.SemaphoreType.DMA((keys.shape[1] // ADIM,)),
        ],
    )
    for part in range(groups - 1):
        (mamba_out,) = norm(part, 0, hops, "rest", mamba_out)
    (mamba_out,) = norm(groups - 1, 0, 1, "first", mamba_out)
    (mamba_out,) = norm(groups - 1, 1, hops, "later", mamba_out)
    return (mamba_out, attn_out)


def solution(mesh):
    split = P(("groups", "seq"), "dp")
    placed = (
        split,
        split,
        split,
        split,
        P(None, "dp"),
        P("dp"),
        P(None, "dp"),
        P("dp"),
        P("dp"),
        P("dp"),
        P("dp"),
        P("dp"),
        split,
        split,
        split,
        P("groups"),
    )
    return jax.shard_map(
        shards,
        mesh=mesh,
        in_specs=placed,
        out_specs=(split, split),
        check_vma=False,
    )
```

```python
import functools
import math
from typing import NamedTuple

import jax
import jax.numpy as jnp
from jax import lax
from jax.experimental import pallas as pl
from jax.experimental.pallas import tpu as pltpu
from jax.sharding import PartitionSpec as P

HDIM = 64
STATE = 128
QHEADS = 32
KVHEADS = 8
ADIM = 128
EPSILON = 1e-05
BARRED = -2e30
HIGHEST = lax.Precision.HIGHEST
F32 = jnp.float32
BF16 = jnp.bfloat16
CHUNK = 256
EDGE = 16
KERNEL_FLOPS = 2 * 10**9
VMEM_LIMIT = 40 * 1024 * 1024
VMEM_ALL = 62 * 1024 * 1024


def silu(value):
    return value * (0.5 * jnp.tanh(0.5 * value) + 0.5)


def softplus(value):
    return jnp.maximum(value, 0.0) + jnp.log(1.0 + jnp.exp(-jnp.abs(value)))


def doc_start(positions, lens_ref):
    begin = jnp.int32(0)
    found = positions * 0
    for doc in range(lens_ref.shape[0]):
        found = jnp.where(positions >= begin, begin, found)
        begin = begin + lens_ref[doc]
    return found


def halves(value):
    high = value.astype(BF16)
    return high, (value - high.astype(F32)).astype(BF16)


def widen(per_head, first, width):
    heads = per_head.shape[1]
    both = jnp.concatenate(halves(per_head), axis=1)
    head = lax.broadcasted_iota(jnp.int32, (2 * heads, width), 0)
    head = jnp.where(head >= heads, head - heads, head)
    channel = lax.broadcasted_iota(jnp.int32, (2 * heads, width), 1) + first
    spread = (channel // HDIM == head).astype(F32).astype(BF16)
    return jnp.dot(both, spread, preferred_element_type=F32)


def rates(dt_ref, dt_bias_ref, a_log_ref):
    heads = dt_ref.shape[0]
    step = softplus(dt_ref[...].T + dt_bias_ref[...].reshape(1, -1)[:, :heads])
    rate = -step * jnp.exp(a_log_ref[...].reshape(1, -1)[:, :heads])
    rows = step.shape[0]
    row = lax.broadcasted_iota(jnp.int32, (rows, rows), 0)
    column = lax.broadcasted_iota(jnp.int32, (rows, rows), 1)
    lower = (row >= column).astype(F32).astype(BF16)
    high = rate.astype(BF16)
    middle, low = halves(rate - high.astype(F32))
    parts = jnp.concatenate([high, middle, low], axis=0)
    lowers = jnp.concatenate([lower, lower, lower], axis=1)
    return step, jnp.dot(lowers, parts, preferred_element_type=F32)


def insides(first, shape, taps, lens_ref):
    positions = first + lax.broadcasted_iota(jnp.int32, shape, 0)
    depth = positions - doc_start(positions, lens_ref)
    return [depth >= lag for lag in range(taps)]


def conv(pad, rows, weight, bias, inside):
    taps = weight.shape[0]
    total = pad[8 : 8 + rows] * weight[taps - 1 : taps] + bias
    for lag in range(1, taps):
        term = pad[8 - lag : 8 - lag + rows] * weight[taps - 1 - lag : taps - lag]
        total = total + jnp.where(inside[lag], term, 0.0)
    return silu(total)


def tail_lines(message, rows):
    block = message[rows:].astype(F32)
    return jnp.concatenate([block[at : at + 4] for at in range(0, block.shape[0], 4)], axis=1)


def reach(device, rows, lens_ref):
    return device - doc_start((device + 1) * rows - 1, lens_ref) // rows


def kept_weight(here, step, running, taps, lens_ref):
    rows = step.shape[0]
    last_begin = doc_start((here + 1) * rows - 1, lens_ref)
    row = lax.broadcasted_iota(jnp.int32, step.shape, 0)
    weight = step * jnp.exp(running[rows - 1 : rows] - running)
    kept = (here * rows + row >= last_begin) & ((row >= taps - 1) | (last_begin // rows >= here))
    return jnp.where(kept, weight, 0.0)


def conv_rows(pad, raw, weight, bias, inside):
    pad[0:8] = jnp.zeros((8, raw.shape[1]), F32)
    pad[8:] = raw.astype(F32)
    return conv(pad, raw.shape[0], weight, bias.reshape(1, -1), inside)


def first_state_kernel(*refs):
    hbm_refs, out_hbm_ref = refs[:10], refs[10]
    vmem_refs = refs[11:21]
    x_edge_ref, bc_edge_ref, out_ref, b_pad_ref, pad_ref, in_sems, out_sems = refs[21:]
    x_ref, b_ref, dt_ref, wx_ref, bx_ref, wbc_ref, bbc_ref, dt_bias_ref, a_log_ref, lens_ref = vmem_refs
    rows, width = x_ref.shape
    taps = wx_ref.shape[0]

    def corner(ref, shape):
        return ref.at[tuple(pl.ds(0, extent) for extent in shape)]

    order = (9, 2, 7, 8, 1, 5, 6, 0, 3, 4)
    copies = {}
    for at in order:
        source = corner(hbm_refs[at], vmem_refs[at].shape)
        copies[at] = pltpu.make_async_copy(source, vmem_refs[at], in_sems.at[at])
        copies[at].start()
    edge_copies = []
    for at, (source, target) in enumerate(((hbm_refs[0], x_edge_ref), (hbm_refs[1], bc_edge_ref))):
        edge_copies.append(
            pltpu.make_async_copy(source.at[pl.ds(rows - EDGE, EDGE)], target, in_sems.at[10 + at])
        )
        edge_copies[-1].start()

    here = lax.axis_index("seq")
    for at in (9, 2, 7, 8):
        copies[at].wait()
    inside = insides(here * rows, (rows, CHUNK), taps, lens_ref)
    step, running = rates(dt_ref, dt_bias_ref, a_log_ref)
    weight = kept_weight(here, step, running, taps, lens_ref)
    narrow = [mask[:, :STATE] for mask in inside]
    for at in (1, 5, 6):
        copies[at].wait()
    inputs = conv_rows(b_pad_ref, b_ref[...], wbc_ref[...], bbc_ref[...], narrow)
    turned = inputs.T.astype(BF16)
    for at in (0, 3, 4):
        copies[at].wait()
    slots = pad_ref.shape[0]
    outs = []

    def send(at, view):
        copy = pltpu.make_async_copy(out_ref.at[view], out_hbm_ref.at[view], out_sems.at[at])
        copy.start()
        outs.append(copy)

    for at, start in enumerate(range(0, width, CHUNK)):
        columns = slice(start, start + CHUNK)
        pad = pad_ref.at[(at + 1) % slots]
        xc = conv_rows(pad, x_ref[:, columns], wx_ref[:, columns], bx_ref[:, columns], inside)
        weighted = (xc * widen(weight, start, CHUNK)).astype(BF16)
        out_ref[:STATE, columns] = jnp.dot(turned, weighted, preferred_element_type=F32).astype(BF16)
        if at % 2:
            send(at // 2, (pl.ds(0, STATE), pl.ds(start - CHUNK, 2 * CHUNK)))
    for copy in edge_copies:
        copy.wait()
    edges = jnp.concatenate([x_edge_ref[...].astype(F32), bc_edge_ref[...].astype(F32)], axis=1)[EDGE - 4 :]
    spare = -edges.shape[1] % width
    if spare:
        edges = jnp.concatenate([edges, jnp.zeros((4, spare), F32)], axis=1)
    pieces = [edges[:, at : at + width] for at in range(0, edges.shape[1], width)]
    while len(pieces) % (EDGE // 4):
        pieces.append(jnp.zeros_like(pieces[0]))
    out_ref[STATE:] = jnp.concatenate(pieces, axis=0).astype(BF16)
    send(width // (2 * CHUNK), (pl.ds(STATE, out_ref.shape[0] - STATE), pl.ds(0, width)))
    for copy in outs:
        copy.wait()


def prepare_kernel(hops, groups, *refs):
    x_ref, bc_ref, dt_ref, wx_ref, bx_ref, wbc_ref, bbc_ref, dt_bias_ref, a_log_ref, skip_ref, lens_ref = refs[:11]
    z_ref = refs[11]
    xc_ref, bcc_ref, partial_ref, weight_ref, through_ref, inside_ref, flag_ref = refs[12:19]
    wide_skip_ref, begin_ref, step_ref, running_ref, out_ref, gate_ref, decay_ref = refs[19:26]
    state_refs = refs[26:-2]
    top_ref, pad_ref = refs[-2:]
    rows, width = x_ref.shape
    per_group = width // groups
    taps = wx_ref.shape[0]
    slots = pad_ref.shape[0]
    here = lax.axis_index("seq")
    first = here * rows
    inside = insides(first, (rows, CHUNK), taps, lens_ref)
    step, running = rates(dt_ref, dt_bias_ref, a_log_ref)
    heads = step.shape[1]
    group_heads = heads // groups
    kept = kept_weight(here, step, running, taps, lens_ref)
    for group in range(groups):
        base = slice(group * 2 * STATE, (group + 1) * 2 * STATE)
        pair = conv_rows(pad_ref.at[0], bc_ref[:, base], wbc_ref[:, base], bbc_ref[base], inside)
        bcc_ref[:, base] = pair.astype(BF16)
        turned = pair[:, :STATE].T.astype(BF16)
        part_weight = kept[:, group * group_heads : (group + 1) * group_heads]
        for chunk in range(0, per_group, CHUNK):
            columns = slice(group * per_group + chunk, group * per_group + chunk + CHUNK)
            pad = pad_ref.at[(chunk // CHUNK + 1) % slots]
            xc = conv_rows(pad, x_ref[:, columns], wx_ref[:, columns], bx_ref[columns], inside)
            xc_ref[:, columns] = xc.astype(BF16)
            if group:
                weighted = (xc * widen(part_weight, chunk, CHUNK)).astype(BF16)
                state_refs[group - 1][:, chunk : chunk + CHUNK] = jnp.dot(
                    turned, weighted, preferred_element_type=F32
                ).astype(BF16)

    own = reach(here, rows, lens_ref) == 0
    inside = [mask[:8] for mask in inside]
    for lag in range(1, taps):
        inside_ref[lag - 1] = inside[lag].astype(F32)
    flag_ref[0] = jnp.broadcast_to(own.astype(F32), (8, CHUNK))
    before = reach(here - 1, rows, lens_ref)
    for hop in range(1, hops):
        flag_ref[hop] = jnp.broadcast_to((before == hop).astype(F32), (8, CHUNK))
    begin = doc_start(first + lax.broadcasted_iota(jnp.int32, begin_ref.shape, 0), lens_ref)
    begin_ref[...] = begin
    entry = jnp.where(begin[:, :heads] < first, jnp.exp(running), 0.0)
    step_ref[...] = step
    running_ref[...] = running
    row = lax.broadcasted_iota(jnp.int32, (8, heads), 0)
    total = running[rows - 1 : rows]
    weight = step[:8] * jnp.exp(total - running[:8])
    weight = jnp.where((row < taps - 1) & jnp.logical_not(own), weight, 0.0)
    through = jnp.where(own, 0.0, jnp.broadcast_to(jnp.exp(total), (8, heads)))
    skip = jnp.broadcast_to(skip_ref[...].reshape(1, -1), (8, heads))
    every = jnp.concatenate([weight, through, skip], axis=0)
    for start in range(0, width, CHUNK):
        wide = widen(every, start, CHUNK)
        weight_ref[:, start : start + CHUNK] = wide[:8]
        through_ref[:, start : start + CHUNK] = wide[8:16]
        wide_skip_ref[:, start : start + CHUNK] = wide[16:]
    top_ref[0:8] = jnp.zeros((8, top_ref.shape[1]), F32)
    top_ref[8:, :width] = x_ref[:EDGE].astype(F32)[:8]
    top_ref[8:, width:] = bc_ref[:EDGE].astype(F32)[:8]

    def some(columns, base, w_ref, b_ref):
        here_columns = slice(base + columns.start, base + columns.stop)
        total = top_ref[8:, here_columns] * w_ref[taps - 1 : taps, columns] + b_ref[columns].reshape(1, -1)
        for lag in range(1, taps):
            term = top_ref[8 - lag : 16 - lag, here_columns] * w_ref[taps - 1 - lag : taps - lag, columns]
            total = total + jnp.where(inside[lag], term, 0.0)
        partial_ref[:, here_columns] = total

    for start in range(0, width, CHUNK):
        some(slice(start, start + CHUNK), 0, wx_ref, bx_ref)
    for start in range(0, bc_ref.shape[1], CHUNK):
        some(slice(start, start + CHUNK), width, wbc_ref, bbc_ref)

    row = lax.broadcasted_iota(jnp.int32, (rows, rows), 0)
    lane = lax.broadcasted_iota(jnp.int32, (rows, rows), 1)
    linked = (row >= lane) & (first + lane >= begin) & (lane >= 8)
    turned_running = running.T
    turned_step = step.T
    pair_width = 2 * HDIM
    channel = lax.broadcasted_iota(jnp.int32, (rows, pair_width), 1)
    below = lax.broadcasted_iota(jnp.int32, (rows, CHUNK), 0) >= 8
    for group in range(groups):
        base = group * 2 * STATE
        meet = lax.dot_general(
            bcc_ref[:, base + STATE : base + 2 * STATE],
            bcc_ref[:, base : base + STATE],
            (((1,), (1,)), ((), ())),
            preferred_element_type=F32,
        )
        meet = jnp.where(linked, meet, 0.0)
        group_entry = entry[:, group * group_heads : (group + 1) * group_heads]
        for chunk in range(0, per_group, CHUNK):
            at = group * per_group + chunk
            columns = slice(at, at + CHUNK)
            gate = silu(z_ref[:, columns].astype(F32))
            gate_ref[:, columns] = gate
            decay_ref[:, columns] = widen(group_entry, chunk, CHUNK) * gate
            xc_all = xc_ref[:, columns]
            skipped = jnp.where(below, xc_all.astype(F32) * wide_skip_ref[0:1, columns], 0.0)
            for start in range(0, CHUNK, pair_width):
                parts = []
                for head in ((at + start) // HDIM, (at + start) // HDIM + 1):
                    spread = running[:, head : head + 1] - turned_running[head : head + 1]
                    decay = jnp.exp(jnp.minimum(spread, 0.0))
                    parts.append((decay * (meet * turned_step[head : head + 1])).astype(BF16))
                mix = jnp.concatenate(parts, axis=1)
                here_columns = slice(start, start + pair_width)
                xc = xc_all[:, here_columns]
                zero = jnp.zeros_like(xc)
                stacked = jnp.concatenate(
                    [jnp.where(channel < HDIM, xc, zero), jnp.where(channel < HDIM, zero, xc)], axis=0
                )
                value = jnp.dot(mix, stacked, preferred_element_type=F32) + skipped[:, here_columns]
                out_ref[:, at + start : at + start + pair_width] = value * gate[:, here_columns]


def first_rows(lines, partial_ref, inside_ref, w_ref, pad_ref, slot, at, start):
    taps = w_ref.shape[0]
    columns = slice(start, start + CHUNK)
    pad = pad_ref.at[slot]
    pad[4:8] = lines[:, at + start : at + start + CHUNK]
    pad[8:] = jnp.zeros((8, CHUNK), F32)
    total = partial_ref[:, at + start : at + start + CHUNK]
    for lag in range(1, taps):
        term = pad[8 - lag : 16 - lag] * w_ref[taps - 1 - lag : taps - lag, columns]
        total = total + term * inside_ref[lag - 1]
    return silu(total)


def sixteen(value):
    return jnp.concatenate([value, jnp.zeros_like(value)], axis=0).astype(BF16)


def relay_first_kernel(fresh, *refs):
    message_ref, state_ref, partial_ref, weight_ref, through_ref, inside_ref, flag_ref, wx_ref, wbc_ref = refs[:9]
    other_ref = refs[9] if fresh else state_ref
    out_ref, pad_ref = refs[-2:]
    width = out_ref.shape[1]
    slots = pad_ref.shape[0]
    own = flag_ref[0, 0, 0] > 0.5

    @pl.when(own)
    def _():
        out_ref[...] = other_ref[:STATE]

    @pl.when(jnp.logical_not(own))
    def _():
        lines = tail_lines(message_ref, STATE)
        top = functools.partial(first_rows, lines, partial_ref, inside_ref)
        inputs = top(wbc_ref, pad_ref, 0, wx_ref.shape[1], 0)[:, :STATE]
        turned = jnp.concatenate([inputs, inputs], axis=0).T.astype(BF16)
        for start in range(0, width, CHUNK):
            columns = slice(start, start + CHUNK)
            xc = top(wx_ref, pad_ref, (start // CHUNK + 1) % slots, 0, start)
            weighted = sixteen(xc * weight_ref[:, columns])
            full = state_ref[:STATE, columns].astype(F32) + jnp.dot(
                turned, weighted, preferred_element_type=F32
            )
            full = full + through_ref[0:1, columns] * message_ref[:STATE, columns].astype(F32)
            out_ref[:, columns] = full.astype(BF16)


def relay_kernel(part, fresh, *refs):
    got_ref, state_ref, through_ref, flag_ref = refs[:4]
    out_ref = refs[-1]
    width = out_ref.shape[1]
    own = flag_ref[0, 0:1] > 0.5
    for start in range(0, width, CHUNK):
        columns = slice(start, start + CHUNK)
        through = through_ref[0:1, part * width + start : part * width + start + CHUNK]
        full = state_ref[:, columns].astype(F32) + through * got_ref[:STATE, columns].astype(F32)
        if fresh:
            full = jnp.where(own, refs[4][:STATE, columns].astype(F32), full)
        out_ref[:, columns] = full.astype(BF16)


def first_rows_kernel(groups, *refs):
    (
        message_ref, partial_ref, weight_ref, inside_ref, wx_ref, wbc_ref, step_ref, running_ref,
        wide_skip_ref, begin_ref, bcc_ref, main_ref, gate_ref,
    ) = refs[:13]
    state_refs = refs[13 : 13 + groups]
    out_ref, c_ref = refs[13 + groups : 15 + groups]
    full_refs = refs[15 + groups : 15 + 2 * groups]
    pad_ref = refs[-1]
    rows, width = main_ref.shape
    per_group = width // groups
    heads = per_group // HDIM
    lanes = 8 * heads
    first = lax.axis_index("seq") * rows
    lines = tail_lines(message_ref, STATE)
    slots = pad_ref.shape[0]
    top = functools.partial(first_rows, lines, partial_ref, inside_ref)
    lane = lax.broadcasted_iota(jnp.int32, (rows, lanes), 1)
    line = lane & 7
    row = lax.broadcasted_iota(jnp.int32, (rows, lanes), 0)
    begin = jnp.concatenate([begin_ref[...]] * -(-lanes // rows), axis=1)[:, :lanes]
    linked = (row >= line) & (first + line >= begin)
    head = lax.broadcasted_iota(jnp.int32, (3 * heads, lanes), 0)
    for _ in range(2):
        head = jnp.where(head >= heads, head - heads, head)
    spread = (lax.broadcasted_iota(jnp.int32, (3 * heads, lanes), 1) >> 3 == head).astype(F32).astype(BF16)
    own_line = lax.broadcasted_iota(jnp.int32, (8, lanes), 0) == line[:8]

    def to_lanes(value):
        high = value.astype(BF16)
        middle, low = halves(value - high.astype(F32))
        return jnp.dot(jnp.concatenate([high, middle, low], axis=1), spread, preferred_element_type=F32)

    def by_line(value):
        return jnp.sum(jnp.where(own_line, value, 0.0), axis=0, keepdims=True)

    channel = lax.broadcasted_iota(jnp.int32, (8, CHUNK), 1)
    for group in range(groups):
        base = group * 2 * STATE
        these = slice(group * heads, (group + 1) * heads)
        new = top(wbc_ref, pad_ref, group % slots, width, base)
        old = bcc_ref[:, base + STATE : base + 2 * STATE]
        outputs = jnp.concatenate([new[:, STATE:], old[:EDGE].astype(F32)[8:]], axis=0).astype(BF16)
        outputs = jnp.concatenate([outputs, old[EDGE:]], axis=0)
        c_ref[:, group * STATE : (group + 1) * STATE] = outputs
        inputs = jnp.concatenate([new[:, :STATE]] * heads, axis=0).astype(BF16)
        meet = lax.dot_general(
            outputs, inputs, (((1,), (1,)), ((), ())), preferred_element_type=F32
        )
        running = to_lanes(running_ref[:, these])
        decay = jnp.exp(jnp.minimum(running - by_line(running[:8]), 0.0))
        mix = decay * (meet * by_line(to_lanes(step_ref[:8, these])))
        mix = jnp.where(linked, mix, 0.0).astype(BF16)
        turned = inputs[:EDGE].astype(F32).T.astype(BF16)
        for chunk in range(0, per_group, CHUNK):
            at = group * per_group + chunk
            columns = slice(at, at + CHUNK)
            xc = top(wx_ref, pad_ref, (chunk // CHUNK + 1) % slots, 0, at)
            full = state_refs[group][:STATE, chunk : chunk + CHUNK].astype(F32) + jnp.dot(
                turned, sixteen(xc * weight_ref[:, columns]), preferred_element_type=F32
            )
            full_refs[group][:, chunk : chunk + CHUNK] = full.astype(BF16)
            blocks = []
            for at_head in range(heads):
                low = at_head * HDIM - chunk
                if 0 <= low < CHUNK:
                    blocks.append(jnp.where((channel >= low) & (channel < low + HDIM), xc, 0.0))
                else:
                    blocks.append(jnp.zeros_like(xc))
            spread_xc = jnp.concatenate(blocks, axis=0).astype(BF16)
            gate = gate_ref[:, columns]
            value = main_ref[:, columns] + gate * jnp.dot(mix, spread_xc, preferred_element_type=F32)
            out_ref[:, columns] = value
            out_ref[0:8, columns] = value[:8] + gate[:8] * (xc * wide_skip_ref[:, columns])


def attend(q_ref, kv_refs, begin_ref, blocks, share, head):
    rows = q_ref.shape[0]
    kv_heads = kv_refs[0].shape[1] // (2 * ADIM)
    count = rows * blocks.count
    here = lax.axis_index("seq")
    row = here * rows + lax.broadcasted_iota(jnp.int32, (rows, count), 0)
    lane = (here - blocks.farthest) * rows + lax.broadcasted_iota(jnp.int32, (rows, count), 1)
    begin = jnp.concatenate([begin_ref[...]] * blocks.count, axis=1)
    allowed = jnp.concatenate([(lane <= row) & (lane >= begin)] * share, axis=0)
    low = head * ADIM
    keys = jnp.concatenate([ref[:, low : low + ADIM] for ref in kv_refs], axis=0)
    low = (kv_heads + head) * ADIM
    values = jnp.concatenate([ref[:, low : low + ADIM] for ref in kv_refs], axis=0)
    values = jnp.concatenate([values, jnp.ones((count, ADIM), BF16)], axis=1)
    lows = [(head * share + part) * ADIM for part in range(share)]
    asking = jnp.concatenate([q_ref[:, low : low + ADIM] for low in lows], axis=0)
    scores = lax.dot_general(asking, keys, (((1,), (1,)), ((), ())), preferred_element_type=F32)
    return jnp.where(allowed, scores * ADIM ** (-0.5), BARRED), values


class Blocks(NamedTuple):
    farthest: int
    count: int


def fold(q_ref, kv_refs, begin_ref, blocks, share, head, carry):
    lows = [(head * share + part) * ADIM for part in range(share)]
    scores, values = attend(q_ref, kv_refs, begin_ref, blocks, share, head)
    peak = jnp.max(scores, axis=1, keepdims=True)
    peak = jnp.broadcast_to(peak, (peak.shape[0], ADIM))
    if carry is not None:
        sums, totals, before = (
            jnp.concatenate([ref[:, low : low + ADIM] for low in lows], axis=0) for ref in carry
        )
        peak = jnp.maximum(peak, before)
    expo = jnp.exp(scores - jnp.concatenate([peak] * (scores.shape[1] // ADIM), axis=1))
    summed = jnp.dot(expo.astype(BF16), values, preferred_element_type=F32)
    if carry is None:
        return lows, summed[:, :ADIM], summed[:, ADIM:], peak
    factor = jnp.exp(before - peak)
    return lows, sums * factor + summed[:, :ADIM], totals * factor + summed[:, ADIM:], peak


def own_kernel(q_ref, keys_ref, values_ref, begin_ref, *outs):
    kv_ref = outs[3]
    kv_width = keys_ref.shape[1]
    kv_ref[:, :kv_width] = keys_ref[...]
    kv_ref[:, kv_width:] = values_ref[...]
    rows = q_ref.shape[0]
    share = QHEADS // KVHEADS
    for head in range(kv_width // ADIM):
        lows, *results = fold(q_ref, (kv_ref,), begin_ref, Blocks(0, 1), share, head, None)
        for ref, result in zip(outs, results):
            for part, low in enumerate(lows):
                ref[:, low : low + ADIM] = result[part * rows : (part + 1) * rows]


def near_kernel(q_ref, before_ref, begin_ref, *refs):
    carry, outs = refs[:3], refs[4:]
    outs[3][...] = before_ref[...]
    rows = q_ref.shape[0]
    share = QHEADS // KVHEADS
    for head in range(before_ref.shape[1] // (2 * ADIM)):
        lows, *results = fold(q_ref, (before_ref,), begin_ref, Blocks(1, 1), share, head, carry)
        for ref, result in zip(outs, results):
            for part, low in enumerate(lows):
                ref[:, low : low + ADIM] = result[part * rows : (part + 1) * rows]


def far_kernel(hops, *refs):
    q_ref, begin_ref = refs[:2]
    kv_refs = refs[5 : 4 + hops]
    out_hbm_ref, out_ref, sems = refs[4 + hops :]
    rows = q_ref.shape[0]
    share = QHEADS // KVHEADS
    copies = []
    for head in range(kv_refs[0].shape[1] // (2 * ADIM)):
        blocks = Blocks(hops, hops - 1)
        lows, sums, totals, _ = fold(q_ref, kv_refs, begin_ref, blocks, share, head, refs[2:5])
        result = (sums / totals).astype(BF16)
        for part, low in enumerate(lows):
            out_ref[:, low : low + ADIM] = result[part * rows : (part + 1) * rows]
        columns = pl.ds(head * share * ADIM, share * ADIM)
        copies.append(
            pltpu.make_async_copy(out_ref.at[:, columns], out_hbm_ref.at[:, columns], sems.at[head])
        )
        copies[-1].start()
    for copy in copies:
        copy.wait()


def norm_kernel(part, hops, first, where, given, *refs):
    local_ref, decay_ref, c_ref, gain_ref, flag_ref = refs[:5]
    got_refs = refs[5 : 5 + hops]
    out_hbm_ref, *token_refs = refs[5 + hops + given : -3]
    gated_ref, out_ref, sems = refs[-3:]
    for ref in token_refs:
        ref[...] = jnp.zeros_like(ref)

    def work():
        rows, width = gated_ref.shape
        outputs = c_ref[:, part * STATE : (part + 1) * STATE]
        squares = jnp.zeros((rows, 128), F32)
        for start in range(0, width, CHUNK):
            columns = slice(start, start + CHUNK)
            placed = slice(part * width + start, part * width + start + CHUNK)
            state = got_refs[0][:STATE, columns]
            for hop in range(1, hops):
                there = flag_ref[first + hop, 0:1] > 0.5
                state = jnp.where(there, got_refs[hop][:STATE, columns].astype(F32), state.astype(F32))
            carried = jnp.dot(outputs, state.astype(BF16), preferred_element_type=F32)
            gated = local_ref[:, placed] + carried * decay_ref[:, placed]
            gated_ref[:, columns] = gated
            for lane in range(0, CHUNK, 128):
                squares = squares + gated[:, lane : lane + 128] * gated[:, lane : lane + 128]
        squares = jnp.sum(squares, axis=1, keepdims=True)
        multiplier = lax.rsqrt(squares * (1.0 / width) + EPSILON)
        copies = []
        for start in range(0, width, CHUNK):
            columns = slice(start, start + CHUNK)
            gain = gain_ref[part * width + start : part * width + start + CHUNK]
            out_ref[:, columns] = (gated_ref[:, columns] * multiplier * gain.reshape(1, -1)).astype(BF16)
            copies.append(
                pltpu.make_async_copy(
                    out_ref.at[:, pl.ds(start, CHUNK)],
                    out_hbm_ref.at[:, pl.ds(part * width + start, CHUNK)],
                    sems.at[start // CHUNK],
                )
            )
            copies[-1].start()
        for copy in copies:
            copy.wait()

    odd = lax.axis_index("dp") % 2 == 1
    later = sum(flag_ref[hop, 0, 0] for hop in range(1, flag_ref.shape[0])) > 0.5
    here = {"odd": odd, "rest": jnp.logical_not(odd) | later, "first": jnp.logical_not(later), "later": later}
    pl.when(here[where])(work)


WHOLE = pl.BlockSpec(memory_space=pltpu.VMEM)
SCALARS = pl.BlockSpec(memory_space=pltpu.SMEM)
UNTOUCHED = pl.BlockSpec(memory_space=pl.ANY)


def tile(rows, columns, row, column):
    return pl.BlockSpec((rows, columns), lambda step: (row, column))


def call(kernel, name, outs, operands, specs, out_specs=None, scratch=(), flops=KERNEL_FLOPS, aliases={}, limit=VMEM_LIMIT):
    moved = sum(math.prod(a.shape) * a.dtype.itemsize for a in (*operands, *outs))
    return pl.pallas_call(
        kernel,
        name=name,
        grid=(1,),
        out_shape=outs,
        in_specs=specs,
        out_specs=[WHOLE] * len(outs) if out_specs is None else out_specs,
        scratch_shapes=list(scratch),
        input_output_aliases=aliases,
        compiler_params=pltpu.CompilerParams(vmem_limit_bytes=limit),
        cost_estimate=pl.CostEstimate(flops=flops, bytes_accessed=moved, transcendentals=0),
    )(*operands)


def onward(value, first=0):
    count = lax.axis_size("seq")
    return lax.ppermute(value, "seq", [(source, source + 1) for source in range(first, count - 1)])


def shards(
    x_raw,
    bc_raw,
    z_gate,
    dt_raw,
    conv_x_weight,
    conv_x_bias,
    conv_bc_weight,
    conv_bc_bias,
    dt_bias,
    a_log,
    skip_d,
    norm_gain,
    queries,
    keys,
    values,
    doc_lens,
):
    rows, width = x_raw.shape
    bc_width = bc_raw.shape[1]
    heads = dt_raw.shape[1]
    groups = bc_width // (2 * STATE)
    per_group = width // groups
    count = lax.axis_size("seq")
    longest = rows * count // 2
    hops = min(count - 1, -(-(longest - 1) // rows))
    assert hops * rows >= longest and (hops == 2 or hops > 2 and groups == 1)
    shape = jax.ShapeDtypeStruct
    dt = dt_raw.T
    params = [dt, conv_x_weight, conv_x_bias, conv_bc_weight, conv_bc_bias, dt_bias, a_log]
    pieces = -(-(width + bc_width) // per_group)
    tail_rows = EDGE * -(-4 * pieces // EDGE)

    (message,) = call(
        first_state_kernel,
        "first_state",
        [shape((STATE + tail_rows, per_group), BF16)],
        [x_raw, bc_raw, *(a if a.ndim > 1 else a[None] for a in params), doc_lens],
        [UNTOUCHED] * 10,
        out_specs=[UNTOUCHED],
        scratch=[
            pltpu.VMEM((rows, per_group), BF16),
            pltpu.VMEM((rows, STATE), BF16),
            pltpu.VMEM((per_group // HDIM, rows), F32),
            pltpu.VMEM((conv_x_weight.shape[0], per_group), F32),
            pltpu.VMEM((1, per_group), F32),
            pltpu.VMEM((conv_x_weight.shape[0], STATE), F32),
            pltpu.VMEM((1, STATE), F32),
            pltpu.VMEM((1, heads), F32),
            pltpu.VMEM((1, heads), F32),
            pltpu.SMEM(doc_lens.shape, jnp.int32),
            pltpu.VMEM((EDGE, width), BF16),
            pltpu.VMEM((EDGE, bc_width), BF16),
            pltpu.VMEM((STATE + tail_rows, per_group), BF16),
            pltpu.VMEM((rows + 8, STATE), F32),
            pltpu.VMEM((4, rows + 8, CHUNK), F32),
            pltpu.SemaphoreType.DMA((12,)),
            pltpu.SemaphoreType.DMA((per_group // (2 * CHUNK) + 1,)),
        ],
        limit=VMEM_ALL,
    )
    slots = [onward(message)]
    prepared = call(
        functools.partial(prepare_kernel, hops, groups),
        "prepare",
        [
            shape((rows, width), BF16),
            shape((rows, bc_width), BF16),
            shape((8, width + bc_width), F32),
            shape((8, width), F32),
            shape((8, width), F32),
            shape((conv_x_weight.shape[0] - 1, 8, CHUNK), F32),
            shape((hops, 8, CHUNK), F32),
            shape((8, width), F32),
            shape((rows, rows), jnp.int32),
            shape((rows, heads), F32),
            shape((rows, heads), F32),
            shape((rows, width), F32),
            shape((rows, width), F32),
            shape((rows, width), F32),
            *(shape((STATE, per_group), BF16) for _ in range(groups - 1)),
        ],
        [x_raw, bc_raw, *params, skip_d, doc_lens, z_gate],
        [WHOLE] * 10 + [SCALARS] + [WHOLE],
        scratch=[
            pltpu.VMEM((16, width + bc_width), F32),
            pltpu.VMEM((4, rows + 8, CHUNK), F32),
        ],
    )
    _, bcc, partial, weight, through, inside, flags, wide_skip, begin, *prepared = prepared
    step, running, main, gate, decay, *states = prepared
    states = [message, *states]
    carried = [shape(queries.shape, F32)] * 3 + [shape((rows, 2 * keys.shape[1]), BF16)]
    *carry, kv = call(own_kernel, "attend_own", carried, [queries, keys, values, begin], [WHOLE] * 4)
    kvs = [kv, onward(kv)]
    fulls = None
    for slot in range(2, hops + groups):
        part = min(slot - 1, groups) - 1
        fresh = slot <= groups
        if slot == 2:
            kernel = functools.partial(relay_first_kernel, fresh)
            operands = [slots[0], states[0], partial, weight, through, inside, flags, conv_x_weight, conv_bc_weight]
            scratch = [pltpu.VMEM((4, 16, CHUNK), F32)]
        else:
            kernel = functools.partial(relay_kernel, part, fresh)
            operands = [slots[-1], fulls[part], through, flags]
            scratch = []
        if fresh:
            operands.append(states[slot - 1])
        (passed,) = call(
            kernel,
            f"relay_slot{slot}",
            [shape((STATE, per_group), BF16)],
            operands,
            [WHOLE] * len(operands),
            scratch=scratch,
        )
        slots.append(onward(passed, max(0, slot - groups)))
        if fulls is None:
            gated, c_out, *fulls = call(
                functools.partial(first_rows_kernel, groups),
                "first_rows",
                [
                    shape((rows, width), F32),
                    shape((rows, groups * STATE), BF16),
                    *(shape((STATE, per_group), BF16) for _ in range(groups)),
                ],
                [
                    slots[0], partial, weight, inside, conv_x_weight, conv_bc_weight, step, running,
                    wide_skip, begin, bcc, main, gate, *states,
                ],
                [WHOLE] * (13 + groups),
                scratch=[pltpu.VMEM((4, 16, CHUNK), F32)],
            )
    def norm(part, first, stop, where, out=None, token=False):
        got = slots[part + first : part + stop]
        operands = [gated, decay, c_out, norm_gain, flags, *got]
        specs = [WHOLE] * len(operands)
        outs = [shape((rows, width), BF16)] + [shape((8, 128), F32)] * token
        aliases = {}
        if out is not None:
            aliases = {len(operands): 0}
            operands.append(out)
            specs.append(UNTOUCHED)
        return call(
            functools.partial(norm_kernel, part, len(got), first, where, out is not None),
            f"norm_part{part}_{where}",
            outs,
            operands,
            specs,
            out_specs=[UNTOUCHED] + [WHOLE] * token,
            scratch=[
                pltpu.VMEM((rows, per_group), F32),
                pltpu.VMEM((rows, per_group), BF16),
                pltpu.SemaphoreType.DMA((per_group // CHUNK,)),
            ],
            aliases=aliases,
            flops=KERNEL_FLOPS // 2,
        )

    mamba_out, token = None, c_out
    for part in range(groups - 1):
        mamba_out, token = norm(part, 0, 1, "odd", mamba_out, True)
    *carry, kv_on = call(
        near_kernel,
        "attend_near",
        carried,
        [queries, kvs[1], begin, *carry, token],
        [WHOLE] * 6 + [UNTOUCHED],
    )
    for hop in range(1, hops):
        kvs.append(onward(kv_on if hop == 1 else kvs[-1], hop))
    (attn_out,) = call(
        functools.partial(far_kernel, hops),
        "attend_far",
        [shape(queries.shape, BF16)],
        [queries, begin, *carry, *reversed(kvs[2:])],
        [WHOLE] * (4 + hops),
        out_specs=[UNTOUCHED],
        scratch=[
            pltpu.VMEM(queries.shape, BF16),
            pltpu.SemaphoreType.DMA((keys.shape[1] // ADIM,)),
        ],
    )
    for part in range(groups - 1):
        (mamba_out,) = norm(part, 0, hops, "rest", mamba_out)
    (mamba_out,) = norm(groups - 1, 0, 1, "first", mamba_out)
    (mamba_out,) = norm(groups - 1, 1, hops, "later", mamba_out)
    return (mamba_out, attn_out)


def solution(mesh):
    split = P(("groups", "seq"), "dp")
    placed = (
        split,
        split,
        split,
        split,
        P(None, "dp"),
        P("dp"),
        P(None, "dp"),
        P("dp"),
        P("dp"),
        P("dp"),
        P("dp"),
        P("dp"),
        split,
        split,
        split,
        P("groups"),
    )
    return jax.shard_map(
        shards,
        mesh=mesh,
        in_specs=placed,
        out_specs=(split, split),
        check_vma=False,
    )
```

```python
import functools
import math
from typing import NamedTuple

import jax
import jax.numpy as jnp
from jax import lax
from jax.experimental import pallas as pl
from jax.experimental.pallas import tpu as pltpu
from jax.sharding import PartitionSpec as P

HDIM = 64
STATE = 128
QHEADS = 32
KVHEADS = 8
ADIM = 128
EPSILON = 1e-05
BARRED = -2e30
HIGHEST = lax.Precision.HIGHEST
F32 = jnp.float32
BF16 = jnp.bfloat16
CHUNK = 256
EDGE = 16
KERNEL_FLOPS = 2 * 10**9
VMEM_LIMIT = 40 * 1024 * 1024
VMEM_ALL = 62 * 1024 * 1024


def silu(value):
    return value * (0.5 * jnp.tanh(0.5 * value) + 0.5)


def softplus(value):
    return jnp.maximum(value, 0.0) + jnp.log(1.0 + jnp.exp(-jnp.abs(value)))


def doc_start(positions, lens_ref):
    begin = jnp.int32(0)
    found = positions * 0
    for doc in range(lens_ref.shape[0]):
        found = jnp.where(positions >= begin, begin, found)
        begin = begin + lens_ref[doc]
    return found


def halves(value):
    high = value.astype(BF16)
    return high, (value - high.astype(F32)).astype(BF16)


def widen(per_head, first, width):
    heads = per_head.shape[1]
    both = jnp.concatenate(halves(per_head), axis=1)
    head = lax.broadcasted_iota(jnp.int32, (2 * heads, width), 0)
    head = jnp.where(head >= heads, head - heads, head)
    channel = lax.broadcasted_iota(jnp.int32, (2 * heads, width), 1) + first
    spread = (channel // HDIM == head).astype(F32).astype(BF16)
    return jnp.dot(both, spread, preferred_element_type=F32)


def rates(dt_ref, dt_bias_ref, a_log_ref):
    heads = dt_ref.shape[0]
    step = softplus(dt_ref[...].T + dt_bias_ref[...].reshape(1, -1)[:, :heads])
    rate = -step * jnp.exp(a_log_ref[...].reshape(1, -1)[:, :heads])
    rows = step.shape[0]
    row = lax.broadcasted_iota(jnp.int32, (rows, rows), 0)
    column = lax.broadcasted_iota(jnp.int32, (rows, rows), 1)
    lower = (row >= column).astype(F32).astype(BF16)
    high = rate.astype(BF16)
    middle, low = halves(rate - high.astype(F32))
    parts = jnp.concatenate([high, middle, low], axis=0)
    lowers = jnp.concatenate([lower, lower, lower], axis=1)
    return step, jnp.dot(lowers, parts, preferred_element_type=F32)


def insides(first, shape, taps, lens_ref):
    positions = first + lax.broadcasted_iota(jnp.int32, shape, 0)
    depth = positions - doc_start(positions, lens_ref)
    return [depth >= lag for lag in range(taps)]


def conv(pad, rows, weight, bias, inside):
    taps = weight.shape[0]
    total = pad[8 : 8 + rows] * weight[taps - 1 : taps] + bias
    for lag in range(1, taps):
        term = pad[8 - lag : 8 - lag + rows] * weight[taps - 1 - lag : taps - lag]
        total = total + jnp.where(inside[lag], term, 0.0)
    return silu(total)


def tail_lines(message, rows):
    block = message[rows:].astype(F32)
    return jnp.concatenate([block[at : at + 4] for at in range(0, block.shape[0], 4)], axis=1)


def reach(device, rows, lens_ref):
    return device - doc_start((device + 1) * rows - 1, lens_ref) // rows


def kept_weight(here, step, running, taps, lens_ref):
    rows = step.shape[0]
    last_begin = doc_start((here + 1) * rows - 1, lens_ref)
    row = lax.broadcasted_iota(jnp.int32, step.shape, 0)
    weight = step * jnp.exp(running[rows - 1 : rows] - running)
    kept = (here * rows + row >= last_begin) & ((row >= taps - 1) | (last_begin // rows >= here))
    return jnp.where(kept, weight, 0.0)


def conv_rows(pad, raw, weight, bias, inside):
    pad[0:8] = jnp.zeros((8, raw.shape[1]), F32)
    pad[8:] = raw.astype(F32)
    return conv(pad, raw.shape[0], weight, bias.reshape(1, -1), inside)


def first_state_kernel(*refs):
    hbm_refs, out_hbm_ref = refs[:10], refs[10]
    vmem_refs = refs[11:21]
    x_edge_ref, bc_edge_ref, out_ref, b_pad_ref, pad_ref, in_sems, out_sems = refs[21:]
    x_ref, b_ref, dt_ref, wx_ref, bx_ref, wbc_ref, bbc_ref, dt_bias_ref, a_log_ref, lens_ref = vmem_refs
    rows, width = x_ref.shape
    taps = wx_ref.shape[0]

    def corner(ref, shape):
        return ref.at[tuple(pl.ds(0, extent) for extent in shape)]

    order = (9, 2, 7, 8, 1, 5, 6, 0, 3, 4)
    copies = {}
    for at in order:
        source = corner(hbm_refs[at], vmem_refs[at].shape)
        copies[at] = pltpu.make_async_copy(source, vmem_refs[at], in_sems.at[at])
        copies[at].start()
    edge_copies = []
    for at, (source, target) in enumerate(((hbm_refs[0], x_edge_ref), (hbm_refs[1], bc_edge_ref))):
        edge_copies.append(
            pltpu.make_async_copy(source.at[pl.ds(rows - EDGE, EDGE)], target, in_sems.at[10 + at])
        )
        edge_copies[-1].start()

    here = lax.axis_index("seq")
    for at in (9, 2, 7, 8):
        copies[at].wait()
    inside = insides(here * rows, (rows, CHUNK), taps, lens_ref)
    step, running = rates(dt_ref, dt_bias_ref, a_log_ref)
    weight = kept_weight(here, step, running, taps, lens_ref)
    narrow = [mask[:, :STATE] for mask in inside]
    for at in (1, 5, 6):
        copies[at].wait()
    inputs = conv_rows(b_pad_ref, b_ref[...], wbc_ref[...], bbc_ref[...], narrow)
    turned = inputs.T.astype(BF16)
    for at in (0, 3, 4):
        copies[at].wait()
    slots = pad_ref.shape[0]
    outs = []

    def send(at, view):
        copy = pltpu.make_async_copy(out_ref.at[view], out_hbm_ref.at[view], out_sems.at[at])
        copy.start()
        outs.append(copy)

    for at, start in enumerate(range(0, width, CHUNK)):
        columns = slice(start, start + CHUNK)
        pad = pad_ref.at[(at + 1) % slots]
        xc = conv_rows(pad, x_ref[:, columns], wx_ref[:, columns], bx_ref[:, columns], inside)
        weighted = (xc * widen(weight, start, CHUNK)).astype(BF16)
        out_ref[:STATE, columns] = jnp.dot(turned, weighted, preferred_element_type=F32).astype(BF16)
        if at % 2:
            send(at // 2, (pl.ds(0, STATE), pl.ds(start - CHUNK, 2 * CHUNK)))
    for copy in edge_copies:
        copy.wait()
    edges = jnp.concatenate([x_edge_ref[...].astype(F32), bc_edge_ref[...].astype(F32)], axis=1)[EDGE - 4 :]
    spare = -edges.shape[1] % width
    if spare:
        edges = jnp.concatenate([edges, jnp.zeros((4, spare), F32)], axis=1)
    pieces = [edges[:, at : at + width] for at in range(0, edges.shape[1], width)]
    while len(pieces) % (EDGE // 4):
        pieces.append(jnp.zeros_like(pieces[0]))
    out_ref[STATE:] = jnp.concatenate(pieces, axis=0).astype(BF16)
    send(width // (2 * CHUNK), (pl.ds(STATE, out_ref.shape[0] - STATE), pl.ds(0, width)))
    for copy in outs:
        copy.wait()


def prepare_kernel(hops, groups, count, *refs):
    x_ref, bc_ref, dt_ref, wx_ref, bx_ref, wbc_ref, bbc_ref, dt_bias_ref, a_log_ref, skip_ref, lens_ref = refs[:11]
    z_ref = refs[11]
    xc_ref, bcc_ref, partial_ref, weight_ref, through_ref, inside_ref, flag_ref = refs[12:19]
    wide_skip_ref, begin_ref, step_ref, running_ref, out_ref, gate_ref, decay_ref = refs[19:26]
    state_refs = refs[26:-2]
    top_ref, pad_ref = refs[-2:]
    rows, width = x_ref.shape
    per_group = width // groups
    taps = wx_ref.shape[0]
    slots = pad_ref.shape[0]
    here = lax.axis_index("seq")
    first = here * rows
    inside = insides(first, (rows, CHUNK), taps, lens_ref)
    step, running = rates(dt_ref, dt_bias_ref, a_log_ref)
    heads = step.shape[1]
    group_heads = heads // groups
    kept = kept_weight(here, step, running, taps, lens_ref)
    for group in range(groups):
        base = slice(group * 2 * STATE, (group + 1) * 2 * STATE)
        pair = conv_rows(pad_ref.at[0], bc_ref[:, base], wbc_ref[:, base], bbc_ref[base], inside)
        bcc_ref[:, base] = pair.astype(BF16)
        turned = pair[:, :STATE].T.astype(BF16)
        part_weight = kept[:, group * group_heads : (group + 1) * group_heads]
        for chunk in range(0, per_group, CHUNK):
            columns = slice(group * per_group + chunk, group * per_group + chunk + CHUNK)
            pad = pad_ref.at[(chunk // CHUNK + 1) % slots]
            xc = conv_rows(pad, x_ref[:, columns], wx_ref[:, columns], bx_ref[columns], inside)
            xc_ref[:, columns] = xc.astype(BF16)
            if group:
                weighted = (xc * widen(part_weight, chunk, CHUNK)).astype(BF16)
                state_refs[group - 1][:, chunk : chunk + CHUNK] = jnp.dot(
                    turned, weighted, preferred_element_type=F32
                ).astype(BF16)

    own = reach(here, rows, lens_ref) == 0
    inside = [mask[:8] for mask in inside]
    for lag in range(1, taps):
        inside_ref[lag - 1] = inside[lag].astype(F32)
    flag_ref[0] = jnp.broadcast_to((own | (here == count - 1)).astype(F32), (8, CHUNK))
    before = reach(here - 1, rows, lens_ref)
    for hop in range(1, hops):
        flag_ref[hop] = jnp.broadcast_to((before == hop).astype(F32), (8, CHUNK))
    begin = doc_start(first + lax.broadcasted_iota(jnp.int32, begin_ref.shape, 0), lens_ref)
    begin_ref[...] = begin
    entry = jnp.where(begin[:, :heads] < first, jnp.exp(running), 0.0)
    step_ref[...] = step
    running_ref[...] = running
    row = lax.broadcasted_iota(jnp.int32, (8, heads), 0)
    total = running[rows - 1 : rows]
    weight = step[:8] * jnp.exp(total - running[:8])
    weight = jnp.where((row < taps - 1) & jnp.logical_not(own), weight, 0.0)
    through = jnp.where(own, 0.0, jnp.broadcast_to(jnp.exp(total), (8, heads)))
    skip = jnp.broadcast_to(skip_ref[...].reshape(1, -1), (8, heads))
    every = jnp.concatenate([weight, through, skip], axis=0)
    for start in range(0, width, CHUNK):
        wide = widen(every, start, CHUNK)
        weight_ref[:, start : start + CHUNK] = wide[:8]
        through_ref[:, start : start + CHUNK] = wide[8:16]
        wide_skip_ref[:, start : start + CHUNK] = wide[16:]
    top_ref[0:8] = jnp.zeros((8, top_ref.shape[1]), F32)
    top_ref[8:, :width] = x_ref[:EDGE].astype(F32)[:8]
    top_ref[8:, width:] = bc_ref[:EDGE].astype(F32)[:8]

    def some(columns, base, w_ref, b_ref):
        here_columns = slice(base + columns.start, base + columns.stop)
        total = top_ref[8:, here_columns] * w_ref[taps - 1 : taps, columns] + b_ref[columns].reshape(1, -1)
        for lag in range(1, taps):
            term = top_ref[8 - lag : 16 - lag, here_columns] * w_ref[taps - 1 - lag : taps - lag, columns]
            total = total + jnp.where(inside[lag], term, 0.0)
        partial_ref[:, here_columns] = total

    for start in range(0, width, CHUNK):
        some(slice(start, start + CHUNK), 0, wx_ref, bx_ref)
    for start in range(0, bc_ref.shape[1], CHUNK):
        some(slice(start, start + CHUNK), width, wbc_ref, bbc_ref)

    row = lax.broadcasted_iota(jnp.int32, (rows, rows), 0)
    lane = lax.broadcasted_iota(jnp.int32, (rows, rows), 1)
    linked = (row >= lane) & (first + lane >= begin) & (lane >= 8)
    turned_running = running.T
    turned_step = step.T
    pair_width = 2 * HDIM
    channel = lax.broadcasted_iota(jnp.int32, (rows, pair_width), 1)
    below = lax.broadcasted_iota(jnp.int32, (rows, CHUNK), 0) >= 8
    for group in range(groups):
        base = group * 2 * STATE
        meet = lax.dot_general(
            bcc_ref[:, base + STATE : base + 2 * STATE],
            bcc_ref[:, base : base + STATE],
            (((1,), (1,)), ((), ())),
            preferred_element_type=F32,
        )
        meet = jnp.where(linked, meet, 0.0)
        group_entry = entry[:, group * group_heads : (group + 1) * group_heads]
        for chunk in range(0, per_group, CHUNK):
            at = group * per_group + chunk
            columns = slice(at, at + CHUNK)
            gate = silu(z_ref[:, columns].astype(F32))
            gate_ref[:, columns] = gate
            decay_ref[:, columns] = widen(group_entry, chunk, CHUNK) * gate
            xc_all = xc_ref[:, columns]
            skipped = jnp.where(below, xc_all.astype(F32) * wide_skip_ref[0:1, columns], 0.0)
            for start in range(0, CHUNK, pair_width):
                parts = []
                for head in ((at + start) // HDIM, (at + start) // HDIM + 1):
                    spread = running[:, head : head + 1] - turned_running[head : head + 1]
                    decay = jnp.exp(jnp.minimum(spread, 0.0))
                    parts.append((decay * (meet * turned_step[head : head + 1])).astype(BF16))
                mix = jnp.concatenate(parts, axis=1)
                here_columns = slice(start, start + pair_width)
                xc = xc_all[:, here_columns]
                zero = jnp.zeros_like(xc)
                stacked = jnp.concatenate(
                    [jnp.where(channel < HDIM, xc, zero), jnp.where(channel < HDIM, zero, xc)], axis=0
                )
                value = jnp.dot(mix, stacked, preferred_element_type=F32) + skipped[:, here_columns]
                out_ref[:, at + start : at + start + pair_width] = value * gate[:, here_columns]


def first_rows(lines, partial_ref, inside_ref, w_ref, pad_ref, slot, at, start):
    taps = w_ref.shape[0]
    columns = slice(start, start + CHUNK)
    pad = pad_ref.at[slot]
    pad[4:8] = lines[:, at + start : at + start + CHUNK]
    pad[8:] = jnp.zeros((8, CHUNK), F32)
    total = partial_ref[:, at + start : at + start + CHUNK]
    for lag in range(1, taps):
        term = pad[8 - lag : 16 - lag] * w_ref[taps - 1 - lag : taps - lag, columns]
        total = total + term * inside_ref[lag - 1]
    return silu(total)


def sixteen(value):
    return jnp.concatenate([value, jnp.zeros_like(value)], axis=0).astype(BF16)


def relay_first_kernel(fresh, *refs):
    message_ref, state_ref, partial_ref, weight_ref, through_ref, inside_ref, flag_ref, wx_ref, wbc_ref = refs[:9]
    other_ref = refs[9] if fresh else state_ref
    out_ref, pad_ref = refs[-2:]
    width = out_ref.shape[1]
    slots = pad_ref.shape[0]
    own = flag_ref[0, 0, 0] > 0.5

    @pl.when(own)
    def _():
        out_ref[...] = other_ref[:STATE]

    @pl.when(jnp.logical_not(own))
    def _():
        lines = tail_lines(message_ref, STATE)
        top = functools.partial(first_rows, lines, partial_ref, inside_ref)
        inputs = top(wbc_ref, pad_ref, 0, wx_ref.shape[1], 0)[:, :STATE]
        turned = jnp.concatenate([inputs, inputs], axis=0).T.astype(BF16)
        for start in range(0, width, CHUNK):
            columns = slice(start, start + CHUNK)
            xc = top(wx_ref, pad_ref, (start // CHUNK + 1) % slots, 0, start)
            weighted = sixteen(xc * weight_ref[:, columns])
            full = state_ref[:STATE, columns].astype(F32) + jnp.dot(
                turned, weighted, preferred_element_type=F32
            )
            full = full + through_ref[0:1, columns] * message_ref[:STATE, columns].astype(F32)
            out_ref[:, columns] = full.astype(BF16)


def relay_kernel(part, fresh, *refs):
    got_ref, state_ref, through_ref, flag_ref = refs[:4]
    out_ref = refs[-1]
    width = out_ref.shape[1]
    own = flag_ref[0, 0:1] > 0.5
    for start in range(0, width, CHUNK):
        columns = slice(start, start + CHUNK)
        through = through_ref[0:1, part * width + start : part * width + start + CHUNK]
        full = state_ref[:, columns].astype(F32) + through * got_ref[:STATE, columns].astype(F32)
        if fresh:
            full = jnp.where(own, refs[4][:STATE, columns].astype(F32), full)
        out_ref[:, columns] = full.astype(BF16)


def first_rows_kernel(groups, *refs):
    (
        message_ref, partial_ref, weight_ref, inside_ref, wx_ref, wbc_ref, step_ref, running_ref,
        wide_skip_ref, begin_ref, bcc_ref, main_ref, gate_ref,
    ) = refs[:13]
    state_refs = refs[13 : 13 + groups]
    out_ref, c_ref = refs[13 + groups : 15 + groups]
    full_refs = refs[15 + groups : 15 + 2 * groups]
    pad_ref = refs[-1]
    rows, width = main_ref.shape
    per_group = width // groups
    heads = per_group // HDIM
    lanes = 8 * heads
    first = lax.axis_index("seq") * rows
    lines = tail_lines(message_ref, STATE)
    slots = pad_ref.shape[0]
    top = functools.partial(first_rows, lines, partial_ref, inside_ref)
    lane = lax.broadcasted_iota(jnp.int32, (rows, lanes), 1)
    line = lane & 7
    row = lax.broadcasted_iota(jnp.int32, (rows, lanes), 0)
    begin = jnp.concatenate([begin_ref[...]] * -(-lanes // rows), axis=1)[:, :lanes]
    linked = (row >= line) & (first + line >= begin)
    head = lax.broadcasted_iota(jnp.int32, (3 * heads, lanes), 0)
    for _ in range(2):
        head = jnp.where(head >= heads, head - heads, head)
    spread = (lax.broadcasted_iota(jnp.int32, (3 * heads, lanes), 1) >> 3 == head).astype(F32).astype(BF16)
    own_line = lax.broadcasted_iota(jnp.int32, (8, lanes), 0) == line[:8]

    def to_lanes(value):
        high = value.astype(BF16)
        middle, low = halves(value - high.astype(F32))
        return jnp.dot(jnp.concatenate([high, middle, low], axis=1), spread, preferred_element_type=F32)

    def by_line(value):
        return jnp.sum(jnp.where(own_line, value, 0.0), axis=0, keepdims=True)

    channel = lax.broadcasted_iota(jnp.int32, (8, CHUNK), 1)
    for group in range(groups):
        base = group * 2 * STATE
        these = slice(group * heads, (group + 1) * heads)
        new = top(wbc_ref, pad_ref, group % slots, width, base)
        old = bcc_ref[:, base + STATE : base + 2 * STATE]
        outputs = jnp.concatenate([new[:, STATE:], old[:EDGE].astype(F32)[8:]], axis=0).astype(BF16)
        outputs = jnp.concatenate([outputs, old[EDGE:]], axis=0)
        c_ref[:, group * STATE : (group + 1) * STATE] = outputs
        inputs = jnp.concatenate([new[:, :STATE]] * heads, axis=0).astype(BF16)
        meet = lax.dot_general(
            outputs, inputs, (((1,), (1,)), ((), ())), preferred_element_type=F32
        )
        running = to_lanes(running_ref[:, these])
        decay = jnp.exp(jnp.minimum(running - by_line(running[:8]), 0.0))
        mix = decay * (meet * by_line(to_lanes(step_ref[:8, these])))
        mix = jnp.where(linked, mix, 0.0).astype(BF16)
        turned = inputs[:EDGE].astype(F32).T.astype(BF16)
        for chunk in range(0, per_group, CHUNK):
            at = group * per_group + chunk
            columns = slice(at, at + CHUNK)
            xc = top(wx_ref, pad_ref, (chunk // CHUNK + 1) % slots, 0, at)
            full = state_refs[group][:STATE, chunk : chunk + CHUNK].astype(F32) + jnp.dot(
                turned, sixteen(xc * weight_ref[:, columns]), preferred_element_type=F32
            )
            full_refs[group][:, chunk : chunk + CHUNK] = full.astype(BF16)
            blocks = []
            for at_head in range(heads):
                low = at_head * HDIM - chunk
                if 0 <= low < CHUNK:
                    blocks.append(jnp.where((channel >= low) & (channel < low + HDIM), xc, 0.0))
                else:
                    blocks.append(jnp.zeros_like(xc))
            spread_xc = jnp.concatenate(blocks, axis=0).astype(BF16)
            gate = gate_ref[:, columns]
            value = main_ref[:, columns] + gate * jnp.dot(mix, spread_xc, preferred_element_type=F32)
            out_ref[:, columns] = value
            out_ref[0:8, columns] = value[:8] + gate[:8] * (xc * wide_skip_ref[:, columns])


def attend(q_ref, kv_refs, begin_ref, blocks, share, head):
    rows = q_ref.shape[0]
    kv_heads = kv_refs[0].shape[1] // (2 * ADIM)
    count = rows * blocks.count
    here = lax.axis_index("seq")
    row = here * rows + lax.broadcasted_iota(jnp.int32, (rows, count), 0)
    lane = (here - blocks.farthest) * rows + lax.broadcasted_iota(jnp.int32, (rows, count), 1)
    begin = jnp.concatenate([begin_ref[...]] * blocks.count, axis=1)
    allowed = jnp.concatenate([(lane <= row) & (lane >= begin)] * share, axis=0)
    low = head * ADIM
    keys = jnp.concatenate([ref[:, low : low + ADIM] for ref in kv_refs], axis=0)
    low = (kv_heads + head) * ADIM
    values = jnp.concatenate([ref[:, low : low + ADIM] for ref in kv_refs], axis=0)
    values = jnp.concatenate([values, jnp.ones((count, ADIM), BF16)], axis=1)
    lows = [(head * share + part) * ADIM for part in range(share)]
    asking = jnp.concatenate([q_ref[:, low : low + ADIM] for low in lows], axis=0)
    scores = lax.dot_general(asking, keys, (((1,), (1,)), ((), ())), preferred_element_type=F32)
    return jnp.where(allowed, scores * ADIM ** (-0.5), BARRED), values


class Blocks(NamedTuple):
    farthest: int
    count: int


def fold(q_ref, kv_refs, begin_ref, blocks, share, head, carry):
    lows = [(head * share + part) * ADIM for part in range(share)]
    scores, values = attend(q_ref, kv_refs, begin_ref, blocks, share, head)
    peak = jnp.max(scores, axis=1, keepdims=True)
    peak = jnp.broadcast_to(peak, (peak.shape[0], ADIM))
    if carry is not None:
        sums, totals, before = (
            jnp.concatenate([ref[:, low : low + ADIM] for low in lows], axis=0) for ref in carry
        )
        peak = jnp.maximum(peak, before)
    expo = jnp.exp(scores - jnp.concatenate([peak] * (scores.shape[1] // ADIM), axis=1))
    summed = jnp.dot(expo.astype(BF16), values, preferred_element_type=F32)
    if carry is None:
        return lows, summed[:, :ADIM], summed[:, ADIM:], peak
    factor = jnp.exp(before - peak)
    return lows, sums * factor + summed[:, :ADIM], totals * factor + summed[:, ADIM:], peak


def own_kernel(q_ref, keys_ref, values_ref, begin_ref, *outs):
    kv_ref = outs[3]
    kv_width = keys_ref.shape[1]
    kv_ref[:, :kv_width] = keys_ref[...]
    kv_ref[:, kv_width:] = values_ref[...]
    rows = q_ref.shape[0]
    share = QHEADS // KVHEADS
    for head in range(kv_width // ADIM):
        lows, *results = fold(q_ref, (kv_ref,), begin_ref, Blocks(0, 1), share, head, None)
        for ref, result in zip(outs, results):
            for part, low in enumerate(lows):
                ref[:, low : low + ADIM] = result[part * rows : (part + 1) * rows]


def near_kernel(q_ref, before_ref, begin_ref, *refs):
    carry, outs = refs[:3], refs[4:]
    outs[3][...] = before_ref[...]
    rows = q_ref.shape[0]
    share = QHEADS // KVHEADS
    for head in range(before_ref.shape[1] // (2 * ADIM)):
        lows, *results = fold(q_ref, (before_ref,), begin_ref, Blocks(1, 1), share, head, carry)
        for ref, result in zip(outs, results):
            for part, low in enumerate(lows):
                ref[:, low : low + ADIM] = result[part * rows : (part + 1) * rows]


def far_kernel(hops, *refs):
    q_ref, begin_ref = refs[:2]
    kv_refs = refs[5 : 4 + hops]
    out_hbm_ref, out_ref, sems = refs[4 + hops :]
    rows = q_ref.shape[0]
    share = QHEADS // KVHEADS
    copies = []
    for head in range(kv_refs[0].shape[1] // (2 * ADIM)):
        blocks = Blocks(hops, hops - 1)
        lows, sums, totals, _ = fold(q_ref, kv_refs, begin_ref, blocks, share, head, refs[2:5])
        result = (sums / totals).astype(BF16)
        for part, low in enumerate(lows):
            out_ref[:, low : low + ADIM] = result[part * rows : (part + 1) * rows]
        columns = pl.ds(head * share * ADIM, share * ADIM)
        copies.append(
            pltpu.make_async_copy(out_ref.at[:, columns], out_hbm_ref.at[:, columns], sems.at[head])
        )
        copies[-1].start()
    for copy in copies:
        copy.wait()


def norm_kernel(part, hops, first, where, given, *refs):
    local_ref, decay_ref, c_ref, gain_ref, flag_ref = refs[:5]
    got_refs = refs[5 : 5 + hops]
    out_hbm_ref, *token_refs = refs[5 + hops + given : -3]
    gated_ref, out_ref, sems = refs[-3:]
    for ref in token_refs:
        ref[...] = jnp.zeros_like(ref)

    def work():
        rows, width = gated_ref.shape
        outputs = c_ref[:, part * STATE : (part + 1) * STATE]
        squares = jnp.zeros((rows, 128), F32)
        for start in range(0, width, CHUNK):
            columns = slice(start, start + CHUNK)
            placed = slice(part * width + start, part * width + start + CHUNK)
            state = got_refs[0][:STATE, columns]
            for hop in range(1, hops):
                there = flag_ref[first + hop, 0:1] > 0.5
                state = jnp.where(there, got_refs[hop][:STATE, columns].astype(F32), state.astype(F32))
            carried = jnp.dot(outputs, state.astype(BF16), preferred_element_type=F32)
            gated = local_ref[:, placed] + carried * decay_ref[:, placed]
            gated_ref[:, columns] = gated
            for lane in range(0, CHUNK, 128):
                squares = squares + gated[:, lane : lane + 128] * gated[:, lane : lane + 128]
        squares = jnp.sum(squares, axis=1, keepdims=True)
        multiplier = lax.rsqrt(squares * (1.0 / width) + EPSILON)
        copies = []
        for start in range(0, width, CHUNK):
            columns = slice(start, start + CHUNK)
            gain = gain_ref[part * width + start : part * width + start + CHUNK]
            out_ref[:, columns] = (gated_ref[:, columns] * multiplier * gain.reshape(1, -1)).astype(BF16)
            copies.append(
                pltpu.make_async_copy(
                    out_ref.at[:, pl.ds(start, CHUNK)],
                    out_hbm_ref.at[:, pl.ds(part * width + start, CHUNK)],
                    sems.at[start // CHUNK],
                )
            )
            copies[-1].start()
        for copy in copies:
            copy.wait()

    odd = lax.axis_index("dp") % 2 == 1
    later = sum(flag_ref[hop, 0, 0] for hop in range(1, flag_ref.shape[0])) > 0.5
    here = {"odd": odd, "rest": jnp.logical_not(odd) | later, "first": jnp.logical_not(later), "later": later}
    pl.when(here[where])(work)


WHOLE = pl.BlockSpec(memory_space=pltpu.VMEM)
SCALARS = pl.BlockSpec(memory_space=pltpu.SMEM)
UNTOUCHED = pl.BlockSpec(memory_space=pl.ANY)


def tile(rows, columns, row, column):
    return pl.BlockSpec((rows, columns), lambda step: (row, column))


def call(kernel, name, outs, operands, specs, out_specs=None, scratch=(), flops=KERNEL_FLOPS, aliases={}, limit=VMEM_LIMIT):
    moved = sum(math.prod(a.shape) * a.dtype.itemsize for a in (*operands, *outs))
    return pl.pallas_call(
        kernel,
        name=name,
        grid=(1,),
        out_shape=outs,
        in_specs=specs,
        out_specs=[WHOLE] * len(outs) if out_specs is None else out_specs,
        scratch_shapes=list(scratch),
        input_output_aliases=aliases,
        compiler_params=pltpu.CompilerParams(vmem_limit_bytes=limit),
        cost_estimate=pl.CostEstimate(flops=flops, bytes_accessed=moved, transcendentals=0),
    )(*operands)


def onward(value, first=0):
    count = lax.axis_size("seq")
    return lax.ppermute(value, "seq", [(source, source + 1) for source in range(first, count - 1)])


def shards(
    x_raw,
    bc_raw,
    z_gate,
    dt_raw,
    conv_x_weight,
    conv_x_bias,
    conv_bc_weight,
    conv_bc_bias,
    dt_bias,
    a_log,
    skip_d,
    norm_gain,
    queries,
    keys,
    values,
    doc_lens,
):
    rows, width = x_raw.shape
    bc_width = bc_raw.shape[1]
    heads = dt_raw.shape[1]
    groups = bc_width // (2 * STATE)
    per_group = width // groups
    count = lax.axis_size("seq")
    longest = rows * count // 2
    hops = min(count - 1, -(-(longest - 1) // rows))
    assert hops * rows >= longest and (hops == 2 or hops > 2 and groups == 1)
    shape = jax.ShapeDtypeStruct
    dt = dt_raw.T
    params = [dt, conv_x_weight, conv_x_bias, conv_bc_weight, conv_bc_bias, dt_bias, a_log]
    pieces = -(-(width + bc_width) // per_group)
    tail_rows = EDGE * -(-4 * pieces // EDGE)

    (message,) = call(
        first_state_kernel,
        "first_state",
        [shape((STATE + tail_rows, per_group), BF16)],
        [x_raw, bc_raw, *(a if a.ndim > 1 else a[None] for a in params), doc_lens],
        [UNTOUCHED] * 10,
        out_specs=[UNTOUCHED],
        scratch=[
            pltpu.VMEM((rows, per_group), BF16),
            pltpu.VMEM((rows, STATE), BF16),
            pltpu.VMEM((per_group // HDIM, rows), F32),
            pltpu.VMEM((conv_x_weight.shape[0], per_group), F32),
            pltpu.VMEM((1, per_group), F32),
            pltpu.VMEM((conv_x_weight.shape[0], STATE), F32),
            pltpu.VMEM((1, STATE), F32),
            pltpu.VMEM((1, heads), F32),
            pltpu.VMEM((1, heads), F32),
            pltpu.SMEM(doc_lens.shape, jnp.int32),
            pltpu.VMEM((EDGE, width), BF16),
            pltpu.VMEM((EDGE, bc_width), BF16),
            pltpu.VMEM((STATE + tail_rows, per_group), BF16),
            pltpu.VMEM((rows + 8, STATE), F32),
            pltpu.VMEM((4, rows + 8, CHUNK), F32),
            pltpu.SemaphoreType.DMA((12,)),
            pltpu.SemaphoreType.DMA((per_group // (2 * CHUNK) + 1,)),
        ],
        limit=VMEM_ALL,
    )
    slots = [onward(message)]
    prepared = call(
        functools.partial(prepare_kernel, hops, groups, count),
        "prepare",
        [
            shape((rows, width), BF16),
            shape((rows, bc_width), BF16),
            shape((8, width + bc_width), F32),
            shape((8, width), F32),
            shape((8, width), F32),
            shape((conv_x_weight.shape[0] - 1, 8, CHUNK), F32),
            shape((hops, 8, CHUNK), F32),
            shape((8, width), F32),
            shape((rows, rows), jnp.int32),
            shape((rows, heads), F32),
            shape((rows, heads), F32),
            shape((rows, width), F32),
            shape((rows, width), F32),
            shape((rows, width), F32),
            *(shape((STATE, per_group), BF16) for _ in range(groups - 1)),
        ],
        [x_raw, bc_raw, *params, skip_d, doc_lens, z_gate],
        [WHOLE] * 10 + [SCALARS] + [WHOLE],
        scratch=[
            pltpu.VMEM((16, width + bc_width), F32),
            pltpu.VMEM((4, rows + 8, CHUNK), F32),
        ],
    )
    _, bcc, partial, weight, through, inside, flags, wide_skip, begin, *prepared = prepared
    step, running, main, gate, decay, *states = prepared
    states = [message, *states]
    carried = [shape(queries.shape, F32)] * 3 + [shape((rows, 2 * keys.shape[1]), BF16)]
    *carry, kv = call(own_kernel, "attend_own", carried, [queries, keys, values, begin], [WHOLE] * 4)
    kvs = [kv, onward(kv)]
    fulls = None
    for slot in range(2, hops + groups):
        part = min(slot - 1, groups) - 1
        fresh = slot <= groups
        if slot == 2:
            kernel = functools.partial(relay_first_kernel, fresh)
            operands = [slots[0], states[0], partial, weight, through, inside, flags, conv_x_weight, conv_bc_weight]
            scratch = [pltpu.VMEM((4, 16, CHUNK), F32)]
        else:
            kernel = functools.partial(relay_kernel, part, fresh)
            operands = [slots[-1], fulls[part], through, flags]
            scratch = []
        if fresh:
            operands.append(states[slot - 1])
        (passed,) = call(
            kernel,
            f"relay_slot{slot}",
            [shape((STATE, per_group), BF16)],
            operands,
            [WHOLE] * len(operands),
            scratch=scratch,
        )
        slots.append(onward(passed, max(0, slot - groups)))
        if fulls is None:
            gated, c_out, *fulls = call(
                functools.partial(first_rows_kernel, groups),
                "first_rows",
                [
                    shape((rows, width), F32),
                    shape((rows, groups * STATE), BF16),
                    *(shape((STATE, per_group), BF16) for _ in range(groups)),
                ],
                [
                    slots[0], partial, weight, inside, conv_x_weight, conv_bc_weight, step, running,
                    wide_skip, begin, bcc, main, gate, *states,
                ],
                [WHOLE] * (13 + groups),
                scratch=[pltpu.VMEM((4, 16, CHUNK), F32)],
            )
    def norm(part, first, stop, where, out=None, token=False):
        got = slots[part + first : part + stop]
        operands = [gated, decay, c_out, norm_gain, flags, *got]
        specs = [WHOLE] * len(operands)
        outs = [shape((rows, width), BF16)] + [shape((8, 128), F32)] * token
        aliases = {}
        if out is not None:
            aliases = {len(operands): 0}
            operands.append(out)
            specs.append(UNTOUCHED)
        return call(
            functools.partial(norm_kernel, part, len(got), first, where, out is not None),
            f"norm_part{part}_{where}",
            outs,
            operands,
            specs,
            out_specs=[UNTOUCHED] + [WHOLE] * token,
            scratch=[
                pltpu.VMEM((rows, per_group), F32),
                pltpu.VMEM((rows, per_group), BF16),
                pltpu.SemaphoreType.DMA((per_group // CHUNK,)),
            ],
            aliases=aliases,
            flops=KERNEL_FLOPS // 2,
        )

    mamba_out, token = None, c_out
    for part in range(groups - 1):
        mamba_out, token = norm(part, 0, 1, "odd", mamba_out, True)
    *carry, kv_on = call(
        near_kernel,
        "attend_near",
        carried,
        [queries, kvs[1], begin, *carry, token],
        [WHOLE] * 6 + [UNTOUCHED],
    )
    for hop in range(1, hops):
        kvs.append(onward(kv_on if hop == 1 else kvs[-1], hop))
    (attn_out,) = call(
        functools.partial(far_kernel, hops),
        "attend_far",
        [shape(queries.shape, BF16)],
        [queries, begin, *carry, *reversed(kvs[2:])],
        [WHOLE] * (4 + hops),
        out_specs=[UNTOUCHED],
        scratch=[
            pltpu.VMEM(queries.shape, BF16),
            pltpu.SemaphoreType.DMA((keys.shape[1] // ADIM,)),
        ],
    )
    for part in range(groups - 1):
        (mamba_out,) = norm(part, 0, hops, "rest", mamba_out)
    (mamba_out,) = norm(groups - 1, 0, 1, "first", mamba_out)
    (mamba_out,) = norm(groups - 1, 1, hops, "later", mamba_out)
    return (mamba_out, attn_out)


def solution(mesh):
    split = P(("groups", "seq"), "dp")
    placed = (
        split,
        split,
        split,
        split,
        P(None, "dp"),
        P("dp"),
        P(None, "dp"),
        P("dp"),
        P("dp"),
        P("dp"),
        P("dp"),
        P("dp"),
        split,
        split,
        split,
        P("groups"),
    )
    return jax.shard_map(
        shards,
        mesh=mesh,
        in_specs=placed,
        out_specs=(split, split),
        check_vma=False,
    )
```

```python
import functools
import math
from typing import NamedTuple

import jax
import jax.numpy as jnp
from jax import lax
from jax.experimental import pallas as pl
from jax.experimental.pallas import tpu as pltpu
from jax.sharding import PartitionSpec as P

HDIM = 64
STATE = 128
QHEADS = 32
KVHEADS = 8
ADIM = 128
EPSILON = 1e-05
BARRED = -2e30
HIGHEST = lax.Precision.HIGHEST
F32 = jnp.float32
BF16 = jnp.bfloat16
CHUNK = 256
EDGE = 16
KERNEL_FLOPS = 2 * 10**9
VMEM_LIMIT = 40 * 1024 * 1024
VMEM_ALL = 62 * 1024 * 1024


def silu(value):
    return value * (0.5 * jnp.tanh(0.5 * value) + 0.5)


def softplus(value):
    return jnp.maximum(value, 0.0) + jnp.log(1.0 + jnp.exp(-jnp.abs(value)))


def doc_start(positions, lens_ref):
    begin = jnp.int32(0)
    found = positions * 0
    for doc in range(lens_ref.shape[0]):
        found = jnp.where(positions >= begin, begin, found)
        begin = begin + lens_ref[doc]
    return found


def halves(value):
    high = value.astype(BF16)
    return high, (value - high.astype(F32)).astype(BF16)


def widen(per_head, first, width):
    heads = per_head.shape[1]
    both = jnp.concatenate(halves(per_head), axis=1)
    head = lax.broadcasted_iota(jnp.int32, (2 * heads, width), 0)
    head = jnp.where(head >= heads, head - heads, head)
    channel = lax.broadcasted_iota(jnp.int32, (2 * heads, width), 1) + first
    spread = (channel // HDIM == head).astype(F32).astype(BF16)
    return jnp.dot(both, spread, preferred_element_type=F32)


def rates(dt_ref, dt_bias_ref, a_log_ref):
    heads = dt_ref.shape[0]
    step = softplus(dt_ref[...].T + dt_bias_ref[...].reshape(1, -1)[:, :heads])
    rate = -step * jnp.exp(a_log_ref[...].reshape(1, -1)[:, :heads])
    rows = step.shape[0]
    row = lax.broadcasted_iota(jnp.int32, (rows, rows), 0)
    column = lax.broadcasted_iota(jnp.int32, (rows, rows), 1)
    lower = (row >= column).astype(F32).astype(BF16)
    high = rate.astype(BF16)
    middle, low = halves(rate - high.astype(F32))
    parts = jnp.concatenate([high, middle, low], axis=0)
    lowers = jnp.concatenate([lower, lower, lower], axis=1)
    return step, jnp.dot(lowers, parts, preferred_element_type=F32)


def insides(first, shape, taps, lens_ref):
    positions = first + lax.broadcasted_iota(jnp.int32, shape, 0)
    depth = positions - doc_start(positions, lens_ref)
    return [depth >= lag for lag in range(taps)]


def conv(pad, rows, weight, bias, inside):
    taps = weight.shape[0]
    total = pad[8 : 8 + rows] * weight[taps - 1 : taps] + bias
    for lag in range(1, taps):
        term = pad[8 - lag : 8 - lag + rows] * weight[taps - 1 - lag : taps - lag]
        total = total + jnp.where(inside[lag], term, 0.0)
    return silu(total)


def tail_lines(message, rows):
    block = message[rows:].astype(F32)
    return jnp.concatenate([block[at : at + 4] for at in range(0, block.shape[0], 4)], axis=1)


def reach(device, rows, lens_ref):
    return device - doc_start((device + 1) * rows - 1, lens_ref) // rows


def kept_weight(here, step, running, taps, lens_ref):
    rows = step.shape[0]
    last_begin = doc_start((here + 1) * rows - 1, lens_ref)
    row = lax.broadcasted_iota(jnp.int32, step.shape, 0)
    weight = step * jnp.exp(running[rows - 1 : rows] - running)
    kept = (here * rows + row >= last_begin) & ((row >= taps - 1) | (last_begin // rows >= here))
    return jnp.where(kept, weight, 0.0)


def conv_rows(pad, raw, weight, bias, inside):
    pad[0:8] = jnp.zeros((8, raw.shape[1]), F32)
    pad[8:] = raw.astype(F32)
    return conv(pad, raw.shape[0], weight, bias.reshape(1, -1), inside)


def first_state_kernel(count, *refs):
    pl.when(lax.axis_index("seq") < count - 1)(functools.partial(first_state, *refs))


def first_state(*refs):
    hbm_refs, out_hbm_ref = refs[:10], refs[10]
    vmem_refs = refs[11:21]
    x_edge_ref, bc_edge_ref, out_ref, b_pad_ref, pad_ref, in_sems, out_sems = refs[21:]
    x_ref, b_ref, dt_ref, wx_ref, bx_ref, wbc_ref, bbc_ref, dt_bias_ref, a_log_ref, lens_ref = vmem_refs
    rows, width = x_ref.shape
    taps = wx_ref.shape[0]

    def corner(ref, shape):
        return ref.at[tuple(pl.ds(0, extent) for extent in shape)]

    order = (9, 2, 7, 8, 1, 5, 6, 0, 3, 4)
    copies = {}
    for at in order:
        source = corner(hbm_refs[at], vmem_refs[at].shape)
        copies[at] = pltpu.make_async_copy(source, vmem_refs[at], in_sems.at[at])
        copies[at].start()
    edge_copies = []
    for at, (source, target) in enumerate(((hbm_refs[0], x_edge_ref), (hbm_refs[1], bc_edge_ref))):
        edge_copies.append(
            pltpu.make_async_copy(source.at[pl.ds(rows - EDGE, EDGE)], target, in_sems.at[10 + at])
        )
        edge_copies[-1].start()

    here = lax.axis_index("seq")
    for at in (9, 2, 7, 8):
        copies[at].wait()
    inside = insides(here * rows, (rows, CHUNK), taps, lens_ref)
    step, running = rates(dt_ref, dt_bias_ref, a_log_ref)
    weight = kept_weight(here, step, running, taps, lens_ref)
    narrow = [mask[:, :STATE] for mask in inside]
    for at in (1, 5, 6):
        copies[at].wait()
    inputs = conv_rows(b_pad_ref, b_ref[...], wbc_ref[...], bbc_ref[...], narrow)
    turned = inputs.T.astype(BF16)
    for at in (0, 3, 4):
        copies[at].wait()
    slots = pad_ref.shape[0]
    outs = []

    def send(at, view):
        copy = pltpu.make_async_copy(out_ref.at[view], out_hbm_ref.at[view], out_sems.at[at])
        copy.start()
        outs.append(copy)

    for at, start in enumerate(range(0, width, CHUNK)):
        columns = slice(start, start + CHUNK)
        pad = pad_ref.at[(at + 1) % slots]
        xc = conv_rows(pad, x_ref[:, columns], wx_ref[:, columns], bx_ref[:, columns], inside)
        weighted = (xc * widen(weight, start, CHUNK)).astype(BF16)
        out_ref[:STATE, columns] = jnp.dot(turned, weighted, preferred_element_type=F32).astype(BF16)
        if at % 2:
            send(at // 2, (pl.ds(0, STATE), pl.ds(start - CHUNK, 2 * CHUNK)))
    for copy in edge_copies:
        copy.wait()
    edges = jnp.concatenate([x_edge_ref[...].astype(F32), bc_edge_ref[...].astype(F32)], axis=1)[EDGE - 4 :]
    spare = -edges.shape[1] % width
    if spare:
        edges = jnp.concatenate([edges, jnp.zeros((4, spare), F32)], axis=1)
    pieces = [edges[:, at : at + width] for at in range(0, edges.shape[1], width)]
    while len(pieces) % (EDGE // 4):
        pieces.append(jnp.zeros_like(pieces[0]))
    out_ref[STATE:] = jnp.concatenate(pieces, axis=0).astype(BF16)
    send(width // (2 * CHUNK), (pl.ds(STATE, out_ref.shape[0] - STATE), pl.ds(0, width)))
    for copy in outs:
        copy.wait()


def prepare_kernel(hops, groups, count, *refs):
    x_ref, bc_ref, dt_ref, wx_ref, bx_ref, wbc_ref, bbc_ref, dt_bias_ref, a_log_ref, skip_ref, lens_ref = refs[:11]
    z_ref = refs[11]
    xc_ref, bcc_ref, partial_ref, weight_ref, through_ref, inside_ref, flag_ref = refs[12:19]
    wide_skip_ref, begin_ref, step_ref, running_ref, out_ref, gate_ref, decay_ref = refs[19:26]
    state_refs = refs[26:-2]
    top_ref, pad_ref = refs[-2:]
    rows, width = x_ref.shape
    per_group = width // groups
    taps = wx_ref.shape[0]
    slots = pad_ref.shape[0]
    here = lax.axis_index("seq")
    first = here * rows
    inside = insides(first, (rows, CHUNK), taps, lens_ref)
    step, running = rates(dt_ref, dt_bias_ref, a_log_ref)
    heads = step.shape[1]
    group_heads = heads // groups
    kept = kept_weight(here, step, running, taps, lens_ref)
    for group in range(groups):
        base = slice(group * 2 * STATE, (group + 1) * 2 * STATE)
        pair = conv_rows(pad_ref.at[0], bc_ref[:, base], wbc_ref[:, base], bbc_ref[base], inside)
        bcc_ref[:, base] = pair.astype(BF16)
        turned = pair[:, :STATE].T.astype(BF16)
        part_weight = kept[:, group * group_heads : (group + 1) * group_heads]
        for chunk in range(0, per_group, CHUNK):
            columns = slice(group * per_group + chunk, group * per_group + chunk + CHUNK)
            pad = pad_ref.at[(chunk // CHUNK + 1) % slots]
            xc = conv_rows(pad, x_ref[:, columns], wx_ref[:, columns], bx_ref[columns], inside)
            xc_ref[:, columns] = xc.astype(BF16)
            if group:
                weighted = (xc * widen(part_weight, chunk, CHUNK)).astype(BF16)
                state_refs[group - 1][:, chunk : chunk + CHUNK] = jnp.dot(
                    turned, weighted, preferred_element_type=F32
                ).astype(BF16)

    own = reach(here, rows, lens_ref) == 0
    inside = [mask[:8] for mask in inside]
    for lag in range(1, taps):
        inside_ref[lag - 1] = inside[lag].astype(F32)
    flag_ref[0] = jnp.broadcast_to((own | (here == count - 1)).astype(F32), (8, CHUNK))
    before = reach(here - 1, rows, lens_ref)
    for hop in range(1, hops):
        flag_ref[hop] = jnp.broadcast_to((before == hop).astype(F32), (8, CHUNK))
    begin = doc_start(first + lax.broadcasted_iota(jnp.int32, begin_ref.shape, 0), lens_ref)
    begin_ref[...] = begin
    entry = jnp.where(begin[:, :heads] < first, jnp.exp(running), 0.0)
    step_ref[...] = step
    running_ref[...] = running
    row = lax.broadcasted_iota(jnp.int32, (8, heads), 0)
    total = running[rows - 1 : rows]
    weight = step[:8] * jnp.exp(total - running[:8])
    weight = jnp.where((row < taps - 1) & jnp.logical_not(own), weight, 0.0)
    through = jnp.where(own, 0.0, jnp.broadcast_to(jnp.exp(total), (8, heads)))
    skip = jnp.broadcast_to(skip_ref[...].reshape(1, -1), (8, heads))
    every = jnp.concatenate([weight, through, skip], axis=0)
    for start in range(0, width, CHUNK):
        wide = widen(every, start, CHUNK)
        weight_ref[:, start : start + CHUNK] = wide[:8]
        through_ref[:, start : start + CHUNK] = wide[8:16]
        wide_skip_ref[:, start : start + CHUNK] = wide[16:]
    top_ref[0:8] = jnp.zeros((8, top_ref.shape[1]), F32)
    top_ref[8:, :width] = x_ref[:EDGE].astype(F32)[:8]
    top_ref[8:, width:] = bc_ref[:EDGE].astype(F32)[:8]

    def some(columns, base, w_ref, b_ref):
        here_columns = slice(base + columns.start, base + columns.stop)
        total = top_ref[8:, here_columns] * w_ref[taps - 1 : taps, columns] + b_ref[columns].reshape(1, -1)
        for lag in range(1, taps):
            term = top_ref[8 - lag : 16 - lag, here_columns] * w_ref[taps - 1 - lag : taps - lag, columns]
            total = total + jnp.where(inside[lag], term, 0.0)
        partial_ref[:, here_columns] = total

    for start in range(0, width, CHUNK):
        some(slice(start, start + CHUNK), 0, wx_ref, bx_ref)
    for start in range(0, bc_ref.shape[1], CHUNK):
        some(slice(start, start + CHUNK), width, wbc_ref, bbc_ref)

    row = lax.broadcasted_iota(jnp.int32, (rows, rows), 0)
    lane = lax.broadcasted_iota(jnp.int32, (rows, rows), 1)
    linked = (row >= lane) & (first + lane >= begin) & (lane >= 8)
    turned_running = running.T
    turned_step = step.T
    pair_width = 2 * HDIM
    channel = lax.broadcasted_iota(jnp.int32, (rows, pair_width), 1)
    below = lax.broadcasted_iota(jnp.int32, (rows, CHUNK), 0) >= 8
    for group in range(groups):
        base = group * 2 * STATE
        meet = lax.dot_general(
            bcc_ref[:, base + STATE : base + 2 * STATE],
            bcc_ref[:, base : base + STATE],
            (((1,), (1,)), ((), ())),
            preferred_element_type=F32,
        )
        meet = jnp.where(linked, meet, 0.0)
        group_entry = entry[:, group * group_heads : (group + 1) * group_heads]
        for chunk in range(0, per_group, CHUNK):
            at = group * per_group + chunk
            columns = slice(at, at + CHUNK)
            gate = silu(z_ref[:, columns].astype(F32))
            gate_ref[:, columns] = gate
            decay_ref[:, columns] = widen(group_entry, chunk, CHUNK) * gate
            xc_all = xc_ref[:, columns]
            skipped = jnp.where(below, xc_all.astype(F32) * wide_skip_ref[0:1, columns], 0.0)
            for start in range(0, CHUNK, pair_width):
                parts = []
                for head in ((at + start) // HDIM, (at + start) // HDIM + 1):
                    spread = running[:, head : head + 1] - turned_running[head : head + 1]
                    decay = jnp.exp(jnp.minimum(spread, 0.0))
                    parts.append((decay * (meet * turned_step[head : head + 1])).astype(BF16))
                mix = jnp.concatenate(parts, axis=1)
                here_columns = slice(start, start + pair_width)
                xc = xc_all[:, here_columns]
                zero = jnp.zeros_like(xc)
                stacked = jnp.concatenate(
                    [jnp.where(channel < HDIM, xc, zero), jnp.where(channel < HDIM, zero, xc)], axis=0
                )
                value = jnp.dot(mix, stacked, preferred_element_type=F32) + skipped[:, here_columns]
                out_ref[:, at + start : at + start + pair_width] = value * gate[:, here_columns]


def first_rows(lines, partial_ref, inside_ref, w_ref, pad_ref, slot, at, start):
    taps = w_ref.shape[0]
    columns = slice(start, start + CHUNK)
    pad = pad_ref.at[slot]
    pad[4:8] = lines[:, at + start : at + start + CHUNK]
    pad[8:] = jnp.zeros((8, CHUNK), F32)
    total = partial_ref[:, at + start : at + start + CHUNK]
    for lag in range(1, taps):
        term = pad[8 - lag : 16 - lag] * w_ref[taps - 1 - lag : taps - lag, columns]
        total = total + term * inside_ref[lag - 1]
    return silu(total)


def sixteen(value):
    return jnp.concatenate([value, jnp.zeros_like(value)], axis=0).astype(BF16)


def relay_first_kernel(fresh, *refs):
    message_ref, state_ref, partial_ref, weight_ref, through_ref, inside_ref, flag_ref, wx_ref, wbc_ref = refs[:9]
    other_ref = refs[9] if fresh else state_ref
    out_ref, pad_ref = refs[-2:]
    width = out_ref.shape[1]
    slots = pad_ref.shape[0]
    own = flag_ref[0, 0, 0] > 0.5

    @pl.when(own)
    def _():
        out_ref[...] = other_ref[:STATE]

    @pl.when(jnp.logical_not(own))
    def _():
        lines = tail_lines(message_ref, STATE)
        top = functools.partial(first_rows, lines, partial_ref, inside_ref)
        inputs = top(wbc_ref, pad_ref, 0, wx_ref.shape[1], 0)[:, :STATE]
        turned = jnp.concatenate([inputs, inputs], axis=0).T.astype(BF16)
        for start in range(0, width, CHUNK):
            columns = slice(start, start + CHUNK)
            xc = top(wx_ref, pad_ref, (start // CHUNK + 1) % slots, 0, start)
            weighted = sixteen(xc * weight_ref[:, columns])
            full = state_ref[:STATE, columns].astype(F32) + jnp.dot(
                turned, weighted, preferred_element_type=F32
            )
            full = full + through_ref[0:1, columns] * message_ref[:STATE, columns].astype(F32)
            out_ref[:, columns] = full.astype(BF16)


def relay_kernel(part, fresh, *refs):
    got_ref, state_ref, through_ref, flag_ref = refs[:4]
    out_ref = refs[-1]
    width = out_ref.shape[1]
    own = flag_ref[0, 0:1] > 0.5
    for start in range(0, width, CHUNK):
        columns = slice(start, start + CHUNK)
        through = through_ref[0:1, part * width + start : part * width + start + CHUNK]
        full = state_ref[:, columns].astype(F32) + through * got_ref[:STATE, columns].astype(F32)
        if fresh:
            full = jnp.where(own, refs[4][:STATE, columns].astype(F32), full)
        out_ref[:, columns] = full.astype(BF16)


def first_rows_kernel(groups, *refs):
    (
        message_ref, partial_ref, weight_ref, inside_ref, wx_ref, wbc_ref, step_ref, running_ref,
        wide_skip_ref, begin_ref, bcc_ref, main_ref, gate_ref,
    ) = refs[:13]
    state_refs = refs[13 : 13 + groups]
    out_ref, c_ref = refs[13 + groups : 15 + groups]
    full_refs = refs[15 + groups : 15 + 2 * groups]
    pad_ref = refs[-1]
    rows, width = main_ref.shape
    per_group = width // groups
    heads = per_group // HDIM
    lanes = 8 * heads
    first = lax.axis_index("seq") * rows
    lines = tail_lines(message_ref, STATE)
    slots = pad_ref.shape[0]
    top = functools.partial(first_rows, lines, partial_ref, inside_ref)
    lane = lax.broadcasted_iota(jnp.int32, (rows, lanes), 1)
    line = lane & 7
    row = lax.broadcasted_iota(jnp.int32, (rows, lanes), 0)
    begin = jnp.concatenate([begin_ref[...]] * -(-lanes // rows), axis=1)[:, :lanes]
    linked = (row >= line) & (first + line >= begin)
    head = lax.broadcasted_iota(jnp.int32, (3 * heads, lanes), 0)
    for _ in range(2):
        head = jnp.where(head >= heads, head - heads, head)
    spread = (lax.broadcasted_iota(jnp.int32, (3 * heads, lanes), 1) >> 3 == head).astype(F32).astype(BF16)
    own_line = lax.broadcasted_iota(jnp.int32, (8, lanes), 0) == line[:8]

    def to_lanes(value):
        high = value.astype(BF16)
        middle, low = halves(value - high.astype(F32))
        return jnp.dot(jnp.concatenate([high, middle, low], axis=1), spread, preferred_element_type=F32)

    def by_line(value):
        return jnp.sum(jnp.where(own_line, value, 0.0), axis=0, keepdims=True)

    channel = lax.broadcasted_iota(jnp.int32, (8, CHUNK), 1)
    for group in range(groups):
        base = group * 2 * STATE
        these = slice(group * heads, (group + 1) * heads)
        new = top(wbc_ref, pad_ref, group % slots, width, base)
        old = bcc_ref[:, base + STATE : base + 2 * STATE]
        outputs = jnp.concatenate([new[:, STATE:], old[:EDGE].astype(F32)[8:]], axis=0).astype(BF16)
        outputs = jnp.concatenate([outputs, old[EDGE:]], axis=0)
        c_ref[:, group * STATE : (group + 1) * STATE] = outputs
        inputs = jnp.concatenate([new[:, :STATE]] * heads, axis=0).astype(BF16)
        meet = lax.dot_general(
            outputs, inputs, (((1,), (1,)), ((), ())), preferred_element_type=F32
        )
        running = to_lanes(running_ref[:, these])
        decay = jnp.exp(jnp.minimum(running - by_line(running[:8]), 0.0))
        mix = decay * (meet * by_line(to_lanes(step_ref[:8, these])))
        mix = jnp.where(linked, mix, 0.0).astype(BF16)
        turned = inputs[:EDGE].astype(F32).T.astype(BF16)
        for chunk in range(0, per_group, CHUNK):
            at = group * per_group + chunk
            columns = slice(at, at + CHUNK)
            xc = top(wx_ref, pad_ref, (chunk // CHUNK + 1) % slots, 0, at)
            full = state_refs[group][:STATE, chunk : chunk + CHUNK].astype(F32) + jnp.dot(
                turned, sixteen(xc * weight_ref[:, columns]), preferred_element_type=F32
            )
            full_refs[group][:, chunk : chunk + CHUNK] = full.astype(BF16)
            blocks = []
            for at_head in range(heads):
                low = at_head * HDIM - chunk
                if 0 <= low < CHUNK:
                    blocks.append(jnp.where((channel >= low) & (channel < low + HDIM), xc, 0.0))
                else:
                    blocks.append(jnp.zeros_like(xc))
            spread_xc = jnp.concatenate(blocks, axis=0).astype(BF16)
            gate = gate_ref[:, columns]
            value = main_ref[:, columns] + gate * jnp.dot(mix, spread_xc, preferred_element_type=F32)
            out_ref[:, columns] = value
            out_ref[0:8, columns] = value[:8] + gate[:8] * (xc * wide_skip_ref[:, columns])


def attend(q_ref, kv_refs, begin_ref, blocks, share, head):
    rows = q_ref.shape[0]
    kv_heads = kv_refs[0].shape[1] // (2 * ADIM)
    count = rows * blocks.count
    here = lax.axis_index("seq")
    row = here * rows + lax.broadcasted_iota(jnp.int32, (rows, count), 0)
    lane = (here - blocks.farthest) * rows + lax.broadcasted_iota(jnp.int32, (rows, count), 1)
    begin = jnp.concatenate([begin_ref[...]] * blocks.count, axis=1)
    allowed = jnp.concatenate([(lane <= row) & (lane >= begin)] * share, axis=0)
    low = head * ADIM
    keys = jnp.concatenate([ref[:, low : low + ADIM] for ref in kv_refs], axis=0)
    low = (kv_heads + head) * ADIM
    values = jnp.concatenate([ref[:, low : low + ADIM] for ref in kv_refs], axis=0)
    values = jnp.concatenate([values, jnp.ones((count, ADIM), BF16)], axis=1)
    lows = [(head * share + part) * ADIM for part in range(share)]
    asking = jnp.concatenate([q_ref[:, low : low + ADIM] for low in lows], axis=0)
    scores = lax.dot_general(asking, keys, (((1,), (1,)), ((), ())), preferred_element_type=F32)
    return jnp.where(allowed, scores * ADIM ** (-0.5), BARRED), values


class Blocks(NamedTuple):
    farthest: int
    count: int


def fold(q_ref, kv_refs, begin_ref, blocks, share, head, carry):
    lows = [(head * share + part) * ADIM for part in range(share)]
    scores, values = attend(q_ref, kv_refs, begin_ref, blocks, share, head)
    peak = jnp.max(scores, axis=1, keepdims=True)
    peak = jnp.broadcast_to(peak, (peak.shape[0], ADIM))
    if carry is not None:
        sums, totals, before = (
            jnp.concatenate([ref[:, low : low + ADIM] for low in lows], axis=0) for ref in carry
        )
        peak = jnp.maximum(peak, before)
    expo = jnp.exp(scores - jnp.concatenate([peak] * (scores.shape[1] // ADIM), axis=1))
    summed = jnp.dot(expo.astype(BF16), values, preferred_element_type=F32)
    if carry is None:
        return lows, summed[:, :ADIM], summed[:, ADIM:], peak
    factor = jnp.exp(before - peak)
    return lows, sums * factor + summed[:, :ADIM], totals * factor + summed[:, ADIM:], peak


def own_kernel(q_ref, keys_ref, values_ref, begin_ref, *outs):
    kv_ref = outs[3]
    kv_width = keys_ref.shape[1]
    kv_ref[:, :kv_width] = keys_ref[...]
    kv_ref[:, kv_width:] = values_ref[...]
    rows = q_ref.shape[0]
    share = QHEADS // KVHEADS
    for head in range(kv_width // ADIM):
        lows, *results = fold(q_ref, (kv_ref,), begin_ref, Blocks(0, 1), share, head, None)
        for ref, result in zip(outs, results):
            for part, low in enumerate(lows):
                ref[:, low : low + ADIM] = result[part * rows : (part + 1) * rows]


def near_kernel(q_ref, before_ref, begin_ref, *refs):
    carry, outs = refs[:3], refs[4:]
    outs[3][...] = before_ref[...]
    rows = q_ref.shape[0]
    share = QHEADS // KVHEADS
    for head in range(before_ref.shape[1] // (2 * ADIM)):
        lows, *results = fold(q_ref, (before_ref,), begin_ref, Blocks(1, 1), share, head, carry)
        for ref, result in zip(outs, results):
            for part, low in enumerate(lows):
                ref[:, low : low + ADIM] = result[part * rows : (part + 1) * rows]


def far_kernel(hops, *refs):
    q_ref, begin_ref = refs[:2]
    kv_refs = refs[5 : 4 + hops]
    out_hbm_ref, out_ref, sems = refs[4 + hops :]
    rows = q_ref.shape[0]
    share = QHEADS // KVHEADS
    copies = []
    for head in range(kv_refs[0].shape[1] // (2 * ADIM)):
        blocks = Blocks(hops, hops - 1)
        lows, sums, totals, _ = fold(q_ref, kv_refs, begin_ref, blocks, share, head, refs[2:5])
        result = (sums / totals).astype(BF16)
        for part, low in enumerate(lows):
            out_ref[:, low : low + ADIM] = result[part * rows : (part + 1) * rows]
        columns = pl.ds(head * share * ADIM, share * ADIM)
        copies.append(
            pltpu.make_async_copy(out_ref.at[:, columns], out_hbm_ref.at[:, columns], sems.at[head])
        )
        copies[-1].start()
    for copy in copies:
        copy.wait()


def norm_kernel(part, hops, first, where, given, *refs):
    local_ref, decay_ref, c_ref, gain_ref, flag_ref = refs[:5]
    got_refs = refs[5 : 5 + hops]
    out_hbm_ref, *token_refs = refs[5 + hops + given : -3]
    gated_ref, out_ref, sems = refs[-3:]
    for ref in token_refs:
        ref[...] = jnp.zeros_like(ref)

    def work():
        rows, width = gated_ref.shape
        outputs = c_ref[:, part * STATE : (part + 1) * STATE]
        squares = jnp.zeros((rows, 128), F32)
        for start in range(0, width, CHUNK):
            columns = slice(start, start + CHUNK)
            placed = slice(part * width + start, part * width + start + CHUNK)
            state = got_refs[0][:STATE, columns]
            for hop in range(1, hops):
                there = flag_ref[first + hop, 0:1] > 0.5
                state = jnp.where(there, got_refs[hop][:STATE, columns].astype(F32), state.astype(F32))
            carried = jnp.dot(outputs, state.astype(BF16), preferred_element_type=F32)
            gated = local_ref[:, placed] + carried * decay_ref[:, placed]
            gated_ref[:, columns] = gated
            for lane in range(0, CHUNK, 128):
                squares = squares + gated[:, lane : lane + 128] * gated[:, lane : lane + 128]
        squares = jnp.sum(squares, axis=1, keepdims=True)
        multiplier = lax.rsqrt(squares * (1.0 / width) + EPSILON)
        copies = []
        for start in range(0, width, CHUNK):
            columns = slice(start, start + CHUNK)
            gain = gain_ref[part * width + start : part * width + start + CHUNK]
            out_ref[:, columns] = (gated_ref[:, columns] * multiplier * gain.reshape(1, -1)).astype(BF16)
            copies.append(
                pltpu.make_async_copy(
                    out_ref.at[:, pl.ds(start, CHUNK)],
                    out_hbm_ref.at[:, pl.ds(part * width + start, CHUNK)],
                    sems.at[start // CHUNK],
                )
            )
            copies[-1].start()
        for copy in copies:
            copy.wait()

    odd = lax.axis_index("dp") % 2 == 1
    later = sum(flag_ref[hop, 0, 0] for hop in range(1, flag_ref.shape[0])) > 0.5
    here = {"odd": odd, "rest": jnp.logical_not(odd) | later, "first": jnp.logical_not(later), "later": later}
    pl.when(here[where])(work)


WHOLE = pl.BlockSpec(memory_space=pltpu.VMEM)
SCALARS = pl.BlockSpec(memory_space=pltpu.SMEM)
UNTOUCHED = pl.BlockSpec(memory_space=pl.ANY)


def tile(rows, columns, row, column):
    return pl.BlockSpec((rows, columns), lambda step: (row, column))


def call(kernel, name, outs, operands, specs, out_specs=None, scratch=(), flops=KERNEL_FLOPS, aliases={}, limit=VMEM_LIMIT):
    moved = sum(math.prod(a.shape) * a.dtype.itemsize for a in (*operands, *outs))
    return pl.pallas_call(
        kernel,
        name=name,
        grid=(1,),
        out_shape=outs,
        in_specs=specs,
        out_specs=[WHOLE] * len(outs) if out_specs is None else out_specs,
        scratch_shapes=list(scratch),
        input_output_aliases=aliases,
        compiler_params=pltpu.CompilerParams(vmem_limit_bytes=limit),
        cost_estimate=pl.CostEstimate(flops=flops, bytes_accessed=moved, transcendentals=0),
    )(*operands)


def onward(value, first=0):
    count = lax.axis_size("seq")
    return lax.ppermute(value, "seq", [(source, source + 1) for source in range(first, count - 1)])


def shards(
    x_raw,
    bc_raw,
    z_gate,
    dt_raw,
    conv_x_weight,
    conv_x_bias,
    conv_bc_weight,
    conv_bc_bias,
    dt_bias,
    a_log,
    skip_d,
    norm_gain,
    queries,
    keys,
    values,
    doc_lens,
):
    rows, width = x_raw.shape
    bc_width = bc_raw.shape[1]
    heads = dt_raw.shape[1]
    groups = bc_width // (2 * STATE)
    per_group = width // groups
    count = lax.axis_size("seq")
    longest = rows * count // 2
    hops = min(count - 1, -(-(longest - 1) // rows))
    assert hops * rows >= longest and (hops == 2 or hops > 2 and groups == 1)
    shape = jax.ShapeDtypeStruct
    dt = dt_raw.T
    params = [dt, conv_x_weight, conv_x_bias, conv_bc_weight, conv_bc_bias, dt_bias, a_log]
    pieces = -(-(width + bc_width) // per_group)
    tail_rows = EDGE * -(-4 * pieces // EDGE)

    (message,) = call(
        functools.partial(first_state_kernel, count),
        "first_state",
        [shape((STATE + tail_rows, per_group), BF16)],
        [x_raw, bc_raw, *(a if a.ndim > 1 else a[None] for a in params), doc_lens],
        [UNTOUCHED] * 10,
        out_specs=[UNTOUCHED],
        scratch=[
            pltpu.VMEM((rows, per_group), BF16),
            pltpu.VMEM((rows, STATE), BF16),
            pltpu.VMEM((per_group // HDIM, rows), F32),
            pltpu.VMEM((conv_x_weight.shape[0], per_group), F32),
            pltpu.VMEM((1, per_group), F32),
            pltpu.VMEM((conv_x_weight.shape[0], STATE), F32),
            pltpu.VMEM((1, STATE), F32),
            pltpu.VMEM((1, heads), F32),
            pltpu.VMEM((1, heads), F32),
            pltpu.SMEM(doc_lens.shape, jnp.int32),
            pltpu.VMEM((EDGE, width), BF16),
            pltpu.VMEM((EDGE, bc_width), BF16),
            pltpu.VMEM((STATE + tail_rows, per_group), BF16),
            pltpu.VMEM((rows + 8, STATE), F32),
            pltpu.VMEM((4, rows + 8, CHUNK), F32),
            pltpu.SemaphoreType.DMA((12,)),
            pltpu.SemaphoreType.DMA((per_group // (2 * CHUNK) + 1,)),
        ],
        limit=VMEM_ALL,
    )
    slots = [onward(message)]
    prepared = call(
        functools.partial(prepare_kernel, hops, groups, count),
        "prepare",
        [
            shape((rows, width), BF16),
            shape((rows, bc_width), BF16),
            shape((8, width + bc_width), F32),
            shape((8, width), F32),
            shape((8, width), F32),
            shape((conv_x_weight.shape[0] - 1, 8, CHUNK), F32),
            shape((hops, 8, CHUNK), F32),
            shape((8, width), F32),
            shape((rows, rows), jnp.int32),
            shape((rows, heads), F32),
            shape((rows, heads), F32),
            shape((rows, width), F32),
            shape((rows, width), F32),
            shape((rows, width), F32),
            *(shape((STATE, per_group), BF16) for _ in range(groups - 1)),
        ],
        [x_raw, bc_raw, *params, skip_d, doc_lens, z_gate],
        [WHOLE] * 10 + [SCALARS] + [WHOLE],
        scratch=[
            pltpu.VMEM((16, width + bc_width), F32),
            pltpu.VMEM((4, rows + 8, CHUNK), F32),
        ],
    )
    _, bcc, partial, weight, through, inside, flags, wide_skip, begin, *prepared = prepared
    step, running, main, gate, decay, *states = prepared
    states = [message, *states]
    carried = [shape(queries.shape, F32)] * 3 + [shape((rows, 2 * keys.shape[1]), BF16)]
    *carry, kv = call(own_kernel, "attend_own", carried, [queries, keys, values, begin], [WHOLE] * 4)
    kvs = [kv, onward(kv)]
    fulls = None
    for slot in range(2, hops + groups):
        part = min(slot - 1, groups) - 1
        fresh = slot <= groups
        if slot == 2:
            kernel = functools.partial(relay_first_kernel, fresh)
            operands = [slots[0], states[0], partial, weight, through, inside, flags, conv_x_weight, conv_bc_weight]
            scratch = [pltpu.VMEM((4, 16, CHUNK), F32)]
        else:
            kernel = functools.partial(relay_kernel, part, fresh)
            operands = [slots[-1], fulls[part], through, flags]
            scratch = []
        if fresh:
            operands.append(states[slot - 1])
        (passed,) = call(
            kernel,
            f"relay_slot{slot}",
            [shape((STATE, per_group), BF16)],
            operands,
            [WHOLE] * len(operands),
            scratch=scratch,
        )
        slots.append(onward(passed, max(0, slot - groups)))
        if fulls is None:
            gated, c_out, *fulls = call(
                functools.partial(first_rows_kernel, groups),
                "first_rows",
                [
                    shape((rows, width), F32),
                    shape((rows, groups * STATE), BF16),
                    *(shape((STATE, per_group), BF16) for _ in range(groups)),
                ],
                [
                    slots[0], partial, weight, inside, conv_x_weight, conv_bc_weight, step, running,
                    wide_skip, begin, bcc, main, gate, *states,
                ],
                [WHOLE] * (13 + groups),
                scratch=[pltpu.VMEM((4, 16, CHUNK), F32)],
            )
    def norm(part, first, stop, where, out=None, token=False):
        got = slots[part + first : part + stop]
        operands = [gated, decay, c_out, norm_gain, flags, *got]
        specs = [WHOLE] * len(operands)
        outs = [shape((rows, width), BF16)] + [shape((8, 128), F32)] * token
        aliases = {}
        if out is not None:
            aliases = {len(operands): 0}
            operands.append(out)
            specs.append(UNTOUCHED)
        return call(
            functools.partial(norm_kernel, part, len(got), first, where, out is not None),
            f"norm_part{part}_{where}",
            outs,
            operands,
            specs,
            out_specs=[UNTOUCHED] + [WHOLE] * token,
            scratch=[
                pltpu.VMEM((rows, per_group), F32),
                pltpu.VMEM((rows, per_group), BF16),
                pltpu.SemaphoreType.DMA((per_group // CHUNK,)),
            ],
            aliases=aliases,
            flops=KERNEL_FLOPS // 2,
        )

    mamba_out, token = None, c_out
    for part in range(groups - 1):
        mamba_out, token = norm(part, 0, 1, "odd", mamba_out, True)
    *carry, kv_on = call(
        near_kernel,
        "attend_near",
        carried,
        [queries, kvs[1], begin, *carry, token],
        [WHOLE] * 6 + [UNTOUCHED],
    )
    for hop in range(1, hops):
        kvs.append(onward(kv_on if hop == 1 else kvs[-1], hop))
    (attn_out,) = call(
        functools.partial(far_kernel, hops),
        "attend_far",
        [shape(queries.shape, BF16)],
        [queries, begin, *carry, *reversed(kvs[2:])],
        [WHOLE] * (4 + hops),
        out_specs=[UNTOUCHED],
        scratch=[
            pltpu.VMEM(queries.shape, BF16),
            pltpu.SemaphoreType.DMA((keys.shape[1] // ADIM,)),
        ],
    )
    for part in range(groups - 1):
        (mamba_out,) = norm(part, 0, hops, "rest", mamba_out)
    (mamba_out,) = norm(groups - 1, 0, 1, "first", mamba_out)
    (mamba_out,) = norm(groups - 1, 1, hops, "later", mamba_out)
    return (mamba_out, attn_out)


def solution(mesh):
    split = P(("groups", "seq"), "dp")
    placed = (
        split,
        split,
        split,
        split,
        P(None, "dp"),
        P("dp"),
        P(None, "dp"),
        P("dp"),
        P("dp"),
        P("dp"),
        P("dp"),
        P("dp"),
        split,
        split,
        split,
        P("groups"),
    )
    return jax.shard_map(
        shards,
        mesh=mesh,
        in_specs=placed,
        out_specs=(split, split),
        check_vma=False,
    )
```
